128 devices in a mesh: dp: 32 (over y_lo, x, z), tensor: 4 (over y_hi, core).
Axes of the slice: x: 4, y: 4 (y_hi: 2, y_lo: 2; y = y_hi * 2 + y_lo), z: 4, core: 2. Of those that a mesh axis runs over, the one named last changes fastest.
Arguments:
- hidden_in: bfloat16 [16384, 2048], P(('dp', 'tensor')), may hold values from -6 to 6
- cotangent: bfloat16 [16384, 2048], P(('dp', 'tensor')), may hold values from -11 to 11
- doc_lengths: int32 [32, 4], P('dp'), may hold values from 0 to 512, as said below
- attn_weights: float32 [4, 2048, 2048], P(None, 'dp', 'tensor'), may hold values from -2 to 2
- attn_first: float32 [4, 2048, 2048], P(None, 'dp', 'tensor'), may hold values from -80 to 80
- attn_second: float32 [4, 2048, 2048], P(None, 'dp', 'tensor'), may hold values from 425.984 to 6881.28
- mlp_weights: float32 [3, 2048, 8192], P(None, 'dp', 'tensor'), may hold values from -2 to 2
- mlp_first: float32 [3, 2048, 8192], P(None, 'dp', 'tensor'), may hold values from -80 to 80
- mlp_second: float32 [3, 2048, 8192], P(None, 'dp', 'tensor'), may hold values from 425.984 to 6881.28
- gains: float32 [4, 2048], P(None, 'dp'), may hold values from 0.5 to 1.5
- gain_first: float32 [4, 2048], P(None, 'dp'), may hold values from -80 to 80
- gain_second: float32 [4, 2048], P(None, 'dp'), may hold values from 425.984 to 6881.28
Outputs:
- hidden_out: bfloat16 [16384, 2048], P(('dp', 'tensor'))
- input_grad: float32 [16384, 2048], P(('dp', 'tensor'))
- attn_grad: float32 [4, 2048, 2048], P(None, 'dp', 'tensor')
- attn_first_new: float32 [4, 2048, 2048], P(None, 'dp', 'tensor')
- attn_second_new: float32 [4, 2048, 2048], P(None, 'dp', 'tensor')
- attn_new: float32 [4, 2048, 2048], P(None, 'dp', 'tensor')
- mlp_grad: float32 [3, 2048, 8192], P(None, 'dp', 'tensor')
- mlp_first_new: float32 [3, 2048, 8192], P(None, 'dp', 'tensor')
- mlp_second_new: float32 [3, 2048, 8192], P(None, 'dp', 'tensor')
- mlp_new: float32 [3, 2048, 8192], P(None, 'dp', 'tensor')
- gain_grad: float32 [4, 2048], P(None, 'dp')
- gain_first_new: float32 [4, 2048], P(None, 'dp')
- gain_second_new: float32 [4, 2048], P(None, 'dp')
- gain_new: float32 [4, 2048], P(None, 'dp')
The draws below stay inside these ranges and needn't reach their ends.
Inputs may be any that keep to these rules, and one draw needn't show every extreme that they name: `doc_lengths`: each row sums to 512; lengths may be 0; the third document of each row starts within the first 128 tokens of its block and ends within the last 128; in some row it fills the whole block.
All inputs are finite; a program needn't handle non-finite values.
Results may differ from the reference program's by a relative error of at most 0.04.
Values may be sent and summed in bfloat16 or wider, within the bound.
A program may use at most 256 MiB of HBM per device.

```python
import math
import jax
import jax.numpy as jnp
from jax import lax

D = 2048
HEAD_DIM = 128
FF = 8192
TOK_DEV = 128
STEP = 10
TOKENS = 16384
N_DP = 32
N_TENSOR = 4


def draw_doc_lengths(key, part):
    key = jax.random.fold_in(key, 5)
    streams = jax.random.split(key, 4)
    group_size = TOK_DEV * N_TENSOR
    leading = jax.random.randint(streams[0], (N_DP,), 0, TOK_DEV)
    trailing = jax.random.randint(streams[1], (N_DP,), 0, TOK_DEV)
    chosen = jax.random.randint(streams[2], (), 0, N_DP)
    single = jnp.arange(N_DP) == chosen
    leading = jnp.where(single, 0, leading)
    trailing = jnp.where(single, 0, trailing)
    first_doc = jax.random.randint(streams[3], (N_DP,), 0, leading + 1)
    second_doc = leading - first_doc
    middle_doc = group_size - leading - trailing
    return jnp.stack([first_doc, second_doc, middle_doc, trailing], axis=1).astype(jnp.int32)


def draw_attn_weights(key, part):
    key = jax.random.fold_in(key, 7)
    column = jnp.arange(D, dtype=jnp.float32) / D - 0.5
    entries = jnp.clip(jax.random.normal(key, (4, D, D), jnp.float32), -6.0, 6.0)
    growth = 3.0
    tilt = growth ** (0.667 * column)
    chosen = (jnp.arange(4) < 2)[:, None, None]
    factor = jnp.where(chosen, tilt[None, None, :], 1.0)
    return entries * factor * D ** (-0.5)


def draw_mlp_weights(key, part):
    key = jax.random.fold_in(key, 9)
    entries = jnp.clip(jax.random.normal(key, (3, D, FF), jnp.float32), -6.0, 6.0)
    factor = jnp.array([D ** (-0.5), D ** (-0.5), FF ** (-0.5)], jnp.float32)
    return entries * factor[:, None, None]


def draw_cotangent(key, part):
    key = jax.random.fold_in(key, 3)
    row_place = jnp.arange(TOKENS, dtype=jnp.float32) / TOKENS - 0.5
    entries = jnp.clip(jax.random.normal(key, (TOKENS, D), jnp.float32), -6.0, 6.0)
    growth = 3.0
    return (entries * (growth ** row_place)[:, None]).astype(jnp.bfloat16)


def level_of(own_key, dims, shards, least, high):
    gain = 1.0
    for position, shards_of in shards:
        heights = jax.random.uniform(jax.random.fold_in(jax.random.fold_in(own_key, 6), position), (shards_of,), jnp.float32, least / len(shards), high / len(shards))
        gain = gain * jnp.repeat(jnp.exp(heights), dims[position] // shards_of).reshape((-1,) + (1,) * (len(dims) - 1 - position))
    return gain


def scatter_about(key, dims, spread, reach, pieces=(), held_as=jnp.bfloat16):
    loudness = level_of(key, dims, pieces, -0.22, 0.18) if pieces else 1.0
    values = jax.random.normal(key, dims, jnp.float32) * spread * loudness
    return jnp.minimum(jnp.maximum(values, -reach), reach).astype(held_as)


def setup_inputs(seed: int = 0) -> dict:
    splits = jax.random.split(jax.random.key(seed), 13)
    return {
        "hidden_in": scatter_about(splits[0], (TOKENS, D), 1.0, 6.0, ((0, 128),)),
        "cotangent": draw_cotangent(jax.random.fold_in(splits[12], 71), 0),
        "doc_lengths": draw_doc_lengths(jax.random.fold_in(splits[12], 71), 0),
        "attn_weights": draw_attn_weights(jax.random.fold_in(splits[12], 71), 0),
        "attn_first": scatter_about(splits[4], (4, D, D), (0.11 * TOKENS ** 0.5), 80.0, ((1, 32), (2, 4)), jnp.float32),
        "attn_second": jnp.clip(jnp.exp(math.log(6881.28) - 2.7821581 * jax.random.uniform(splits[5], (4, D, D), jnp.float32) ** level_of(splits[5], (4, D, D), ((1, 32), (2, 4)), -0.2, 0.2)), 425.984, 6881.28),
        "mlp_weights": draw_mlp_weights(jax.random.fold_in(splits[12], 71), 0),
        "mlp_first": scatter_about(splits[7], (3, D, FF), (0.11 * TOKENS ** 0.5), 80.0, ((1, 32), (2, 4)), jnp.float32),
        "mlp_second": jnp.clip(jnp.exp(math.log(6881.28) - 2.7821581 * jax.random.uniform(splits[8], (3, D, FF), jnp.float32) ** level_of(splits[8], (3, D, FF), ((1, 32), (2, 4)), -0.2, 0.2)), 425.984, 6881.28),
        "gains": jnp.clip(1.0 + 0.1 * jax.random.normal(splits[9], (4, D), jnp.float32), 0.5, 1.5),
        "gain_first": scatter_about(splits[10], (4, D), (0.11 * TOKENS ** 0.5), 80.0, ((1, 32),), jnp.float32),
        "gain_second": jnp.clip(jnp.exp(math.log(6881.28) - 2.7821581 * jax.random.uniform(splits[11], (4, D), jnp.float32) ** level_of(splits[11], (4, D), ((1, 32),), -0.2, 0.2)), 425.984, 6881.28),
    }


@jax.custom_vjp
def low(v):
    return lax.optimization_barrier(v.astype(jnp.bfloat16)).astype(jnp.float32)

@jax.custom_vjp
def low_back(v):
    return v

def low_keep(v):
    return (low(v), None)

def low_pass(kept, grad):
    return (grad,)

def back_keep(v):
    return (v, None)

def back_low(kept, grad):
    return (low(grad),)
low.defvjp(low_keep, low_pass)
low_back.defvjp(back_keep, back_low)
NORM_EPS = 1e-06
ROPE_BASE = 500000.0
BETA_ONE = 0.9
BETA_TWO = 0.95
ADAM_EPS = 1e-08
WEIGHT_RATE = 0.03
GAIN_RATE = 1.0
WEIGHT_DECAY = 0.1
HIGHEST = lax.Precision.HIGHEST

def exact_dot(left, right):
    return jnp.dot(left, right, precision=HIGHEST)

def norm_scale(values):
    return lax.rsqrt(lax.optimization_barrier(jnp.mean(values * values, axis=-1, keepdims=True)) + NORM_EPS)

def doc_layout(lengths, group_size):
    positions = jnp.arange(group_size, dtype=jnp.int32)
    doc_ends = jnp.cumsum(lengths).astype(jnp.int32)
    passed = (positions[:, None] >= doc_ends[None, :]).astype(jnp.int32)
    segment = lax.optimization_barrier(jnp.sum(passed, axis=-1))
    begins = lax.optimization_barrier(jnp.sum(passed * lengths[None, :], axis=-1))
    return (segment, positions - begins)

def rope_tables(offsets):
    frequency = ROPE_BASE ** (-jnp.arange(0, HEAD_DIM, 2).astype(jnp.float32) / HEAD_DIM)
    angles = offsets.astype(jnp.float32)[:, None] * frequency[None, :]
    angles = jnp.concatenate([angles, angles], axis=-1)
    return (jnp.cos(angles)[:, None, :], jnp.sin(angles)[:, None, :])

def half_turn(values):
    middle = values.shape[-1] // 2
    return jnp.concatenate([-values[..., middle:], values[..., :middle]], axis=-1)

def rotate(values, cosine_table, sine_table):
    return values * cosine_table + half_turn(values) * sine_table

def layer(inputs, attn_all, mlp_all, gain_all, lengths):
    group_size, model_width = inputs.shape
    head_count = model_width // HEAD_DIM
    attn_low = low(attn_all)
    mlp_low = low(mlp_all)
    gain_low = low(gain_all)
    queries = low_back(exact_dot(inputs, attn_low[0]))
    key_raw = low_back(exact_dot(inputs, attn_low[1]))
    value_side = low(low_back(exact_dot(inputs, attn_low[2])))
    query_norm = queries * norm_scale(queries) * gain_low[0]
    key_norm = key_raw * norm_scale(key_raw) * gain_low[1]
    segment, offsets = doc_layout(lengths, group_size)
    cosine_table, sine_table = rope_tables(offsets)
    query_rot = low(rotate(query_norm.reshape(group_size, head_count, HEAD_DIM), cosine_table, sine_table))
    key_rot = low(rotate(key_norm.reshape(group_size, head_count, HEAD_DIM), cosine_table, sine_table))
    raw_scores = low_back(jnp.einsum('qhd,khd->hqk', query_rot, key_rot, precision=HIGHEST))
    positions = jnp.arange(group_size)
    allowed = (segment[:, None] == segment[None, :]) & (positions[None, :] <= positions[:, None])
    scores = jnp.where(allowed[None], raw_scores * HEAD_DIM ** (-0.5), -1e+30)
    attn_probs = low(jax.nn.softmax(scores, axis=-1))
    attended = jnp.einsum('hqk,khd->qhd', attn_probs, value_side.reshape(group_size, head_count, HEAD_DIM), precision=HIGHEST)
    attended = low(low_back(attended.reshape(group_size, model_width)))
    attn_proj = low_back(jnp.einsum('qf,of->qo', attended, attn_low[3], precision=HIGHEST))
    mixed = inputs + attn_proj * norm_scale(attn_proj) * gain_low[2]
    mixed_low = low(mixed)
    gate_proj = low_back(exact_dot(mixed_low, mlp_low[0]))
    up_proj = low_back(exact_dot(mixed_low, mlp_low[1]))
    hidden_act = low(jax.nn.silu(gate_proj) * up_proj)
    down_proj = low_back(jnp.einsum('qf,of->qo', hidden_act, mlp_low[2], precision=HIGHEST))
    return mixed + down_proj * norm_scale(down_proj) * gain_low[3]

def adam_update(weights_old, first_old, second_old, gradient, rate, decay):
    first_new = BETA_ONE * first_old + (1.0 - BETA_ONE) * gradient
    second_new = BETA_TWO * second_old + (1.0 - BETA_TWO) * gradient * gradient
    ratio = first_new / (1.0 - BETA_ONE ** STEP) / (jnp.sqrt(second_new / (1.0 - BETA_TWO ** STEP)) + ADAM_EPS)
    return (first_new, second_new, weights_old - rate * (ratio + decay * weights_old))

def reference(hidden_in, cotangent, doc_lengths, attn_weights, attn_first, attn_second, mlp_weights, mlp_first, mlp_second, gains, gain_first, gain_second):
    group_size = TOK_DEV * N_TENSOR
    model_width = hidden_in.shape[1]
    block_count = hidden_in.shape[0] // group_size
    inputs = hidden_in.astype(jnp.float32).reshape(block_count, group_size, model_width)
    upstream = cotangent.astype(jnp.float32).reshape(block_count, group_size, model_width)

    def one_block(totals, item):
        block_in, block_back, lengths = item

        def forward(inside, attn_all, mlp_all, gain_all):
            return layer(inside, attn_all, mlp_all, gain_all, lengths)
        output, pullback = jax.vjp(forward, block_in, attn_weights, mlp_weights, gains)
        d_input, d_attn, d_mlp, d_gain = pullback(block_back)
        totals = (totals[0] + d_attn, totals[1] + d_mlp, totals[2] + d_gain)
        return (totals, (output, d_input))
    zeros = (jnp.zeros_like(attn_weights), jnp.zeros_like(mlp_weights), jnp.zeros_like(gains))
    totals, (outputs, d_inputs) = lax.scan(one_block, zeros, (inputs, upstream, doc_lengths))
    attn_grad, mlp_grad, gain_grad = totals
    attn_first_new, attn_second_new, attn_new = adam_update(attn_weights, attn_first, attn_second, attn_grad, WEIGHT_RATE, WEIGHT_DECAY)
    mlp_first_new, mlp_second_new, mlp_new = adam_update(mlp_weights, mlp_first, mlp_second, mlp_grad, WEIGHT_RATE, WEIGHT_DECAY)
    gain_first_new, gain_second_new, gain_new = adam_update(gains, gain_first, gain_second, gain_grad, GAIN_RATE, 0.0)
    hidden_out = outputs.reshape(-1, model_width).astype(jnp.bfloat16)
    input_grad = d_inputs.reshape(-1, model_width)
    return (hidden_out, input_grad, attn_grad, attn_first_new, attn_second_new, attn_new, mlp_grad, mlp_first_new, mlp_second_new, mlp_new, gain_grad, gain_first_new, gain_second_new, gain_new)
```

```python
import functools

import jax
import jax.numpy as jnp
from jax import lax
from jax.experimental import pallas as pl
from jax.experimental.pallas import tpu as pltpu
from jax.sharding import Mesh
from jax.sharding import PartitionSpec as P

HEAD_DIM = 128
STEP = 10
DP = ("yl", "x", "z")
TENSOR = ("yh", "c")
EVERY = ("yl", "x", "z", "yh", "c")
RING = 4
MESH = pl.DeviceIdType.MESH

NORM_EPS = 1e-06
ROPE_BASE = 500000.0
BETA_ONE = 0.9
BETA_TWO = 0.95
ADAM_EPS = 1e-08
WEIGHT_RATE = 0.03
GAIN_RATE = 1.0
WEIGHT_DECAY = 0.1

BF16 = jnp.bfloat16
F32 = jnp.float32
IN_VMEM = pl.BlockSpec(memory_space=pltpu.VMEM)
ANYWHERE = pl.BlockSpec(memory_space=pl.ANY)
VMEM_LIMIT = 56 * 1024 * 1024


class Place:
    def __init__(self):
        self.x, self.z, self.c = (lax.axis_index(a) for a in ("x", "z", "c"))
        self.yl, self.yh = (lax.axis_index(a) for a in ("yl", "yh"))
        self.y = self.yh * 2 + self.yl

    def at(self, axis, step):
        if axis == "y":
            there = (self.y + step + RING) % RING
            return {"yl": there % 2, "yh": there // 2}
        if axis == "c":
            return {"c": 1 - self.c}
        return {axis: (getattr(self, axis) + step + RING) % RING}

    def shift(self, axis, step):
        return (getattr(self, axis) + step + RING) % RING


def greet(devices):
    barrier = pltpu.get_barrier_semaphore()
    for device in devices:
        pl.semaphore_signal(barrier, inc=1, device_id=device, device_id_type=MESH)
    pl.semaphore_wait(barrier, len(devices))


def greet_all(place, axes):
    devices = []
    for axis in axes:
        devices += [place.at(axis, 1)] if axis == "c" else [place.at(axis, 1), place.at(axis, -1)]
    greet(devices)


class Sender:
    def __init__(self, sems):
        self.sems, self.open = sems, []

    def push(self, src, dst, recv_sem, device):
        copy = pltpu.make_async_remote_copy(
            src_ref=src,
            dst_ref=dst,
            send_sem=self.sems.at[len(self.open)],
            recv_sem=recv_sem,
            device_id=device,
            device_id_type=MESH,
        )
        copy.start()
        self.open.append(copy.wait_send)

    def keep(self, src, dst):
        copy = pltpu.make_async_copy(src, dst, self.sems.at[len(self.open)])
        copy.start()
        self.open.append(copy.wait)

    def keep_first(self, src, dst):
        copy = pltpu.make_async_copy(src, dst, self.sems.at[len(self.open)])
        copy.start()
        self.open.append(lambda: None)
        return copy

    def arrived(self, dst, recv_sem, device):
        pltpu.make_async_remote_copy(
            src_ref=dst,
            dst_ref=dst,
            send_sem=self.sems.at[0],
            recv_sem=recv_sem,
            device_id=device,
            device_id_type=MESH,
        ).wait_recv()

    def finish(self):
        for wait in self.open:
            wait()


def take_turns(tasks):
    tasks = list(tasks)
    while tasks:
        for task in list(tasks):
            if next(task, "done") == "done":
                tasks.remove(task)


WHOLE, LOW, HIGH = 0, 1, 2


def part_of(ref, part, cut):
    rows = ref.shape[-2]
    if part == WHOLE:
        return ref
    return ref.at[pl.ds(0, cut)] if part == LOW else ref.at[pl.ds(cut, rows - cut)]


def plane_gather(place, sender, sems, out, cut):
    rows = out.shape[-2]
    axes = (("x", "z"), ("z", "x"))

    def piece(half, dp, dq):
        p, q = (place.shift(a, d) for a, d in zip(axes[half], (dp, dq)))
        return out.at[half, p, q] if half == 0 else out.at[half, q, p]

    def parts(part):
        if part == WHOLE:
            return True
        return cut > 0 if part == LOW else cut < rows

    def send(half, dp, dq, part, along, step):
        if parts(part):
            ref = part_of(piece(half, dp, dq), part, cut)
            sp, sq = ((dp - step) % RING, dq % RING) if along == 0 else (dp % RING, (dq - step) % RING)
            sender.push(ref, ref, sems.at[half, sp, sq, part], place.at(axes[half][along], step))

    def wait(half, dp, dq, part):
        if parts(part):
            ref = part_of(piece(half, dp, dq), part, cut)
            sender.arrived(ref, sems.at[half, dp % RING, dq % RING, part], place.at("x", 1))

    both = (0, 1)
    for half in both:
        for step in (1, -1):
            send(half, 0, 0, WHOLE, 0, step)
    for half in both:
        for step in (1, -1):
            send(half, 0, 0, WHOLE, 1, step)
    yield
    for step, part in ((1, LOW), (-1, HIGH)):
        for half in both:
            wait(half, -step, 0, WHOLE)
            send(half, -step, 0, part, 0, step)
            for side in (1, -1):
                send(half, -step, 0, WHOLE, 1, side)
    yield
    for half in both:
        for step, part in ((1, LOW), (-1, HIGH)):
            wait(half, 0, -step, WHOLE)
            send(half, 0, -step, part, 1, step)
    yield
    for half in both:
        wait(half, 2, 0, LOW)
        wait(half, 2, 0, HIGH)
        for side in (1, -1):
            send(half, 2, 0, WHOLE, 1, side)
    yield
    for dp in (-1, 1, 2):
        for half in both:
            for step, part in ((1, LOW), (-1, HIGH)):
                wait(half, dp, -step, WHOLE)
                send(half, dp, -step, part, 1, step)
        yield
    for dp in (0, -1, 1, 2):
        for half in both:
            wait(half, dp, 2, LOW)
            wait(half, dp, 2, HIGH)


def ring_gather(place, sender, sems, own, out):
    rows = own.shape[0]
    cut = rows // 2

    def piece(dy, core):
        y = place.shift("y", dy)
        return out.at[y % 2, y // 2, core]

    other = place.at("c", 1)
    sender.keep(own, piece(0, place.c))
    for step in (1, -1):
        sender.push(own, piece(0, place.c), sems.at[(-step) % RING, WHOLE], place.at("y", step))
    sender.push(own, piece(0, place.c), sems.at[0, 3], other)
    yield
    for step, part in ((1, LOW), (-1, HIGH)):
        ref = piece(-step, place.c)
        sender.arrived(ref, sems.at[(-step) % RING, WHOLE], other)
        half = part_of(ref, part, cut)
        sender.push(half, half, sems.at[2, part], place.at("y", step))
        sender.push(ref, ref, sems.at[(-step) % RING, 3], other)
    yield
    ref = piece(2, place.c)
    for part in (LOW, HIGH):
        sender.arrived(part_of(ref, part, cut), sems.at[2, part], other)
    sender.push(ref, ref, sems.at[2, 3], other)
    yield
    for dy in (0, 1, -1, 2):
        sender.arrived(piece(dy, 1 - place.c), sems.at[dy % RING, 3], other)


def add_rows(out, terms, rows):
    def step(i, carry):
        window = pl.ds(pl.multiple_of(i * 16, 16), 16)
        total = terms[0][window, :].astype(F32)
        for term in terms[1:]:
            total = total + term[window, :].astype(F32)
        out[window, :] = total.astype(out.dtype)
        return carry

    lax.fori_loop(0, rows // 16, step, 0)


def ring_scatter(place, sender, sems, partial, out, kept, from_core, hop, last):
    rows = out.shape[0]
    cut = rows // 2
    low, high = pl.ds(0, cut), pl.ds(cut, cut)
    other = place.at("c", 1)

    def mine(dy, core):
        y = place.shift("y", dy)
        return partial.at[y % 2, y // 2, core]

    for dy in (2, 1, -1, 0):
        sender.push(mine(dy, 1 - place.c), from_core.at[dy % RING], sems.at[0, dy % RING], other)
    yield
    sender.arrived(from_core.at[2], sems.at[0, 2], other)
    add_rows(kept.at[2], (mine(2, place.c), from_core.at[2]), rows)
    sender.push(kept.at[2, low], hop.at[0], sems.at[1, 0], place.at("y", 1))
    sender.push(kept.at[2, high], hop.at[1], sems.at[1, 1], place.at("y", -1))
    for step in (1, -1):
        sender.arrived(from_core.at[step % RING], sems.at[0, step % RING], other)
        add_rows(kept.at[step % RING], (mine(step, place.c), from_core.at[step % RING]), rows)
        if step == 1:
            sender.push(kept.at[1, high], last.at[0, high], sems.at[2, 1], place.at("y", 1))
        else:
            sender.push(kept.at[3, low], last.at[1, low], sems.at[2, 2], place.at("y", -1))
    sender.arrived(from_core.at[0], sems.at[0, 0], other)
    yield
    sender.arrived(hop.at[0], sems.at[1, 0], other)
    add_rows(kept.at[1, low], (kept.at[1, low], hop.at[0]), cut)
    sender.push(kept.at[1, low], last.at[0, low], sems.at[2, 0], place.at("y", 1))
    sender.arrived(hop.at[1], sems.at[1, 1], other)
    add_rows(kept.at[3, high], (kept.at[3, high], hop.at[1]), cut)
    sender.push(kept.at[3, high], last.at[1, high], sems.at[2, 3], place.at("y", -1))
    yield
    sender.arrived(last.at[0, low], sems.at[2, 0], other)
    sender.arrived(last.at[0, high], sems.at[2, 1], other)
    sender.arrived(last.at[1, low], sems.at[2, 2], other)
    sender.arrived(last.at[1, high], sems.at[2, 3], other)
    add_rows(out, (mine(0, place.c), from_core.at[0], last.at[0], last.at[1]), rows)


def plane_scatter(place, sender, sems, partial, done, cut, bufs):
    rows = partial.shape[-2]
    hop, send_on, last, middle, hop2, send_on2, last2 = bufs
    low, high = pl.ds(0, cut), pl.ds(cut, rows - cut)
    axes = (("z", "x"), ("x", "z"))
    two_parts = cut < rows
    both = (0, 1)
    other = place.at("x", 1)

    def row(half, du, window):
        u = place.shift(axes[half][0], du)
        return partial.at[half, :, u, window] if half == 0 else partial.at[half, u, :, window]

    def line(half, du, v):
        u = place.shift(axes[half][0], du)
        return partial.at[half, v, u] if half == 0 else partial.at[half, u, v]

    def add(out, terms, count):
        if count % 16:
            total = terms[0][...].astype(F32)
            for term in terms[1:]:
                total = total + term[...].astype(F32)
            out[...] = total.astype(out.dtype)
        else:
            add_rows(out, terms, count)

    for half in both:
        u = axes[half][0]
        sender.push(row(half, 2, low), hop.at[half, 0, :, low], sems.at[half, 0], place.at(u, 1))
        if two_parts:
            sender.push(row(half, 2, high), hop.at[half, 1, :, high], sems.at[half, 1], place.at(u, -1))
    for half in both:
        u = axes[half][0]
        if two_parts:
            sender.push(row(half, 1, high), last.at[half, 0, :, high], sems.at[half, 2], place.at(u, 1))
        sender.push(row(half, -1, low), last.at[half, 1, :, low], sems.at[half, 3], place.at(u, -1))
    yield
    for half in both:
        u = axes[half][0]
        sender.arrived(hop.at[half, 0, :, low], sems.at[half, 0], other)
        for v in range(RING):
            add(send_on.at[half, 0, v, low], (line(half, 1, v).at[low], hop.at[half, 0, v, low]), cut)
        sender.push(send_on.at[half, 0, :, low], last.at[half, 0, :, low], sems.at[half, 4], place.at(u, 1))
        if two_parts:
            sender.arrived(hop.at[half, 1, :, high], sems.at[half, 1], other)
            for v in range(RING):
                add(
                    send_on.at[half, 1, v, high],
                    (line(half, -1, v).at[high], hop.at[half, 1, v, high]),
                    rows - cut,
                )
            sender.push(
                send_on.at[half, 1, :, high], last.at[half, 1, :, high], sems.at[half, 5], place.at(u, -1)
            )
    yield
    for half in both:
        v_axis = axes[half][1]
        if two_parts:
            sender.arrived(last.at[half, 0, :, high], sems.at[half, 2], other)
        sender.arrived(last.at[half, 1, :, low], sems.at[half, 3], other)
        sender.arrived(last.at[half, 0, :, low], sems.at[half, 4], other)
        if two_parts:
            sender.arrived(last.at[half, 1, :, high], sems.at[half, 5], other)
        for dv in (2, 1, -1, 0):
            v = place.shift(v_axis, dv)
            terms = (line(half, 0, v), last.at[half, 0, v], last.at[half, 1, v])
            add(middle.at[half, dv % RING], terms, rows)
            if dv == 2:
                sender.push(
                    middle.at[half, 2, low], hop2.at[half, 0, low], sems.at[half, 6], place.at(v_axis, 1)
                )
                if two_parts:
                    sender.push(
                        middle.at[half, 2, high],
                        hop2.at[half, 1, high],
                        sems.at[half, 7],
                        place.at(v_axis, -1),
                    )
            elif dv == 1 and two_parts:
                sender.push(
                    middle.at[half, 1, high], last2.at[half, 0, high], sems.at[half, 8], place.at(v_axis, 1)
                )
            elif dv == -1:
                sender.push(
                    middle.at[half, 3, low], last2.at[half, 1, low], sems.at[half, 9], place.at(v_axis, -1)
                )
    yield
    for half in both:
        v_axis = axes[half][1]
        sender.arrived(hop2.at[half, 0, low], sems.at[half, 6], other)
        add(send_on2.at[half, 0, low], (middle.at[half, 1, low], hop2.at[half, 0, low]), cut)
        sender.push(
            send_on2.at[half, 0, low], last2.at[half, 0, low], sems.at[half, 10], place.at(v_axis, 1)
        )
        if two_parts:
            sender.arrived(hop2.at[half, 1, high], sems.at[half, 7], other)
            add(send_on2.at[half, 1, high], (middle.at[half, 3, high], hop2.at[half, 1, high]), rows - cut)
            sender.push(
                send_on2.at[half, 1, high], last2.at[half, 1, high], sems.at[half, 11], place.at(v_axis, -1)
            )
    yield
    for half in both:
        if two_parts:
            sender.arrived(last2.at[half, 0, high], sems.at[half, 8], other)
        sender.arrived(last2.at[half, 1, low], sems.at[half, 9], other)
        sender.arrived(last2.at[half, 0, low], sems.at[half, 10], other)
        if two_parts:
            sender.arrived(last2.at[half, 1, high], sems.at[half, 11], other)
        add(done.at[half], (middle.at[half, 0], last2.at[half, 0], last2.at[half, 1]), rows)


def scatter_buffers(rows, columns, dtype):
    line = (2, 2, RING, rows, columns)
    one = (2, 2, rows, columns)
    return [
        pltpu.VMEM(line, dtype),
        pltpu.VMEM(line, dtype),
        pltpu.VMEM(line, dtype),
        pltpu.VMEM((2, RING, rows, columns), dtype),
        pltpu.VMEM(one, dtype),
        pltpu.VMEM(one, dtype),
        pltpu.VMEM(one, dtype),
    ]


def ring_buffers(rows, columns):
    return [
        pltpu.VMEM((RING, rows, columns), BF16),
        pltpu.VMEM((RING, rows, columns), BF16),
        pltpu.VMEM((2, rows // 2, columns), BF16),
        pltpu.VMEM((2, rows, columns), BF16),
    ]


def dma_sems(*shape):
    return pltpu.SemaphoreType.DMA(shape)


def shape_of(*shape, dtype=BF16):
    return jax.ShapeDtypeStruct(shape, dtype)


def call(kernel, number, out_shape, in_specs, out_specs, scratch, args):
    return pl.pallas_call(
        kernel,
        out_shape=out_shape,
        in_specs=in_specs,
        out_specs=out_specs,
        scratch_shapes=scratch,
        compiler_params=pltpu.CompilerParams(
            collective_id=number, has_side_effects=True, vmem_limit_bytes=VMEM_LIMIT
        ),
    )(*args)


def first_kernel(hidden, attn, mlp, gain, doc, hidden_all, attn_all, mlp_pair, gain_all, doc_pair, sends, ring, plane, plane_gain, swap):
    place = Place()
    greet_all(place, ("x", "z", "y", "c"))
    sender = Sender(sends)
    partner = {"yl": 1 - place.yl}
    me, you = place.yl, 1 - place.yl
    own_attn = attn_all.at[:, place.x, place.z]
    own_gain = gain_all.at[:, place.x, place.z]
    sender.push(attn.at[you], own_attn.at[me], swap.at[0], partner)
    sender.push(gain, own_gain.at[me], swap.at[1], partner)
    first = sender.keep_first(attn.at[me], own_attn.at[me])
    second = sender.keep_first(gain, own_gain.at[me])
    gather = ring_gather(place, sender, ring, hidden, hidden_all)
    next(gather)
    first.wait()
    second.wait()
    sender.arrived(own_attn.at[you], swap.at[0], partner)
    sender.arrived(own_gain.at[you], swap.at[1], partner)
    planes = plane_gather(place, sender, plane, attn_all, attn_all.shape[-2] // 2)
    gains = plane_gather(place, sender, plane_gain, gain_all, gain_all.shape[-2])
    next(planes)
    next(gains)
    sender.push(mlp.at[:, you], mlp_pair.at[:, me], swap.at[2], partner)
    sender.push(doc, doc_pair.at[me], swap.at[3], partner)
    sender.keep(mlp.at[:, me], mlp_pair.at[:, me])
    sender.keep(doc, doc_pair.at[me])
    take_turns((gains, planes, gather))
    sender.arrived(mlp_pair.at[:, you], swap.at[2], partner)
    sender.arrived(doc_pair.at[you], swap.at[3], partner)
    sender.finish()


def sums_kernel(own, total, slots, sends, recvs):
    place = Place()
    peers = [(dy, dc) for dy in (0, 1, 3, 2) for dc in (0, 1) if dy or dc]

    def device(dy, dc):
        y = place.shift("y", dy)
        return {"yl": y % 2, "yh": y // 2, "c": (place.c + dc) % 2}

    greet([device(*peer) for peer in peers])
    sender = Sender(sends)
    for dy, dc in peers:
        slot = ((RING - dy) % RING) * 2 + dc
        sender.push(own, slots.at[slot], recvs.at[slot], device(dy, dc))
    for dy, dc in peers:
        slot = dy * 2 + dc
        sender.arrived(slots.at[slot], recvs.at[slot], device(dy, dc))
    subtotal = own[...]
    for dy, dc in peers:
        subtotal = subtotal + slots[dy * 2 + dc]
    total[...] = subtotal
    sender.finish()


def sum_over_eight(own, number):
    return call(
        sums_kernel,
        number,
        shape_of(*own.shape, dtype=F32),
        [IN_VMEM],
        IN_VMEM,
        [pltpu.VMEM((8, *own.shape), F32), dma_sems(8), dma_sems(8)],
        (own,),
    )


def scatter_and_gather_kernel(counts, *refs):
    refs = list(refs)

    def take(n):
        out = refs[:n]
        del refs[:n]
        return out

    (partial,), pairs, (out,), weights = take(1), take(counts), take(1), take(counts)
    (sends, ring), planes, buffers = take(2), take(counts), take(4)
    place = Place()
    greet_all(place, ("x", "z", "y", "c") if counts else ("y", "c"))
    sender = Sender(sends)
    started = [sender.keep_first(p, w.at[:, place.x, place.z]) for p, w in zip(pairs, weights)]
    task = ring_scatter(place, sender, ring, partial, out, *buffers)
    next(task)
    for copy in started:
        copy.wait()
    tasks = [
        plane_gather(place, sender, sems, w, w.shape[-2] // 2) for sems, w in zip(planes, weights)
    ]
    take_turns([*tasks, task])
    sender.finish()


def scatter_and_gather(partial, pairs, number):
    rows, columns = partial.shape[-2:]
    count = len(pairs)
    weights = [shape_of(2, RING, RING, *p.shape[-2:]) for p in pairs]
    out = call(
        functools.partial(scatter_and_gather_kernel, count),
        number,
        (shape_of(rows, columns, dtype=F32), *weights),
        [IN_VMEM] + [ANYWHERE] * count,
        (IN_VMEM, *[ANYWHERE] * count),
        [dma_sems(16 + 48 * count), dma_sems(3, RING)]
        + [dma_sems(2, RING, RING, 3)] * count
        + ring_buffers(rows, columns),
        (partial, *pairs),
    )
    return out[0], [flat(w) for w in out[1:]]


def gather_and_gather_kernel(counts, *refs):
    refs = list(refs)

    def take(n):
        out = refs[:n]
        del refs[:n]
        return out

    (own,), pairs, (out,), weights = take(1), take(counts), take(1), take(counts)
    (sends, ring), planes = take(2), take(counts)
    place = Place()
    greet_all(place, ("x", "z", "y", "c") if counts else ("y", "c"))
    sender = Sender(sends)
    started = [sender.keep_first(p, w.at[:, place.x, place.z]) for p, w in zip(pairs, weights)]
    task = ring_gather(place, sender, ring, own, out)
    next(task)
    for copy in started:
        copy.wait()
    tasks = [
        plane_gather(place, sender, sems, w, w.shape[-2] // 2) for sems, w in zip(planes, weights)
    ]
    take_turns([*tasks, task])
    sender.finish()


def gather_and_gather(own, pairs, number):
    rows, columns = own.shape
    count = len(pairs)
    weights = [shape_of(2, RING, RING, *p.shape[-2:]) for p in pairs]
    out = call(
        functools.partial(gather_and_gather_kernel, count),
        number,
        (shape_of(2, 2, 2, rows, columns), *weights),
        [ANYWHERE] * (1 + count),
        (ANYWHERE, *[ANYWHERE] * count),
        [dma_sems(16 + 48 * count), dma_sems(RING, 4)] + [dma_sems(2, RING, RING, 3)] * count,
        (own, *pairs),
    )
    return out[0].reshape(8 * rows, columns), [flat(w) for w in out[1:]]


def flat(weight):
    return weight.reshape(-1, weight.shape[-1])


def sums_of_gradients_kernel(mode, shapes, *refs):
    refs = list(refs)

    def take(n):
        out = refs[:n]
        del refs[:n]
        return out

    count = len(shapes)
    (own,), partials, (out,), sums = take(1), take(count), take(1), take(count)
    (sends, ring, swap), planes = take(3), take(count)
    done, buffers = take(count), [take(7) for _ in range(count)]
    place = Place()
    greet_all(place, ("x", "z", "y", "c"))
    sender = Sender(sends)
    if mode == "gather":
        task = ring_gather(place, sender, ring, own, out)
    else:
        task = ring_scatter(place, sender, ring, own, out, *take(4))
    next(task)
    tasks = []
    for k, (rows, _, dtype) in enumerate(shapes):
        cut = rows // 2 if dtype == BF16 else rows
        tasks.append(plane_scatter(place, sender, planes[k], partials[k], done[k], cut, buffers[k]))
    take_turns([*tasks, task])
    partner = {"yl": 1 - place.yl}
    me, you = place.yl, 1 - place.yl
    for k, (rows, _, dtype) in enumerate(shapes):
        if dtype == BF16:
            sender.push(done[k].at[you], sums[k].at[me], swap.at[k], partner)
            sender.keep(done[k].at[me], sums[k].at[me])
        else:
            sender.keep(done[k].at[me], sums[k])
    for k, (rows, _, dtype) in enumerate(shapes):
        if dtype == BF16:
            sender.arrived(sums[k].at[you], swap.at[k], partner)
    sender.finish()


def sums_of_gradients(mode, own, partials, number):
    rows, columns = own.shape[-2:]
    shapes = [(*p.shape[-2:], p.dtype) for p in partials]
    count = len(shapes)
    sums = [
        shape_of(2, r, c) if dtype == BF16 else shape_of(r, c, dtype=dtype) for r, c, dtype in shapes
    ]
    scratch = [dma_sems(20 + 30 * count), dma_sems(RING, 4), dma_sems(count)]
    scratch += [dma_sems(2, 12)] * count
    scratch += [pltpu.VMEM((2, r, c), dtype) for r, c, dtype in shapes]
    for shape in shapes:
        scratch += scatter_buffers(*shape)
    if mode == "gather":
        result, ring_spec = shape_of(2, 2, 2, rows, columns), ANYWHERE
    else:
        result, ring_spec = shape_of(rows, columns, dtype=F32), IN_VMEM
        scratch += ring_buffers(rows, columns)
    out = call(
        functools.partial(sums_of_gradients_kernel, mode, shapes),
        number,
        (result, *sums),
        [ring_spec] + [IN_VMEM] * count,
        (ring_spec, *[IN_VMEM] * count),
        scratch,
        (own, *partials),
    )
    first = out[0].reshape(8 * rows, columns) if mode == "gather" else out[0]
    return first, out[1:]


def norm_scale(values):
    return lax.rsqrt(jnp.mean(values * values, axis=-1, keepdims=True) + NORM_EPS)


def norm_back(upstream, values, scales, gain_row):
    scaled_grad = upstream * gain_row
    return scales * scaled_grad - values * scales**3 * jnp.mean(
        scaled_grad * values, axis=-1, keepdims=True
    )


def doc_layout(lengths, group_size):
    positions = jnp.arange(group_size, dtype=jnp.int32)
    doc_ends = jnp.cumsum(lengths)
    passed = (positions[:, None] >= doc_ends[None, :]).astype(jnp.int32)
    segment = jnp.sum(passed, axis=-1)
    begins = jnp.sum(passed * lengths[None, :], axis=-1)
    return (segment, positions - begins)


def rope_tables(offsets):
    frequency = ROPE_BASE ** (-jnp.arange(0, HEAD_DIM, 2).astype(jnp.float32) / HEAD_DIM)
    angles = offsets.astype(jnp.float32)[:, None] * frequency[None, :]
    cosine, sine = jnp.cos(angles), jnp.sin(angles)
    return (
        jnp.concatenate([cosine, cosine], axis=-1),
        jnp.concatenate([sine, sine], axis=-1),
    )


def half_turn(values):
    middle = values.shape[-1] // 2
    return jnp.concatenate([-values[..., middle:], values[..., :middle]], axis=-1)


def rotate(values, cosine_table, sine_table):
    return values * cosine_table + half_turn(values) * sine_table


def unrotate(values, cosine_table, sine_table):
    return values * cosine_table - half_turn(values) * sine_table


def product(left, right):
    return jnp.dot(left, right, preferred_element_type=F32)


def row_product(left, right):
    return lax.dot_general(left, right, (((1,), (1,)), ((), ())), preferred_element_type=F32)


def col_product(left, right):
    return lax.dot_general(left, right, (((0,), (0,)), ((), ())), preferred_element_type=F32)


def adam_update(weights_old, first_old, second_old, gradient, rate, decay):
    first_new = BETA_ONE * first_old + (1.0 - BETA_ONE) * gradient
    second_new = BETA_TWO * second_old + (1.0 - BETA_TWO) * gradient * gradient
    ratio = (
        first_new
        / (1.0 - BETA_ONE**STEP)
        / (jnp.sqrt(second_new / (1.0 - BETA_TWO**STEP)) + ADAM_EPS)
    )
    return (first_new, second_new, weights_old - rate * (ratio + decay * weights_old))


def body(
    hidden_in,
    cotangent,
    doc_lengths,
    attn_weights,
    attn_first,
    attn_second,
    mlp_weights,
    mlp_first,
    mlp_second,
    gains,
    gain_first,
    gain_second,
):
    row_count, model_width = hidden_in.shape
    shard_rows = attn_weights.shape[1]
    heads_width = attn_weights.shape[2] // 2
    hidden_width = mlp_weights.shape[2] // 2
    token_count = 8 * row_count
    block_rows = token_count // 2
    head_count = heads_width // HEAD_DIM
    score_factor = HEAD_DIM ** (-0.5)
    yl, yh, core = (lax.axis_index(a) for a in ("yl", "yh", "c"))

    attn_halves = (
        attn_weights.astype(BF16)
        .reshape(4, shard_rows, 2, heads_width)
        .transpose(2, 1, 0, 3)
        .reshape(2, shard_rows, 4 * heads_width)
    )
    mlp_halves = mlp_weights.astype(BF16).reshape(3, shard_rows, 2, hidden_width).transpose(0, 2, 1, 3)
    gain_tile = jnp.pad(gains.astype(BF16).astype(F32), ((0, 4), (0, 128 - shard_rows)))
    doc_tile = jnp.pad(doc_lengths.astype(F32), ((0, 7), (0, 124)))
    every_input, attn_all, mlp_pair, gain_all, doc_pair = call(
        first_kernel,
        0,
        (
            shape_of(2, 2, 2, row_count, model_width),
            shape_of(2, RING, RING, shard_rows, 4 * heads_width),
            shape_of(3, 2, shard_rows, hidden_width),
            shape_of(2, RING, RING, 8, 128, dtype=F32),
            shape_of(2, 8, 128, dtype=F32),
        ),
        [ANYWHERE] * 5,
        (ANYWHERE,) * 5,
        [
            dma_sems(112),
            dma_sems(RING, 4),
            dma_sems(2, RING, RING, 3),
            dma_sems(2, RING, RING, 3),
            dma_sems(4),
        ],
        (hidden_in, attn_halves, mlp_halves, gain_tile, doc_tile),
    )
    every_input = every_input.reshape(token_count, model_width)
    attn_all = flat(attn_all)
    qkv_weight, out_weight = attn_all[:, : 3 * heads_width], attn_all[:, 3 * heads_width :]
    gain_full = gain_all[..., :4, :shard_rows].transpose(3, 0, 1, 2, 4).reshape(4, model_width)
    lengths = doc_pair[:, 0, :4].astype(jnp.int32)

    qkv = product(every_input, qkv_weight)
    queries, key_raw = qkv[:, :heads_width], qkv[:, heads_width : 2 * heads_width]
    value_side = qkv[:, 2 * heads_width :].astype(BF16)
    squares = jnp.stack([jnp.sum(queries * queries, axis=-1), jnp.sum(key_raw * key_raw, axis=-1)])
    totals = sum_over_eight(squares.reshape(-1, 128), 1).reshape(2, token_count)
    scales = lax.rsqrt(totals / model_width + NORM_EPS)
    query_scale, key_scale = scales[0][:, None], scales[1][:, None]
    first_column = (yh * 2 + core) * (2 * heads_width) + yl * heads_width
    query_gain = lax.dynamic_slice_in_dim(gain_full[0], first_column, heads_width)
    key_gain = lax.dynamic_slice_in_dim(gain_full[1], first_column, heads_width)

    segment, offsets = jax.vmap(lambda one: doc_layout(one, block_rows))(lengths)
    cosine_table, sine_table = rope_tables(offsets.reshape(-1))
    cosine_table = cosine_table.reshape(2, block_rows, HEAD_DIM)
    sine_table = sine_table.reshape(2, block_rows, HEAD_DIM)
    positions = jnp.arange(block_rows)
    allowed = (segment[:, :, None] == segment[:, None, :]) & (
        positions[None, None, :] <= positions[None, :, None]
    )

    def by_head(values):
        return jnp.stack(
            [
                values[:, h * HEAD_DIM : (h + 1) * HEAD_DIM].reshape(2, block_rows, HEAD_DIM)
                for h in range(head_count)
            ]
        )

    def by_token(values):
        return jnp.concatenate([v.reshape(token_count, HEAD_DIM) for v in values], axis=-1)

    query_rot = rotate(by_head(queries * query_scale * query_gain), cosine_table, sine_table).astype(BF16)
    key_rot = rotate(by_head(key_raw * key_scale * key_gain), cosine_table, sine_table).astype(BF16)
    value_heads = by_head(value_side)

    def scores_of():
        raw = jnp.einsum("hbqd,hbkd->hbqk", query_rot, key_rot, preferred_element_type=F32)
        return jnp.where(allowed[None], raw * score_factor, -1e30)

    scores = scores_of()
    maxima = jnp.max(scores, axis=-1, keepdims=True)
    exponent = jnp.exp(scores - maxima)
    normaliser = jnp.sum(exponent, axis=-1, keepdims=True)
    probs_low = (exponent / normaliser).astype(BF16)
    log_totals = maxima + jnp.log(normaliser)
    attended = by_token(
        jnp.einsum("hbqk,hbkd->hbqd", probs_low, value_heads, preferred_element_type=F32).astype(BF16)
    )

    def for_ring(values):
        return values.astype(BF16).reshape(2, 2, 2, row_count, model_width)

    attn_proj, (gate_weight, down_weight) = scatter_and_gather(
        for_ring(row_product(attended, out_weight)), [mlp_pair[0], mlp_pair[2]], 2
    )
    proj_scale = norm_scale(attn_proj)
    mixed = hidden_in.astype(F32) + attn_proj * proj_scale * gain_full[2]
    every_mixed, (up_weight,) = gather_and_gather(mixed.astype(BF16), [mlp_pair[1]], 3)
    gate_proj = product(every_mixed, gate_weight)
    up_proj = product(every_mixed, up_weight)
    sigmoid_gate = jax.nn.sigmoid(gate_proj)
    hidden_act = (gate_proj * sigmoid_gate * up_proj).astype(BF16)
    down_proj, _ = scatter_and_gather(for_ring(row_product(hidden_act, down_weight)), [], 4)
    down_scale = norm_scale(down_proj)
    hidden_out = (mixed + down_proj * down_scale * gain_full[3]).astype(BF16)

    upstream = cotangent.astype(F32)
    d_down = norm_back(upstream, down_proj, down_scale, gain_full[3]).astype(BF16)
    gain_mlp = jnp.sum(upstream * down_proj * down_scale, axis=0)
    every_down, _ = gather_and_gather(d_down, [], 5)
    d_act = product(every_down, down_weight)
    d_gate = (d_act * up_proj * sigmoid_gate * (1.0 + gate_proj * (1.0 - sigmoid_gate))).astype(BF16)
    d_up = (d_act * gate_proj * sigmoid_gate).astype(BF16)

    def for_plane(values):
        return values.astype(BF16).reshape(2, RING, RING, shard_rows, values.shape[-1])

    down_partial = for_plane(col_product(every_down, hidden_act))
    gate_partial = for_plane(col_product(every_mixed, d_gate))
    up_partial = for_plane(col_product(every_mixed, d_up))
    d_mixed_sum, (down_sum,) = sums_of_gradients(
        "scatter",
        for_ring(row_product(d_gate, gate_weight) + row_product(d_up, up_weight)),
        [down_partial],
        6,
    )
    d_mixed = upstream + d_mixed_sum
    gain_attn = jnp.sum(d_mixed * attn_proj * proj_scale, axis=0)
    d_proj = norm_back(d_mixed, attn_proj, proj_scale, gain_full[2]).astype(BF16)
    every_proj, (gate_sum,) = sums_of_gradients("gather", d_proj, [gate_partial], 7)
    d_att = by_head(product(every_proj, out_weight).astype(BF16))
    out_weight_grad = col_product(every_proj, attended).astype(BF16)

    attn_probs = jnp.exp(scores_of() - log_totals)
    d_probs = jnp.einsum("hbqd,hbkd->hbqk", d_att, value_heads, preferred_element_type=F32)
    row_dot = jnp.sum(attn_probs * d_probs, axis=-1, keepdims=True)
    d_scores = (attn_probs * (d_probs - row_dot) * score_factor).astype(BF16)
    d_query_rot = jnp.einsum("hbqk,hbkd->hbqd", d_scores, key_rot, preferred_element_type=F32)
    d_key_rot = jnp.einsum("hbqk,hbqd->hbkd", d_scores, query_rot, preferred_element_type=F32)
    d_value = by_token(
        jnp.einsum(
            "hbqk,hbqd->hbkd", attn_probs.astype(BF16), d_att, preferred_element_type=F32
        ).astype(BF16)
    )
    d_query_norm = by_token(unrotate(d_query_rot, cosine_table, sine_table))
    d_key_norm = by_token(unrotate(d_key_rot, cosine_table, sine_table))
    gain_query = jnp.sum(d_query_norm * queries * query_scale, axis=0)
    gain_key = jnp.sum(d_key_norm * key_raw * key_scale, axis=0)
    query_back = d_query_norm * query_gain
    key_back = d_key_norm * key_gain
    gain_heads = lax.dynamic_update_slice(
        jnp.zeros((2, model_width), F32), jnp.stack([gain_query, gain_key]), (0, first_column)
    )
    row_sums = jnp.stack([jnp.sum(query_back * queries, axis=-1), jnp.sum(key_back * key_raw, axis=-1)])
    together = jnp.concatenate(
        [row_sums.reshape(-1), gain_heads.reshape(-1), gain_attn, gain_mlp]
    ).reshape(-1, 128)
    together = sum_over_eight(together, 8).reshape(-1)
    row_sums = together[: 2 * token_count].reshape(2, token_count)
    gain_sums = together[2 * token_count :].reshape(4, model_width)
    d_query = (
        query_scale * query_back - queries * query_scale**3 * row_sums[0][:, None] / model_width
    ).astype(BF16)
    d_key = (
        key_scale * key_back - key_raw * key_scale**3 * row_sums[1][:, None] / model_width
    ).astype(BF16)
    d_qkv = jnp.concatenate([d_query, d_key, d_value], axis=-1)
    attn_partial = for_plane(
        jnp.concatenate([col_product(every_input, d_qkv).astype(BF16), out_weight_grad], axis=-1)
    )
    gain_partial = jnp.pad(
        gain_sums.reshape(4, 2, RING, RING, shard_rows).transpose(1, 2, 3, 0, 4),
        ((0, 0), (0, 0), (0, 0), (0, 4), (0, 128 - shard_rows)),
    )
    input_sum, (up_sum, attn_sum, gain_sum) = sums_of_gradients(
        "scatter", for_ring(row_product(d_qkv, qkv_weight)), [up_partial, attn_partial, gain_partial], 9
    )
    input_grad = d_mixed + input_sum

    attn_grad = (
        attn_sum.astype(F32)
        .reshape(2, shard_rows, 4, heads_width)
        .transpose(2, 1, 0, 3)
        .reshape(4, shard_rows, 2 * heads_width)
    )
    mlp_grad = jnp.stack(
        [
            s.astype(F32).transpose(1, 0, 2).reshape(shard_rows, 2 * hidden_width)
            for s in (gate_sum, up_sum, down_sum)
        ]
    )
    gain_grad = gain_sum[:4, :shard_rows]
    attn_first_new, attn_second_new, attn_new = adam_update(
        attn_weights, attn_first, attn_second, attn_grad, WEIGHT_RATE, WEIGHT_DECAY
    )
    mlp_first_new, mlp_second_new, mlp_new = adam_update(
        mlp_weights, mlp_first, mlp_second, mlp_grad, WEIGHT_RATE, WEIGHT_DECAY
    )
    gain_first_new, gain_second_new, gain_new = adam_update(
        gains, gain_first, gain_second, gain_grad, GAIN_RATE, 0.0
    )
    return (
        hidden_out,
        input_grad,
        attn_grad,
        attn_first_new,
        attn_second_new,
        attn_new,
        mlp_grad,
        mlp_first_new,
        mlp_second_new,
        mlp_new,
        gain_grad,
        gain_first_new,
        gain_second_new,
        gain_new,
    )


def solution(mesh):
    split = Mesh(mesh.devices.reshape(2, 4, 4, 2, 2), EVERY)
    tokens, shards, rows = P(EVERY, None), P(None, DP, TENSOR), P(None, DP)
    return jax.shard_map(
        body,
        mesh=split,
        in_specs=(tokens, tokens, P(DP, None), *[shards] * 6, *[rows] * 3),
        out_specs=(tokens, tokens, *[shards] * 8, *[rows] * 4),
        check_vma=False,
    )
```

```python
import functools

import jax
import jax.numpy as jnp
from jax import lax
from jax.experimental import pallas as pl
from jax.experimental.pallas import tpu as pltpu
from jax.sharding import Mesh
from jax.sharding import PartitionSpec as P

HEAD_DIM = 128
STEP = 10
DP = ("yl", "x", "z")
TENSOR = ("yh", "c")
EVERY = ("yl", "x", "z", "yh", "c")
RING = 4
MESH = pl.DeviceIdType.MESH

NORM_EPS = 1e-06
ROPE_BASE = 500000.0
BETA_ONE = 0.9
BETA_TWO = 0.95
ADAM_EPS = 1e-08
WEIGHT_RATE = 0.03
GAIN_RATE = 1.0
WEIGHT_DECAY = 0.1

BF16 = jnp.bfloat16
F32 = jnp.float32
IN_VMEM = pl.BlockSpec(memory_space=pltpu.VMEM)
ANYWHERE = pl.BlockSpec(memory_space=pl.ANY)
VMEM_LIMIT = 56 * 1024 * 1024


class Place:
    def __init__(self):
        self.x, self.z, self.c = (lax.axis_index(a) for a in ("x", "z", "c"))
        self.yl, self.yh = (lax.axis_index(a) for a in ("yl", "yh"))
        self.y = self.yh * 2 + self.yl

    def at(self, axis, step):
        if axis == "y":
            there = (self.y + step + RING) % RING
            return {"yl": there % 2, "yh": there // 2}
        if axis == "c":
            return {"c": 1 - self.c}
        return {axis: (getattr(self, axis) + step + RING) % RING}

    def shift(self, axis, step):
        return (getattr(self, axis) + step + RING) % RING


def greet(devices):
    barrier = pltpu.get_barrier_semaphore()
    for device in devices:
        pl.semaphore_signal(barrier, inc=1, device_id=device, device_id_type=MESH)
    pl.semaphore_wait(barrier, len(devices))


def greet_all(place, axes):
    devices = []
    for axis in axes:
        devices += [place.at(axis, 1)] if axis == "c" else [place.at(axis, 1), place.at(axis, -1)]
    greet(devices)


class Sender:
    def __init__(self, sems):
        self.sems, self.open = sems, []

    def push(self, src, dst, recv_sem, device):
        copy = pltpu.make_async_remote_copy(
            src_ref=src,
            dst_ref=dst,
            send_sem=self.sems.at[len(self.open)],
            recv_sem=recv_sem,
            device_id=device,
            device_id_type=MESH,
        )
        copy.start()
        self.open.append(copy.wait_send)

    def keep(self, src, dst):
        copy = pltpu.make_async_copy(src, dst, self.sems.at[len(self.open)])
        copy.start()
        self.open.append(copy.wait)

    def keep_first(self, src, dst):
        copy = pltpu.make_async_copy(src, dst, self.sems.at[len(self.open)])
        copy.start()
        self.open.append(lambda: None)
        return copy

    def arrived(self, dst, recv_sem, device):
        pltpu.make_async_remote_copy(
            src_ref=dst,
            dst_ref=dst,
            send_sem=self.sems.at[0],
            recv_sem=recv_sem,
            device_id=device,
            device_id_type=MESH,
        ).wait_recv()

    def finish(self):
        for wait in self.open:
            wait()


def take_turns(tasks):
    tasks = list(tasks)
    while tasks:
        for task in list(tasks):
            if next(task, "done") == "done":
                tasks.remove(task)


WHOLE, LOW, HIGH = 0, 1, 2


def part_of(ref, part, cut):
    rows = ref.shape[-2]
    if part == WHOLE:
        return ref
    return ref.at[pl.ds(0, cut)] if part == LOW else ref.at[pl.ds(cut, rows - cut)]


def plane_gather(place, sender, sems, out, cut):
    rows = out.shape[-2]
    axes = (("x", "z"), ("z", "x"))

    def piece(half, dp, dq):
        p, q = (place.shift(a, d) for a, d in zip(axes[half], (dp, dq)))
        return out.at[half, p, q] if half == 0 else out.at[half, q, p]

    def parts(part):
        if part == WHOLE:
            return True
        return cut > 0 if part == LOW else cut < rows

    def send(half, dp, dq, part, along, step):
        if parts(part):
            ref = part_of(piece(half, dp, dq), part, cut)
            sp, sq = ((dp - step) % RING, dq % RING) if along == 0 else (dp % RING, (dq - step) % RING)
            sender.push(ref, ref, sems.at[half, sp, sq, part], place.at(axes[half][along], step))

    def wait(half, dp, dq, part):
        if parts(part):
            ref = part_of(piece(half, dp, dq), part, cut)
            sender.arrived(ref, sems.at[half, dp % RING, dq % RING, part], place.at("x", 1))

    both = (0, 1)
    for half in both:
        for step in (1, -1):
            send(half, 0, 0, WHOLE, 0, step)
    for half in both:
        for step in (1, -1):
            send(half, 0, 0, WHOLE, 1, step)
    yield
    for step, part in ((1, LOW), (-1, HIGH)):
        for half in both:
            wait(half, -step, 0, WHOLE)
            send(half, -step, 0, part, 0, step)
            for side in (1, -1):
                send(half, -step, 0, WHOLE, 1, side)
    yield
    for half in both:
        for step, part in ((1, LOW), (-1, HIGH)):
            wait(half, 0, -step, WHOLE)
            send(half, 0, -step, part, 1, step)
    yield
    for half in both:
        wait(half, 2, 0, LOW)
        wait(half, 2, 0, HIGH)
        for side in (1, -1):
            send(half, 2, 0, WHOLE, 1, side)
    yield
    for dp in (-1, 1, 2):
        for half in both:
            for step, part in ((1, LOW), (-1, HIGH)):
                wait(half, dp, -step, WHOLE)
                send(half, dp, -step, part, 1, step)
        yield
    for dp in (0, -1, 1, 2):
        for half in both:
            wait(half, dp, 2, LOW)
            wait(half, dp, 2, HIGH)


class RingGather:
    def __init__(self, place, sender, sems, own, out):
        self.place, self.sender, self.sems, self.own, self.out = place, sender, sems, own, out
        self.rows = own.shape[0]
        self.other = place.at("c", 1)

    def piece(self, dy, core, part=WHOLE):
        y = self.place.shift("y", dy)
        half = self.rows // 2
        start, size = {WHOLE: (0, self.rows), LOW: (0, half), HIGH: (half, half)}[part]
        return self.out.at[y % 2, y // 2, pl.ds(pl.multiple_of(core * self.rows + start, 16), size)]

    def begin(self):
        place, mine = self.place, self.piece(0, self.place.c)
        for step in (1, -1):
            self.sender.push(self.own, mine, self.sems.at[(-step) % RING, WHOLE], place.at("y", step))
        self.sender.push(self.own, mine, self.sems.at[0, 3], self.other)
        self.kept = self.sender.keep_first(self.own, mine)

    def relay(self):
        for step, part in ((1, LOW), (-1, HIGH)):
            ref = self.piece(-step, self.place.c)
            self.sender.arrived(ref, self.sems.at[(-step) % RING, WHOLE], self.other)
            half = self.piece(-step, self.place.c, part)
            self.sender.push(half, half, self.sems.at[2, part], self.place.at("y", step))
            self.sender.push(ref, ref, self.sems.at[(-step) % RING, 3], self.other)

    def relay_far(self):
        for part in (LOW, HIGH):
            self.sender.arrived(self.piece(2, self.place.c, part), self.sems.at[2, part], self.other)
        ref = self.piece(2, self.place.c)
        self.sender.push(ref, ref, self.sems.at[2, 3], self.other)

    def ready(self, dy):
        if dy == 0:
            self.kept.wait()
        self.sender.arrived(self.piece(dy, 1 - self.place.c), self.sems.at[dy % RING, 3], self.other)


def ring_gather(place, sender, sems, own, out):
    gather = RingGather(place, sender, sems, own, out)
    gather.begin()
    yield
    gather.relay()
    yield
    gather.relay_far()
    yield
    for dy in (0, 1, -1, 2):
        gather.ready(dy)


def add_rows(out, terms, rows):
    def step(i, carry):
        window = pl.ds(pl.multiple_of(i * 16, 16), 16)
        total = terms[0][window, :].astype(F32)
        for term in terms[1:]:
            total = total + term[window, :].astype(F32)
        out[window, :] = total.astype(out.dtype)
        return carry

    lax.fori_loop(0, rows // 16, step, 0)


class RingSum:
    def __init__(self, place, sender, sems, partial, kept, from_core, hop, last):
        self.place, self.sender, self.sems, self.partial = place, sender, sems, partial
        self.kept, self.from_core, self.hop, self.last = kept, from_core, hop, last
        self.rows = kept.shape[1]
        self.low, self.high = pl.ds(0, self.rows // 2), pl.ds(self.rows // 2, self.rows // 2)
        self.other = place.at("c", 1)

    def mine(self, dy, core):
        y = self.place.shift("y", dy)
        return self.partial.at[y % 2, y // 2, pl.ds(pl.multiple_of(core * self.rows, 16), self.rows)]

    def offer(self, dy):
        slot = dy % RING
        self.sender.push(
            self.mine(dy, 1 - self.place.c), self.from_core.at[slot], self.sems.at[0, slot], self.other
        )

    def collect(self, dy):
        slot = dy % RING
        kept, low, high = self.kept.at[slot], self.low, self.high
        self.sender.arrived(self.from_core.at[slot], self.sems.at[0, slot], self.other)
        if dy == 0:
            return
        add_rows(kept, (self.mine(dy, self.place.c), self.from_core.at[slot]), self.rows)
        up, down = self.place.at("y", 1), self.place.at("y", -1)
        if dy == 2:
            self.sender.push(kept.at[low], self.hop.at[0], self.sems.at[1, 0], up)
            self.sender.push(kept.at[high], self.hop.at[1], self.sems.at[1, 1], down)
        elif dy == 1:
            self.sender.push(kept.at[high], self.last.at[0, high], self.sems.at[2, 1], up)
        else:
            self.sender.push(kept.at[low], self.last.at[1, low], self.sems.at[2, 2], down)

    def relay(self):
        for k, slot, part, step, sem in ((0, 1, self.low, 1, 0), (1, 3, self.high, -1, 3)):
            self.sender.arrived(self.hop.at[k], self.sems.at[1, k], self.other)
            rows = self.kept.at[slot, part]
            add_rows(rows, (rows, self.hop.at[k]), self.rows // 2)
            self.sender.push(rows, self.last.at[k, part], self.sems.at[2, sem], self.place.at("y", step))

    def finish(self, out):
        for k, part, sem in ((0, self.low, 0), (0, self.high, 1), (1, self.low, 2), (1, self.high, 3)):
            self.sender.arrived(self.last.at[k, part], self.sems.at[2, sem], self.other)
        add_rows(
            out, (self.mine(0, self.place.c), self.from_core.at[0], self.last.at[0], self.last.at[1]), self.rows
        )


def plane_scatter(place, sender, sems, partial, done, cut, bufs):
    rows = partial.shape[-2]
    hop, send_on, last, middle, hop2, send_on2, last2 = bufs
    low, high = pl.ds(0, cut), pl.ds(cut, rows - cut)
    axes = (("z", "x"), ("x", "z"))
    two_parts = cut < rows
    both = (0, 1)
    other = place.at("x", 1)

    def row(half, du, window):
        u = place.shift(axes[half][0], du)
        return partial.at[half, :, u, window] if half == 0 else partial.at[half, u, :, window]

    def line(half, du, v):
        u = place.shift(axes[half][0], du)
        return partial.at[half, v, u] if half == 0 else partial.at[half, u, v]

    def add(out, terms, count):
        if count % 16:
            total = terms[0][...].astype(F32)
            for term in terms[1:]:
                total = total + term[...].astype(F32)
            out[...] = total.astype(out.dtype)
        else:
            add_rows(out, terms, count)

    for half in both:
        u = axes[half][0]
        sender.push(row(half, 2, low), hop.at[half, 0, :, low], sems.at[half, 0], place.at(u, 1))
        if two_parts:
            sender.push(row(half, 2, high), hop.at[half, 1, :, high], sems.at[half, 1], place.at(u, -1))
    for half in both:
        u = axes[half][0]
        if two_parts:
            sender.push(row(half, 1, high), last.at[half, 0, :, high], sems.at[half, 2], place.at(u, 1))
        sender.push(row(half, -1, low), last.at[half, 1, :, low], sems.at[half, 3], place.at(u, -1))
    yield
    for half in both:
        u = axes[half][0]
        sender.arrived(hop.at[half, 0, :, low], sems.at[half, 0], other)
        for v in range(RING):
            add(send_on.at[half, 0, v, low], (line(half, 1, v).at[low], hop.at[half, 0, v, low]), cut)
        sender.push(send_on.at[half, 0, :, low], last.at[half, 0, :, low], sems.at[half, 4], place.at(u, 1))
        if two_parts:
            sender.arrived(hop.at[half, 1, :, high], sems.at[half, 1], other)
            for v in range(RING):
                add(
                    send_on.at[half, 1, v, high],
                    (line(half, -1, v).at[high], hop.at[half, 1, v, high]),
                    rows - cut,
                )
            sender.push(
                send_on.at[half, 1, :, high], last.at[half, 1, :, high], sems.at[half, 5], place.at(u, -1)
            )
    yield
    for half in both:
        v_axis = axes[half][1]
        if two_parts:
            sender.arrived(last.at[half, 0, :, high], sems.at[half, 2], other)
        sender.arrived(last.at[half, 1, :, low], sems.at[half, 3], other)
        sender.arrived(last.at[half, 0, :, low], sems.at[half, 4], other)
        if two_parts:
            sender.arrived(last.at[half, 1, :, high], sems.at[half, 5], other)
        for dv in (2, 1, -1, 0):
            v = place.shift(v_axis, dv)
            terms = (line(half, 0, v), last.at[half, 0, v], last.at[half, 1, v])
            add(middle.at[half, dv % RING], terms, rows)
            if dv == 2:
                sender.push(
                    middle.at[half, 2, low], hop2.at[half, 0, low], sems.at[half, 6], place.at(v_axis, 1)
                )
                if two_parts:
                    sender.push(
                        middle.at[half, 2, high],
                        hop2.at[half, 1, high],
                        sems.at[half, 7],
                        place.at(v_axis, -1),
                    )
            elif dv == 1 and two_parts:
                sender.push(
                    middle.at[half, 1, high], last2.at[half, 0, high], sems.at[half, 8], place.at(v_axis, 1)
                )
            elif dv == -1:
                sender.push(
                    middle.at[half, 3, low], last2.at[half, 1, low], sems.at[half, 9], place.at(v_axis, -1)
                )
    yield
    for half in both:
        v_axis = axes[half][1]
        sender.arrived(hop2.at[half, 0, low], sems.at[half, 6], other)
        add(send_on2.at[half, 0, low], (middle.at[half, 1, low], hop2.at[half, 0, low]), cut)
        sender.push(
            send_on2.at[half, 0, low], last2.at[half, 0, low], sems.at[half, 10], place.at(v_axis, 1)
        )
        if two_parts:
            sender.arrived(hop2.at[half, 1, high], sems.at[half, 7], other)
            add(send_on2.at[half, 1, high], (middle.at[half, 3, high], hop2.at[half, 1, high]), rows - cut)
            sender.push(
                send_on2.at[half, 1, high], last2.at[half, 1, high], sems.at[half, 11], place.at(v_axis, -1)
            )
    yield
    for half in both:
        if two_parts:
            sender.arrived(last2.at[half, 0, high], sems.at[half, 8], other)
        sender.arrived(last2.at[half, 1, low], sems.at[half, 9], other)
        sender.arrived(last2.at[half, 0, low], sems.at[half, 10], other)
        if two_parts:
            sender.arrived(last2.at[half, 1, high], sems.at[half, 11], other)
        add(done.at[half], (middle.at[half, 0], last2.at[half, 0], last2.at[half, 1]), rows)


def scatter_buffers(rows, columns, dtype):
    line = (2, 2, RING, rows, columns)
    one = (2, 2, rows, columns)
    return [
        pltpu.VMEM(line, dtype),
        pltpu.VMEM(line, dtype),
        pltpu.VMEM(line, dtype),
        pltpu.VMEM((2, RING, rows, columns), dtype),
        pltpu.VMEM(one, dtype),
        pltpu.VMEM(one, dtype),
        pltpu.VMEM(one, dtype),
    ]


def ring_buffers(rows, columns):
    return [
        pltpu.VMEM((RING, rows, columns), BF16),
        pltpu.VMEM((RING, rows, columns), BF16),
        pltpu.VMEM((2, rows // 2, columns), BF16),
        pltpu.VMEM((2, rows, columns), BF16),
    ]


def dma_sems(*shape):
    return pltpu.SemaphoreType.DMA(shape)


def shape_of(*shape, dtype=BF16):
    return jax.ShapeDtypeStruct(shape, dtype)


def call(kernel, number, out_shape, in_specs, out_specs, scratch, args):
    return pl.pallas_call(
        kernel,
        out_shape=out_shape,
        in_specs=in_specs,
        out_specs=out_specs,
        scratch_shapes=scratch,
        compiler_params=pltpu.CompilerParams(
            collective_id=number, has_side_effects=True, vmem_limit_bytes=VMEM_LIMIT
        ),
    )(*args)


def first_kernel(hidden, attn, gain, doc, hidden_all, attn_all, gain_all, doc_pair, sends, ring, plane, plane_gain, swap):
    place = Place()
    greet_all(place, ("x", "z", "y", "c"))
    sender = Sender(sends)
    partner = {"yl": 1 - place.yl}
    me, you = place.yl, 1 - place.yl
    own_attn = attn_all.at[:, place.x, place.z]
    own_gain = gain_all.at[:, place.x, place.z]
    sender.push(attn.at[you], own_attn.at[me], swap.at[0], partner)
    sender.push(gain, own_gain.at[me], swap.at[1], partner)
    first = sender.keep_first(attn.at[me], own_attn.at[me])
    second = sender.keep_first(gain, own_gain.at[me])
    gather = ring_gather(place, sender, ring, hidden, hidden_all)
    next(gather)
    first.wait()
    second.wait()
    sender.arrived(own_attn.at[you], swap.at[0], partner)
    sender.arrived(own_gain.at[you], swap.at[1], partner)
    planes = plane_gather(place, sender, plane, attn_all, attn_all.shape[-2] // 2)
    gains = plane_gather(place, sender, plane_gain, gain_all, gain_all.shape[-2])
    next(planes)
    next(gains)
    sender.push(doc, doc_pair.at[me], swap.at[3], partner)
    sender.keep(doc, doc_pair.at[me])
    take_turns((gains, planes, gather))
    sender.arrived(doc_pair.at[you], swap.at[3], partner)
    sender.finish()


def sums_kernel(own, total, slots, sends, recvs):
    place = Place()
    peers = [(dy, dc) for dy in (0, 1, 3, 2) for dc in (0, 1) if dy or dc]

    def device(dy, dc):
        y = place.shift("y", dy)
        return {"yl": y % 2, "yh": y // 2, "c": (place.c + dc) % 2}

    greet([device(*peer) for peer in peers])
    sender = Sender(sends)
    for dy, dc in peers:
        slot = ((RING - dy) % RING) * 2 + dc
        sender.push(own, slots.at[slot], recvs.at[slot], device(dy, dc))
    for dy, dc in peers:
        slot = dy * 2 + dc
        sender.arrived(slots.at[slot], recvs.at[slot], device(dy, dc))
    subtotal = own[...]
    for dy, dc in peers:
        subtotal = subtotal + slots[dy * 2 + dc]
    total[...] = subtotal
    sender.finish()


def sum_over_eight(own, number):
    return call(
        sums_kernel,
        number,
        shape_of(*own.shape, dtype=F32),
        [IN_VMEM],
        IN_VMEM,
        [pltpu.VMEM((8, *own.shape), F32), dma_sems(8), dma_sems(8)],
        (own,),
    )


NN = (((1,), (0,)), ((), ()))
NT = (((1,), (1,)), ((), ()))
TN = (((0,), (0,)), ((), ()))


def dot(left, right, dims=NN):
    return lax.dot_general(left, right, dims, preferred_element_type=F32)


def in_tiles(width, tile, work):
    def step(n, carry):
        work(pl.ds(pl.multiple_of(n * tile, tile), tile))
        return carry

    lax.fori_loop(0, width // tile, step, 0)


def refs_of(refs, *counts):
    refs, out = list(refs), []
    for n in counts:
        out.append(refs[:n])
        del refs[:n]
    return out


def load_weights(sender, source, targets):
    copies = []
    for k, target in targets:
        for yl in range(2):
            copies.append(sender.keep_first(source.at[:, k, yl], target.at[yl]))
    return copies


def rows_of(weight, window):
    piece = weight.shape[2]
    per_half = weight.shape[1] * piece
    start, size = window.start, window.size
    block = weight[start // per_half, pl.ds((start % per_half) // piece, size // piece), :, :]
    return block.reshape(size, weight.shape[3])


def columns_of(weight, window):
    block = weight[:, :, :, window]
    return block.reshape(-1, window.size)


def mlp_forward_kernel(own, weights, x_out, gate_out, up_out, act_out, down_out, *refs):
    (x_all, w_gate, w_up, w_down, gate, up, act, partial), ring, (sends, gather_sems, sum_sems) = refs_of(
        refs, 8, 4, 3
    )
    place = Place()
    greet_all(place, ("y", "c"))
    sender = Sender(sends)
    gather = RingGather(place, sender, gather_sems, own, x_all)
    total = RingSum(place, sender, sum_sems, partial, *ring)
    gather.begin()
    for copy in load_weights(sender, weights, ((0, w_gate), (1, w_up), (2, w_down))):
        copy.wait()
    tile = 512

    def compute(dy):
        gather.ready(dy)
        y = place.shift("y", dy)
        at = (y % 2, y // 2)

        def hidden(columns):
            rows = x_all[at]
            g = dot(rows, columns_of(w_gate, columns))
            u = dot(rows, columns_of(w_up, columns))
            here = (*at, slice(None), columns)
            gate[here], up[here] = g.astype(BF16), u.astype(BF16)
            act[here] = (g * jax.nn.sigmoid(g) * u).astype(BF16)

        in_tiles(act.shape[-1], tile, hidden)

        def down(columns):
            partial[(*at, slice(None), columns)] = dot(act[at], rows_of(w_down, columns), NT).astype(BF16)

        in_tiles(partial.shape[-1], tile, down)
        total.offer(dy)
        for values, out in ((x_all, x_out), (gate, gate_out), (up, up_out), (act, act_out)):
            sender.keep(values.at[at], out.at[at])

    compute(0)
    gather.relay()
    compute(1)
    gather.relay_far()
    compute(-1)
    total.collect(1)
    compute(2)
    total.collect(-1)
    total.collect(2)
    total.collect(0)
    total.relay()
    total.finish(down_out)
    sender.finish()


def mlp_forward(own, weights, number):
    rows, width = own.shape
    hidden = weights.shape[-1]
    tokens = (2, 2, 2 * rows)
    weight = pltpu.VMEM((2, 16, *weights.shape[-2:]), BF16)
    return call(
        mlp_forward_kernel,
        number,
        (
            shape_of(*tokens, width),
            shape_of(*tokens, hidden),
            shape_of(*tokens, hidden),
            shape_of(*tokens, hidden),
            shape_of(rows, width, dtype=F32),
        ),
        [ANYWHERE, ANYWHERE],
        (ANYWHERE, ANYWHERE, ANYWHERE, ANYWHERE, IN_VMEM),
        [
            pltpu.VMEM((*tokens, width), BF16),
            *[weight] * 3,
            *[pltpu.VMEM((*tokens, hidden), BF16)] * 3,
            pltpu.VMEM((*tokens, width), BF16),
            *ring_buffers(rows, width),
            dma_sems(56),
            dma_sems(RING, 4),
            dma_sems(3, RING),
        ],
        (own, weights),
    )


def mlp_backward_kernel(own, weights, x_in, gate_in, up_in, act_in, d_x_out, grads_out, *refs):
    (
        (d_all, w_gate, w_up, w_down, x_all, gate, up, act, d_gate, d_up, partial, tiles),
        ring,
        (sends, gather_sems, sum_sems, tile_sems),
    ) = refs_of(refs, 12, 4, 4)
    place = Place()
    greet_all(place, ("y", "c"))
    sender = Sender(sends)
    gather = RingGather(place, sender, gather_sems, own, d_all)
    total = RingSum(place, sender, sum_sems, partial, *ring)
    gather.begin()
    first = load_weights(sender, weights, ((2, w_down),))
    first += [sender.keep_first(gate_in, gate), sender.keep_first(up_in, up)]
    second = load_weights(sender, weights, ((0, w_gate), (1, w_up)))
    third = [sender.keep_first(x_in, x_all), sender.keep_first(act_in, act)]
    for copy in first + second:
        copy.wait()
    tile = 512

    def compute(dy):
        gather.ready(dy)
        y = place.shift("y", dy)
        at = (y % 2, y // 2)

        def hidden(columns):
            d_act = dot(d_all[at], columns_of(w_down, columns))
            here = (*at, slice(None), columns)
            g, u = gate[here].astype(F32), up[here].astype(F32)
            s = jax.nn.sigmoid(g)
            d_gate[here] = (d_act * u * s * (1.0 + g * (1.0 - s))).astype(BF16)
            d_up[here] = (d_act * g * s).astype(BF16)

        in_tiles(act.shape[-1], tile, hidden)

        def back(columns):
            value = dot(d_gate[at], rows_of(w_gate, columns), NT) + dot(d_up[at], rows_of(w_up, columns), NT)
            partial[(*at, slice(None), columns)] = value.astype(BF16)

        in_tiles(partial.shape[-1], tile, back)
        total.offer(dy)

    block = 4 * tiles.shape[3]

    def all_rows(ref, columns=slice(None)):
        value = ref[:, :, :, columns]
        return value.reshape(-1, value.shape[-1])

    def sent(slot, k, i):
        return pltpu.make_async_copy(
            tiles.at[slot, k], grads_out.at[pl.ds((i % RING) * 4, 4), k, i // RING], tile_sems.at[slot, k]
        )

    def weight_grads(begin, end):
        def step(i, carry):
            slot = i % 2
            columns = pl.ds(pl.multiple_of(i * block, block), block)
            for k, (left, right) in enumerate(((x_all, d_gate), (x_all, d_up), (d_all, act))):

                @pl.when(i >= 2)
                def _():
                    sent(slot, k, i - 2).wait()

                value = dot(all_rows(left, columns), all_rows(right), TN)
                tiles[slot, k] = value.astype(BF16).reshape(tiles.shape[2:])
                sent(slot, k, i).start()
            return carry

        lax.fori_loop(begin, end, step, 0)

    compute(0)
    gather.relay()
    compute(1)
    gather.relay_far()
    compute(-1)
    total.collect(1)
    compute(2)
    total.collect(-1)
    for copy in third:
        copy.wait()
    total.collect(2)
    total.collect(0)
    weight_grads(0, 3)
    total.relay()
    weight_grads(3, 8)
    total.finish(d_x_out)
    for i in (6, 7):
        for k in range(3):
            sent(i % 2, k, i).wait()
    sender.finish()


def mlp_backward(own, weights, x_all, gate, up, act, number):
    rows, width = own.shape
    piece, hidden = weights.shape[-2:]
    tokens = (2, 2, 2 * rows)
    weight = pltpu.VMEM((2, 16, piece, hidden), BF16)
    wide, narrow = pltpu.VMEM((*tokens, width), BF16), pltpu.VMEM((*tokens, hidden), BF16)
    return call(
        mlp_backward_kernel,
        number,
        (shape_of(rows, width, dtype=F32), shape_of(*weights.shape)),
        [ANYWHERE] * 6,
        (IN_VMEM, ANYWHERE),
        [
            wide,
            *[weight] * 3,
            wide,
            *[narrow] * 5,
            wide,
            pltpu.VMEM((2, 3, 4, piece, hidden), BF16),
            *ring_buffers(rows, width),
            dma_sems(48),
            dma_sems(RING, 4),
            dma_sems(3, RING),
            dma_sems(2, 3),
        ],
        (own, weights, x_all, gate, up, act),
    )


def project_out_kernel(values, weight, out, *refs):
    (own_weight, partial), ring, (sends, sum_sems) = refs_of(refs, 2, 4, 2)
    place = Place()
    sender = Sender(sends)
    load = sender.keep_first(last_columns(weight, own_weight), own_weight)
    greet_all(place, ("y", "c"))
    total = RingSum(place, sender, sum_sems, partial, *ring)
    load.wait()
    ring_product(place, total, values, own_weight, partial, ())
    total.finish(out)
    sender.finish()


def last_columns(weight, part):
    width = part.shape[1]
    return weight.at[:, pl.ds(weight.shape[1] - width, width)]


def ring_product(place, total, values, weight, partial, others):
    def compute(dy):
        y = place.shift("y", dy)
        at = (y % 2, y // 2)

        def tile(columns):
            partial[(*at, slice(None), columns)] = dot(values[at], weight[columns, :], NT).astype(BF16)

        in_tiles(partial.shape[-1], 512, tile)
        total.offer(dy)

    compute(2)
    compute(1)
    total.collect(2)
    compute(-1)
    total.collect(1)
    compute(0)
    total.collect(-1)
    total.collect(0)
    for task in others:
        next(task)
    total.relay()
    take_turns(others)


def project_out(values, weight, number):
    rows, width = values.shape[2] // 2, weight.shape[0]
    return call(
        project_out_kernel,
        number,
        shape_of(rows, width, dtype=F32),
        [IN_VMEM, ANYWHERE],
        IN_VMEM,
        [
            pltpu.VMEM((width, values.shape[3]), BF16),
            pltpu.VMEM((2, 2, 2 * rows, width), BF16),
            *ring_buffers(rows, width),
            dma_sems(17),
            dma_sems(3, RING),
        ],
        (values, weight),
    )


def project_back_kernel(own, weight, values, d_values_out, grad_out, d_all, own_weight, sends, gather_sems):
    place = Place()
    sender = Sender(sends)
    load = sender.keep_first(last_columns(weight, own_weight), own_weight)
    greet_all(place, ("y", "c"))
    gather = RingGather(place, sender, gather_sems, own, d_all)
    gather.begin()
    load.wait()

    def compute(dy):
        gather.ready(dy)
        y = place.shift("y", dy)
        at = (y % 2, y // 2)
        d_values_out[at] = dot(d_all[at], own_weight[...]).astype(BF16)

    compute(0)
    gather.relay()
    compute(1)
    gather.relay_far()
    compute(-1)
    compute(2)
    flat_values = values[...].reshape(-1, values.shape[-1])

    block = 4 * grad_out.shape[3]

    def grad(i, carry):
        left = d_all[:, :, :, pl.ds(pl.multiple_of(i * block, block), block)]
        value = dot(left.reshape(-1, block), flat_values, TN).astype(BF16)
        grad_out[i // RING, i % RING] = value.reshape(grad_out.shape[2:])
        return carry

    lax.fori_loop(0, 2 * RING, grad, 0)
    sender.finish()


def project_back(own, weight, values, number):
    rows, width = own.shape
    tokens = (2, 2, 2 * rows)
    return call(
        project_back_kernel,
        number,
        (shape_of(*values.shape), shape_of(2, RING, RING, width // 32, values.shape[3])),
        [ANYWHERE, ANYWHERE, IN_VMEM],
        (IN_VMEM, IN_VMEM),
        [
            pltpu.VMEM((*tokens, width), BF16),
            pltpu.VMEM((width, values.shape[3]), BF16),
            dma_sems(16),
            dma_sems(RING, 4),
        ],
        (own, weight, values),
    )


def flat(weight):
    return weight.reshape(-1, weight.shape[-1])


def last_kernel(values, weight, inputs, out_grad, gain_partial, out, attn_out, gain_out, *refs):
    (own_weight, x_all, attn_partial, partial, attn_done, gain_done), ring, buffers, gain_buffers, sems = refs_of(
        refs, 6, 4, 7, 7, 5
    )
    sends, sum_sems, swap, plane, gain_plane = sems
    place = Place()
    sender = Sender(sends)
    width = own_weight.shape[1]
    rows = attn_partial.shape[3]
    block = RING * rows
    loads = [
        sender.keep_first(inputs, x_all),
        sender.keep_first(out_grad, attn_partial.at[:, :, :, :, pl.ds(width, out_grad.shape[4])]),
        sender.keep_first(weight.at[:, pl.ds(0, width)], own_weight),
    ]
    greet_all(place, ("x", "z", "y", "c"))
    total = RingSum(place, sender, sum_sems, partial, *ring)
    gains = plane_scatter(place, sender, gain_plane, gain_partial, gain_done, gain_done.shape[1], gain_buffers)
    next(gains)
    for load in loads:
        load.wait()
    flat_values = values[...].reshape(-1, width)

    def grad(i, carry):
        left = x_all[:, :, :, pl.ds(pl.multiple_of(i * block, block), block)]
        value = dot(left.reshape(-1, block), flat_values, TN).astype(BF16)
        attn_partial[i // RING, i % RING, :, :, pl.ds(0, width)] = value.reshape(RING, rows, width)
        return carry

    lax.fori_loop(0, 2 * RING, grad, 0)
    grads = plane_scatter(place, sender, plane, attn_partial, attn_done, rows // 2, buffers)
    next(grads)
    ring_product(place, total, values, own_weight, partial, (grads, gains))
    partner = {"yl": 1 - place.yl}
    me, you = place.yl, 1 - place.yl
    sender.push(attn_done.at[you], attn_out.at[me], swap.at[0], partner)
    sender.keep(attn_done.at[me], attn_out.at[me])
    sender.keep(gain_done.at[me], gain_out)
    total.finish(out)
    sender.arrived(attn_out.at[you], swap.at[0], partner)
    sender.finish()


def last_sums(values, weight, inputs, out_grad, gain_partial, number):
    rows, width = values.shape[2] // 2, weight.shape[0]
    tokens = (2, 2, 2 * rows)
    shard = out_grad.shape[3], weight.shape[1]
    gain_tile = gain_partial.shape[-2:]
    return call(
        last_kernel,
        number,
        (shape_of(rows, width, dtype=F32), shape_of(2, *shard), shape_of(*gain_tile, dtype=F32)),
        [IN_VMEM, ANYWHERE, ANYWHERE, ANYWHERE, IN_VMEM],
        (IN_VMEM,) * 3,
        [
            pltpu.VMEM((width, values.shape[3]), BF16),
            pltpu.VMEM((*tokens, width), BF16),
            pltpu.VMEM((2, RING, RING, *shard), BF16),
            pltpu.VMEM((*tokens, width), BF16),
            pltpu.VMEM((2, *shard), BF16),
            pltpu.VMEM((2, *gain_tile), F32),
            *ring_buffers(rows, width),
            *scatter_buffers(*shard, BF16),
            *scatter_buffers(*gain_tile, F32),
            dma_sems(80),
            dma_sems(3, RING),
            dma_sems(1),
            dma_sems(2, 12),
            dma_sems(2, 12),
        ],
        (values, weight, inputs, out_grad, gain_partial),
    )


def norm_scale(values):
    return lax.rsqrt(jnp.mean(values * values, axis=-1, keepdims=True) + NORM_EPS)


def norm_back(upstream, values, scales, gain_row):
    scaled_grad = upstream * gain_row
    return scales * scaled_grad - values * scales**3 * jnp.mean(
        scaled_grad * values, axis=-1, keepdims=True
    )


def doc_layout(lengths, group_size):
    positions = jnp.arange(group_size, dtype=jnp.int32)
    doc_ends = jnp.cumsum(lengths)
    passed = (positions[:, None] >= doc_ends[None, :]).astype(jnp.int32)
    segment = jnp.sum(passed, axis=-1)
    begins = jnp.sum(passed * lengths[None, :], axis=-1)
    return (segment, positions - begins)


def rope_tables(offsets):
    frequency = ROPE_BASE ** (-jnp.arange(0, HEAD_DIM, 2).astype(jnp.float32) / HEAD_DIM)
    angles = offsets.astype(jnp.float32)[:, None] * frequency[None, :]
    cosine, sine = jnp.cos(angles), jnp.sin(angles)
    return (
        jnp.concatenate([cosine, cosine], axis=-1),
        jnp.concatenate([sine, sine], axis=-1),
    )


def half_turn(values):
    middle = values.shape[-1] // 2
    return jnp.concatenate([-values[..., middle:], values[..., :middle]], axis=-1)


def rotate(values, cosine_table, sine_table):
    return values * cosine_table + half_turn(values) * sine_table


def unrotate(values, cosine_table, sine_table):
    return values * cosine_table - half_turn(values) * sine_table


def product(left, right):
    return jnp.dot(left, right, preferred_element_type=F32)


def row_product(left, right):
    return lax.dot_general(left, right, (((1,), (1,)), ((), ())), preferred_element_type=F32)


def col_product(left, right):
    return lax.dot_general(left, right, (((0,), (0,)), ((), ())), preferred_element_type=F32)


def adam_update(weights_old, first_old, second_old, gradient, rate, decay):
    first_new = BETA_ONE * first_old + (1.0 - BETA_ONE) * gradient
    second_new = BETA_TWO * second_old + (1.0 - BETA_TWO) * gradient * gradient
    ratio = (
        first_new
        / (1.0 - BETA_ONE**STEP)
        / (jnp.sqrt(second_new / (1.0 - BETA_TWO**STEP)) + ADAM_EPS)
    )
    return (first_new, second_new, weights_old - rate * (ratio + decay * weights_old))


def body(
    hidden_in,
    cotangent,
    doc_lengths,
    attn_weights,
    attn_first,
    attn_second,
    mlp_weights,
    mlp_first,
    mlp_second,
    gains,
    gain_first,
    gain_second,
):
    row_count, model_width = hidden_in.shape
    shard_rows = attn_weights.shape[1]
    heads_width = attn_weights.shape[2] // 2
    hidden_width = mlp_weights.shape[2] // 2
    token_count = 8 * row_count
    block_rows = token_count // 2
    head_count = heads_width // HEAD_DIM
    score_factor = HEAD_DIM ** (-0.5)
    yl, yh, core = (lax.axis_index(a) for a in ("yl", "yh", "c"))

    attn_halves = (
        attn_weights.astype(BF16)
        .reshape(4, shard_rows, 2, heads_width)
        .transpose(2, 1, 0, 3)
        .reshape(2, shard_rows, 4 * heads_width)
    )
    mlp_halves = mlp_weights.astype(BF16).reshape(3, shard_rows, 2, hidden_width).transpose(0, 2, 1, 3)
    mine = lax.dynamic_index_in_dim(mlp_halves, yl, 1, keepdims=False)
    yours = lax.dynamic_index_in_dim(mlp_halves, 1 - yl, 1, keepdims=False)
    arrived = lax.ppermute(yours, "yl", [(0, 1), (1, 0)])
    mlp_pair = jnp.stack(
        [jnp.where(yl == 0, mine, arrived), jnp.where(yl == 0, arrived, mine)], axis=1
    )
    mlp_all = lax.all_gather(mlp_pair.reshape(-1, hidden_width), ("x", "z"), tiled=True)
    mlp_all = mlp_all.reshape(16, 3, 2, shard_rows, hidden_width)
    gain_tile = jnp.pad(gains.astype(BF16).astype(F32), ((0, 4), (0, 128 - shard_rows)))
    doc_tile = jnp.pad(doc_lengths.astype(F32), ((0, 7), (0, 124)))
    every_input, attn_all, gain_all, doc_pair = call(
        first_kernel,
        0,
        (
            shape_of(2, 2, 2 * row_count, model_width),
            shape_of(2, RING, RING, shard_rows, 4 * heads_width),
            shape_of(2, RING, RING, 8, 128, dtype=F32),
            shape_of(2, 8, 128, dtype=F32),
        ),
        [ANYWHERE] * 4,
        (ANYWHERE, IN_VMEM, ANYWHERE, ANYWHERE),
        [
            dma_sems(112),
            dma_sems(RING, 4),
            dma_sems(2, RING, RING, 3),
            dma_sems(2, RING, RING, 3),
            dma_sems(4),
        ],
        (hidden_in, attn_halves, gain_tile, doc_tile),
    )
    attn_all = flat(attn_all)
    gain_full = gain_all[..., :4, :shard_rows].transpose(3, 0, 1, 2, 4).reshape(4, model_width)
    lengths = doc_pair[:, 0, :4].astype(jnp.int32)

    qkv = product(every_input.reshape(token_count, model_width), attn_all[:, : 3 * heads_width])
    queries, key_raw = qkv[:, :heads_width], qkv[:, heads_width : 2 * heads_width]
    value_side = qkv[:, 2 * heads_width :].astype(BF16)
    squares = jnp.stack([jnp.sum(queries * queries, axis=-1), jnp.sum(key_raw * key_raw, axis=-1)])
    totals = sum_over_eight(squares.reshape(-1, 128), 1).reshape(2, token_count)
    scales = lax.rsqrt(totals / model_width + NORM_EPS)
    query_scale, key_scale = scales[0][:, None], scales[1][:, None]
    first_column = (yh * 2 + core) * (2 * heads_width) + yl * heads_width
    query_gain = lax.dynamic_slice_in_dim(gain_full[0], first_column, heads_width)
    key_gain = lax.dynamic_slice_in_dim(gain_full[1], first_column, heads_width)

    segment, offsets = jax.vmap(lambda one: doc_layout(one, block_rows))(lengths)
    cosine_table, sine_table = rope_tables(offsets.reshape(-1))
    cosine_table = cosine_table.reshape(2, block_rows, HEAD_DIM)
    sine_table = sine_table.reshape(2, block_rows, HEAD_DIM)
    positions = jnp.arange(block_rows)
    allowed = (segment[:, :, None] == segment[:, None, :]) & (
        positions[None, None, :] <= positions[None, :, None]
    )

    def by_head(values):
        return jnp.stack(
            [
                values[:, h * HEAD_DIM : (h + 1) * HEAD_DIM].reshape(2, block_rows, HEAD_DIM)
                for h in range(head_count)
            ]
        )

    def by_token(values):
        return jnp.concatenate([v.reshape(token_count, HEAD_DIM) for v in values], axis=-1)

    query_rot = rotate(by_head(queries * query_scale * query_gain), cosine_table, sine_table).astype(BF16)
    key_rot = rotate(by_head(key_raw * key_scale * key_gain), cosine_table, sine_table).astype(BF16)
    value_heads = by_head(value_side)

    def scores_of():
        raw = jnp.einsum("hbqd,hbkd->hbqk", query_rot, key_rot, preferred_element_type=F32)
        return jnp.where(allowed[None], raw * score_factor, -1e30)

    scores = scores_of()
    maxima = jnp.max(scores, axis=-1, keepdims=True)
    exponent = jnp.exp(scores - maxima)
    normaliser = jnp.sum(exponent, axis=-1, keepdims=True)
    probs_low = (exponent / normaliser).astype(BF16)
    log_totals = maxima + jnp.log(normaliser)
    attended = by_token(
        jnp.einsum("hbqk,hbkd->hbqd", probs_low, value_heads, preferred_element_type=F32).astype(BF16)
    )

    def for_ring(values):
        return values.reshape(2, 2, 2 * row_count, -1)

    attended = for_ring(attended)
    attn_proj = project_out(attended, attn_all, 2)
    proj_scale = norm_scale(attn_proj)
    mixed = hidden_in.astype(F32) + attn_proj * proj_scale * gain_full[2]
    every_mixed, gate_proj, up_proj, hidden_act, down_proj = mlp_forward(mixed.astype(BF16), mlp_all, 3)
    down_scale = norm_scale(down_proj)
    hidden_out = (mixed + down_proj * down_scale * gain_full[3]).astype(BF16)

    upstream = cotangent.astype(F32)
    d_down = norm_back(upstream, down_proj, down_scale, gain_full[3]).astype(BF16)
    gain_mlp = jnp.sum(upstream * down_proj * down_scale, axis=0)
    d_mixed_sum, mlp_partial = mlp_backward(
        d_down, mlp_all, every_mixed, gate_proj, up_proj, hidden_act, 4
    )
    mlp_sum = lax.psum_scatter(
        mlp_partial.reshape(16 * 3 * 2, shard_rows, hidden_width),
        ("x", "z"),
        scatter_dimension=0,
        tiled=True,
    ).reshape(3, 2, shard_rows, hidden_width)
    d_mixed = upstream + d_mixed_sum
    gain_attn = jnp.sum(d_mixed * attn_proj * proj_scale, axis=0)
    d_proj = norm_back(d_mixed, attn_proj, proj_scale, gain_full[2]).astype(BF16)
    d_att, out_weight_grad = project_back(d_proj, attn_all, attended, 5)
    d_att = by_head(d_att.reshape(token_count, heads_width))

    attn_probs = jnp.exp(scores_of() - log_totals)
    d_probs = jnp.einsum("hbqd,hbkd->hbqk", d_att, value_heads, preferred_element_type=F32)
    row_dot = jnp.sum(attn_probs * d_probs, axis=-1, keepdims=True)
    d_scores = (attn_probs * (d_probs - row_dot) * score_factor).astype(BF16)
    d_query_rot = jnp.einsum("hbqk,hbkd->hbqd", d_scores, key_rot, preferred_element_type=F32)
    d_key_rot = jnp.einsum("hbqk,hbqd->hbkd", d_scores, query_rot, preferred_element_type=F32)
    d_value = by_token(
        jnp.einsum(
            "hbqk,hbqd->hbkd", attn_probs.astype(BF16), d_att, preferred_element_type=F32
        ).astype(BF16)
    )
    d_query_norm = by_token(unrotate(d_query_rot, cosine_table, sine_table))
    d_key_norm = by_token(unrotate(d_key_rot, cosine_table, sine_table))
    gain_query = jnp.sum(d_query_norm * queries * query_scale, axis=0)
    gain_key = jnp.sum(d_key_norm * key_raw * key_scale, axis=0)
    query_back = d_query_norm * query_gain
    key_back = d_key_norm * key_gain
    gain_heads = lax.dynamic_update_slice(
        jnp.zeros((2, model_width), F32), jnp.stack([gain_query, gain_key]), (0, first_column)
    )
    row_sums = jnp.stack([jnp.sum(query_back * queries, axis=-1), jnp.sum(key_back * key_raw, axis=-1)])
    together = jnp.concatenate(
        [row_sums.reshape(-1), gain_heads.reshape(-1), gain_attn, gain_mlp]
    ).reshape(-1, 128)
    together = sum_over_eight(together, 6).reshape(-1)
    row_sums = together[: 2 * token_count].reshape(2, token_count)
    gain_sums = together[2 * token_count :].reshape(4, model_width)
    d_query = (
        query_scale * query_back - queries * query_scale**3 * row_sums[0][:, None] / model_width
    ).astype(BF16)
    d_key = (
        key_scale * key_back - key_raw * key_scale**3 * row_sums[1][:, None] / model_width
    ).astype(BF16)
    d_qkv = jnp.concatenate([d_query, d_key, d_value], axis=-1)
    gain_partial = jnp.pad(
        gain_sums.reshape(4, 2, RING, RING, shard_rows).transpose(1, 2, 3, 0, 4),
        ((0, 0), (0, 0), (0, 0), (0, 4), (0, 128 - shard_rows)),
    )
    input_sum, attn_sum, gain_sum = last_sums(
        for_ring(d_qkv), attn_all, every_input, out_weight_grad, gain_partial, 7
    )
    input_grad = d_mixed + input_sum

    own_half = lax.dynamic_index_in_dim(mlp_sum, yl, 1, keepdims=False)
    other_half = lax.ppermute(
        lax.dynamic_index_in_dim(mlp_sum, 1 - yl, 1, keepdims=False), "yl", [(0, 1), (1, 0)]
    )
    mlp_sums = jnp.stack([jnp.where(yl == 0, own_half, other_half), jnp.where(yl == 0, other_half, own_half)], axis=1)
    attn_grad = (
        attn_sum.astype(F32)
        .reshape(2, shard_rows, 4, heads_width)
        .transpose(2, 1, 0, 3)
        .reshape(4, shard_rows, 2 * heads_width)
    )
    mlp_grad = jnp.stack(
        [
            s.astype(F32).transpose(1, 0, 2).reshape(shard_rows, 2 * hidden_width)
            for s in mlp_sums
        ]
    )
    gain_grad = gain_sum[:4, :shard_rows]
    attn_first_new, attn_second_new, attn_new = adam_update(
        attn_weights, attn_first, attn_second, attn_grad, WEIGHT_RATE, WEIGHT_DECAY
    )
    mlp_first_new, mlp_second_new, mlp_new = adam_update(
        mlp_weights, mlp_first, mlp_second, mlp_grad, WEIGHT_RATE, WEIGHT_DECAY
    )
    gain_first_new, gain_second_new, gain_new = adam_update(
        gains, gain_first, gain_second, gain_grad, GAIN_RATE, 0.0
    )
    return (
        hidden_out,
        input_grad,
        attn_grad,
        attn_first_new,
        attn_second_new,
        attn_new,
        mlp_grad,
        mlp_first_new,
        mlp_second_new,
        mlp_new,
        gain_grad,
        gain_first_new,
        gain_second_new,
        gain_new,
    )


def solution(mesh):
    split = Mesh(mesh.devices.reshape(2, 4, 4, 2, 2), EVERY)
    tokens, shards, rows = P(EVERY, None), P(None, DP, TENSOR), P(None, DP)
    return jax.shard_map(
        body,
        mesh=split,
        in_specs=(tokens, tokens, P(DP, None), *[shards] * 6, *[rows] * 3),
        out_specs=(tokens, tokens, *[shards] * 8, *[rows] * 4),
        check_vma=False,
    )
```

```python
import functools

import jax
import jax.numpy as jnp
from jax import lax
from jax.experimental import pallas as pl
from jax.experimental.pallas import tpu as pltpu
from jax.sharding import Mesh
from jax.sharding import PartitionSpec as P

HEAD_DIM = 128
STEP = 10
DP = ("yl", "x", "z")
TENSOR = ("yh", "c")
EVERY = ("yl", "x", "z", "yh", "c")
RING = 4
MESH = pl.DeviceIdType.MESH

NORM_EPS = 1e-06
ROPE_BASE = 500000.0
BETA_ONE = 0.9
BETA_TWO = 0.95
ADAM_EPS = 1e-08
WEIGHT_RATE = 0.03
GAIN_RATE = 1.0
WEIGHT_DECAY = 0.1

BF16 = jnp.bfloat16
F32 = jnp.float32
IN_VMEM = pl.BlockSpec(memory_space=pltpu.VMEM)
ANYWHERE = pl.BlockSpec(memory_space=pl.ANY)
VMEM_LIMIT = 58 * 1024 * 1024


class Place:
    def __init__(self):
        self.x, self.z, self.c = (lax.axis_index(a) for a in ("x", "z", "c"))
        self.yl, self.yh = (lax.axis_index(a) for a in ("yl", "yh"))
        self.y = self.yh * 2 + self.yl

    def at(self, axis, step):
        if axis == "y":
            there = (self.y + step + RING) % RING
            return {"yl": there % 2, "yh": there // 2}
        if axis == "c":
            return {"c": 1 - self.c}
        return {axis: (getattr(self, axis) + step + RING) % RING}

    def shift(self, axis, step):
        return (getattr(self, axis) + step + RING) % RING


def greet(devices):
    barrier = pltpu.get_barrier_semaphore()
    for device in devices:
        pl.semaphore_signal(barrier, inc=1, device_id=device, device_id_type=MESH)
    pl.semaphore_wait(barrier, len(devices))


def greet_all(place, axes):
    devices = []
    for axis in axes:
        devices += [place.at(axis, 1)] if axis == "c" else [place.at(axis, 1), place.at(axis, -1)]
    greet(devices)


class Sender:
    def __init__(self, sems):
        self.sems, self.open = sems, []

    def push(self, src, dst, recv_sem, device):
        copy = pltpu.make_async_remote_copy(
            src_ref=src,
            dst_ref=dst,
            send_sem=self.sems.at[len(self.open)],
            recv_sem=recv_sem,
            device_id=device,
            device_id_type=MESH,
        )
        copy.start()
        self.open.append(copy.wait_send)
        return len(self.open) - 1

    def settle(self, numbers):
        for number in numbers:
            self.open[number]()
            self.open[number] = lambda: None

    def keep(self, src, dst):
        copy = pltpu.make_async_copy(src, dst, self.sems.at[len(self.open)])
        copy.start()
        self.open.append(copy.wait)

    def keep_first(self, src, dst):
        copy = pltpu.make_async_copy(src, dst, self.sems.at[len(self.open)])
        copy.start()
        self.open.append(lambda: None)
        return copy

    def arrived(self, dst, recv_sem, device):
        pltpu.make_async_remote_copy(
            src_ref=dst,
            dst_ref=dst,
            send_sem=self.sems.at[0],
            recv_sem=recv_sem,
            device_id=device,
            device_id_type=MESH,
        ).wait_recv()

    def finish(self):
        for wait in self.open:
            wait()


def take_turns(tasks):
    tasks = list(tasks)
    while tasks:
        for task in list(tasks):
            if next(task, "done") == "done":
                tasks.remove(task)


WHOLE, LOW, HIGH = 0, 1, 2
PIECES = 2


def part_of(ref, part, cut):
    rows = ref.shape[-2]
    if part == WHOLE:
        return ref
    return ref.at[pl.ds(0, cut)] if part == LOW else ref.at[pl.ds(cut, rows - cut)]


def plane_gather(place, sender, sems, out, cut):
    rows = out.shape[-2]
    axes = (("x", "z"), ("z", "x"))

    def piece(half, dp, dq):
        p, q = (place.shift(a, d) for a, d in zip(axes[half], (dp, dq)))
        return out.at[half, p, q] if half == 0 else out.at[half, q, p]

    def parts(part):
        if part == WHOLE:
            return True
        return cut > 0 if part == LOW else cut < rows

    def send(half, dp, dq, part, along, step):
        if parts(part):
            ref = part_of(piece(half, dp, dq), part, cut)
            sp, sq = ((dp - step) % RING, dq % RING) if along == 0 else (dp % RING, (dq - step) % RING)
            sender.push(ref, ref, sems.at[half, sp, sq, part], place.at(axes[half][along], step))

    def wait(half, dp, dq, part):
        if parts(part):
            ref = part_of(piece(half, dp, dq), part, cut)
            sender.arrived(ref, sems.at[half, dp % RING, dq % RING, part], place.at("x", 1))

    both = (0, 1)
    for half in both:
        for step in (1, -1):
            send(half, 0, 0, WHOLE, 0, step)
    for half in both:
        for step in (1, -1):
            send(half, 0, 0, WHOLE, 1, step)
    yield
    for step, part in ((1, LOW), (-1, HIGH)):
        for half in both:
            wait(half, -step, 0, WHOLE)
            send(half, -step, 0, part, 0, step)
            for side in (1, -1):
                send(half, -step, 0, WHOLE, 1, side)
    yield
    for half in both:
        for step, part in ((1, LOW), (-1, HIGH)):
            wait(half, 0, -step, WHOLE)
            send(half, 0, -step, part, 1, step)
    yield
    for half in both:
        wait(half, 2, 0, LOW)
        wait(half, 2, 0, HIGH)
        for side in (1, -1):
            send(half, 2, 0, WHOLE, 1, side)
    yield
    for dp in (-1, 1, 2):
        for half in both:
            for step, part in ((1, LOW), (-1, HIGH)):
                wait(half, dp, -step, WHOLE)
                send(half, dp, -step, part, 1, step)
        yield
    for dp in (0, -1, 1, 2):
        for half in both:
            wait(half, dp, 2, LOW)
            wait(half, dp, 2, HIGH)


class RingGather:
    def __init__(self, place, sender, sems, own, out):
        self.place, self.sender, self.sems, self.own, self.out = place, sender, sems, own, out
        self.rows = own.shape[0]
        self.other = place.at("c", 1)
        self.forwarded = []

    def piece(self, dy, core, part=WHOLE):
        y = self.place.shift("y", dy)
        half = self.rows // 2
        start, size = {WHOLE: (0, self.rows), LOW: (0, half), HIGH: (half, half)}[part]
        return self.out.at[y % 2, y // 2, pl.ds(pl.multiple_of(core * self.rows + start, 16), size)]

    def begin(self):
        place, mine = self.place, self.piece(0, self.place.c)
        for step in (1, -1):
            self.sender.push(self.own, mine, self.sems.at[(-step) % RING, WHOLE], place.at("y", step))
        self.sender.push(self.own, mine, self.sems.at[0, 3], self.other)
        self.kept = self.sender.keep_first(self.own, mine)

    def relay(self):
        for step, part in ((1, LOW), (-1, HIGH)):
            ref = self.piece(-step, self.place.c)
            self.sender.arrived(ref, self.sems.at[(-step) % RING, WHOLE], self.other)
            half = self.piece(-step, self.place.c, part)
            self.forwarded += [
                self.sender.push(half, half, self.sems.at[2, part], self.place.at("y", step)),
                self.sender.push(ref, ref, self.sems.at[(-step) % RING, 3], self.other),
            ]

    def relay_far(self):
        for part in (LOW, HIGH):
            self.sender.arrived(self.piece(2, self.place.c, part), self.sems.at[2, part], self.other)
        ref = self.piece(2, self.place.c)
        self.forwarded += [self.sender.push(ref, ref, self.sems.at[2, 3], self.other)]

    def ready(self, dy):
        if dy == 0:
            self.kept.wait()
        self.sender.arrived(self.piece(dy, 1 - self.place.c), self.sems.at[dy % RING, 3], self.other)


def ring_gather(place, sender, sems, own, out):
    gather = RingGather(place, sender, sems, own, out)
    gather.begin()
    yield
    gather.relay()
    yield
    gather.relay_far()
    yield
    for dy in (0, 1, -1, 2):
        gather.ready(dy)


def add_rows(out, terms, rows):
    def step(i, carry):
        window = pl.ds(pl.multiple_of(i * 16, 16), 16)
        total = terms[0][window, :].astype(F32)
        for term in terms[1:]:
            total = total + term[window, :].astype(F32)
        out[window, :] = total.astype(out.dtype)
        return carry

    lax.fori_loop(0, rows // 16, step, 0)


class RingSum:
    def __init__(self, place, sender, sems, partial, kept, from_core, hop, last):
        self.place, self.sender, self.sems, self.partial = place, sender, sems, partial
        self.kept, self.from_core, self.hop, self.last = kept, from_core, hop, last
        self.rows = kept.shape[1]
        self.low, self.high = pl.ds(0, self.rows // 2), pl.ds(self.rows // 2, self.rows // 2)
        self.other = place.at("c", 1)

    def mine(self, dy, core):
        y = self.place.shift("y", dy)
        return self.partial.at[y % 2, y // 2, pl.ds(pl.multiple_of(core * self.rows, 16), self.rows)]

    def offer(self, dy):
        slot = dy % RING
        self.sender.push(
            self.mine(dy, 1 - self.place.c), self.from_core.at[slot], self.sems.at[0, slot], self.other
        )

    def pieces(self):
        columns = self.kept.shape[2]
        return [pl.ds(p * columns // PIECES, columns // PIECES) for p in range(PIECES)]

    def collect(self, dy):
        slot = dy % RING
        kept, low, high = self.kept.at[slot], self.low, self.high
        self.sender.arrived(self.from_core.at[slot], self.sems.at[0, slot], self.other)
        if dy == 0:
            return
        up, down = self.place.at("y", 1), self.place.at("y", -1)
        mine = self.mine(dy, self.place.c)
        if dy == 2:
            for p, columns in enumerate(self.pieces()):
                add_rows(kept.at[:, columns], (mine.at[:, columns], self.from_core.at[slot, :, columns]), self.rows)
                self.sender.push(kept.at[low, columns], self.hop.at[0, :, columns], self.sems.at[1, p], up)
                self.sender.push(
                    kept.at[high, columns], self.hop.at[1, :, columns], self.sems.at[1, PIECES + p], down
                )
            return
        add_rows(kept, (mine, self.from_core.at[slot]), self.rows)
        if dy == 1:
            self.sender.push(kept.at[high], self.last.at[0, high], self.sems.at[2, 1], up)
        else:
            self.sender.push(kept.at[low], self.last.at[1, low], self.sems.at[2, 2], down)

    def relay(self):
        for p, columns in enumerate(self.pieces()):
            for k, slot, part, step in ((0, 1, self.low, 1), (1, 3, self.high, -1)):
                number = k * PIECES + p
                self.sender.arrived(self.hop.at[k, :, columns], self.sems.at[1, number], self.other)
                rows = self.kept.at[slot, part, columns]
                add_rows(rows, (rows, self.hop.at[k, :, columns]), self.rows // 2)
                self.sender.push(
                    rows, self.last.at[k, part, columns], self.sems.at[3, number], self.place.at("y", step)
                )

    def finish(self, out):
        self.sender.arrived(self.last.at[0, self.high], self.sems.at[2, 1], self.other)
        self.sender.arrived(self.last.at[1, self.low], self.sems.at[2, 2], self.other)
        mine = self.mine(0, self.place.c)
        for p, columns in enumerate(self.pieces()):
            for k, part in ((0, self.low), (1, self.high)):
                self.sender.arrived(
                    self.last.at[k, part, columns], self.sems.at[3, k * PIECES + p], self.other
                )
            terms = (mine, self.from_core.at[0], self.last.at[0], self.last.at[1])
            add_rows(out.at[:, columns], [term.at[:, columns] for term in terms], self.rows)


def plane_scatter(place, sender, sems, partial, done, cut, bufs):
    rows = partial.shape[-2]
    hop, last, middle, hop2, last2 = bufs
    low, high = pl.ds(0, cut), pl.ds(cut, rows - cut)
    axes = (("z", "x"), ("x", "z"))
    two_parts = cut < rows
    both = (0, 1)
    other = place.at("x", 1)

    def row(half, du, window):
        u = place.shift(axes[half][0], du)
        return partial.at[half, :, u, window] if half == 0 else partial.at[half, u, :, window]

    def line(half, du, v):
        u = place.shift(axes[half][0], du)
        return partial.at[half, v, u] if half == 0 else partial.at[half, u, v]

    def add(out, terms, count):
        if count % 16:
            total = terms[0][...].astype(F32)
            for term in terms[1:]:
                total = total + term[...].astype(F32)
            out[...] = total.astype(out.dtype)
        else:
            add_rows(out, terms, count)

    for half in both:
        u = axes[half][0]
        sender.push(row(half, 2, low), hop.at[half, 0], sems.at[half, 0], place.at(u, 1))
        if two_parts:
            sender.push(row(half, 2, high), hop.at[half, 1], sems.at[half, 1], place.at(u, -1))
    for half in both:
        u = axes[half][0]
        if two_parts:
            sender.push(row(half, 1, high), last.at[half, 0, :, high], sems.at[half, 2], place.at(u, 1))
        sender.push(row(half, -1, low), last.at[half, 1, :, low], sems.at[half, 3], place.at(u, -1))
    yield
    for half in both:
        u = axes[half][0]
        sender.arrived(hop.at[half, 0], sems.at[half, 0], other)
        for v in range(RING):
            add(hop.at[half, 0, v], (line(half, 1, v).at[low], hop.at[half, 0, v]), cut)
        sender.push(hop.at[half, 0], last.at[half, 0, :, low], sems.at[half, 4], place.at(u, 1))
        if two_parts:
            sender.arrived(hop.at[half, 1], sems.at[half, 1], other)
            for v in range(RING):
                add(
                    hop.at[half, 1, v],
                    (line(half, -1, v).at[high], hop.at[half, 1, v]),
                    rows - cut,
                )
            sender.push(
                hop.at[half, 1], last.at[half, 1, :, high], sems.at[half, 5], place.at(u, -1)
            )
    yield
    for half in both:
        v_axis = axes[half][1]
        if two_parts:
            sender.arrived(last.at[half, 0, :, high], sems.at[half, 2], other)
        sender.arrived(last.at[half, 1, :, low], sems.at[half, 3], other)
        sender.arrived(last.at[half, 0, :, low], sems.at[half, 4], other)
        if two_parts:
            sender.arrived(last.at[half, 1, :, high], sems.at[half, 5], other)
        for dv in (2, 1, -1, 0):
            v = place.shift(v_axis, dv)
            terms = (line(half, 0, v), last.at[half, 0, v], last.at[half, 1, v])
            add(middle.at[half, dv % RING], terms, rows)
            if dv == 2:
                sender.push(
                    middle.at[half, 2, low], hop2.at[half, 0], sems.at[half, 6], place.at(v_axis, 1)
                )
                if two_parts:
                    sender.push(
                        middle.at[half, 2, high],
                        hop2.at[half, 1],
                        sems.at[half, 7],
                        place.at(v_axis, -1),
                    )
            elif dv == 1 and two_parts:
                sender.push(
                    middle.at[half, 1, high], last2.at[half, 0, high], sems.at[half, 8], place.at(v_axis, 1)
                )
            elif dv == -1:
                sender.push(
                    middle.at[half, 3, low], last2.at[half, 1, low], sems.at[half, 9], place.at(v_axis, -1)
                )
    yield
    for half in both:
        v_axis = axes[half][1]
        sender.arrived(hop2.at[half, 0], sems.at[half, 6], other)
        add(hop2.at[half, 0], (middle.at[half, 1, low], hop2.at[half, 0]), cut)
        sender.push(
            hop2.at[half, 0], last2.at[half, 0, low], sems.at[half, 10], place.at(v_axis, 1)
        )
        if two_parts:
            sender.arrived(hop2.at[half, 1], sems.at[half, 7], other)
            add(hop2.at[half, 1], (middle.at[half, 3, high], hop2.at[half, 1]), rows - cut)
            sender.push(
                hop2.at[half, 1], last2.at[half, 1, high], sems.at[half, 11], place.at(v_axis, -1)
            )
    yield
    for half in both:
        if two_parts:
            sender.arrived(last2.at[half, 0, high], sems.at[half, 8], other)
        sender.arrived(last2.at[half, 1, low], sems.at[half, 9], other)
        sender.arrived(last2.at[half, 0, low], sems.at[half, 10], other)
        if two_parts:
            sender.arrived(last2.at[half, 1, high], sems.at[half, 11], other)
        add(done.at[half], (middle.at[half, 0], last2.at[half, 0], last2.at[half, 1]), rows)


def scatter_buffers(rows, columns, dtype):
    cut = rows // 2 if dtype == BF16 else rows
    return [
        pltpu.VMEM((2, 2, RING, cut, columns), dtype),
        pltpu.VMEM((2, 2, RING, rows, columns), dtype),
        pltpu.VMEM((2, RING, rows, columns), dtype),
        pltpu.VMEM((2, 2, cut, columns), dtype),
        pltpu.VMEM((2, 2, rows, columns), dtype),
    ]


def ring_buffers(rows, columns):
    return [
        pltpu.VMEM((RING, rows, columns), BF16),
        pltpu.VMEM((RING, rows, columns), BF16),
        pltpu.VMEM((2, rows // 2, columns), BF16),
        pltpu.VMEM((2, rows, columns), BF16),
    ]


def dma_sems(*shape):
    return pltpu.SemaphoreType.DMA(shape)


def shape_of(*shape, dtype=BF16):
    return jax.ShapeDtypeStruct(shape, dtype)


def call(kernel, number, out_shape, in_specs, out_specs, scratch, args):
    return pl.pallas_call(
        kernel,
        out_shape=out_shape,
        in_specs=in_specs,
        out_specs=out_specs,
        scratch_shapes=scratch,
        compiler_params=pltpu.CompilerParams(
            collective_id=number, has_side_effects=True, vmem_limit_bytes=VMEM_LIMIT
        ),
    )(*args)


def first_kernel(hidden, attn, gain, hidden_all, attn_all, gain_all, sends, ring, plane, plane_gain, swap):
    place = Place()
    greet_all(place, ("x", "z", "y", "c"))
    sender = Sender(sends)
    partner = {"yl": 1 - place.yl}
    me, you = place.yl, 1 - place.yl
    own_attn = attn_all.at[:, place.x, place.z]
    own_gain = gain_all.at[:, place.x, place.z]
    sender.push(attn.at[you], own_attn.at[me], swap.at[0], partner)
    sender.push(gain, own_gain.at[me], swap.at[1], partner)
    first = sender.keep_first(attn.at[me], own_attn.at[me])
    second = sender.keep_first(gain, own_gain.at[me])
    gather = ring_gather(place, sender, ring, hidden, hidden_all)
    next(gather)
    first.wait()
    second.wait()
    sender.arrived(own_attn.at[you], swap.at[0], partner)
    sender.arrived(own_gain.at[you], swap.at[1], partner)
    planes = plane_gather(place, sender, plane, attn_all, attn_all.shape[-2] // 2)
    gains = plane_gather(place, sender, plane_gain, gain_all, gain_all.shape[-2])
    next(planes)
    next(gains)
    take_turns((gains, planes, gather))
    sender.finish()


NN = (((1,), (0,)), ((), ()))
NT = (((1,), (1,)), ((), ()))
TN = (((0,), (0,)), ((), ()))


def dot(left, right, dims=NN):
    return lax.dot_general(left, right, dims, preferred_element_type=F32)


def in_tiles(width, tile, work):
    for n in range(width // tile):
        work(pl.ds(n * tile, tile))


def refs_of(refs, *counts):
    refs, out = list(refs), []
    for n in counts:
        out.append(refs[:n])
        del refs[:n]
    return out


def load_weights(sender, source, targets):
    copies = []
    for k, target in targets:
        for yl in range(2):
            copies.append(sender.keep_first(source.at[:, k, yl], target.at[yl]))
    return copies


def rows_of(weight, window):
    piece = weight.shape[2]
    per_half = weight.shape[1] * piece
    start, size = window.start, window.size
    block = weight[start // per_half, pl.ds((start % per_half) // piece, size // piece), :, :]
    return block.reshape(size, weight.shape[3])


def columns_of(weight, window):
    block = weight[:, :, :, window]
    return block.reshape(-1, window.size)


def mlp_forward_kernel(own, weights, x_out, gate_out, up_out, act_out, down_out, *refs):
    (x_all, w_gate, w_up, w_down, gate, up, act, partial), ring, (sends, gather_sems, sum_sems) = refs_of(
        refs, 8, 4, 3
    )
    place = Place()
    sender = Sender(sends)
    loads = load_weights(sender, weights, ((0, w_gate), (1, w_up), (2, w_down)))
    greet_all(place, ("y", "c"))
    gather = RingGather(place, sender, gather_sems, own, x_all)
    total = RingSum(place, sender, sum_sems, partial, *ring)
    gather.begin()
    for copy in loads:
        copy.wait()
    tile = 512

    def compute(dy):
        gather.ready(dy)
        y = place.shift("y", dy)
        at = (y % 2, y // 2)

        def hidden(columns):
            rows = x_all[at]
            g = dot(rows, columns_of(w_gate, columns))
            u = dot(rows, columns_of(w_up, columns))
            here = (*at, slice(None), columns)
            gate[here], up[here] = g.astype(BF16), u.astype(BF16)
            act[here] = (g * jax.nn.sigmoid(g) * u).astype(BF16)

        in_tiles(act.shape[-1], tile, hidden)

        def down(columns):
            partial[(*at, slice(None), columns)] = dot(act[at], rows_of(w_down, columns), NT).astype(BF16)

        in_tiles(partial.shape[-1], tile, down)
        total.offer(dy)
        for values, out in ((x_all, x_out), (gate, gate_out), (up, up_out), (act, act_out)):
            sender.keep(values.at[at], out.at[at])

    compute(0)
    gather.relay()
    compute(1)
    gather.relay_far()
    compute(-1)
    total.collect(1)
    compute(2)
    total.collect(-1)
    total.collect(2)
    total.collect(0)
    total.relay()
    total.finish(down_out)
    sender.finish()


def mlp_forward(own, weights, number):
    rows, width = own.shape
    hidden = weights.shape[-1]
    tokens = (2, 2, 2 * rows)
    weight = pltpu.VMEM((2, 16, *weights.shape[-2:]), BF16)
    return call(
        mlp_forward_kernel,
        number,
        (
            shape_of(*tokens, width),
            shape_of(*tokens, hidden),
            shape_of(*tokens, hidden),
            shape_of(*tokens, hidden),
            shape_of(rows, width, dtype=F32),
        ),
        [ANYWHERE, ANYWHERE],
        (ANYWHERE, ANYWHERE, ANYWHERE, ANYWHERE, IN_VMEM),
        [
            pltpu.VMEM((*tokens, width), BF16),
            *[weight] * 3,
            *[pltpu.VMEM((*tokens, hidden), BF16)] * 3,
            pltpu.VMEM((*tokens, width), BF16),
            *ring_buffers(rows, width),
            dma_sems(56),
            dma_sems(RING, 4),
            dma_sems(4, RING),
        ],
        (own, weights),
    )


def mlp_backward_kernel(own, weights, x_in, gate_in, up_in, act_in, d_x_out, grads_out, down_out, *refs):
    (
        (d_all, w_gate, w_up, w_down, x_all, gate, up, act, d_gate, d_up, partial, tiles, down_partial),
        ring,
        buffers,
        (sends, gather_sems, sum_sems, tile_sems, plane),
    ) = refs_of(refs, 13, 4, 5, 5)
    place = Place()
    sender = Sender(sends)
    first = load_weights(sender, weights, ((2, w_down),))
    first += [sender.keep_first(gate_in, gate), sender.keep_first(up_in, up)]
    second = load_weights(sender, weights, ((0, w_gate), (1, w_up)))
    greet_all(place, ("x", "z", "y", "c"))
    gather = RingGather(place, sender, gather_sems, own, d_all)
    total = RingSum(place, sender, sum_sems, partial, *ring)
    gather.begin()
    third = [sender.keep_first(x_in, x_all), sender.keep_first(act_in, act)]
    for copy in first + second:
        copy.wait()
    tile = 512

    def compute(dy, wait=True):
        if wait:
            gather.ready(dy)
        y = place.shift("y", dy)
        at = (y % 2, y // 2)

        def hidden(columns):
            d_act = dot(d_all[at], columns_of(w_down, columns))
            here = (*at, slice(None), columns)
            g, u = gate[here].astype(F32), up[here].astype(F32)
            s = jax.nn.sigmoid(g)
            d_gate[here] = (d_act * u * s * (1.0 + g * (1.0 - s))).astype(BF16)
            d_up[here] = (d_act * g * s).astype(BF16)

        in_tiles(act.shape[-1], tile, hidden)

        def back(columns):
            value = dot(d_gate[at], rows_of(w_gate, columns), NT) + dot(d_up[at], rows_of(w_up, columns), NT)
            partial[(*at, slice(None), columns)] = value.astype(BF16)

        in_tiles(partial.shape[-1], tile, back)
        total.offer(dy)

    block = 4 * tiles.shape[3]

    def all_rows(ref, columns=slice(None)):
        value = ref[:, :, :, columns]
        return value.reshape(-1, value.shape[-1])

    def sent(slot, k, i):
        return pltpu.make_async_copy(
            tiles.at[slot, k], grads_out.at[k, i // RING, i % RING], tile_sems.at[slot, k]
        )

    def weight_grads(begin, end):
        def step(i, carry):
            slot = i % 2
            columns = pl.ds(pl.multiple_of(i * block, block), block)
            for k, right in enumerate((d_gate, d_up)):

                @pl.when(i >= 2)
                def _():
                    sent(slot, k, i - 2).wait()

                value = dot(all_rows(x_all, columns), all_rows(right), TN)
                tiles[slot, k] = value.astype(BF16).reshape(tiles.shape[2:])
                sent(slot, k, i).start()
            return carry

        lax.fori_loop(begin, end, step, 0)

    def down_grad(i, carry):
        columns = pl.ds(pl.multiple_of(i * block, block), block)
        value = dot(all_rows(d_all, columns), all_rows(act), TN).astype(BF16)
        down_partial[i // RING, i % RING] = value.reshape(down_partial.shape[2:])
        return carry

    compute(0)
    gather.relay()
    compute(1)
    gather.relay_far()
    compute(-1)
    total.collect(1)
    gather.ready(2)
    for copy in third:
        copy.wait()
    lax.fori_loop(0, 2 * RING, down_grad, 0)
    grads = plane_scatter(
        place, sender, plane, down_partial, down_out, down_partial.shape[3] // 2, buffers
    )
    next(grads)
    compute(2, False)
    total.collect(-1)
    next(grads)
    total.collect(2)
    total.collect(0)
    weight_grads(0, 3)
    total.relay()
    weight_grads(3, 6)
    next(grads)
    weight_grads(6, 8)
    next(grads)
    total.finish(d_x_out)
    take_turns((grads,))
    for i in (6, 7):
        for k in range(2):
            sent(i % 2, k, i).wait()
    sender.finish()


def mlp_backward(own, weights, x_all, gate, up, act, number):
    rows, width = own.shape
    piece, hidden = weights.shape[-2:]
    tokens = (2, 2, 2 * rows)
    weight = pltpu.VMEM((2, 16, piece, hidden), BF16)
    wide, narrow = pltpu.VMEM((*tokens, width), BF16), pltpu.VMEM((*tokens, hidden), BF16)
    return call(
        mlp_backward_kernel,
        number,
        (
            shape_of(rows, width, dtype=F32),
            shape_of(2, 2, RING, RING, piece, hidden),
            shape_of(2, piece, hidden),
        ),
        [ANYWHERE] * 6,
        (IN_VMEM, ANYWHERE, IN_VMEM),
        [
            wide,
            *[weight] * 3,
            wide,
            *[narrow] * 5,
            wide,
            pltpu.VMEM((2, 2, 4, piece, hidden), BF16),
            pltpu.VMEM((2, RING, RING, piece, hidden), BF16),
            *ring_buffers(rows, width),
            *scatter_buffers(piece, hidden, BF16),
            dma_sems(72),
            dma_sems(RING, 4),
            dma_sems(4, RING),
            dma_sems(2, 2),
            dma_sems(2, 12),
        ],
        (own, weights, x_all, gate, up, act),
    )


def ring_product(place, total, values, weight, partial, others, before_near=lambda: None):
    def compute(dy):
        y = place.shift("y", dy)
        at = (y % 2, y // 2)

        def tile(columns):
            partial[(*at, slice(None), columns)] = dot(values[at], weight[columns, :], NT).astype(BF16)

        in_tiles(partial.shape[-1], 512, tile)
        total.offer(dy)

    compute(2)
    before_near()
    compute(1)
    total.collect(2)
    compute(-1)
    total.collect(1)
    compute(0)
    total.collect(-1)
    total.collect(0)
    for task in others:
        next(task)
    total.relay()


def flat(weight):
    return weight.reshape(-1, weight.shape[-1])


def exact(left, right, dims):
    return lax.dot_general(
        left, right, dims, precision=lax.Precision.HIGHEST, preferred_element_type=F32
    )


def half_roll(values):
    return pltpu.roll(values, HEAD_DIM // 2, 1)


class Octet:
    peers = [(dy, dc) for dy in (0, 1, 3, 2) for dc in (0, 1) if dy or dc]

    def __init__(self, place, sender, own, slots, sems):
        self.place, self.sender, self.own, self.slots, self.sems = place, sender, own, slots, sems

    @staticmethod
    def device(place, dy, dc):
        y = place.shift("y", dy)
        return {"yl": y % 2, "yh": y // 2, "c": (place.c + dc) % 2}

    def send(self):
        for dy, dc in self.peers:
            slot = ((RING - dy) % RING) * 2 + dc
            device = self.device(self.place, dy, dc)
            self.sender.push(self.own, self.slots.at[slot], self.sems.at[slot], device)

    def total(self):
        for dy, dc in self.peers:
            slot = dy * 2 + dc
            self.sender.arrived(self.slots.at[slot], self.sems.at[slot], self.device(self.place, dy, dc))
        value = self.own[...]
        for dy, dc in self.peers:
            value = value + self.slots[dy * 2 + dc]
        return value


def one_hot_rows(k):
    return (lax.broadcasted_iota(jnp.int32, (8, HEAD_DIM), 0) == k).astype(F32)


def masked(scores, starts, i):
    tile, count = scores.shape
    keys = lax.broadcasted_iota(jnp.int32, (tile, count), 1)
    queries = lax.broadcasted_iota(jnp.int32, (tile, count), 0) + i * tile
    return jnp.where((keys >= starts) & (keys <= queries), scores, -1e30)


def softmax(scores):
    exponent = jnp.exp(scores - jnp.max(scores, axis=-1, keepdims=True))
    return exponent / jnp.sum(exponent, axis=-1, keepdims=True)


def attention_forward_kernel(
    inputs, weight, cosine, sine, starts, head_gains, proj_out, raw_out, rot_out, value_out, scale_out,
    attended_out, *refs
):
    (
        (x_all, own_weight, raw, rot, values, scales, attended, partial, sums, slots),
        ring,
        (sends, sum_sems, octet_sems),
    ) = refs_of(refs, 10, 4, 3)
    place = Place()
    sender = Sender(sends)
    loads = [sender.keep_first(weight, own_weight), sender.keep_first(inputs, x_all)]
    _, heads, _, block_rows, _ = raw.shape
    inner = heads * HEAD_DIM
    tile = block_rows // 2
    greet([Octet.device(place, *peer) for peer in Octet.peers])
    total = RingSum(place, sender, sum_sems, partial, *ring)
    ones = [one_hot_rows(k) for k in range(2)]
    for load in loads:
        load.wait()

    def project(t, carry):
        a, b = t // 2, t % 2
        window = pl.ds(pl.multiple_of(b * tile, tile), tile)
        value = dot(x_all[a, b], own_weight[:, pl.ds(0, 2 * inner)])
        row_sums = jnp.zeros((8, tile), F32)
        for k in range(2):
            for h in range(heads):
                column = k * inner + h * HEAD_DIM
                part = value[:, column : column + HEAD_DIM]
                raw[k, h, a, window, :] = part
                row_sums = row_sums + exact(ones[k], part * part, NT)
        sums[:, pl.ds(pl.multiple_of(t * tile, tile), tile)] = row_sums
        return carry

    def project_value(t, carry):
        a, b = t // 2, t % 2
        window = pl.ds(pl.multiple_of(b * tile, tile), tile)
        value = dot(x_all[a, b], own_weight[:, pl.ds(2 * inner, inner)]).astype(BF16)
        for h in range(heads):
            values[h, a, window, :] = value[:, h * HEAD_DIM : (h + 1) * HEAD_DIM]
        return carry

    lax.fori_loop(0, 4, project, 0)
    octet = Octet(place, sender, sums, slots, octet_sems)
    octet.send()
    sender.keep(raw, raw_out)
    lax.fori_loop(0, 4, project_value, 0)
    sender.keep(values, value_out)
    row_scales = lax.rsqrt(octet.total() / x_all.shape[3] + NORM_EPS)
    for b in range(2):
        for k in range(2):
            scale = exact(row_scales[:, b * block_rows : (b + 1) * block_rows], ones[k], TN)
            scales[k, b] = scale
            for h in range(heads):
                lanes = slice(h * HEAD_DIM, (h + 1) * HEAD_DIM)
                value = raw[k, h, b] * scale * head_gains[k : k + 1, lanes]
                rot[k, h, b] = (value * cosine[b] + half_roll(value) * sine[b]).astype(BF16)
    sender.keep(scales, scale_out)
    sender.keep(rot, rot_out)

    def attention(b):
        for h in range(heads):
            key, value = rot[1, h, b], values[h, b]
            for i in range(2):
                window, count = pl.ds(i * tile, tile), (i + 1) * tile
                scores = dot(rot[0, h, b, window, :], key[:count], NT) * HEAD_DIM ** (-0.5)
                probs = softmax(masked(scores, starts[b, window, 0:1], i)).astype(BF16)
                attended[b, i, :, pl.ds(h * HEAD_DIM, HEAD_DIM)] = dot(probs, value[:count]).astype(BF16)

    attention(place.yl)
    out_weight = own_weight.at[:, pl.ds(3 * inner, inner)]
    ring_product(
        place, total, attended, out_weight, partial, (), lambda: attention(1 - place.yl)
    )
    sender.keep(attended, attended_out)
    total.finish(proj_out)
    sender.finish()


def attention_forward(number, inputs, weight, cosine, sine, starts, head_gains):
    _, _, pair_rows, width = inputs.shape
    inner = weight.shape[1] // 4
    heads = inner // HEAD_DIM
    raw, rot = (2, heads, 2, 2 * pair_rows, HEAD_DIM), (2, heads, 2, 2 * pair_rows, HEAD_DIM)
    values, scales, attended = rot[1:], (2, 2, 2 * pair_rows, HEAD_DIM), (2, 2, pair_rows, inner)
    return call(
        attention_forward_kernel,
        number,
        (
            shape_of(pair_rows // 2, width, dtype=F32),
            shape_of(*raw, dtype=F32),
            shape_of(*rot),
            shape_of(*values),
            shape_of(*scales, dtype=F32),
            shape_of(*attended),
        ),
        [ANYWHERE, ANYWHERE] + [IN_VMEM] * 4,
        (IN_VMEM,) + (ANYWHERE,) * 5,
        [
            pltpu.VMEM(inputs.shape, BF16),
            pltpu.VMEM(weight.shape, BF16),
            pltpu.VMEM(raw, F32),
            pltpu.VMEM(rot, BF16),
            pltpu.VMEM(values, BF16),
            pltpu.VMEM(scales, F32),
            pltpu.VMEM(attended, BF16),
            pltpu.VMEM(inputs.shape, BF16),
            pltpu.VMEM((8, 4 * pair_rows), F32),
            pltpu.VMEM((8, 8, 4 * pair_rows), F32),
            *ring_buffers(pair_rows // 2, width),
            dma_sems(48),
            dma_sems(4, RING),
            dma_sems(8),
        ],
        (inputs, weight, cosine, sine, starts, head_gains),
    )


def attention_backward_kernel(
    own, weight, attended, inputs, mlp_in, down, raw_all, rot, values, scales, cosines, sines, starts,
    head_gains, token_gains, out, attn_out, gain_out, mlp_out, *refs
):
    (
        (shared, own_weight, attn_partial, mlp_partial, d_att, back, d_qkv, sums, slots),
        (gain_partial, gain_rows, gain_slots, attn_done, gain_done, mlp_done),
        ring,
        buffers,
        gate_buffers,
        up_buffers,
        gain_buffers,
        (sends, gather_sems, sum_sems, octet_sems, gain_sems, swap, plane, gain_plane, gate_plane, up_plane),
    ) = refs_of(refs, 9, 6, 4, 5, 5, 5, 5, 10)
    d_all = x_all = partial = shared
    place = Place()
    sender = Sender(sends)
    _, heads, _, block_rows, _ = rot.shape
    width = d_qkv.shape[-1]
    inner = heads * HEAD_DIM
    rows = attn_partial.shape[3]
    block = RING * rows
    mlp_loads = [sender.keep_first(mlp_in.at[k], mlp_partial.at[k]) for k in range(2)]
    load = sender.keep_first(weight, own_weight)
    partner = {"yl": 1 - place.yl}
    me, you = place.yl, 1 - place.yl
    near = [place.at(axis, step) for axis in ("x", "z") for step in (1, -1)]
    greet(near + [Octet.device(place, *peer) for peer in Octet.peers])
    gather = RingGather(place, sender, gather_sems, own, d_all)
    total = RingSum(place, sender, sum_sems, partial, *ring)
    gather.begin()
    sender.push(down.at[you], mlp_out.at[2, me], swap.at[3], partner)
    sender.keep(down.at[me], mlp_out.at[2, me])
    mlp = []
    for k, (sems, bufs) in enumerate(((gate_plane, gate_buffers), (up_plane, up_buffers))):
        mlp_loads[k].wait()
        task = plane_scatter(place, sender, sems, mlp_partial.at[k], mlp_done.at[k], rows // 2, bufs)
        next(task)
        mlp.append(task)
    gate_task, up_task = mlp
    load.wait()
    gain_partial[...] = jnp.zeros_like(gain_partial)
    gain_rows[...] = jnp.zeros_like(gain_rows)
    for k in range(2 * RING):
        for z in range(RING):
            gain_partial[k // RING, k % RING, z, 2:4, :] = token_gains[:, k * block : (k + 1) * block]

    def compute(dy):
        gather.ready(dy)
        y = place.shift("y", dy)
        at = (y % 2, y // 2)
        d_att[at] = dot(d_all[at], own_weight[:, pl.ds(width, inner)]).astype(BF16)

    tile = block_rows // 2
    score_factor = HEAD_DIM ** (-0.5)
    ones = [one_hot_rows(k) for k in range(2)]

    def attention(b):
        row_sums = jnp.zeros((8, block_rows), F32)
        cosine, sine = cosines[b], sines[b]
        for h in range(heads):
            lanes = pl.ds(h * HEAD_DIM, HEAD_DIM)
            key, value = rot[1, h, b], values[h, b]
            d_query, d_key, d_value = [], [None, None], [None, None]
            for i in range(2):
                window = pl.ds(i * tile, tile)
                query, upstream = rot[0, h, b, window, :], d_att[b, i, :, lanes]
                count = (i + 1) * tile
                scores = dot(query, key[:count], NT) * score_factor
                probs = softmax(masked(scores, starts[b, window, 0:1], i))
                d_probs = dot(upstream, value[:count], NT)
                row_dot = jnp.sum(probs * d_probs, axis=-1, keepdims=True)
                d_scores = (probs * (d_probs - row_dot) * score_factor).astype(BF16)
                probs = probs.astype(BF16)
                d_query.append(dot(d_scores, key[:count]))
                for j in range(i + 1):
                    part = slice(j * tile, (j + 1) * tile)
                    for sums_of, left, right in ((d_key, d_scores, query), (d_value, probs, upstream)):
                        term = dot(left[:, part], right, TN)
                        sums_of[j] = term if sums_of[j] is None else sums_of[j] + term
            for i in range(2):
                d_qkv[b, i, :, pl.ds(2 * inner + h * HEAD_DIM, HEAD_DIM)] = d_value[i].astype(BF16)
            for k, parts in enumerate((d_query, d_key)):
                turned = jnp.concatenate(parts, axis=0)
                turned = turned * cosine - half_roll(turned) * sine
                raw = raw_all[k, h, b]
                gain_rows[k : k + 1, lanes] += jnp.sum(turned * raw * scales[k, b], axis=0, keepdims=True)
                turned = turned * head_gains[k : k + 1, lanes]
                back[k, h, b] = turned
                row_sums = row_sums + exact(ones[k], turned * raw, NT)
        sums[:, pl.ds(pl.multiple_of(b * block_rows, block_rows), block_rows)] = row_sums

    compute(0)
    gather.relay()
    compute(1)
    compute(-1)
    next(gate_task)
    attention(1 - place.yl)
    gather.relay_far()
    compute(2)
    next(up_task)
    attention(place.yl)
    octet = Octet(place, sender, sums, slots, octet_sems)
    octet.send()
    first = (place.yh * 2 + place.c) * 2 + place.yl
    for z in range(RING):
        gain_partial[first // RING, first % RING, z, 0:2, :] = gain_rows[0:2, :]
    gains = plane_scatter(place, sender, gain_plane, gain_partial, gain_done, gain_done.shape[1], gain_buffers)
    next(gains)

    def flat_tokens(ref, columns=slice(None)):
        value = ref[:, :, :, columns]
        return value.reshape(-1, value.shape[-1])

    def weight_grads(left_ref, right, start):
        size = right.shape[1]
        for i in range(2 * RING):
            left = flat_tokens(left_ref, pl.ds(i * block, block))
            value = dot(left, right, TN).astype(BF16)
            attn_partial[i // RING, i % RING, :, :, pl.ds(start, size)] = value.reshape(RING, rows, size)

    weight_grads(d_all, flat_tokens(attended), width)
    sender.settle(gather.forwarded)
    load = sender.keep_first(inputs, x_all)
    next(gate_task)
    row_sums = octet.total()
    for b in range(2):
        for k in range(2):
            column = exact(row_sums[:, b * block_rows : (b + 1) * block_rows], ones[k], TN)
            for h in range(heads):
                scale = scales[k, b]
                value = scale * back[k, h, b] - raw_all[k, h, b] * (scale * scale * scale * column / own.shape[1])
                value = value.astype(BF16)
                for i in range(2):
                    d_qkv[b, i, :, pl.ds(k * inner + h * HEAD_DIM, HEAD_DIM)] = value[
                        i * tile : (i + 1) * tile
                    ]
    load.wait()
    weight_grads(x_all, flat_tokens(d_qkv), 0)
    grads = plane_scatter(place, sender, plane, attn_partial, attn_done, rows // 2, buffers)
    next(grads)
    next(gate_task)
    next(up_task)
    ring_product(place, total, d_qkv, own_weight.at[:, pl.ds(0, width)], partial, (up_task, grads, gains))
    take_turns((gate_task, up_task))
    for k in range(2):
        sender.push(mlp_done.at[k, you], mlp_out.at[k, me], swap.at[1 + k], partner)
        sender.keep(mlp_done.at[k, me], mlp_out.at[k, me])
    take_turns((gains, grads))
    sender.push(attn_done.at[you], attn_out.at[me], swap.at[0], partner)
    sender.keep(attn_done.at[me], attn_out.at[me])
    everyone = Octet(place, sender, gain_done, gain_slots, gain_sems)
    everyone.send()
    total.finish(out)
    gain_out[...] = everyone.total()
    sender.arrived(attn_out.at[you], swap.at[0], partner)
    for k in range(3):
        sender.arrived(mlp_out.at[k, you], swap.at[1 + k], partner)
    sender.finish()


def attention_backward(number, own, weight, attended, inputs, mlp_partial, *others):
    rows, width = own.shape
    tokens = (2, 2, 2 * rows)
    inner = attended.shape[3]
    heads = inner // HEAD_DIM
    shard = width // 32, weight.shape[1]
    gain_tile = (8, 4 * shard[0])
    return call(
        attention_backward_kernel,
        number,
        (
            shape_of(rows, width, dtype=F32),
            shape_of(2, *shard),
            shape_of(2, *gain_tile, dtype=F32),
            shape_of(3, 2, *shard),
        ),
        [ANYWHERE, ANYWHERE, IN_VMEM, ANYWHERE, ANYWHERE] + [IN_VMEM] * len(others),
        (IN_VMEM,) * 4,
        [
            pltpu.VMEM((*tokens, width), BF16),
            pltpu.VMEM(weight.shape, BF16),
            pltpu.VMEM((2, RING, RING, *shard), BF16),
            pltpu.VMEM((2, 2, RING, RING, *shard), BF16),
            pltpu.VMEM((*tokens, inner), BF16),
            pltpu.VMEM((2, heads, 2, 4 * rows, HEAD_DIM), F32),
            pltpu.VMEM((*tokens, 3 * inner), BF16),
            pltpu.VMEM((8, 8 * rows), F32),
            pltpu.VMEM((8, 8, 8 * rows), F32),
            pltpu.VMEM((2, RING, RING, *gain_tile), F32),
            pltpu.VMEM((8, inner), F32),
            pltpu.VMEM((8, 2, *gain_tile), F32),
            pltpu.VMEM((2, *shard), BF16),
            pltpu.VMEM((2, *gain_tile), F32),
            pltpu.VMEM((2, 2, *shard), BF16),
            *ring_buffers(rows, width),
            *scatter_buffers(*shard, BF16),
            *scatter_buffers(*shard, BF16),
            *scatter_buffers(*shard, BF16),
            *scatter_buffers(*gain_tile, F32),
            dma_sems(176),
            dma_sems(RING, 4),
            dma_sems(4, RING),
            dma_sems(8),
            dma_sems(8),
            dma_sems(4),
            dma_sems(2, 12),
            dma_sems(2, 12),
            dma_sems(2, 12),
            dma_sems(2, 12),
        ],
        (own, weight, attended, inputs, mlp_partial, *others),
    )


def norm_scale(values):
    return lax.rsqrt(jnp.mean(values * values, axis=-1, keepdims=True) + NORM_EPS)


def norm_back(upstream, values, scales, gain_row):
    scaled_grad = upstream * gain_row
    return scales * scaled_grad - values * scales**3 * jnp.mean(
        scaled_grad * values, axis=-1, keepdims=True
    )


def doc_layout(lengths, group_size):
    positions = jnp.arange(group_size, dtype=jnp.int32)
    doc_ends = jnp.cumsum(lengths)
    passed = (positions[:, None] >= doc_ends[None, :]).astype(jnp.int32)
    segment = jnp.sum(passed, axis=-1)
    begins = jnp.sum(passed * lengths[None, :], axis=-1)
    return (segment, positions - begins)


def rope_tables(offsets):
    frequency = ROPE_BASE ** (-jnp.arange(0, HEAD_DIM, 2).astype(jnp.float32) / HEAD_DIM)
    angles = offsets.astype(jnp.float32)[:, None] * frequency[None, :]
    cosine, sine = jnp.cos(angles), jnp.sin(angles)
    return (
        jnp.concatenate([cosine, cosine], axis=-1),
        jnp.concatenate([sine, sine], axis=-1),
    )


def half_turn(values):
    middle = values.shape[-1] // 2
    return jnp.concatenate([-values[..., middle:], values[..., :middle]], axis=-1)


def rotate(values, cosine_table, sine_table):
    return values * cosine_table + half_turn(values) * sine_table


def unrotate(values, cosine_table, sine_table):
    return values * cosine_table - half_turn(values) * sine_table


def product(left, right):
    return jnp.dot(left, right, preferred_element_type=F32)


def row_product(left, right):
    return lax.dot_general(left, right, (((1,), (1,)), ((), ())), preferred_element_type=F32)


def col_product(left, right):
    return lax.dot_general(left, right, (((0,), (0,)), ((), ())), preferred_element_type=F32)


def adam_update(weights_old, first_old, second_old, gradient, rate, decay):
    first_new = BETA_ONE * first_old + (1.0 - BETA_ONE) * gradient
    second_new = BETA_TWO * second_old + (1.0 - BETA_TWO) * gradient * gradient
    ratio = (
        first_new
        / (1.0 - BETA_ONE**STEP)
        / (jnp.sqrt(second_new / (1.0 - BETA_TWO**STEP)) + ADAM_EPS)
    )
    return (first_new, second_new, weights_old - rate * (ratio + decay * weights_old))


def mlp_adam_kernel(weights, first, second, sums, grad_out, first_out, second_out, new_out):
    gradient = sums[0].astype(F32)
    grad_out[...] = gradient
    first_out[...], second_out[...], new_out[...] = adam_update(
        weights[...], first[...], second[...], gradient, WEIGHT_RATE, WEIGHT_DECAY
    )


def mlp_adam(weights, first, second, sums):
    count, rows, columns = weights.shape
    half = columns // 2
    state = pl.BlockSpec((1, rows, half), lambda m, h: (m, 0, h))
    return pl.pallas_call(
        mlp_adam_kernel,
        out_shape=(shape_of(*weights.shape, dtype=F32),) * 4,
        grid=(count, 2),
        in_specs=[state] * 3 + [pl.BlockSpec((1, 1, rows, half), lambda m, h: (m, h, 0, 0))],
        out_specs=(state,) * 4,
        compiler_params=pltpu.CompilerParams(vmem_limit_bytes=VMEM_LIMIT),
    )(weights, first, second, sums)


def attn_adam_kernel(weights, first, second, sums, grad_out, first_out, second_out, new_out):
    inner = weights.shape[2]
    for m in range(weights.shape[0]):
        gradient = sums[0, :, m * inner : (m + 1) * inner].astype(F32)
        grad_out[m] = gradient
        first_out[m], second_out[m], new_out[m] = adam_update(
            weights[m], first[m], second[m], gradient, WEIGHT_RATE, WEIGHT_DECAY
        )


def attn_adam(weights, first, second, sums):
    count, rows, columns = weights.shape
    state = pl.BlockSpec((count, rows, columns // 2), lambda h: (0, 0, h))
    return pl.pallas_call(
        attn_adam_kernel,
        out_shape=(shape_of(*weights.shape, dtype=F32),) * 4,
        grid=(2,),
        in_specs=[state] * 3 + [pl.BlockSpec((1, *sums.shape[1:]), lambda h: (h, 0, 0))],
        out_specs=(state,) * 4,
        compiler_params=pltpu.CompilerParams(vmem_limit_bytes=VMEM_LIMIT),
    )(weights, first, second, sums)


def body(
    hidden_in,
    cotangent,
    doc_lengths,
    attn_weights,
    attn_first,
    attn_second,
    mlp_weights,
    mlp_first,
    mlp_second,
    gains,
    gain_first,
    gain_second,
):
    row_count, model_width = hidden_in.shape
    shard_rows = attn_weights.shape[1]
    heads_width = attn_weights.shape[2] // 2
    hidden_width = mlp_weights.shape[2] // 2
    token_count = 8 * row_count
    block_rows = token_count // 2
    head_count = heads_width // HEAD_DIM
    score_factor = HEAD_DIM ** (-0.5)
    yl, yh, core = (lax.axis_index(a) for a in ("yl", "yh", "c"))

    attn_halves = (
        attn_weights.astype(BF16)
        .reshape(4, shard_rows, 2, heads_width)
        .transpose(2, 1, 0, 3)
        .reshape(2, shard_rows, 4 * heads_width)
    )
    mlp_halves = mlp_weights.astype(BF16).reshape(3, shard_rows, 2, hidden_width).transpose(0, 2, 1, 3)
    mine = lax.dynamic_index_in_dim(mlp_halves, yl, 1, keepdims=False)
    yours = lax.dynamic_index_in_dim(mlp_halves, 1 - yl, 1, keepdims=False)
    arrived = lax.ppermute(yours, "yl", [(0, 1), (1, 0)])
    mlp_pair = jnp.stack(
        [jnp.where(yl == 0, mine, arrived), jnp.where(yl == 0, arrived, mine)], axis=1
    )
    mlp_all = lax.all_gather(mlp_pair.reshape(-1, hidden_width), ("x", "z"), tiled=True)
    mlp_all = mlp_all.reshape(16, 3, 2, shard_rows, hidden_width)
    gain_tile = jnp.pad(gains.astype(BF16).astype(F32), ((0, 4), (0, 128 - shard_rows)))
    theirs = lax.ppermute(doc_lengths, "yl", [(0, 1), (1, 0)])
    lengths = jnp.where(yl == 0, jnp.stack([doc_lengths[0], theirs[0]]), jnp.stack([theirs[0], doc_lengths[0]]))
    _, offsets = jax.vmap(lambda one: doc_layout(one, block_rows))(lengths)
    cosine_table, sine_table = rope_tables(offsets.reshape(-1))
    sine_table = sine_table * jnp.where(jnp.arange(HEAD_DIM) < HEAD_DIM // 2, -1.0, 1.0)
    cosine_table = cosine_table.reshape(2, block_rows, HEAD_DIM)
    sine_table = sine_table.reshape(2, block_rows, HEAD_DIM)
    starts = jnp.broadcast_to((jnp.arange(block_rows) - offsets)[:, :, None], (2, block_rows, HEAD_DIM))

    own_input, cosine_table, sine_table, starts = lax.optimization_barrier(
        (hidden_in, cosine_table, sine_table, starts)
    )
    every_input, attn_all, gain_all = call(
        first_kernel,
        0,
        (
            shape_of(2, 2, 2 * row_count, model_width),
            shape_of(2, RING, RING, shard_rows, 4 * heads_width),
            shape_of(2, RING, RING, 8, 128, dtype=F32),
        ),
        [ANYWHERE] * 3,
        (ANYWHERE, IN_VMEM, ANYWHERE),
        [
            dma_sems(112),
            dma_sems(RING, 4),
            dma_sems(2, RING, RING, 3),
            dma_sems(2, RING, RING, 3),
            dma_sems(2),
        ],
        (own_input, attn_halves, gain_tile),
    )
    attn_all = flat(attn_all)
    gain_full = gain_all[..., :4, :shard_rows].transpose(3, 0, 1, 2, 4).reshape(4, model_width)
    first_column = (yh * 2 + core) * (2 * heads_width) + yl * heads_width
    head_gains = lax.dynamic_slice(gain_full, (0, first_column), (2, heads_width))
    attn_proj, raw, rotated, values, head_scales, attended = attention_forward(
        1, every_input, attn_all, cosine_table, sine_table, starts, head_gains
    )
    proj_scale = norm_scale(attn_proj)
    mixed = hidden_in.astype(F32) + attn_proj * proj_scale * gain_full[2]
    every_mixed, gate_proj, up_proj, hidden_act, down_proj = mlp_forward(mixed.astype(BF16), mlp_all, 3)
    down_scale = norm_scale(down_proj)
    hidden_out = (mixed + down_proj * down_scale * gain_full[3]).astype(BF16)

    upstream = cotangent.astype(F32)
    d_down = norm_back(upstream, down_proj, down_scale, gain_full[3]).astype(BF16)
    gain_mlp = jnp.sum(upstream * down_proj * down_scale, axis=0)
    d_mixed_sum, mlp_partial, down_sum = mlp_backward(
        d_down, mlp_all, every_mixed, gate_proj, up_proj, hidden_act, 4
    )
    d_mixed = upstream + d_mixed_sum
    gain_attn = jnp.sum(d_mixed * attn_proj * proj_scale, axis=0)
    d_proj = norm_back(d_mixed, attn_proj, proj_scale, gain_full[2]).astype(BF16)

    input_sum, attn_sum, gain_sum, mlp_sum = attention_backward(
        5,
        d_proj,
        attn_all,
        attended,
        every_input,
        mlp_partial,
        down_sum,
        raw,
        rotated,
        values,
        head_scales,
        cosine_table,
        sine_table,
        starts,
        head_gains,
        jnp.stack([gain_attn, gain_mlp]),
    )
    input_grad = d_mixed + input_sum

    gain_sum = lax.dynamic_index_in_dim(gain_sum, yl, 0, keepdims=False)[:4]
    gain_grad = lax.dynamic_slice_in_dim(gain_sum, lax.axis_index("z") * shard_rows, shard_rows, axis=1)
    attn_grad, attn_first_new, attn_second_new, attn_new = attn_adam(
        attn_weights, attn_first, attn_second, attn_sum
    )
    mlp_grad, mlp_first_new, mlp_second_new, mlp_new = mlp_adam(
        mlp_weights, mlp_first, mlp_second, mlp_sum
    )
    gain_first_new, gain_second_new, gain_new = adam_update(
        gains, gain_first, gain_second, gain_grad, GAIN_RATE, 0.0
    )
    return (
        hidden_out,
        input_grad,
        attn_grad,
        attn_first_new,
        attn_second_new,
        attn_new,
        mlp_grad,
        mlp_first_new,
        mlp_second_new,
        mlp_new,
        gain_grad,
        gain_first_new,
        gain_second_new,
        gain_new,
    )


def solution(mesh):
    split = Mesh(mesh.devices.reshape(2, 4, 4, 2, 2), EVERY)
    tokens, shards, rows = P(EVERY, None), P(None, DP, TENSOR), P(None, DP)
    return jax.shard_map(
        body,
        mesh=split,
        in_specs=(tokens, tokens, P(DP, None), *[shards] * 6, *[rows] * 3),
        out_specs=(tokens, tokens, *[shards] * 8, *[rows] * 4),
        check_vma=False,
    )
```

```python
import functools

import jax
import jax.numpy as jnp
from jax import lax
from jax.experimental import pallas as pl
from jax.experimental.pallas import tpu as pltpu
from jax.sharding import Mesh
from jax.sharding import PartitionSpec as P

HEAD_DIM = 128
STEP = 10
DP = ("yl", "x", "z")
TENSOR = ("yh", "c")
EVERY = ("yl", "x", "z", "yh", "c")
RING = 4
MESH = pl.DeviceIdType.MESH

NORM_EPS = 1e-06
ROPE_BASE = 500000.0
BETA_ONE = 0.9
BETA_TWO = 0.95
ADAM_EPS = 1e-08
WEIGHT_RATE = 0.03
GAIN_RATE = 1.0
WEIGHT_DECAY = 0.1

BF16 = jnp.bfloat16
F32 = jnp.float32
IN_VMEM = pl.BlockSpec(memory_space=pltpu.VMEM)
ANYWHERE = pl.BlockSpec(memory_space=pl.ANY)
VMEM_LIMIT = 60 * 1024 * 1024


class Place:
    def __init__(self):
        self.x, self.z, self.c = (lax.axis_index(a) for a in ("x", "z", "c"))
        self.yl, self.yh = (lax.axis_index(a) for a in ("yl", "yh"))
        self.y = self.yh * 2 + self.yl

    def at(self, axis, step):
        if axis == "y":
            there = (self.y + step + RING) % RING
            return {"yl": there % 2, "yh": there // 2}
        if axis == "c":
            return {"c": 1 - self.c}
        return {axis: (getattr(self, axis) + step + RING) % RING}

    def shift(self, axis, step):
        return (getattr(self, axis) + step + RING) % RING


def greet(devices):
    barrier = pltpu.get_barrier_semaphore()
    for device in devices:
        pl.semaphore_signal(barrier, inc=1, device_id=device, device_id_type=MESH)
    pl.semaphore_wait(barrier, len(devices))


def greet_all(place, axes):
    devices = []
    for axis in axes:
        devices += [place.at(axis, 1)] if axis == "c" else [place.at(axis, 1), place.at(axis, -1)]
    greet(devices)


class Sender:
    def __init__(self, sems):
        self.sems, self.open = sems, []

    def push(self, src, dst, recv_sem, device):
        copy = pltpu.make_async_remote_copy(
            src_ref=src,
            dst_ref=dst,
            send_sem=self.sems.at[len(self.open)],
            recv_sem=recv_sem,
            device_id=device,
            device_id_type=MESH,
        )
        copy.start()
        self.open.append(copy.wait_send)
        return len(self.open) - 1

    def settle(self, numbers):
        for number in numbers:
            self.open[number]()
            self.open[number] = lambda: None

    def keep(self, src, dst):
        copy = pltpu.make_async_copy(src, dst, self.sems.at[len(self.open)])
        copy.start()
        self.open.append(copy.wait)

    def keep_first(self, src, dst):
        copy = pltpu.make_async_copy(src, dst, self.sems.at[len(self.open)])
        copy.start()
        self.open.append(lambda: None)
        return copy

    def arrived(self, dst, recv_sem, device):
        pltpu.make_async_remote_copy(
            src_ref=dst,
            dst_ref=dst,
            send_sem=self.sems.at[0],
            recv_sem=recv_sem,
            device_id=device,
            device_id_type=MESH,
        ).wait_recv()

    def finish(self):
        for wait in self.open:
            wait()


def take_turns(tasks):
    tasks = list(tasks)
    while tasks:
        for task in list(tasks):
            if next(task, "done") == "done":
                tasks.remove(task)


WHOLE, LOW, HIGH = 0, 1, 2
PIECES = 4


def part_of(ref, part, cut):
    rows = ref.shape[-2]
    if part == WHOLE:
        return ref
    return ref.at[pl.ds(0, cut)] if part == LOW else ref.at[pl.ds(cut, rows - cut)]


def plane_gather(place, sender, sems, out, cut):
    rows = out.shape[-2]
    axes = (("x", "z"), ("z", "x"))

    def piece(half, dp, dq):
        p, q = (place.shift(a, d) for a, d in zip(axes[half], (dp, dq)))
        return out.at[half, p, q] if half == 0 else out.at[half, q, p]

    def parts(part):
        if part == WHOLE:
            return True
        return cut > 0 if part == LOW else cut < rows

    def send(half, dp, dq, part, along, step):
        if parts(part):
            ref = part_of(piece(half, dp, dq), part, cut)
            sp, sq = ((dp - step) % RING, dq % RING) if along == 0 else (dp % RING, (dq - step) % RING)
            sender.push(ref, ref, sems.at[half, sp, sq, part], place.at(axes[half][along], step))

    def wait(half, dp, dq, part):
        if parts(part):
            ref = part_of(piece(half, dp, dq), part, cut)
            sender.arrived(ref, sems.at[half, dp % RING, dq % RING, part], place.at("x", 1))

    both = (0, 1)
    for half in both:
        for step in (1, -1):
            send(half, 0, 0, WHOLE, 0, step)
    for half in both:
        for step in (1, -1):
            send(half, 0, 0, WHOLE, 1, step)
    yield
    for step, part in ((1, LOW), (-1, HIGH)):
        for half in both:
            wait(half, -step, 0, WHOLE)
            send(half, -step, 0, part, 0, step)
            for side in (1, -1):
                send(half, -step, 0, WHOLE, 1, side)
    yield
    for half in both:
        for step, part in ((1, LOW), (-1, HIGH)):
            wait(half, 0, -step, WHOLE)
            send(half, 0, -step, part, 1, step)
    yield
    for half in both:
        wait(half, 2, 0, LOW)
        wait(half, 2, 0, HIGH)
        for side in (1, -1):
            send(half, 2, 0, WHOLE, 1, side)
    yield
    for dp in (-1, 1, 2):
        for half in both:
            for step, part in ((1, LOW), (-1, HIGH)):
                wait(half, dp, -step, WHOLE)
                send(half, dp, -step, part, 1, step)
        yield
    for dp in (0, -1, 1, 2):
        for half in both:
            wait(half, dp, 2, LOW)
            wait(half, dp, 2, HIGH)


class RingGather:
    def __init__(self, place, sender, sems, own, out):
        self.place, self.sender, self.sems, self.own, self.out = place, sender, sems, own, out
        self.rows = own.shape[0]
        self.other = place.at("c", 1)
        self.begun, self.forwarded = [], []

    def piece(self, dy, core, part=WHOLE):
        y = self.place.shift("y", dy)
        half = self.rows // 2
        start, size = {WHOLE: (0, self.rows), LOW: (0, half), HIGH: (half, half)}[part]
        return self.out.at[y % 2, y // 2, pl.ds(pl.multiple_of(core * self.rows + start, 16), size)]

    def begin(self):
        place, mine = self.place, self.piece(0, self.place.c)
        for step in (1, -1):
            number = self.sender.push(self.own, mine, self.sems.at[(-step) % RING, WHOLE], place.at("y", step))
            self.begun.append(number)
        self.begun.append(self.sender.push(self.own, mine, self.sems.at[0, 3], self.other))
        self.kept = self.sender.keep_first(self.own, mine)

    def relay(self):
        for step, part in ((1, LOW), (-1, HIGH)):
            ref = self.piece(-step, self.place.c)
            self.sender.arrived(ref, self.sems.at[(-step) % RING, WHOLE], self.other)
            half = self.piece(-step, self.place.c, part)
            self.forwarded += [
                self.sender.push(half, half, self.sems.at[2, part], self.place.at("y", step)),
                self.sender.push(ref, ref, self.sems.at[(-step) % RING, 3], self.other),
            ]

    def relay_far(self):
        for part in (LOW, HIGH):
            self.sender.arrived(self.piece(2, self.place.c, part), self.sems.at[2, part], self.other)
        ref = self.piece(2, self.place.c)
        self.forwarded += [self.sender.push(ref, ref, self.sems.at[2, 3], self.other)]

    def ready(self, dy):
        if dy == 0:
            self.kept.wait()
        self.sender.arrived(self.piece(dy, 1 - self.place.c), self.sems.at[dy % RING, 3], self.other)


def ring_gather(place, sender, sems, own, out):
    gather = RingGather(place, sender, sems, own, out)
    gather.begin()
    yield
    gather.relay()
    yield
    gather.relay_far()
    yield
    for dy in (0, 1, -1, 2):
        gather.ready(dy)


def add_rows(out, terms, rows):
    def step(i, carry):
        window = pl.ds(pl.multiple_of(i * 16, 16), 16)
        total = terms[0][window, :].astype(F32)
        for term in terms[1:]:
            total = total + term[window, :].astype(F32)
        out[window, :] = total.astype(out.dtype)
        return carry

    lax.fori_loop(0, rows // 16, step, 0)


class RingSum:
    def __init__(self, place, sender, sems, partial, kept, from_core, hop, last):
        self.place, self.sender, self.sems, self.partial = place, sender, sems, partial
        self.kept, self.from_core, self.hop, self.last = kept, from_core, hop, last
        self.rows = kept.shape[1]
        self.low, self.high = pl.ds(0, self.rows // 2), pl.ds(self.rows // 2, self.rows // 2)
        self.other = place.at("c", 1)

    def mine(self, dy, core):
        y = self.place.shift("y", dy)
        return self.partial.at[y % 2, y // 2, pl.ds(pl.multiple_of(core * self.rows, 16), self.rows)]

    def offer(self, dy):
        slot = dy % RING
        self.sender.push(
            self.mine(dy, 1 - self.place.c), self.from_core.at[slot], self.sems.at[0, slot], self.other
        )

    def pieces(self):
        columns = self.kept.shape[2]
        return [pl.ds(p * columns // PIECES, columns // PIECES) for p in range(PIECES)]

    def collect(self, dy):
        slot = dy % RING
        kept, low, high = self.kept.at[slot], self.low, self.high
        self.sender.arrived(self.from_core.at[slot], self.sems.at[0, slot], self.other)
        if dy == 0:
            return
        up, down = self.place.at("y", 1), self.place.at("y", -1)
        mine = self.mine(dy, self.place.c)
        if dy == 2:
            for p, columns in enumerate(self.pieces()):
                add_rows(kept.at[:, columns], (mine.at[:, columns], self.from_core.at[slot, :, columns]), self.rows)
                self.sender.push(kept.at[low, columns], self.hop.at[0, :, columns], self.sems.at[1, p], up)
                self.sender.push(
                    kept.at[high, columns], self.hop.at[1, :, columns], self.sems.at[1, PIECES + p], down
                )
            return
        add_rows(kept, (mine, self.from_core.at[slot]), self.rows)
        if dy == 1:
            self.sender.push(kept.at[high], self.last.at[0, high], self.sems.at[2, 1], up)
        else:
            self.sender.push(kept.at[low], self.last.at[1, low], self.sems.at[2, 2], down)

    def relay(self):
        for p, columns in enumerate(self.pieces()):
            for k, slot, part, step in ((0, 1, self.low, 1), (1, 3, self.high, -1)):
                number = k * PIECES + p
                self.sender.arrived(self.hop.at[k, :, columns], self.sems.at[1, number], self.other)
                rows = self.kept.at[slot, part, columns]
                add_rows(rows, (rows, self.hop.at[k, :, columns]), self.rows // 2)
                self.sender.push(
                    rows, self.last.at[k, part, columns], self.sems.at[3, number], self.place.at("y", step)
                )

    def finish(self, out):
        self.sender.arrived(self.last.at[0, self.high], self.sems.at[2, 1], self.other)
        self.sender.arrived(self.last.at[1, self.low], self.sems.at[2, 2], self.other)
        mine = self.mine(0, self.place.c)
        for p, columns in enumerate(self.pieces()):
            for k, part in ((0, self.low), (1, self.high)):
                self.sender.arrived(
                    self.last.at[k, part, columns], self.sems.at[3, k * PIECES + p], self.other
                )
            terms = (mine, self.from_core.at[0], self.last.at[0], self.last.at[1])
            add_rows(out.at[:, columns], [term.at[:, columns] for term in terms], self.rows)


def plane_scatter(place, sender, sems, partial, done, cut, bufs):
    rows = partial.shape[-2]
    hop, last, middle, hop2, last2 = bufs
    low, high = pl.ds(0, cut), pl.ds(cut, rows - cut)
    axes = (("z", "x"), ("x", "z"))
    two_parts = cut < rows
    both = (0, 1)
    other = place.at("x", 1)

    def row(half, du, window):
        u = place.shift(axes[half][0], du)
        return partial.at[half, :, u, window] if half == 0 else partial.at[half, u, :, window]

    def line(half, du, v):
        u = place.shift(axes[half][0], du)
        return partial.at[half, v, u] if half == 0 else partial.at[half, u, v]

    def add(out, terms, count):
        if count % 16:
            total = terms[0][...].astype(F32)
            for term in terms[1:]:
                total = total + term[...].astype(F32)
            out[...] = total.astype(out.dtype)
        else:
            add_rows(out, terms, count)

    for half in both:
        u = axes[half][0]
        sender.push(row(half, 2, low), hop.at[half, 0], sems.at[half, 0], place.at(u, 1))
        if two_parts:
            sender.push(row(half, 2, high), hop.at[half, 1], sems.at[half, 1], place.at(u, -1))
    for half in both:
        u = axes[half][0]
        if two_parts:
            sender.push(row(half, 1, high), last.at[half, 0, :, high], sems.at[half, 2], place.at(u, 1))
        sender.push(row(half, -1, low), last.at[half, 1, :, low], sems.at[half, 3], place.at(u, -1))
    yield
    for half in both:
        u = axes[half][0]
        sender.arrived(hop.at[half, 0], sems.at[half, 0], other)
        for v in range(RING):
            add(hop.at[half, 0, v], (line(half, 1, v).at[low], hop.at[half, 0, v]), cut)
        sender.push(hop.at[half, 0], last.at[half, 0, :, low], sems.at[half, 4], place.at(u, 1))
        if two_parts:
            sender.arrived(hop.at[half, 1], sems.at[half, 1], other)
            for v in range(RING):
                add(
                    hop.at[half, 1, v],
                    (line(half, -1, v).at[high], hop.at[half, 1, v]),
                    rows - cut,
                )
            sender.push(
                hop.at[half, 1], last.at[half, 1, :, high], sems.at[half, 5], place.at(u, -1)
            )
    yield
    for half in both:
        v_axis = axes[half][1]
        if two_parts:
            sender.arrived(last.at[half, 0, :, high], sems.at[half, 2], other)
        sender.arrived(last.at[half, 1, :, low], sems.at[half, 3], other)
        sender.arrived(last.at[half, 0, :, low], sems.at[half, 4], other)
        if two_parts:
            sender.arrived(last.at[half, 1, :, high], sems.at[half, 5], other)
        for dv in (2, 1, -1, 0):
            v = place.shift(v_axis, dv)
            terms = (line(half, 0, v), last.at[half, 0, v], last.at[half, 1, v])
            add(middle.at[half, dv % RING], terms, rows)
            if dv == 2:
                sender.push(
                    middle.at[half, 2, low], hop2.at[half, 0], sems.at[half, 6], place.at(v_axis, 1)
                )
                if two_parts:
                    sender.push(
                        middle.at[half, 2, high],
                        hop2.at[half, 1],
                        sems.at[half, 7],
                        place.at(v_axis, -1),
                    )
            elif dv == 1 and two_parts:
                sender.push(
                    middle.at[half, 1, high], last2.at[half, 0, high], sems.at[half, 8], place.at(v_axis, 1)
                )
            elif dv == -1:
                sender.push(
                    middle.at[half, 3, low], last2.at[half, 1, low], sems.at[half, 9], place.at(v_axis, -1)
                )
    yield
    for half in both:
        v_axis = axes[half][1]
        sender.arrived(hop2.at[half, 0], sems.at[half, 6], other)
        add(hop2.at[half, 0], (middle.at[half, 1, low], hop2.at[half, 0]), cut)
        sender.push(
            hop2.at[half, 0], last2.at[half, 0, low], sems.at[half, 10], place.at(v_axis, 1)
        )
        if two_parts:
            sender.arrived(hop2.at[half, 1], sems.at[half, 7], other)
            add(hop2.at[half, 1], (middle.at[half, 3, high], hop2.at[half, 1]), rows - cut)
            sender.push(
                hop2.at[half, 1], last2.at[half, 1, high], sems.at[half, 11], place.at(v_axis, -1)
            )
    yield
    for half in both:
        if two_parts:
            sender.arrived(last2.at[half, 0, high], sems.at[half, 8], other)
        sender.arrived(last2.at[half, 1, low], sems.at[half, 9], other)
        sender.arrived(last2.at[half, 0, low], sems.at[half, 10], other)
        if two_parts:
            sender.arrived(last2.at[half, 1, high], sems.at[half, 11], other)
        add(done.at[half], (middle.at[half, 0], last2.at[half, 0], last2.at[half, 1]), rows)


def scatter_buffers(rows, columns, dtype):
    cut = rows // 2 if dtype == BF16 else rows
    return [
        pltpu.VMEM((2, 2, RING, cut, columns), dtype),
        pltpu.VMEM((2, 2, RING, rows, columns), dtype),
        pltpu.VMEM((2, RING, rows, columns), dtype),
        pltpu.VMEM((2, 2, cut, columns), dtype),
        pltpu.VMEM((2, 2, rows, columns), dtype),
    ]


def ring_buffers(rows, columns):
    return [
        pltpu.VMEM((RING, rows, columns), BF16),
        pltpu.VMEM((RING, rows, columns), BF16),
        pltpu.VMEM((2, rows // 2, columns), BF16),
        pltpu.VMEM((2, rows, columns), BF16),
    ]


def dma_sems(*shape):
    return pltpu.SemaphoreType.DMA(shape)


def shape_of(*shape, dtype=BF16):
    return jax.ShapeDtypeStruct(shape, dtype)


def call(kernel, number, out_shape, in_specs, out_specs, scratch, args):
    return pl.pallas_call(
        kernel,
        out_shape=out_shape,
        in_specs=in_specs,
        out_specs=out_specs,
        scratch_shapes=scratch,
        compiler_params=pltpu.CompilerParams(
            collective_id=number, has_side_effects=True, vmem_limit_bytes=VMEM_LIMIT
        ),
    )(*args)


def first_kernel(hidden, attn, gain, down, hidden_all, attn_all, gain_all, down_pair, sends, ring, plane, plane_gain, swap):
    place = Place()
    greet_all(place, ("x", "z", "y", "c"))
    sender = Sender(sends)
    partner = {"yl": 1 - place.yl}
    me, you = place.yl, 1 - place.yl
    own_attn = attn_all.at[:, place.x, place.z]
    own_gain = gain_all.at[:, place.x, place.z]
    sender.push(attn.at[you], own_attn.at[me], swap.at[0], partner)
    sender.push(gain, own_gain.at[me], swap.at[1], partner)
    first = sender.keep_first(attn.at[me], own_attn.at[me])
    second = sender.keep_first(gain, own_gain.at[me])
    gather = ring_gather(place, sender, ring, hidden, hidden_all)
    next(gather)
    first.wait()
    second.wait()
    sender.arrived(own_attn.at[you], swap.at[0], partner)
    sender.arrived(own_gain.at[you], swap.at[1], partner)
    planes = plane_gather(place, sender, plane, attn_all, attn_all.shape[-2] // 2)
    gains = plane_gather(place, sender, plane_gain, gain_all, gain_all.shape[-2])
    next(planes)
    next(gains)
    sender.push(down.at[you], down_pair.at[me], swap.at[2], partner)
    sender.keep(down.at[me], down_pair.at[me])
    take_turns((gains, planes, gather))
    sender.arrived(down_pair.at[you], swap.at[2], partner)
    sender.finish()


NN = (((1,), (0,)), ((), ()))
NT = (((1,), (1,)), ((), ()))
TN = (((0,), (0,)), ((), ()))


def dot(left, right, dims=NN):
    return lax.dot_general(left, right, dims, preferred_element_type=F32)


def in_tiles(width, tile, work):
    for n in range(width // tile):
        work(pl.ds(n * tile, tile))


def refs_of(refs, *counts):
    refs, out = list(refs), []
    for n in counts:
        out.append(refs[:n])
        del refs[:n]
    return out


def by_rows(count, work):
    def step(i, carry):
        work(pl.ds(pl.multiple_of(i * 16, 16), 16))
        return carry

    lax.fori_loop(0, count // 16, step, 0)


def load_weights(sender, source, targets):
    copies = []
    for k, target in targets:
        for yl in range(2):
            copies.append(sender.keep_first(source.at[:, k, yl], target.at[yl]))
    return copies


def rows_of(weight, window):
    piece = weight.shape[2]
    per_half = weight.shape[1] * piece
    start, size = window.start, window.size
    block = weight[start // per_half, pl.ds((start % per_half) // piece, size // piece), :, :]
    return block.reshape(size, weight.shape[3])


def columns_of(weight, window):
    block = weight[:, :, :, window]
    return block.reshape(-1, window.size)


def mlp_kernel(
    own, gate_up, down, mixed, cotangent, proj, gain_rows, hidden_out, d_mixed_out, d_proj_out, gains_out,
    grads_out, down_out, *refs
):
    (
        (x_all, d_all, w_gate, w_up, w_down, gate, up, act, partial, tiles, down_partial),
        (down_proj,),
        ring,
        first_buffers,
        second_buffers,
        (sends, gather_sems, sum_sems, gather_sems2, sum_sems2, tile_sems, plane, plane2),
    ) = refs_of(refs, 11, 1, 4, 5, 5, 8)
    d_own = d_proj_out
    d_gate, d_up = gate, up
    place = Place()
    sender = Sender(sends)
    loads = load_weights(sender, gate_up, ((0, w_gate), (1, w_up)))
    load_down = sender.keep_first(down, w_down)
    greet_all(place, ("x", "z", "y", "c"))
    gather = RingGather(place, sender, gather_sems, own, x_all)
    total = RingSum(place, sender, sum_sems, partial, *ring)
    gather.begin()
    for copy in loads:
        copy.wait()
    load_down.wait()
    tile = 512

    def where(dy):
        y = place.shift("y", dy)
        return y % 2, y // 2

    def at_chip(dy):
        at = where(dy)
        return (*at, slice(None)), (2 * rows, hidden_width)

    def at_neighbours(_):
        return (1 - place.yl, slice(None), slice(None)), (4 * rows, hidden_width)

    rows, hidden_width = own.shape[0], act.shape[-1]

    def forward(index, shape):
        count = shape[0]

        def hidden(columns):
            tokens = x_all[(*index, slice(None))].reshape(count, -1)
            g = dot(tokens, columns_of(w_gate, columns))
            u = dot(tokens, columns_of(w_up, columns))
            here = (*index, columns)
            held = act[here].shape
            gate[here], up[here] = g.astype(BF16).reshape(held), u.astype(BF16).reshape(held)
            act[here] = (g * jax.nn.sigmoid(g) * u).astype(BF16).reshape(held)

        in_tiles(hidden_width, tile, hidden)

        def project(columns):
            left = act[(*index, slice(None))].reshape(shape)
            value = dot(left, rows_of(w_down, columns), NT).astype(BF16)
            here = (*index, columns)
            partial[here] = value.reshape(partial[here].shape)

        in_tiles(partial.shape[-1], tile, project)

    def in_turn(gather, total, work, before_far=lambda: None):
        gather.ready(0)
        work(*at_chip(0))
        total.offer(0)
        gather.relay()
        gather.ready(1)
        gather.ready(-1)
        work(*at_neighbours(0))
        total.offer(1)
        total.offer(-1)
        gather.relay_far()
        total.collect(1)
        total.collect(-1)
        gather.ready(2)
        before_far()
        work(*at_chip(2))
        total.offer(2)

    in_turn(gather, total, forward)
    total.collect(2)
    total.collect(0)
    total.relay()
    total.finish(down_proj)
    sender.settle(range(len(sender.open)))
    gains_out[...] = jnp.zeros_like(gains_out)

    def output_norm(rows):
        value, upstream, gain = down_proj[rows, :], cotangent[rows, :].astype(F32), gain_rows[3:4, :]
        scale = norm_scale(value)
        hidden_out[rows, :] = (mixed[rows, :] + value * scale * gain).astype(BF16)
        d_own[rows, :] = norm_back(upstream, value, scale, gain).astype(BF16)
        gains_out[1:2, :] += jnp.sum(upstream * value * scale, axis=0, keepdims=True)

    by_rows(down_proj.shape[0], output_norm)

    gather = RingGather(place, sender, gather_sems2, d_own, d_all)
    total = RingSum(place, sender, sum_sems2, partial, *ring)
    gather.begin()

    def backward(index, shape):
        count = shape[0]

        def hidden(columns):
            d_act = dot(d_all[(*index, slice(None))].reshape(count, -1), columns_of(w_down, columns))
            here = (*index, columns)
            held = gate[here].shape
            g, u = gate[here].astype(F32).reshape(d_act.shape), up[here].astype(F32).reshape(d_act.shape)
            s = jax.nn.sigmoid(g)
            d_gate[here] = (d_act * u * s * (1.0 + g * (1.0 - s))).astype(BF16).reshape(held)
            d_up[here] = (d_act * g * s).astype(BF16).reshape(held)

        in_tiles(hidden_width, tile, hidden)

        def back(columns):
            whole = (*index, slice(None))
            value = dot(d_gate[whole].reshape(shape), rows_of(w_gate, columns), NT)
            value = value + dot(d_up[whole].reshape(shape), rows_of(w_up, columns), NT)
            here = (*index, columns)
            partial[here] = value.astype(BF16).reshape(partial[here].shape)

        in_tiles(partial.shape[-1], tile, back)

    block = 4 * tiles.shape[3]

    def all_rows(ref, columns=slice(None)):
        value = ref[:, :, :, columns]
        return value.reshape(-1, value.shape[-1])

    def sent(slot, k, i):
        return pltpu.make_async_copy(
            tiles.at[slot, k], grads_out.at[k, i // RING, i % RING], tile_sems.at[slot, k]
        )

    def weight_grads(begin, end):
        def step(i, carry):
            slot = i % 2
            columns = pl.ds(pl.multiple_of(i * block, block), block)
            for k, right in enumerate((d_gate, d_up)):

                @pl.when(i >= 2)
                def _():
                    sent(slot, k, i - 2).wait()

                value = dot(all_rows(x_all, columns), all_rows(right), TN)
                tiles[slot, k] = value.astype(BF16).reshape(tiles.shape[2:])
                sent(slot, k, i).start()
            return carry

        lax.fori_loop(begin, end, step, 0)

    half = act.shape[-1] // 2

    def down_grad(p, sems, buffers):
        columns = pl.ds(p * half, half)
        right = all_rows(act, columns)
        for i in range(2 * RING):
            value = dot(all_rows(d_all, pl.ds(i * block, block)), right, TN).astype(BF16)
            down_partial[i // RING, i % RING, :, :, columns] = value.reshape(*down_partial.shape[2:4], half)
        task = plane_scatter(
            place,
            sender,
            sems,
            down_partial.at[:, :, :, :, columns],
            down_out.at[:, :, columns],
            down_partial.shape[3] // 2,
            buffers,
        )
        next(task)
        return task

    tasks = []

    def down_grads():
        tasks.append(down_grad(0, plane, first_buffers))
        tasks.append(down_grad(1, plane2, second_buffers))

    in_turn(gather, total, backward, down_grads)
    task, task2 = tasks
    total.collect(2)
    next(task)
    total.collect(0)
    next(task2)
    weight_grads(0, 3)
    total.relay()
    weight_grads(3, 4)
    next(task)
    weight_grads(4, 6)
    next(task2)
    weight_grads(6, 7)
    next(task)
    weight_grads(7, 8)
    next(task2)
    total.finish(d_mixed_out)
    sender.settle(gather.begun)

    def attention_norm(rows):
        value, gain = proj[rows, :], gain_rows[2:3, :]
        d_mixed = cotangent[rows, :].astype(F32) + d_mixed_out[rows, :]
        d_mixed_out[rows, :] = d_mixed
        scale = norm_scale(value)
        d_proj_out[rows, :] = norm_back(d_mixed, value, scale, gain).astype(BF16)
        gains_out[0:1, :] += jnp.sum(d_mixed * value * scale, axis=0, keepdims=True)

    by_rows(down_proj.shape[0], attention_norm)
    take_turns((task, task2))
    for i in (6, 7):
        for k in range(2):
            sent(i % 2, k, i).wait()
    sender.finish()


def mlp(number, own, gate_up, down, mixed, cotangent, proj, gain_rows):
    rows, width = own.shape
    piece, hidden = down.shape[-2:]
    tokens = (2, 2, 2 * rows)
    weight = pltpu.VMEM((2, 16, piece, hidden), BF16)
    wide, narrow = pltpu.VMEM((*tokens, width), BF16), pltpu.VMEM((*tokens, hidden), BF16)
    return call(
        mlp_kernel,
        number,
        (
            shape_of(rows, width),
            shape_of(rows, width, dtype=F32),
            shape_of(rows, width),
            shape_of(8, width, dtype=F32),
            shape_of(2, 2, RING, RING, piece, hidden),
            shape_of(2, piece, hidden),
        ),
        [ANYWHERE] * 3 + [IN_VMEM] * 4,
        (IN_VMEM, IN_VMEM, IN_VMEM, IN_VMEM, ANYWHERE, IN_VMEM),
        [
            wide,
            wide,
            *[weight] * 3,
            *[narrow] * 3,
            wide,
            pltpu.VMEM((2, 2, 4, piece, hidden), BF16),
            pltpu.VMEM((2, RING, RING, piece, hidden), BF16),
            pltpu.VMEM((rows, width), F32),
            *ring_buffers(rows, width),
            *scatter_buffers(piece, hidden // 2, BF16),
            *scatter_buffers(piece, hidden // 2, BF16),
            dma_sems(128),
            dma_sems(RING, 4),
            dma_sems(4, 2 * PIECES),
            dma_sems(RING, 4),
            dma_sems(4, 2 * PIECES),
            dma_sems(2, 2),
            dma_sems(2, 12),
            dma_sems(2, 12),
        ],
        (own, gate_up, down.reshape(2, 16, piece, hidden), mixed, cotangent, proj, gain_rows),
    )


def ring_product(place, total, values, weight, partial, others, before_near=lambda: None):
    def compute(dy):
        y = place.shift("y", dy)
        at = (y % 2, y // 2)

        def tile(columns):
            partial[(*at, slice(None), columns)] = dot(values[at], weight[columns, :], NT).astype(BF16)

        in_tiles(partial.shape[-1], 512, tile)
        total.offer(dy)

    compute(2)
    before_near()
    compute(1)
    total.collect(2)
    compute(-1)
    total.collect(1)
    compute(0)
    total.collect(-1)
    total.collect(0)
    for task in others:
        next(task)
    total.relay()


def flat(weight):
    return weight.reshape(-1, weight.shape[-1])


def exact(left, right, dims):
    return lax.dot_general(
        left, right, dims, precision=lax.Precision.HIGHEST, preferred_element_type=F32
    )


def half_roll(values):
    return pltpu.roll(values, HEAD_DIM // 2, 1)


def near_devices(place):
    return [place.at(axis, step) for axis in ("x", "z") for step in (1, -1)]


class Octet:
    peers = [(dy, dc) for dy in (0, 1, 3, 2) for dc in (0, 1) if dy or dc]

    def __init__(self, place, sender, own, slots, sems):
        self.place, self.sender, self.own, self.slots, self.sems = place, sender, own, slots, sems

    @staticmethod
    def device(place, dy, dc):
        y = place.shift("y", dy)
        return {"yl": y % 2, "yh": y // 2, "c": (place.c + dc) % 2}

    def send(self):
        for dy, dc in self.peers:
            slot = ((RING - dy) % RING) * 2 + dc
            device = self.device(self.place, dy, dc)
            self.sender.push(self.own, self.slots.at[slot], self.sems.at[slot], device)

    def total(self):
        for dy, dc in self.peers:
            slot = dy * 2 + dc
            self.sender.arrived(self.slots.at[slot], self.sems.at[slot], self.device(self.place, dy, dc))
        value = self.own[...]
        for dy, dc in self.peers:
            value = value + self.slots[dy * 2 + dc]
        return value


def one_hot_rows(k):
    return (lax.broadcasted_iota(jnp.int32, (8, HEAD_DIM), 0) == k).astype(F32)


def masked(scores, starts, i):
    tile, count = scores.shape
    keys = lax.broadcasted_iota(jnp.int32, (tile, count), 1)
    queries = lax.broadcasted_iota(jnp.int32, (tile, count), 0) + i * tile
    return jnp.where((keys >= starts) & (keys <= queries), scores, -1e30)


def softmax(scores):
    exponent = jnp.exp(scores - jnp.max(scores, axis=-1, keepdims=True))
    return exponent / jnp.sum(exponent, axis=-1, keepdims=True)


def attention_forward_kernel(
    inputs, weight, down_pair, cosine, sine, starts, head_gains, hidden, gain_rows, proj_out, mixed_out,
    low_out, raw_out, rot_out, value_out, scale_out, attended_out, down_out, *refs
):
    (
        (x_all, own_weight, raw, rot, values, scales, attended, partial, sums, slots, down_all),
        ring,
        (sends, sum_sems, octet_sems, plane),
    ) = refs_of(refs, 11, 4, 4)
    place = Place()
    sender = Sender(sends)
    loads = [sender.keep_first(weight, own_weight), sender.keep_first(inputs, x_all)]
    _, heads, _, block_rows, _ = raw.shape
    inner = heads * HEAD_DIM
    tile = block_rows // 2
    pair = sender.keep_first(down_pair, down_all.at[:, place.x, place.z])
    greet(near_devices(place) + [Octet.device(place, *peer) for peer in Octet.peers])
    total = RingSum(place, sender, sum_sems, partial, *ring)
    ones = [one_hot_rows(k) for k in range(2)]
    pair.wait()
    down_task = plane_gather(place, sender, plane, down_all, down_all.shape[3] // 2)
    next(down_task)
    for load in loads:
        load.wait()

    def project(t, carry):
        a, b = t // 2, t % 2
        window = pl.ds(pl.multiple_of(b * tile, tile), tile)
        value = dot(x_all[a, b], own_weight[:, pl.ds(0, 2 * inner)])
        row_sums = jnp.zeros((8, tile), F32)
        for k in range(2):
            for h in range(heads):
                column = k * inner + h * HEAD_DIM
                part = value[:, column : column + HEAD_DIM]
                raw[k, h, a, window, :] = part
                row_sums = row_sums + exact(ones[k], part * part, NT)
        sums[:, pl.ds(pl.multiple_of(t * tile, tile), tile)] = row_sums
        return carry

    def project_value(t, carry):
        a, b = t // 2, t % 2
        window = pl.ds(pl.multiple_of(b * tile, tile), tile)
        value = dot(x_all[a, b], own_weight[:, pl.ds(2 * inner, inner)]).astype(BF16)
        for h in range(heads):
            values[h, a, window, :] = value[:, h * HEAD_DIM : (h + 1) * HEAD_DIM]
        return carry

    lax.fori_loop(0, 4, project, 0)
    octet = Octet(place, sender, sums, slots, octet_sems)
    octet.send()
    sender.keep(raw, raw_out)
    lax.fori_loop(0, 4, project_value, 0)
    sender.keep(values, value_out)
    next(down_task)
    row_scales = lax.rsqrt(octet.total() / x_all.shape[3] + NORM_EPS)
    for b in range(2):
        for k in range(2):
            scale = exact(row_scales[:, b * block_rows : (b + 1) * block_rows], ones[k], TN)
            scales[k, b] = scale
            for h in range(heads):
                lanes = slice(h * HEAD_DIM, (h + 1) * HEAD_DIM)
                value = raw[k, h, b] * scale * head_gains[k : k + 1, lanes]
                rot[k, h, b] = (value * cosine[b] + half_roll(value) * sine[b]).astype(BF16)
    sender.keep(scales, scale_out)
    sender.keep(rot, rot_out)
    next(down_task)

    def attention(b):
        for h in range(heads):
            key, value = rot[1, h, b], values[h, b]
            for i in range(2):
                window, count = pl.ds(i * tile, tile), (i + 1) * tile
                scores = dot(rot[0, h, b, window, :], key[:count], NT) * HEAD_DIM ** (-0.5)
                probs = softmax(masked(scores, starts[b, window, 0:1], i)).astype(BF16)
                attended[b, i, :, pl.ds(h * HEAD_DIM, HEAD_DIM)] = dot(probs, value[:count]).astype(BF16)

    attention(place.yl)
    out_weight = own_weight.at[:, pl.ds(3 * inner, inner)]
    ring_product(
        place, total, attended, out_weight, partial, (), lambda: attention(1 - place.yl)
    )
    sender.keep(attended, attended_out)
    take_turns((down_task,))
    sender.keep(down_all, down_out)
    total.finish(proj_out)

    def mix(rows):
        value = proj_out[rows, :]
        mixed = hidden[rows, :].astype(F32) + value * norm_scale(value) * gain_rows[2:3, :]
        mixed_out[rows, :] = mixed
        low_out[rows, :] = mixed.astype(BF16)

    by_rows(proj_out.shape[0], mix)
    sender.finish()


def attention_forward(number, inputs, weight, down_pair, *others):
    _, _, pair_rows, width = inputs.shape
    inner = weight.shape[1] // 4
    heads = inner // HEAD_DIM
    raw, rot = (2, heads, 2, 2 * pair_rows, HEAD_DIM), (2, heads, 2, 2 * pair_rows, HEAD_DIM)
    values, scales, attended = rot[1:], (2, 2, 2 * pair_rows, HEAD_DIM), (2, 2, pair_rows, inner)
    return call(
        attention_forward_kernel,
        number,
        (
            shape_of(pair_rows // 2, width, dtype=F32),
            shape_of(pair_rows // 2, width, dtype=F32),
            shape_of(pair_rows // 2, width),
            shape_of(*raw, dtype=F32),
            shape_of(*rot),
            shape_of(*values),
            shape_of(*scales, dtype=F32),
            shape_of(*attended),
            shape_of(2, RING, RING, *down_pair.shape[1:]),
        ),
        [ANYWHERE] * 3 + [IN_VMEM] * len(others),
        (IN_VMEM,) * 3 + (ANYWHERE,) * 6,
        [
            pltpu.VMEM(inputs.shape, BF16),
            pltpu.VMEM(weight.shape, BF16),
            pltpu.VMEM(raw, F32),
            pltpu.VMEM(rot, BF16),
            pltpu.VMEM(values, BF16),
            pltpu.VMEM(scales, F32),
            pltpu.VMEM(attended, BF16),
            pltpu.VMEM(inputs.shape, BF16),
            pltpu.VMEM((8, 4 * pair_rows), F32),
            pltpu.VMEM((8, 8, 4 * pair_rows), F32),
            pltpu.VMEM((2, RING, RING, *down_pair.shape[1:]), BF16),
            *ring_buffers(pair_rows // 2, width),
            dma_sems(96),
            dma_sems(4, 2 * PIECES),
            dma_sems(8),
            dma_sems(2, RING, RING, 3),
        ],
        (inputs, weight, down_pair, *others),
    )


def attention_backward_kernel(
    own, weight, attended, inputs, mlp_in, down, raw_all, rot, values, scales, cosines, sines, starts,
    head_gains, token_gains, out, attn_out, gain_out, mlp_out, *refs
):
    (
        (shared, own_weight, attn_partial, mlp_partial, d_att, back, d_qkv, sums, slots),
        (gain_partial, gain_rows, gain_slots, attn_done, gain_done, mlp_done),
        ring,
        buffers,
        late_buffers,
        gate_buffers,
        up_buffers,
        gain_buffers,
        (sends, gather_sems, sum_sems, octet_sems, gain_sems, swap, plane, late_plane, gain_plane, gate_plane),
        (up_plane,),
    ) = refs_of(refs, 9, 6, 4, 5, 5, 5, 5, 5, 10, 1)
    d_all = x_all = partial = shared
    place = Place()
    sender = Sender(sends)
    _, heads, _, block_rows, _ = rot.shape
    width = d_qkv.shape[-1]
    inner = heads * HEAD_DIM
    rows = attn_partial.shape[3]
    block = RING * rows
    mlp_loads = [sender.keep_first(mlp_in.at[k], mlp_partial.at[k]) for k in range(2)]
    load = sender.keep_first(weight, own_weight)
    partner = {"yl": 1 - place.yl}
    me, you = place.yl, 1 - place.yl
    greet(near_devices(place) + [Octet.device(place, *peer) for peer in Octet.peers])
    gather = RingGather(place, sender, gather_sems, own, d_all)
    total = RingSum(place, sender, sum_sems, partial, *ring)
    gather.begin()
    sender.push(down.at[you], mlp_out.at[2, me], swap.at[3], partner)
    sender.keep(down.at[me], mlp_out.at[2, me])
    mlp = []
    for k, (sems, bufs) in enumerate(((gate_plane, gate_buffers), (up_plane, up_buffers))):
        mlp_loads[k].wait()
        task = plane_scatter(place, sender, sems, mlp_partial.at[k], mlp_done.at[k], rows // 2, bufs)
        next(task)
        mlp.append(task)
    gate_task, up_task = mlp
    load.wait()
    gain_partial[...] = jnp.zeros_like(gain_partial)
    gain_rows[...] = jnp.zeros_like(gain_rows)
    for k in range(2 * RING):
        for z in range(RING):
            gain_partial[k // RING, k % RING, z, 2:4, :] = token_gains[0:2, k * block : (k + 1) * block]

    def compute(dy):
        gather.ready(dy)
        y = place.shift("y", dy)
        at = (y % 2, y // 2)
        d_att[at] = dot(d_all[at], own_weight[:, pl.ds(width, inner)]).astype(BF16)

    tile = block_rows // 2
    score_factor = HEAD_DIM ** (-0.5)
    ones = [one_hot_rows(k) for k in range(2)]

    def attention(b):
        row_sums = jnp.zeros((8, block_rows), F32)
        cosine, sine = cosines[b], sines[b]
        for h in range(heads):
            lanes = pl.ds(h * HEAD_DIM, HEAD_DIM)
            key, value = rot[1, h, b], values[h, b]
            d_query, d_key, d_value = [], [None, None], [None, None]
            for i in range(2):
                window = pl.ds(i * tile, tile)
                query, upstream = rot[0, h, b, window, :], d_att[b, i, :, lanes]
                count = (i + 1) * tile
                scores = dot(query, key[:count], NT) * score_factor
                probs = softmax(masked(scores, starts[b, window, 0:1], i))
                d_probs = dot(upstream, value[:count], NT)
                row_dot = jnp.sum(probs * d_probs, axis=-1, keepdims=True)
                d_scores = (probs * (d_probs - row_dot) * score_factor).astype(BF16)
                probs = probs.astype(BF16)
                d_query.append(dot(d_scores, key[:count]))
                for j in range(i + 1):
                    part = slice(j * tile, (j + 1) * tile)
                    for sums_of, left, right in ((d_key, d_scores, query), (d_value, probs, upstream)):
                        term = dot(left[:, part], right, TN)
                        sums_of[j] = term if sums_of[j] is None else sums_of[j] + term
            for i in range(2):
                d_qkv[b, i, :, pl.ds(2 * inner + h * HEAD_DIM, HEAD_DIM)] = d_value[i].astype(BF16)
            for k, parts in enumerate((d_query, d_key)):
                turned = jnp.concatenate(parts, axis=0)
                turned = turned * cosine - half_roll(turned) * sine
                raw = raw_all[k, h, b]
                gain_rows[k : k + 1, lanes] += jnp.sum(turned * raw * scales[k, b], axis=0, keepdims=True)
                turned = turned * head_gains[k : k + 1, lanes]
                back[k, h, b] = turned
                row_sums = row_sums + exact(ones[k], turned * raw, NT)
        sums[:, pl.ds(pl.multiple_of(b * block_rows, block_rows), block_rows)] = row_sums

    compute(0)
    gather.relay()
    compute(1)
    compute(-1)
    next(gate_task)
    attention(1 - place.yl)
    gather.relay_far()
    compute(2)
    next(up_task)
    attention(place.yl)
    octet = Octet(place, sender, sums, slots, octet_sems)
    octet.send()
    first = (place.yh * 2 + place.c) * 2 + place.yl
    for z in range(RING):
        gain_partial[first // RING, first % RING, z, 0:2, :] = gain_rows[0:2, :]
    gains = plane_scatter(place, sender, gain_plane, gain_partial, gain_done, gain_done.shape[1], gain_buffers)
    next(gains)

    def flat_tokens(ref, columns=slice(None)):
        value = ref[:, :, :, columns]
        return value.reshape(-1, value.shape[-1])

    def weight_grads(left_ref, right, start):
        size = right.shape[1]
        for i in range(2 * RING):
            left = flat_tokens(left_ref, pl.ds(i * block, block))
            value = dot(left, right, TN).astype(BF16)
            attn_partial[i // RING, i % RING, :, :, pl.ds(start, size)] = value.reshape(RING, rows, size)

    weight_grads(d_all, flat_tokens(attended), width)
    sender.settle(gather.forwarded)
    load = sender.keep_first(inputs, x_all)
    next(gate_task)
    load.wait()

    def attn_scatter(columns, sems, bufs):
        task = plane_scatter(
            place,
            sender,
            sems,
            attn_partial.at[:, :, :, :, columns],
            attn_done.at[:, :, columns],
            rows // 2,
            bufs,
        )
        next(task)
        return task

    weight_grads(x_all, flat_tokens(d_qkv, pl.ds(2 * inner, inner)), 2 * inner)
    early = attn_scatter(pl.ds(2 * inner, 2 * inner), plane, buffers)
    row_sums = octet.total()
    for b in range(2):
        for k in range(2):
            column = exact(row_sums[:, b * block_rows : (b + 1) * block_rows], ones[k], TN)
            for h in range(heads):
                scale = scales[k, b]
                value = scale * back[k, h, b] - raw_all[k, h, b] * (scale * scale * scale * column / own.shape[1])
                value = value.astype(BF16)
                for i in range(2):
                    d_qkv[b, i, :, pl.ds(k * inner + h * HEAD_DIM, HEAD_DIM)] = value[
                        i * tile : (i + 1) * tile
                    ]
    weight_grads(x_all, flat_tokens(d_qkv, pl.ds(0, 2 * inner)), 0)
    late = attn_scatter(pl.ds(0, 2 * inner), late_plane, late_buffers)
    next(gate_task)
    next(up_task)
    next(early)
    ring_product(
        place, total, d_qkv, own_weight.at[:, pl.ds(0, width)], partial, (late, up_task, gains)
    )
    take_turns((gate_task, up_task))
    for k in range(2):
        sender.push(mlp_done.at[k, you], mlp_out.at[k, me], swap.at[1 + k], partner)
        sender.keep(mlp_done.at[k, me], mlp_out.at[k, me])
    take_turns((early, gains, late))
    sender.push(attn_done.at[you], attn_out.at[me], swap.at[0], partner)
    sender.keep(attn_done.at[me], attn_out.at[me])
    everyone = Octet(place, sender, gain_done, gain_slots, gain_sems)
    everyone.send()
    total.finish(out)
    gain_out[...] = everyone.total()
    sender.arrived(attn_out.at[you], swap.at[0], partner)
    for k in range(3):
        sender.arrived(mlp_out.at[k, you], swap.at[1 + k], partner)
    sender.finish()


def attention_backward(number, own, weight, attended, inputs, mlp_partial, *others):
    rows, width = own.shape
    tokens = (2, 2, 2 * rows)
    inner = attended.shape[3]
    heads = inner // HEAD_DIM
    shard = width // 32, weight.shape[1]
    gain_tile = (8, 4 * shard[0])
    return call(
        attention_backward_kernel,
        number,
        (
            shape_of(rows, width, dtype=F32),
            shape_of(2, *shard),
            shape_of(2, *gain_tile, dtype=F32),
            shape_of(3, 2, *shard),
        ),
        [ANYWHERE, ANYWHERE, IN_VMEM, ANYWHERE, ANYWHERE] + [IN_VMEM] * len(others),
        (IN_VMEM,) * 4,
        [
            pltpu.VMEM((*tokens, width), BF16),
            pltpu.VMEM(weight.shape, BF16),
            pltpu.VMEM((2, RING, RING, *shard), BF16),
            pltpu.VMEM((2, 2, RING, RING, *shard), BF16),
            pltpu.VMEM((*tokens, inner), BF16),
            pltpu.VMEM((2, heads, 2, 4 * rows, HEAD_DIM), F32),
            pltpu.VMEM((*tokens, 3 * inner), BF16),
            pltpu.VMEM((8, 8 * rows), F32),
            pltpu.VMEM((8, 8, 8 * rows), F32),
            pltpu.VMEM((2, RING, RING, *gain_tile), F32),
            pltpu.VMEM((8, inner), F32),
            pltpu.VMEM((8, 2, *gain_tile), F32),
            pltpu.VMEM((2, *shard), BF16),
            pltpu.VMEM((2, *gain_tile), F32),
            pltpu.VMEM((2, 2, *shard), BF16),
            *ring_buffers(rows, width),
            *scatter_buffers(shard[0], shard[1] // 2, BF16),
            *scatter_buffers(shard[0], shard[1] // 2, BF16),
            *scatter_buffers(*shard, BF16),
            *scatter_buffers(*shard, BF16),
            *scatter_buffers(*gain_tile, F32),
            dma_sems(208),
            dma_sems(RING, 4),
            dma_sems(4, 2 * PIECES),
            dma_sems(8),
            dma_sems(8),
            dma_sems(4),
            dma_sems(2, 12),
            dma_sems(2, 12),
            dma_sems(2, 12),
            dma_sems(2, 12),
            dma_sems(2, 12),
        ],
        (own, weight, attended, inputs, mlp_partial, *others),
    )


def norm_scale(values):
    return lax.rsqrt(jnp.mean(values * values, axis=-1, keepdims=True) + NORM_EPS)


def norm_back(upstream, values, scales, gain_row):
    scaled_grad = upstream * gain_row
    return scales * scaled_grad - values * scales**3 * jnp.mean(
        scaled_grad * values, axis=-1, keepdims=True
    )


def doc_layout(lengths, group_size):
    positions = jnp.arange(group_size, dtype=jnp.int32)
    doc_ends = jnp.cumsum(lengths)
    passed = (positions[:, None] >= doc_ends[None, :]).astype(jnp.int32)
    segment = jnp.sum(passed, axis=-1)
    begins = jnp.sum(passed * lengths[None, :], axis=-1)
    return (segment, positions - begins)


def rope_tables(offsets):
    frequency = ROPE_BASE ** (-jnp.arange(0, HEAD_DIM, 2).astype(jnp.float32) / HEAD_DIM)
    angles = offsets.astype(jnp.float32)[:, None] * frequency[None, :]
    cosine, sine = jnp.cos(angles), jnp.sin(angles)
    return (
        jnp.concatenate([cosine, cosine], axis=-1),
        jnp.concatenate([sine, sine], axis=-1),
    )


def half_turn(values):
    middle = values.shape[-1] // 2
    return jnp.concatenate([-values[..., middle:], values[..., :middle]], axis=-1)


def rotate(values, cosine_table, sine_table):
    return values * cosine_table + half_turn(values) * sine_table


def unrotate(values, cosine_table, sine_table):
    return values * cosine_table - half_turn(values) * sine_table


def product(left, right):
    return jnp.dot(left, right, preferred_element_type=F32)


def row_product(left, right):
    return lax.dot_general(left, right, (((1,), (1,)), ((), ())), preferred_element_type=F32)


def col_product(left, right):
    return lax.dot_general(left, right, (((0,), (0,)), ((), ())), preferred_element_type=F32)


def adam_update(weights_old, first_old, second_old, gradient, rate, decay):
    first_new = BETA_ONE * first_old + (1.0 - BETA_ONE) * gradient
    second_new = BETA_TWO * second_old + (1.0 - BETA_TWO) * gradient * gradient
    ratio = (
        first_new
        / (1.0 - BETA_ONE**STEP)
        / (jnp.sqrt(second_new / (1.0 - BETA_TWO**STEP)) + ADAM_EPS)
    )
    return (first_new, second_new, weights_old - rate * (ratio + decay * weights_old))


def mlp_adam_kernel(weights, first, second, sums, grad_out, first_out, second_out, new_out):
    gradient = sums[0].astype(F32)
    grad_out[...] = gradient
    first_out[...], second_out[...], new_out[...] = adam_update(
        weights[...], first[...], second[...], gradient, WEIGHT_RATE, WEIGHT_DECAY
    )


def mlp_adam(weights, first, second, sums):
    count, rows, columns = weights.shape
    half = columns // 2
    state = pl.BlockSpec((1, rows, half), lambda m, h: (m, 0, h))
    return pl.pallas_call(
        mlp_adam_kernel,
        out_shape=(shape_of(*weights.shape, dtype=F32),) * 4,
        grid=(count, 2),
        in_specs=[state] * 3 + [pl.BlockSpec((1, 1, rows, half), lambda m, h: (m, h, 0, 0))],
        out_specs=(state,) * 4,
        compiler_params=pltpu.CompilerParams(vmem_limit_bytes=VMEM_LIMIT),
    )(weights, first, second, sums)


def attn_adam_kernel(weights, first, second, sums, grad_out, first_out, second_out, new_out):
    inner = weights.shape[2]
    for m in range(weights.shape[0]):
        gradient = sums[0, :, m * inner : (m + 1) * inner].astype(F32)
        grad_out[m] = gradient
        first_out[m], second_out[m], new_out[m] = adam_update(
            weights[m], first[m], second[m], gradient, WEIGHT_RATE, WEIGHT_DECAY
        )


def attn_adam(weights, first, second, sums):
    count, rows, columns = weights.shape
    state = pl.BlockSpec((count, rows, columns // 2), lambda h: (0, 0, h))
    return pl.pallas_call(
        attn_adam_kernel,
        out_shape=(shape_of(*weights.shape, dtype=F32),) * 4,
        grid=(2,),
        in_specs=[state] * 3 + [pl.BlockSpec((1, *sums.shape[1:]), lambda h: (h, 0, 0))],
        out_specs=(state,) * 4,
        compiler_params=pltpu.CompilerParams(vmem_limit_bytes=VMEM_LIMIT),
    )(weights, first, second, sums)


def body(
    hidden_in,
    cotangent,
    doc_lengths,
    attn_weights,
    attn_first,
    attn_second,
    mlp_weights,
    mlp_first,
    mlp_second,
    gains,
    gain_first,
    gain_second,
):
    row_count, model_width = hidden_in.shape
    shard_rows = attn_weights.shape[1]
    heads_width = attn_weights.shape[2] // 2
    hidden_width = mlp_weights.shape[2] // 2
    token_count = 8 * row_count
    block_rows = token_count // 2
    head_count = heads_width // HEAD_DIM
    score_factor = HEAD_DIM ** (-0.5)
    yl, yh, core = (lax.axis_index(a) for a in ("yl", "yh", "c"))

    attn_halves = (
        attn_weights.astype(BF16)
        .reshape(4, shard_rows, 2, heads_width)
        .transpose(2, 1, 0, 3)
        .reshape(2, shard_rows, 4 * heads_width)
    )
    gate_up = mlp_weights[:2].astype(BF16).reshape(2, shard_rows, 2, hidden_width)
    mine = lax.dynamic_index_in_dim(gate_up, yl, 2, keepdims=False)
    yours = lax.dynamic_index_in_dim(gate_up, 1 - yl, 2, keepdims=False)
    arrived = lax.ppermute(yours, "yl", [(0, 1), (1, 0)])
    down_halves = mlp_weights[2].astype(BF16).reshape(shard_rows, 2, hidden_width).transpose(1, 0, 2)
    gain_tile = jnp.pad(gains.astype(BF16).astype(F32), ((0, 4), (0, 128 - shard_rows)))
    theirs = lax.ppermute(doc_lengths, "yl", [(0, 1), (1, 0)])
    lengths = jnp.where(yl == 0, jnp.stack([doc_lengths[0], theirs[0]]), jnp.stack([theirs[0], doc_lengths[0]]))
    _, offsets = jax.vmap(lambda one: doc_layout(one, block_rows))(lengths)
    cosine_table, sine_table = rope_tables(offsets.reshape(-1))
    sine_table = sine_table * jnp.where(jnp.arange(HEAD_DIM) < HEAD_DIM // 2, -1.0, 1.0)
    cosine_table = cosine_table.reshape(2, block_rows, HEAD_DIM)
    sine_table = sine_table.reshape(2, block_rows, HEAD_DIM)
    starts = jnp.broadcast_to((jnp.arange(block_rows) - offsets)[:, :, None], (2, block_rows, HEAD_DIM))

    arrived, cosine_table, sine_table, starts, attn_halves, gain_tile, down_halves = lax.optimization_barrier(
        (arrived, cosine_table, sine_table, starts, attn_halves, gain_tile, down_halves)
    )
    pair = jnp.stack(
        [jnp.where(yl == 0, mine, arrived), jnp.where(yl == 0, arrived, mine)], axis=1
    )
    gate_up = lax.all_gather(pair.reshape(-1, hidden_width), ("x", "z"), tiled=True)
    gate_up = gate_up.reshape(16, 2, 2, shard_rows, hidden_width)

    every_input, attn_all, gain_all, down_pair = call(
        first_kernel,
        0,
        (
            shape_of(2, 2, 2 * row_count, model_width),
            shape_of(2, RING, RING, shard_rows, 4 * heads_width),
            shape_of(2, RING, RING, 8, 128, dtype=F32),
            shape_of(2, shard_rows, hidden_width),
        ),
        [ANYWHERE] * 4,
        (ANYWHERE, IN_VMEM, ANYWHERE, ANYWHERE),
        [
            dma_sems(112),
            dma_sems(RING, 4),
            dma_sems(2, RING, RING, 3),
            dma_sems(2, RING, RING, 3),
            dma_sems(3),
        ],
        (hidden_in, attn_halves, gain_tile, down_halves),
    )
    attn_all = flat(attn_all)
    gain_full = gain_all[..., :4, :shard_rows].transpose(3, 0, 1, 2, 4).reshape(4, model_width)
    first_column = (yh * 2 + core) * (2 * heads_width) + yl * heads_width
    head_gains = lax.dynamic_slice(gain_full, (0, first_column), (2, heads_width))
    attn_proj, mixed, mixed_low, raw, rotated, values, head_scales, attended, down_all = attention_forward(
        1,
        every_input,
        attn_all,
        down_pair,
        cosine_table,
        sine_table,
        starts,
        head_gains,
        hidden_in,
        gain_full,
    )
    hidden_out, d_mixed, d_proj, token_gains, mlp_partial, down_sum = mlp(
        2, mixed_low, gate_up, down_all, mixed, cotangent, attn_proj, gain_full
    )
    input_sum, attn_sum, gain_sum, mlp_sum = attention_backward(
        3,
        d_proj,
        attn_all,
        attended,
        every_input,
        mlp_partial,
        down_sum,
        raw,
        rotated,
        values,
        head_scales,
        cosine_table,
        sine_table,
        starts,
        head_gains,
        token_gains,
    )
    input_grad = d_mixed + input_sum

    gain_sum = lax.dynamic_index_in_dim(gain_sum, yl, 0, keepdims=False)[:4]
    gain_grad = lax.dynamic_slice_in_dim(gain_sum, lax.axis_index("z") * shard_rows, shard_rows, axis=1)
    attn_grad, attn_first_new, attn_second_new, attn_new = attn_adam(
        attn_weights, attn_first, attn_second, attn_sum
    )
    mlp_grad, mlp_first_new, mlp_second_new, mlp_new = mlp_adam(
        mlp_weights, mlp_first, mlp_second, mlp_sum
    )
    gain_first_new, gain_second_new, gain_new = adam_update(
        gains, gain_first, gain_second, gain_grad, GAIN_RATE, 0.0
    )
    return (
        hidden_out,
        input_grad,
        attn_grad,
        attn_first_new,
        attn_second_new,
        attn_new,
        mlp_grad,
        mlp_first_new,
        mlp_second_new,
        mlp_new,
        gain_grad,
        gain_first_new,
        gain_second_new,
        gain_new,
    )


def solution(mesh):
    split = Mesh(mesh.devices.reshape(2, 4, 4, 2, 2), EVERY)
    tokens, shards, rows = P(EVERY, None), P(None, DP, TENSOR), P(None, DP)
    return jax.shard_map(
        body,
        mesh=split,
        in_specs=(tokens, tokens, P(DP, None), *[shards] * 6, *[rows] * 3),
        out_specs=(tokens, tokens, *[shards] * 8, *[rows] * 4),
        check_vma=False,
    )
```

```python
import functools

import jax
import jax.numpy as jnp
from jax import lax
from jax.experimental import pallas as pl
from jax.experimental.pallas import tpu as pltpu
from jax.sharding import Mesh
from jax.sharding import PartitionSpec as P

HEAD_DIM = 128
STEP = 10
DP = ("yl", "x", "z")
TENSOR = ("yh", "c")
EVERY = ("yl", "x", "z", "yh", "c")
RING = 4
MESH = pl.DeviceIdType.MESH

NORM_EPS = 1e-06
ROPE_BASE = 500000.0
BETA_ONE = 0.9
BETA_TWO = 0.95
ADAM_EPS = 1e-08
WEIGHT_RATE = 0.03
GAIN_RATE = 1.0
WEIGHT_DECAY = 0.1

BF16 = jnp.bfloat16
F32 = jnp.float32
IN_VMEM = pl.BlockSpec(memory_space=pltpu.VMEM)
ANYWHERE = pl.BlockSpec(memory_space=pl.ANY)
VMEM_LIMIT = 60 * 1024 * 1024


class Place:
    def __init__(self):
        self.x, self.z, self.c = (lax.axis_index(a) for a in ("x", "z", "c"))
        self.yl, self.yh = (lax.axis_index(a) for a in ("yl", "yh"))
        self.y = self.yh * 2 + self.yl

    def at(self, axis, step):
        if axis == "y":
            there = (self.y + step + RING) % RING
            return {"yl": there % 2, "yh": there // 2}
        if axis == "c":
            return {"c": 1 - self.c}
        return {axis: (getattr(self, axis) + step + RING) % RING}

    def shift(self, axis, step):
        return (getattr(self, axis) + step + RING) % RING


def greet(devices):
    barrier = pltpu.get_barrier_semaphore()
    for device in devices:
        pl.semaphore_signal(barrier, inc=1, device_id=device, device_id_type=MESH)
    pl.semaphore_wait(barrier, len(devices))


def greet_all(place, axes):
    devices = []
    for axis in axes:
        devices += [place.at(axis, 1)] if axis == "c" else [place.at(axis, 1), place.at(axis, -1)]
    greet(devices)


class Sender:
    def __init__(self, sems):
        self.sems, self.open = sems, []

    def push(self, src, dst, recv_sem, device):
        copy = pltpu.make_async_remote_copy(
            src_ref=src,
            dst_ref=dst,
            send_sem=self.sems.at[len(self.open)],
            recv_sem=recv_sem,
            device_id=device,
            device_id_type=MESH,
        )
        copy.start()
        self.open.append(copy.wait_send)
        return len(self.open) - 1

    def settle(self, numbers):
        for number in numbers:
            self.open[number]()
            self.open[number] = lambda: None

    def keep(self, src, dst):
        copy = pltpu.make_async_copy(src, dst, self.sems.at[len(self.open)])
        copy.start()
        self.open.append(copy.wait)

    def keep_first(self, src, dst):
        copy = pltpu.make_async_copy(src, dst, self.sems.at[len(self.open)])
        copy.start()
        self.open.append(lambda: None)
        return copy

    def arrived(self, dst, recv_sem, device):
        pltpu.make_async_remote_copy(
            src_ref=dst,
            dst_ref=dst,
            send_sem=self.sems.at[0],
            recv_sem=recv_sem,
            device_id=device,
            device_id_type=MESH,
        ).wait_recv()

    def finish(self):
        for wait in self.open:
            wait()


def take_turns(tasks):
    tasks = list(tasks)
    while tasks:
        for task in list(tasks):
            if next(task, "done") == "done":
                tasks.remove(task)


WHOLE, LOW, HIGH = 0, 1, 2
PIECES = 4


def part_of(ref, part, cut):
    rows = ref.shape[-2]
    if part == WHOLE:
        return ref
    return ref.at[pl.ds(0, cut)] if part == LOW else ref.at[pl.ds(cut, rows - cut)]


def plane_gather(place, sender, sems, out, cut):
    rows = out.shape[-2]
    axes = (("x", "z"), ("z", "x"))

    def piece(half, dp, dq):
        p, q = (place.shift(a, d) for a, d in zip(axes[half], (dp, dq)))
        return out.at[half, p, q] if half == 0 else out.at[half, q, p]

    def parts(part):
        if part == WHOLE:
            return True
        return cut > 0 if part == LOW else cut < rows

    def send(half, dp, dq, part, along, step):
        if parts(part):
            ref = part_of(piece(half, dp, dq), part, cut)
            sp, sq = ((dp - step) % RING, dq % RING) if along == 0 else (dp % RING, (dq - step) % RING)
            sender.push(ref, ref, sems.at[half, sp, sq, part], place.at(axes[half][along], step))

    def wait(half, dp, dq, part):
        if parts(part):
            ref = part_of(piece(half, dp, dq), part, cut)
            sender.arrived(ref, sems.at[half, dp % RING, dq % RING, part], place.at("x", 1))

    both = (0, 1)
    for half in both:
        for step in (1, -1):
            send(half, 0, 0, WHOLE, 0, step)
    for half in both:
        for step in (1, -1):
            send(half, 0, 0, WHOLE, 1, step)
    yield
    for step, part in ((1, LOW), (-1, HIGH)):
        for half in both:
            wait(half, -step, 0, WHOLE)
            send(half, -step, 0, part, 0, step)
            for side in (1, -1):
                send(half, -step, 0, WHOLE, 1, side)
    yield
    for half in both:
        for step, part in ((1, LOW), (-1, HIGH)):
            wait(half, 0, -step, WHOLE)
            send(half, 0, -step, part, 1, step)
    yield
    for half in both:
        wait(half, 2, 0, LOW)
        wait(half, 2, 0, HIGH)
        for side in (1, -1):
            send(half, 2, 0, WHOLE, 1, side)
    yield
    for dp in (-1, 1, 2):
        for half in both:
            for step, part in ((1, LOW), (-1, HIGH)):
                wait(half, dp, -step, WHOLE)
                send(half, dp, -step, part, 1, step)
        yield
    for dp in (0, -1, 1, 2):
        for half in both:
            wait(half, dp, 2, LOW)
            wait(half, dp, 2, HIGH)


class RingGather:
    def __init__(self, place, sender, sems, own, out):
        self.place, self.sender, self.sems, self.own, self.out = place, sender, sems, own, out
        self.rows = own.shape[0]
        self.other = place.at("c", 1)
        self.begun, self.forwarded = [], []

    def piece(self, dy, core, part=WHOLE):
        y = self.place.shift("y", dy)
        half = self.rows // 2
        start, size = {WHOLE: (0, self.rows), LOW: (0, half), HIGH: (half, half)}[part]
        return self.out.at[y % 2, y // 2, pl.ds(pl.multiple_of(core * self.rows + start, 16), size)]

    def begin(self):
        place, mine = self.place, self.piece(0, self.place.c)
        for step in (1, -1):
            number = self.sender.push(self.own, mine, self.sems.at[(-step) % RING, WHOLE], place.at("y", step))
            self.begun.append(number)
        self.begun.append(self.sender.push(self.own, mine, self.sems.at[0, 3], self.other))
        self.kept = self.sender.keep_first(self.own, mine)

    def relay(self):
        for step, part in ((1, LOW), (-1, HIGH)):
            ref = self.piece(-step, self.place.c)
            self.sender.arrived(ref, self.sems.at[(-step) % RING, WHOLE], self.other)
            half = self.piece(-step, self.place.c, part)
            self.forwarded += [
                self.sender.push(half, half, self.sems.at[2, part], self.place.at("y", step)),
                self.sender.push(ref, ref, self.sems.at[(-step) % RING, 3], self.other),
            ]

    def relay_far(self):
        for part in (LOW, HIGH):
            self.sender.arrived(self.piece(2, self.place.c, part), self.sems.at[2, part], self.other)
        ref = self.piece(2, self.place.c)
        self.forwarded += [self.sender.push(ref, ref, self.sems.at[2, 3], self.other)]

    def ready(self, dy):
        if dy == 0:
            self.kept.wait()
        self.sender.arrived(self.piece(dy, 1 - self.place.c), self.sems.at[dy % RING, 3], self.other)


def ring_gather(place, sender, sems, own, out):
    gather = RingGather(place, sender, sems, own, out)
    gather.begin()
    yield
    gather.relay()
    yield
    gather.relay_far()
    yield
    for dy in (0, 1, -1, 2):
        gather.ready(dy)


def add_rows(out, terms, rows):
    def step(i, carry):
        window = pl.ds(pl.multiple_of(i * 16, 16), 16)
        total = terms[0][window, :].astype(F32)
        for term in terms[1:]:
            total = total + term[window, :].astype(F32)
        out[window, :] = total.astype(out.dtype)
        return carry

    lax.fori_loop(0, rows // 16, step, 0)


class RingSum:
    def __init__(self, place, sender, sems, partial, kept, from_core, hop, last):
        self.place, self.sender, self.sems, self.partial = place, sender, sems, partial
        self.kept, self.from_core, self.hop, self.last = kept, from_core, hop, last
        self.rows = kept.shape[1]
        self.low, self.high = pl.ds(0, self.rows // 2), pl.ds(self.rows // 2, self.rows // 2)
        self.other = place.at("c", 1)

    def mine(self, dy, core):
        y = self.place.shift("y", dy)
        return self.partial.at[y % 2, y // 2, pl.ds(pl.multiple_of(core * self.rows, 16), self.rows)]

    def offer(self, dy):
        slot = dy % RING
        self.sender.push(
            self.mine(dy, 1 - self.place.c), self.from_core.at[slot], self.sems.at[0, slot], self.other
        )

    def pieces(self):
        columns = self.kept.shape[2]
        return [pl.ds(p * columns // PIECES, columns // PIECES) for p in range(PIECES)]

    def collect(self, dy):
        slot = dy % RING
        kept, low, high = self.kept.at[slot], self.low, self.high
        self.sender.arrived(self.from_core.at[slot], self.sems.at[0, slot], self.other)
        if dy == 0:
            return
        up, down = self.place.at("y", 1), self.place.at("y", -1)
        mine = self.mine(dy, self.place.c)
        if dy == 2:
            for p, columns in enumerate(self.pieces()):
                add_rows(kept.at[:, columns], (mine.at[:, columns], self.from_core.at[slot, :, columns]), self.rows)
                self.sender.push(kept.at[low, columns], self.hop.at[0, :, columns], self.sems.at[1, p], up)
                self.sender.push(
                    kept.at[high, columns], self.hop.at[1, :, columns], self.sems.at[1, PIECES + p], down
                )
            return
        add_rows(kept, (mine, self.from_core.at[slot]), self.rows)
        if dy == 1:
            self.sender.push(kept.at[high], self.last.at[0, high], self.sems.at[2, 1], up)
        else:
            self.sender.push(kept.at[low], self.last.at[1, low], self.sems.at[2, 2], down)

    def relay(self):
        for p, columns in enumerate(self.pieces()):
            for k, slot, part, step in ((0, 1, self.low, 1), (1, 3, self.high, -1)):
                number = k * PIECES + p
                self.sender.arrived(self.hop.at[k, :, columns], self.sems.at[1, number], self.other)
                rows = self.kept.at[slot, part, columns]
                add_rows(rows, (rows, self.hop.at[k, :, columns]), self.rows // 2)
                self.sender.push(
                    rows, self.last.at[k, part, columns], self.sems.at[3, number], self.place.at("y", step)
                )

    def finish(self, out):
        self.sender.arrived(self.last.at[0, self.high], self.sems.at[2, 1], self.other)
        self.sender.arrived(self.last.at[1, self.low], self.sems.at[2, 2], self.other)
        mine = self.mine(0, self.place.c)
        for p, columns in enumerate(self.pieces()):
            for k, part in ((0, self.low), (1, self.high)):
                self.sender.arrived(
                    self.last.at[k, part, columns], self.sems.at[3, k * PIECES + p], self.other
                )
            terms = (mine, self.from_core.at[0], self.last.at[0], self.last.at[1])
            add_rows(out.at[:, columns], [term.at[:, columns] for term in terms], self.rows)


def plane_scatter(place, sender, sems, partial, done, cut, bufs):
    rows = partial.shape[-2]
    hop, last, middle, hop2, last2 = bufs
    low, high = pl.ds(0, cut), pl.ds(cut, rows - cut)
    axes = (("z", "x"), ("x", "z"))
    two_parts = cut < rows
    both = (0, 1)
    other = place.at("x", 1)

    def row(half, du, window):
        u = place.shift(axes[half][0], du)
        return partial.at[half, :, u, window] if half == 0 else partial.at[half, u, :, window]

    def line(half, du, v):
        u = place.shift(axes[half][0], du)
        return partial.at[half, v, u] if half == 0 else partial.at[half, u, v]

    def add(out, terms, count):
        if count % 16:
            total = terms[0][...].astype(F32)
            for term in terms[1:]:
                total = total + term[...].astype(F32)
            out[...] = total.astype(out.dtype)
        else:
            add_rows(out, terms, count)

    for half in both:
        u = axes[half][0]
        sender.push(row(half, 2, low), hop.at[half, 0], sems.at[half, 0], place.at(u, 1))
        if two_parts:
            sender.push(row(half, 2, high), hop.at[half, 1], sems.at[half, 1], place.at(u, -1))
    for half in both:
        u = axes[half][0]
        if two_parts:
            sender.push(row(half, 1, high), last.at[half, 0, :, high], sems.at[half, 2], place.at(u, 1))
        sender.push(row(half, -1, low), last.at[half, 1, :, low], sems.at[half, 3], place.at(u, -1))
    yield
    for half in both:
        u = axes[half][0]
        sender.arrived(hop.at[half, 0], sems.at[half, 0], other)
        for v in range(RING):
            add(hop.at[half, 0, v], (line(half, 1, v).at[low], hop.at[half, 0, v]), cut)
        sender.push(hop.at[half, 0], last.at[half, 0, :, low], sems.at[half, 4], place.at(u, 1))
        if two_parts:
            sender.arrived(hop.at[half, 1], sems.at[half, 1], other)
            for v in range(RING):
                add(
                    hop.at[half, 1, v],
                    (line(half, -1, v).at[high], hop.at[half, 1, v]),
                    rows - cut,
                )
            sender.push(
                hop.at[half, 1], last.at[half, 1, :, high], sems.at[half, 5], place.at(u, -1)
            )
    yield
    for half in both:
        v_axis = axes[half][1]
        if two_parts:
            sender.arrived(last.at[half, 0, :, high], sems.at[half, 2], other)
        sender.arrived(last.at[half, 1, :, low], sems.at[half, 3], other)
        sender.arrived(last.at[half, 0, :, low], sems.at[half, 4], other)
        if two_parts:
            sender.arrived(last.at[half, 1, :, high], sems.at[half, 5], other)
        for dv in (2, 1, -1, 0):
            v = place.shift(v_axis, dv)
            terms = (line(half, 0, v), last.at[half, 0, v], last.at[half, 1, v])
            add(middle.at[half, dv % RING], terms, rows)
            if dv == 2:
                sender.push(
                    middle.at[half, 2, low], hop2.at[half, 0], sems.at[half, 6], place.at(v_axis, 1)
                )
                if two_parts:
                    sender.push(
                        middle.at[half, 2, high],
                        hop2.at[half, 1],
                        sems.at[half, 7],
                        place.at(v_axis, -1),
                    )
            elif dv == 1 and two_parts:
                sender.push(
                    middle.at[half, 1, high], last2.at[half, 0, high], sems.at[half, 8], place.at(v_axis, 1)
                )
            elif dv == -1:
                sender.push(
                    middle.at[half, 3, low], last2.at[half, 1, low], sems.at[half, 9], place.at(v_axis, -1)
                )
    yield
    for half in both:
        v_axis = axes[half][1]
        sender.arrived(hop2.at[half, 0], sems.at[half, 6], other)
        add(hop2.at[half, 0], (middle.at[half, 1, low], hop2.at[half, 0]), cut)
        sender.push(
            hop2.at[half, 0], last2.at[half, 0, low], sems.at[half, 10], place.at(v_axis, 1)
        )
        if two_parts:
            sender.arrived(hop2.at[half, 1], sems.at[half, 7], other)
            add(hop2.at[half, 1], (middle.at[half, 3, high], hop2.at[half, 1]), rows - cut)
            sender.push(
                hop2.at[half, 1], last2.at[half, 1, high], sems.at[half, 11], place.at(v_axis, -1)
            )
    yield
    for half in both:
        if two_parts:
            sender.arrived(last2.at[half, 0, high], sems.at[half, 8], other)
        sender.arrived(last2.at[half, 1, low], sems.at[half, 9], other)
        sender.arrived(last2.at[half, 0, low], sems.at[half, 10], other)
        if two_parts:
            sender.arrived(last2.at[half, 1, high], sems.at[half, 11], other)
        add(done.at[half], (middle.at[half, 0], last2.at[half, 0], last2.at[half, 1]), rows)


def scatter_buffers(rows, columns, dtype):
    cut = rows // 2 if dtype == BF16 else rows
    return [
        pltpu.VMEM((2, 2, RING, cut, columns), dtype),
        pltpu.VMEM((2, 2, RING, rows, columns), dtype),
        pltpu.VMEM((2, RING, rows, columns), dtype),
        pltpu.VMEM((2, 2, cut, columns), dtype),
        pltpu.VMEM((2, 2, rows, columns), dtype),
    ]


def ring_buffers(rows, columns):
    return [
        pltpu.VMEM((RING, rows, columns), BF16),
        pltpu.VMEM((RING, rows, columns), BF16),
        pltpu.VMEM((2, rows // 2, columns), BF16),
        pltpu.VMEM((2, rows, columns), BF16),
    ]


def dma_sems(*shape):
    return pltpu.SemaphoreType.DMA(shape)


def shape_of(*shape, dtype=BF16):
    return jax.ShapeDtypeStruct(shape, dtype)


def call(kernel, number, out_shape, in_specs, out_specs, scratch, args):
    return pl.pallas_call(
        kernel,
        out_shape=out_shape,
        in_specs=in_specs,
        out_specs=out_specs,
        scratch_shapes=scratch,
        compiler_params=pltpu.CompilerParams(
            collective_id=number, has_side_effects=True, vmem_limit_bytes=VMEM_LIMIT
        ),
    )(*args)


NN = (((1,), (0,)), ((), ()))
NT = (((1,), (1,)), ((), ()))
TN = (((0,), (0,)), ((), ()))


def dot(left, right, dims=NN):
    return lax.dot_general(left, right, dims, preferred_element_type=F32)


def in_tiles(width, tile, work):
    for n in range(width // tile):
        work(pl.ds(n * tile, tile))


def refs_of(refs, *counts):
    refs, out = list(refs), []
    for n in counts:
        out.append(refs[:n])
        del refs[:n]
    return out


def by_rows(count, work):
    def step(i, carry):
        work(pl.ds(pl.multiple_of(i * 16, 16), 16))
        return carry

    lax.fori_loop(0, count // 16, step, 0)


def load_weights(sender, source, targets):
    copies = []
    for k, target in targets:
        for yl in range(2):
            copies.append(sender.keep_first(source.at[:, :, k, yl], target.at[yl]))
    return copies


def rows_of(weight, window):
    if len(weight.shape) == 2:
        return weight[window, :]
    run = weight.shape[2] * weight.shape[3]
    first, count = window.start // run, window.size // run
    block = weight[first // RING, pl.ds(first % RING, count), :, :, :]
    return block.reshape(window.size, weight.shape[4])


def columns_of(weight, window):
    block = weight[:, :, :, :, window]
    return block.reshape(-1, window.size)


def mlp_kernel(
    own, gate_up, down, mixed_in, cotangent_in, proj_in, gain_rows, hidden_out, d_mixed_out, d_proj_out,
    gains_out, grads_out, down_out, *refs
):
    (
        (x_all, d_all, w_gate, w_up, w_down, gate, up, act, partial, down_partial, tiles),
        (down_proj, mixed, cotangent, proj),
        ring,
        first_buffers,
        second_buffers,
        (sends, gather_sems, sum_sems, gather_sems2, sum_sems2, plane, plane2, tile_sems),
    ) = refs_of(refs, 11, 4, 4, 5, 5, 8)
    d_own = d_proj_out
    d_gate, d_up = gate, up
    place = Place()
    sender = Sender(sends)
    loads = load_weights(sender, gate_up, ((0, w_gate), (1, w_up)))
    load_down = sender.keep_first(down, w_down)
    pairs = ((mixed_in, mixed), (cotangent_in, cotangent), (proj_in, proj))
    later = [sender.keep_first(source, target) for source, target in pairs]
    greet_all(place, ("x", "z", "y", "c"))
    gather = RingGather(place, sender, gather_sems, own, x_all)
    total = RingSum(place, sender, sum_sems, partial, *ring)
    gather.begin()
    for copy in loads:
        copy.wait()
    load_down.wait()
    tile = 512

    def where(dy):
        y = place.shift("y", dy)
        return y % 2, y // 2

    def at_chip(dy):
        at = where(dy)
        return (*at, slice(None)), (2 * rows, hidden_width)

    def at_neighbours(_):
        return (1 - place.yl, slice(None), slice(None)), (4 * rows, hidden_width)

    rows, hidden_width = own.shape[0], act.shape[-1]

    def forward(index, shape):
        count = shape[0]

        def hidden(columns):
            tokens = x_all[(*index, slice(None))].reshape(count, -1)
            g = dot(tokens, columns_of(w_gate, columns))
            u = dot(tokens, columns_of(w_up, columns))
            here = (*index, columns)
            held = act[here].shape
            gate[here], up[here] = g.astype(BF16).reshape(held), u.astype(BF16).reshape(held)
            act[here] = (g * jax.nn.sigmoid(g) * u).astype(BF16).reshape(held)

        in_tiles(hidden_width, tile, hidden)

        def project(columns):
            left = act[(*index, slice(None))].reshape(shape)
            value = dot(left, rows_of(w_down, columns), NT).astype(BF16)
            here = (*index, columns)
            partial[here] = value.reshape(partial[here].shape)

        in_tiles(partial.shape[-1], tile, project)

    def in_turn(gather, total, work, before_far=lambda: None):
        gather.ready(0)
        work(*at_chip(0))
        total.offer(0)
        gather.relay()
        gather.ready(1)
        gather.ready(-1)
        work(*at_neighbours(0))
        total.offer(1)
        total.offer(-1)
        gather.relay_far()
        total.collect(1)
        total.collect(-1)
        gather.ready(2)
        before_far()
        work(*at_chip(2))
        total.offer(2)

    in_turn(gather, total, forward)
    total.collect(2)
    total.collect(0)
    total.relay()
    total.finish(down_proj)
    for copy in later:
        copy.wait()
    sender.settle(range(len(sender.open)))
    gains_out[...] = jnp.zeros_like(gains_out)

    def output_norm(rows):
        value, upstream, gain = down_proj[rows, :], cotangent[rows, :].astype(F32), gain_rows[3:4, :]
        scale = norm_scale(value)
        hidden_out[rows, :] = (mixed[rows, :] + value * scale * gain).astype(BF16)
        d_own[rows, :] = norm_back(upstream, value, scale, gain).astype(BF16)
        gains_out[1:2, :] += jnp.sum(upstream * value * scale, axis=0, keepdims=True)

    by_rows(down_proj.shape[0], output_norm)

    gather = RingGather(place, sender, gather_sems2, d_own, d_all)
    total = RingSum(place, sender, sum_sems2, partial, *ring)
    gather.begin()

    def backward(index, shape):
        count = shape[0]

        def hidden(columns):
            d_act = dot(d_all[(*index, slice(None))].reshape(count, -1), columns_of(w_down, columns))
            here = (*index, columns)
            held = gate[here].shape
            g, u = gate[here].astype(F32).reshape(d_act.shape), up[here].astype(F32).reshape(d_act.shape)
            s = jax.nn.sigmoid(g)
            d_gate[here] = (d_act * u * s * (1.0 + g * (1.0 - s))).astype(BF16).reshape(held)
            d_up[here] = (d_act * g * s).astype(BF16).reshape(held)

        in_tiles(hidden_width, tile, hidden)

        def back(columns):
            whole = (*index, slice(None))
            value = dot(d_gate[whole].reshape(shape), rows_of(w_gate, columns), NT)
            value = value + dot(d_up[whole].reshape(shape), rows_of(w_up, columns), NT)
            here = (*index, columns)
            partial[here] = value.astype(BF16).reshape(partial[here].shape)

        in_tiles(partial.shape[-1], tile, back)

    block = 4 * down_partial.shape[3]

    def all_rows(ref, columns=slice(None)):
        value = ref[:, :, :, columns]
        return value.reshape(-1, value.shape[-1])

    def sent(slot, k, i):
        return pltpu.make_async_copy(
            tiles.at[slot, k], grads_out.at[k, i // RING, i % RING], tile_sems.at[slot, k]
        )

    def weight_grads(begin, end):
        def step(i, carry):
            slot = i % 2
            columns = pl.ds(pl.multiple_of(i * block, block), block)
            for k, right in enumerate((d_gate, d_up)):

                @pl.when(i >= 2)
                def _():
                    sent(slot, k, i - 2).wait()

                value = dot(all_rows(x_all, columns), all_rows(right), TN)
                tiles[slot, k] = value.astype(BF16).reshape(tiles.shape[2:])
                sent(slot, k, i).start()
            return carry

        lax.fori_loop(begin, end, step, 0)

    half = act.shape[-1] // 2

    def down_grad(p, sems, buffers):
        columns = pl.ds(p * half, half)
        right = all_rows(act, columns)
        for i in range(2 * RING):
            value = dot(all_rows(d_all, pl.ds(i * block, block)), right, TN).astype(BF16)
            down_partial[i // RING, i % RING, :, :, columns] = value.reshape(*down_partial.shape[2:4], half)
        task = plane_scatter(
            place,
            sender,
            sems,
            down_partial.at[:, :, :, :, columns],
            down_out.at[:, :, columns],
            down_partial.shape[3] // 2,
            buffers,
        )
        next(task)
        return task

    tasks = []

    def down_grads():
        tasks.append(down_grad(0, plane, first_buffers))
        tasks.append(down_grad(1, plane2, second_buffers))

    in_turn(gather, total, backward, down_grads)
    task, task2 = tasks
    total.collect(2)
    next(task)
    total.collect(0)
    next(task2)
    weight_grads(0, 3)
    total.relay()
    weight_grads(3, 4)
    next(task)
    weight_grads(4, 6)
    next(task2)
    weight_grads(6, 7)
    next(task)
    weight_grads(7, 8)
    next(task2)
    total.finish(d_mixed_out)
    sender.settle(gather.begun)

    def attention_norm(rows):
        value, gain = proj[rows, :], gain_rows[2:3, :]
        d_mixed = cotangent[rows, :].astype(F32) + d_mixed_out[rows, :]
        d_mixed_out[rows, :] = d_mixed
        scale = norm_scale(value)
        d_proj_out[rows, :] = norm_back(d_mixed, value, scale, gain).astype(BF16)
        gains_out[0:1, :] += jnp.sum(d_mixed * value * scale, axis=0, keepdims=True)

    by_rows(down_proj.shape[0], attention_norm)
    take_turns((task, task2))
    for i in (6, 7):
        for k in range(2):
            sent(i % 2, k, i).wait()
    sender.finish()


def mlp(number, own, gate_up, down, mixed, cotangent, proj, gain_rows):
    rows, width = own.shape
    piece, hidden = down.shape[-2:]
    tokens = (2, 2, 2 * rows)
    weight = pltpu.VMEM((2, RING, RING, piece, hidden), BF16)
    wide, narrow = pltpu.VMEM((*tokens, width), BF16), pltpu.VMEM((*tokens, hidden), BF16)
    return call(
        mlp_kernel,
        number,
        (
            shape_of(rows, width),
            shape_of(rows, width, dtype=F32),
            shape_of(rows, width),
            shape_of(8, width, dtype=F32),
            shape_of(2, 2, RING, RING, piece, hidden),
            shape_of(2, piece, hidden),
        ),
        [ANYWHERE] * 6 + [IN_VMEM],
        (IN_VMEM,) * 4 + (ANYWHERE, IN_VMEM),
        [
            wide,
            wide,
            *[weight] * 3,
            *[narrow] * 3,
            wide,
            weight,
            pltpu.VMEM((2, 2, RING, piece, hidden), BF16),
            pltpu.VMEM((rows, width), F32),
            pltpu.VMEM((rows, width), F32),
            pltpu.VMEM((rows, width), BF16),
            pltpu.VMEM((rows, width), F32),
            *ring_buffers(rows, width),
            *scatter_buffers(piece, hidden // 2, BF16),
            *scatter_buffers(piece, hidden // 2, BF16),
            dma_sems(128),
            dma_sems(RING, 4),
            dma_sems(4, 2 * PIECES),
            dma_sems(RING, 4),
            dma_sems(4, 2 * PIECES),
            dma_sems(2, 12),
            dma_sems(2, 12),
            dma_sems(2, 2),
        ],
        (own, gate_up, down, mixed, cotangent, proj, gain_rows),
    )


def ring_product(place, total, values, weight, partial, others, before_near=lambda: None):
    def compute(dy):
        y = place.shift("y", dy)
        at = (y % 2, y // 2)

        def tile(columns):
            partial[(*at, slice(None), columns)] = dot(values[at], rows_of(weight, columns), NT).astype(BF16)

        in_tiles(partial.shape[-1], 512, tile)
        total.offer(dy)

    compute(2)
    before_near()
    compute(1)
    total.collect(2)
    compute(-1)
    total.collect(1)
    compute(0)
    total.collect(-1)
    total.collect(0)
    for task in others:
        next(task)
    total.relay()


def flat(weight):
    return weight.reshape(-1, weight.shape[-1])


def exact(left, right, dims):
    return lax.dot_general(
        left, right, dims, precision=lax.Precision.HIGHEST, preferred_element_type=F32
    )


def half_roll(values):
    return pltpu.roll(values, HEAD_DIM // 2, 1)


def near_devices(place):
    return [place.at(axis, step) for axis in ("x", "z") for step in (1, -1)]


class Octet:
    peers = [(dy, dc) for dy in (0, 1, 3, 2) for dc in (0, 1) if dy or dc]

    def __init__(self, place, sender, own, slots, sems):
        self.place, self.sender, self.own, self.slots, self.sems = place, sender, own, slots, sems

    @staticmethod
    def device(place, dy, dc):
        y = place.shift("y", dy)
        return {"yl": y % 2, "yh": y // 2, "c": (place.c + dc) % 2}

    def send(self):
        for dy, dc in self.peers:
            slot = ((RING - dy) % RING) * 2 + dc
            device = self.device(self.place, dy, dc)
            self.sender.push(self.own, self.slots.at[slot], self.sems.at[slot], device)

    def total(self):
        for dy, dc in self.peers:
            slot = dy * 2 + dc
            self.sender.arrived(self.slots.at[slot], self.sems.at[slot], self.device(self.place, dy, dc))
        value = self.own[...]
        for dy, dc in self.peers:
            value = value + self.slots[dy * 2 + dc]
        return value


def one_hot_rows(k):
    return (lax.broadcasted_iota(jnp.int32, (8, HEAD_DIM), 0) == k).astype(F32)


def masked(scores, starts, i):
    tile, count = scores.shape
    keys = lax.broadcasted_iota(jnp.int32, (tile, count), 1)
    queries = lax.broadcasted_iota(jnp.int32, (tile, count), 0) + i * tile
    return jnp.where((keys >= starts) & (keys <= queries), scores, -1e30)


def softmax(scores):
    exponent = jnp.exp(scores - jnp.max(scores, axis=-1, keepdims=True))
    return exponent / jnp.sum(exponent, axis=-1, keepdims=True)


def attention_forward_kernel(
    own, attn, down, gain, cosine_in, sine_in, starts_in, proj_out, mixed_out, low_out, gain_rows, x_out,
    weight_out, raw_out, rot_out, value_out, scale_out, attended_out, down_out, *refs
):
    (
        (x_all, weight, raw, rot, values, scales, attended, partial, sums, slots, down_all, gain_all),
        (cosine, sine, starts, hidden),
        ring,
        (sends, gather_sems, sum_sems, octet_sems, attn_plane, gain_plane, plane, swap),
    ) = refs_of(refs, 12, 4, 4, 8)
    place = Place()
    sender = Sender(sends)
    _, heads, _, block_rows, _ = raw.shape
    inner = heads * HEAD_DIM
    tile = block_rows // 2
    pairs = ((cosine_in, cosine), (sine_in, sine), (starts_in, starts), (own, hidden))
    later = [sender.keep_first(source, target) for source, target in pairs]
    partner = {"yl": 1 - place.yl}
    me, you = place.yl, 1 - place.yl
    shards = ((attn, weight), (gain, gain_all), (down, down_all))
    mine = [
        sender.keep_first(source if k == 1 else source.at[me], target.at[me, place.x, place.z])
        for k, (source, target) in enumerate(shards)
    ]
    greet(near_devices(place) + [Octet.device(place, *peer) for peer in Octet.peers])
    for k, (source, target) in enumerate(shards[:2]):
        sender.push(
            source if k == 1 else source.at[you], target.at[me, place.x, place.z], swap.at[k], partner
        )
    gather = RingGather(place, sender, gather_sems, own, x_all)
    gather.begin()
    for copy in mine:
        copy.wait()
    for k, (_, target) in enumerate(shards[:2]):
        sender.arrived(target.at[you, place.x, place.z], swap.at[k], partner)
    attn_task = plane_gather(place, sender, attn_plane, weight, weight.shape[3] // 2)
    gain_task = plane_gather(place, sender, gain_plane, gain_all, gain_all.shape[3])
    next(attn_task)
    next(gain_task)
    sender.push(down.at[you], down_all.at[me, place.x, place.z], swap.at[2], partner)

    def gather_all():
        gather.relay()
        yield
        gather.relay_far()
        yield
        for dy in (0, 1, -1, 2):
            gather.ready(dy)

    take_turns((gain_task, attn_task, gather_all()))
    sender.keep(x_all, x_out)
    sender.keep(weight, weight_out)
    for yl in range(2):
        for x in range(RING):
            for h in range(2):
                lanes = pl.ds(((yl * RING + x) * 2 + h) * HEAD_DIM, HEAD_DIM)
                gain_rows[:, lanes] = gain_all[yl, x, 2 * h] + gain_all[yl, x, 2 * h + 1]
    first_column = (place.yh * 2 + place.c) * (2 * inner) + place.yl * inner

    def head_gain(k, h):
        start = pl.multiple_of(first_column + h * HEAD_DIM, HEAD_DIM)
        return gain_rows[k : k + 1, pl.ds(start, HEAD_DIM)]

    sender.arrived(down_all.at[you, place.x, place.z], swap.at[2], partner)
    down_task = plane_gather(place, sender, plane, down_all, down_all.shape[3] // 2)
    next(down_task)
    total = RingSum(place, sender, sum_sems, partial, *ring)
    ones = [one_hot_rows(k) for k in range(2)]

    def project(t, carry):
        a, b = t // 2, t % 2
        window = pl.ds(pl.multiple_of(b * tile, tile), tile)
        value = dot(x_all[a, b], columns_of(weight, pl.ds(0, 2 * inner)))
        row_sums = jnp.zeros((8, tile), F32)
        for k in range(2):
            for h in range(heads):
                column = k * inner + h * HEAD_DIM
                part = value[:, column : column + HEAD_DIM]
                raw[k, h, a, window, :] = part
                row_sums = row_sums + exact(ones[k], part * part, NT)
        sums[:, pl.ds(pl.multiple_of(t * tile, tile), tile)] = row_sums
        return carry

    def project_value(t, carry):
        a, b = t // 2, t % 2
        window = pl.ds(pl.multiple_of(b * tile, tile), tile)
        value = dot(x_all[a, b], columns_of(weight, pl.ds(2 * inner, inner))).astype(BF16)
        for h in range(heads):
            values[h, a, window, :] = value[:, h * HEAD_DIM : (h + 1) * HEAD_DIM]
        return carry

    lax.fori_loop(0, 4, project, 0)
    octet = Octet(place, sender, sums, slots, octet_sems)
    octet.send()
    sender.keep(raw, raw_out)
    lax.fori_loop(0, 4, project_value, 0)
    sender.keep(values, value_out)
    next(down_task)
    for copy in later:
        copy.wait()
    row_scales = lax.rsqrt(octet.total() / x_all.shape[3] + NORM_EPS)
    for b in range(2):
        for k in range(2):
            scale = exact(row_scales[:, b * block_rows : (b + 1) * block_rows], ones[k], TN)
            scales[k, b] = scale
            for h in range(heads):
                value = raw[k, h, b] * scale * head_gain(k, h)
                rot[k, h, b] = (value * cosine[b] + half_roll(value) * sine[b]).astype(BF16)
    sender.keep(scales, scale_out)
    sender.keep(rot, rot_out)
    next(down_task)

    def attention(b):
        for h in range(heads):
            key, value = rot[1, h, b], values[h, b]
            for i in range(2):
                window, count = pl.ds(i * tile, tile), (i + 1) * tile
                scores = dot(rot[0, h, b, window, :], key[:count], NT) * HEAD_DIM ** (-0.5)
                probs = softmax(masked(scores, starts[b, window, 0:1], i)).astype(BF16)
                attended[b, i, :, pl.ds(h * HEAD_DIM, HEAD_DIM)] = dot(probs, value[:count]).astype(BF16)

    attention(place.yl)
    out_weight = weight.at[:, :, :, :, pl.ds(3 * inner, inner)]
    ring_product(place, total, attended, out_weight, partial, (), lambda: attention(1 - place.yl))
    sender.keep(attended, attended_out)
    take_turns((down_task,))
    sender.keep(down_all, down_out)
    total.finish(proj_out)

    def mix(rows):
        value = proj_out[rows, :]
        mixed = hidden[rows, :].astype(F32) + value * norm_scale(value) * gain_rows[2:3, :]
        mixed_out[rows, :] = mixed
        low_out[rows, :] = mixed.astype(BF16)

    by_rows(proj_out.shape[0], mix)
    sender.finish()


def attention_forward(number, own, attn, down, gain, cosine, sine, starts):
    rows, width = own.shape
    inner = attn.shape[2] // 4
    heads = inner // HEAD_DIM
    tokens = (2, 2, 2 * rows)
    raw = (2, heads, 2, 4 * rows, HEAD_DIM)
    values, scales, attended = raw[1:], (2, 2, 4 * rows, HEAD_DIM), (*tokens, inner)
    weight, down_all = (2, RING, RING, *attn.shape[1:]), (2, RING, RING, *down.shape[1:])
    return call(
        attention_forward_kernel,
        number,
        (
            shape_of(rows, width, dtype=F32),
            shape_of(rows, width, dtype=F32),
            shape_of(rows, width),
            shape_of(8, width, dtype=F32),
            shape_of(*tokens, width),
            shape_of(*weight),
            shape_of(*raw, dtype=F32),
            shape_of(*raw),
            shape_of(*values),
            shape_of(*scales, dtype=F32),
            shape_of(*attended),
            shape_of(*down_all),
        ),
        [ANYWHERE] * 7,
        (IN_VMEM,) * 4 + (ANYWHERE,) * 8,
        [
            pltpu.VMEM((*tokens, width), BF16),
            pltpu.VMEM(weight, BF16),
            pltpu.VMEM(raw, F32),
            pltpu.VMEM(raw, BF16),
            pltpu.VMEM(values, BF16),
            pltpu.VMEM(scales, F32),
            pltpu.VMEM(attended, BF16),
            pltpu.VMEM((*tokens, width), BF16),
            pltpu.VMEM((8, 8 * rows), F32),
            pltpu.VMEM((8, 8, 8 * rows), F32),
            pltpu.VMEM(down_all, BF16),
            pltpu.VMEM((2, RING, RING, *gain.shape), F32),
            *[pltpu.VMEM(other.shape, other.dtype) for other in (cosine, sine, starts, own)],
            *ring_buffers(rows, width),
            dma_sems(208),
            dma_sems(RING, 4),
            dma_sems(4, 2 * PIECES),
            dma_sems(8),
            dma_sems(2, RING, RING, 3),
            dma_sems(2, RING, RING, 3),
            dma_sems(2, RING, RING, 3),
            dma_sems(3),
        ],
        (own, attn, down, gain, cosine, sine, starts),
    )


def attention_backward_kernel(
    own, weight, inputs, mlp_in, down, attended_in, raw_in, rot_in, values_in, scales_in,
    cosines_in, sines_in, starts_in, head_gains, token_gains, out, attn_out, gain_out, mlp_out, *refs
):
    (
        (shared, own_weight, attn_partial, gate_partial, up_partial, d_att, back, d_qkv, sums, slots),
        staged,
        (gain_partial, gain_rows, gain_slots, attn_done, gain_done, mlp_done),
        ring,
        buffers,
        late_buffers,
        gate_buffers,
        up_buffers,
        gain_buffers,
        (sends, gather_sems, sum_sems, octet_sems, gain_sems, swap, plane, late_plane, gain_plane, gate_plane),
        (up_plane,),
    ) = refs_of(refs, 10, 8, 6, 4, 5, 5, 5, 5, 5, 10, 1)
    attended, raw_all, rot, values, scales, cosines, sines, starts = staged
    d_all = x_all = partial = shared
    place = Place()
    sender = Sender(sends)
    _, heads, _, block_rows, _ = rot.shape
    width = d_qkv.shape[-1]
    inner = heads * HEAD_DIM
    rows = attn_partial.shape[3]
    block = RING * rows
    mlp_loads = [sender.keep_first(mlp_in.at[0], gate_partial), sender.keep_first(mlp_in.at[1], up_partial)]
    load = sender.keep_first(weight, own_weight)
    sources = (attended_in, raw_in, rot_in, values_in, scales_in, cosines_in, sines_in, starts_in)
    later = [sender.keep_first(source, target) for source, target in zip(sources, staged)]
    partner = {"yl": 1 - place.yl}
    me, you = place.yl, 1 - place.yl
    greet(near_devices(place) + [Octet.device(place, *peer) for peer in Octet.peers])
    gather = RingGather(place, sender, gather_sems, own, d_all)
    total = RingSum(place, sender, sum_sems, partial, *ring)
    gather.begin()
    sender.push(down.at[you], mlp_out.at[2, me], swap.at[3], partner)
    sender.keep(down.at[me], mlp_out.at[2, me])
    mlp = []
    for k, (sems, bufs, summand) in enumerate(
        ((gate_plane, gate_buffers, gate_partial), (up_plane, up_buffers, up_partial))
    ):
        mlp_loads[k].wait()
        task = plane_scatter(place, sender, sems, summand, mlp_done.at[k], rows // 2, bufs)
        next(task)
        mlp.append(task)
    gate_task, up_task = mlp
    load.wait()
    gain_partial[...] = jnp.zeros_like(gain_partial)
    gain_rows[...] = jnp.zeros_like(gain_rows)
    for k in range(2 * RING):
        for z in range(RING):
            gain_partial[k // RING, k % RING, z, 2:4, :] = token_gains[0:2, k * block : (k + 1) * block]

    def compute(dy):
        gather.ready(dy)
        y = place.shift("y", dy)
        at = (y % 2, y // 2)
        d_att[at] = dot(d_all[at], own_weight[:, pl.ds(width, inner)]).astype(BF16)

    tile = block_rows // 2
    score_factor = HEAD_DIM ** (-0.5)
    ones = [one_hot_rows(k) for k in range(2)]

    def attention(b):
        row_sums = jnp.zeros((8, block_rows), F32)
        cosine, sine = cosines[b], sines[b]
        for h in range(heads):
            lanes = pl.ds(h * HEAD_DIM, HEAD_DIM)
            key, value = rot[1, h, b], values[h, b]
            d_query, d_key, d_value = [], [None, None], [None, None]
            for i in range(2):
                window = pl.ds(i * tile, tile)
                query, upstream = rot[0, h, b, window, :], d_att[b, i, :, lanes]
                count = (i + 1) * tile
                scores = dot(query, key[:count], NT) * score_factor
                probs = softmax(masked(scores, starts[b, window, 0:1], i))
                d_probs = dot(upstream, value[:count], NT)
                row_dot = jnp.sum(probs * d_probs, axis=-1, keepdims=True)
                d_scores = (probs * (d_probs - row_dot) * score_factor).astype(BF16)
                probs = probs.astype(BF16)
                d_query.append(dot(d_scores, key[:count]))
                for j in range(i + 1):
                    part = slice(j * tile, (j + 1) * tile)
                    for sums_of, left, right in ((d_key, d_scores, query), (d_value, probs, upstream)):
                        term = dot(left[:, part], right, TN)
                        sums_of[j] = term if sums_of[j] is None else sums_of[j] + term
            for i in range(2):
                d_qkv[b, i, :, pl.ds(2 * inner + h * HEAD_DIM, HEAD_DIM)] = d_value[i].astype(BF16)
            for k, parts in enumerate((d_query, d_key)):
                turned = jnp.concatenate(parts, axis=0)
                turned = turned * cosine - half_roll(turned) * sine
                raw = raw_all[k, h, b]
                gain_rows[k : k + 1, lanes] += jnp.sum(turned * raw * scales[k, b], axis=0, keepdims=True)
                turned = turned * head_gains[k : k + 1, lanes]
                back[k, h, b] = turned
                row_sums = row_sums + exact(ones[k], turned * raw, NT)
        sums[:, pl.ds(pl.multiple_of(b * block_rows, block_rows), block_rows)] = row_sums

    compute(0)
    gather.relay()
    compute(1)
    compute(-1)
    next(gate_task)
    for copy in later:
        copy.wait()
    attention(1 - place.yl)
    gather.relay_far()
    compute(2)
    next(up_task)
    attention(place.yl)
    octet = Octet(place, sender, sums, slots, octet_sems)
    octet.send()
    first = (place.yh * 2 + place.c) * 2 + place.yl
    for z in range(RING):
        gain_partial[first // RING, first % RING, z, 0:2, :] = gain_rows[0:2, :]
    gains = plane_scatter(place, sender, gain_plane, gain_partial, gain_done, gain_done.shape[1], gain_buffers)
    next(gains)

    def flat_tokens(ref, columns=slice(None)):
        value = ref[:, :, :, columns]
        return value.reshape(-1, value.shape[-1])

    def weight_grads(left_ref, right, start):
        size = right.shape[1]
        for i in range(2 * RING):
            left = flat_tokens(left_ref, pl.ds(i * block, block))
            value = dot(left, right, TN).astype(BF16)
            attn_partial[i // RING, i % RING, :, :, pl.ds(start, size)] = value.reshape(RING, rows, size)

    weight_grads(d_all, flat_tokens(attended), width)
    sender.settle(gather.forwarded)
    load = sender.keep_first(inputs, x_all)
    next(gate_task)
    load.wait()

    def attn_scatter(columns, sems, bufs):
        task = plane_scatter(
            place,
            sender,
            sems,
            attn_partial.at[:, :, :, :, columns],
            attn_done.at[:, :, columns],
            rows // 2,
            bufs,
        )
        next(task)
        return task

    weight_grads(x_all, flat_tokens(d_qkv, pl.ds(2 * inner, inner)), 2 * inner)
    early = attn_scatter(pl.ds(2 * inner, 2 * inner), plane, buffers)
    row_sums = octet.total()
    for b in range(2):
        for k in range(2):
            column = exact(row_sums[:, b * block_rows : (b + 1) * block_rows], ones[k], TN)
            for h in range(heads):
                scale = scales[k, b]
                value = scale * back[k, h, b] - raw_all[k, h, b] * (scale * scale * scale * column / own.shape[1])
                value = value.astype(BF16)
                for i in range(2):
                    d_qkv[b, i, :, pl.ds(k * inner + h * HEAD_DIM, HEAD_DIM)] = value[
                        i * tile : (i + 1) * tile
                    ]
    weight_grads(x_all, flat_tokens(d_qkv, pl.ds(0, 2 * inner)), 0)
    late = attn_scatter(pl.ds(0, 2 * inner), late_plane, late_buffers)
    next(gate_task)
    next(up_task)
    next(early)
    ring_product(
        place, total, d_qkv, own_weight.at[:, pl.ds(0, width)], partial, (late, up_task, gains)
    )
    take_turns((gate_task, up_task))
    for k in range(2):
        sender.push(mlp_done.at[k, you], mlp_out.at[k, me], swap.at[1 + k], partner)
        sender.keep(mlp_done.at[k, me], mlp_out.at[k, me])
    take_turns((early, gains, late))
    sender.push(attn_done.at[you], attn_out.at[me], swap.at[0], partner)
    sender.keep(attn_done.at[me], attn_out.at[me])
    everyone = Octet(place, sender, gain_done, gain_slots, gain_sems)
    everyone.send()
    total.finish(out)
    gain_out[...] = everyone.total()
    sender.arrived(attn_out.at[you], swap.at[0], partner)
    for k in range(3):
        sender.arrived(mlp_out.at[k, you], swap.at[1 + k], partner)
    sender.finish()


def attention_backward(number, own, weight, inputs, mlp_partial, down, attended, *others):
    rows, width = own.shape
    tokens = (2, 2, 2 * rows)
    inner = attended.shape[3]
    heads = inner // HEAD_DIM
    shard = width // 32, weight.shape[1]
    gain_tile = (8, 4 * shard[0])
    return call(
        attention_backward_kernel,
        number,
        (
            shape_of(rows, width, dtype=F32),
            shape_of(2, *shard),
            shape_of(2, *gain_tile, dtype=F32),
            shape_of(3, 2, *shard),
        ),
        [ANYWHERE] * 13 + [IN_VMEM] * 2,
        (IN_VMEM,) * 4,
        [
            pltpu.VMEM((*tokens, width), BF16),
            pltpu.VMEM(weight.shape, BF16),
            pltpu.VMEM((2, RING, RING, *shard), BF16),
            pltpu.VMEM(mlp_partial.shape[1:], BF16),
            pltpu.VMEM(mlp_partial.shape[1:], BF16),
            pltpu.VMEM((*tokens, inner), BF16),
            pltpu.VMEM((2, heads, 2, 4 * rows, HEAD_DIM), F32),
            pltpu.VMEM((*tokens, 3 * inner), BF16),
            pltpu.VMEM((8, 8 * rows), F32),
            pltpu.VMEM((8, 8, 8 * rows), F32),
            *[pltpu.VMEM(other.shape, other.dtype) for other in (attended, *others[:7])],
            pltpu.VMEM((2, RING, RING, *gain_tile), F32),
            pltpu.VMEM((8, inner), F32),
            pltpu.VMEM((8, 2, *gain_tile), F32),
            pltpu.VMEM((2, *shard), BF16),
            pltpu.VMEM((2, *gain_tile), F32),
            pltpu.VMEM((2, 2, *shard), BF16),
            *ring_buffers(rows, width),
            *scatter_buffers(shard[0], shard[1] // 2, BF16),
            *scatter_buffers(shard[0], shard[1] // 2, BF16),
            *scatter_buffers(*shard, BF16),
            *scatter_buffers(*shard, BF16),
            *scatter_buffers(*gain_tile, F32),
            dma_sems(224),
            dma_sems(RING, 4),
            dma_sems(4, 2 * PIECES),
            dma_sems(8),
            dma_sems(8),
            dma_sems(5),
            dma_sems(2, 12),
            dma_sems(2, 12),
            dma_sems(2, 12),
            dma_sems(2, 12),
            dma_sems(2, 12),
        ],
        (own, weight, inputs, mlp_partial, down, attended, *others),
    )


def norm_scale(values):
    return lax.rsqrt(jnp.mean(values * values, axis=-1, keepdims=True) + NORM_EPS)


def norm_back(upstream, values, scales, gain_row):
    scaled_grad = upstream * gain_row
    return scales * scaled_grad - values * scales**3 * jnp.mean(
        scaled_grad * values, axis=-1, keepdims=True
    )


def doc_layout(lengths, group_size):
    positions = jnp.arange(group_size, dtype=jnp.int32)
    doc_ends = jnp.cumsum(lengths)
    passed = (positions[:, None] >= doc_ends[None, :]).astype(jnp.int32)
    segment = jnp.sum(passed, axis=-1)
    begins = jnp.sum(passed * lengths[None, :], axis=-1)
    return (segment, positions - begins)


def rope_tables(offsets):
    frequency = ROPE_BASE ** (-jnp.arange(0, HEAD_DIM, 2).astype(jnp.float32) / HEAD_DIM)
    angles = offsets.astype(jnp.float32)[:, None] * frequency[None, :]
    cosine, sine = jnp.cos(angles), jnp.sin(angles)
    return (
        jnp.concatenate([cosine, cosine], axis=-1),
        jnp.concatenate([sine, sine], axis=-1),
    )


def half_turn(values):
    middle = values.shape[-1] // 2
    return jnp.concatenate([-values[..., middle:], values[..., :middle]], axis=-1)


def rotate(values, cosine_table, sine_table):
    return values * cosine_table + half_turn(values) * sine_table


def unrotate(values, cosine_table, sine_table):
    return values * cosine_table - half_turn(values) * sine_table


def product(left, right):
    return jnp.dot(left, right, preferred_element_type=F32)


def row_product(left, right):
    return lax.dot_general(left, right, (((1,), (1,)), ((), ())), preferred_element_type=F32)


def col_product(left, right):
    return lax.dot_general(left, right, (((0,), (0,)), ((), ())), preferred_element_type=F32)


def adam_update(weights_old, first_old, second_old, gradient, rate, decay):
    first_new = BETA_ONE * first_old + (1.0 - BETA_ONE) * gradient
    second_new = BETA_TWO * second_old + (1.0 - BETA_TWO) * gradient * gradient
    ratio = (
        first_new
        / (1.0 - BETA_ONE**STEP)
        / (jnp.sqrt(second_new / (1.0 - BETA_TWO**STEP)) + ADAM_EPS)
    )
    return (first_new, second_new, weights_old - rate * (ratio + decay * weights_old))


def mlp_adam_kernel(weights, first, second, sums, grad_out, first_out, second_out, new_out):
    gradient = sums[0].astype(F32)
    grad_out[...] = gradient
    first_out[...], second_out[...], new_out[...] = adam_update(
        weights[...], first[...], second[...], gradient, WEIGHT_RATE, WEIGHT_DECAY
    )


def mlp_adam(weights, first, second, sums):
    count, rows, columns = weights.shape
    half = columns // 2
    state = pl.BlockSpec((1, rows, half), lambda m, h: (m, 0, h))
    return pl.pallas_call(
        mlp_adam_kernel,
        out_shape=(shape_of(*weights.shape, dtype=F32),) * 4,
        grid=(count, 2),
        in_specs=[state] * 3 + [pl.BlockSpec((1, 1, rows, half), lambda m, h: (m, h, 0, 0))],
        out_specs=(state,) * 4,
        compiler_params=pltpu.CompilerParams(vmem_limit_bytes=VMEM_LIMIT),
    )(weights, first, second, sums)


def attn_adam_kernel(weights, first, second, sums, grad_out, first_out, second_out, new_out):
    inner = weights.shape[2]
    for m in range(weights.shape[0]):
        gradient = sums[0, :, m * inner : (m + 1) * inner].astype(F32)
        grad_out[m] = gradient
        first_out[m], second_out[m], new_out[m] = adam_update(
            weights[m], first[m], second[m], gradient, WEIGHT_RATE, WEIGHT_DECAY
        )


def attn_adam(weights, first, second, sums):
    count, rows, columns = weights.shape
    state = pl.BlockSpec((count, rows, columns // 2), lambda h: (0, 0, h))
    return pl.pallas_call(
        attn_adam_kernel,
        out_shape=(shape_of(*weights.shape, dtype=F32),) * 4,
        grid=(2,),
        in_specs=[state] * 3 + [pl.BlockSpec((1, *sums.shape[1:]), lambda h: (h, 0, 0))],
        out_specs=(state,) * 4,
        compiler_params=pltpu.CompilerParams(vmem_limit_bytes=VMEM_LIMIT),
    )(weights, first, second, sums)


def body(
    hidden_in,
    cotangent,
    doc_lengths,
    attn_weights,
    attn_first,
    attn_second,
    mlp_weights,
    mlp_first,
    mlp_second,
    gains,
    gain_first,
    gain_second,
):
    row_count, model_width = hidden_in.shape
    shard_rows = attn_weights.shape[1]
    heads_width = attn_weights.shape[2] // 2
    hidden_width = mlp_weights.shape[2] // 2
    token_count = 8 * row_count
    block_rows = token_count // 2
    head_count = heads_width // HEAD_DIM
    score_factor = HEAD_DIM ** (-0.5)
    yl, yh, core = (lax.axis_index(a) for a in ("yl", "yh", "c"))

    attn_halves = (
        attn_weights.astype(BF16)
        .reshape(4, shard_rows, 2, heads_width)
        .transpose(2, 1, 0, 3)
        .reshape(2, shard_rows, 4 * heads_width)
    )
    gate_up = mlp_weights[:2].astype(BF16).reshape(2, shard_rows, 2, hidden_width)
    mine = lax.dynamic_index_in_dim(gate_up, yl, 2, keepdims=False)
    yours = lax.dynamic_index_in_dim(gate_up, 1 - yl, 2, keepdims=False)
    arrived = lax.ppermute(yours, "yl", [(0, 1), (1, 0)])
    down_halves = mlp_weights[2].astype(BF16).reshape(shard_rows, 2, hidden_width).transpose(1, 0, 2)
    gain_low = lax.reduce_precision(gains, 8, 7)
    odd = lax.axis_index("z") % 2
    gain_tile = jnp.concatenate([jnp.where(odd == 0, gain_low, 0.0), jnp.where(odd == 1, gain_low, 0.0)], axis=1)
    gain_tile = jnp.pad(gain_tile, ((0, 4), (0, 0)))
    theirs = lax.ppermute(doc_lengths, "yl", [(0, 1), (1, 0)])
    lengths = jnp.where(yl == 0, jnp.stack([doc_lengths[0], theirs[0]]), jnp.stack([theirs[0], doc_lengths[0]]))
    _, offsets = jax.vmap(lambda one: doc_layout(one, block_rows))(lengths)
    cosine_table, sine_table = rope_tables(offsets.reshape(-1))
    sine_table = sine_table * jnp.where(jnp.arange(HEAD_DIM) < HEAD_DIM // 2, -1.0, 1.0)
    cosine_table = cosine_table.reshape(2, block_rows, HEAD_DIM)
    sine_table = sine_table.reshape(2, block_rows, HEAD_DIM)
    starts = jnp.broadcast_to((jnp.arange(block_rows) - offsets)[:, :, None], (2, block_rows, HEAD_DIM))

    arrived, cosine_table, sine_table, starts, attn_halves, gain_tile, down_halves = lax.optimization_barrier(
        (arrived, cosine_table, sine_table, starts, attn_halves, gain_tile, down_halves)
    )
    pair = jnp.stack(
        [jnp.where(yl == 0, mine, arrived), jnp.where(yl == 0, arrived, mine)], axis=1
    )
    gate_up = lax.all_gather(pair.reshape(-1, hidden_width), ("x", "z"), tiled=True)
    gate_up = gate_up.reshape(RING, RING, 2, 2, shard_rows, hidden_width)

    (
        attn_proj, mixed, mixed_low, gain_full, every_input, attn_all, raw, rotated, values, head_scales,
        attended, down_all,
    ) = attention_forward(
        1, hidden_in, attn_halves, down_halves, gain_tile, cosine_table, sine_table, starts
    )
    attn_all = flat(attn_all)
    first_column = (yh * 2 + core) * (2 * heads_width) + yl * heads_width
    head_gains = lax.dynamic_slice(gain_full, (0, first_column), (2, heads_width))
    hidden_out, d_mixed, d_proj, token_gains, mlp_partial, down_sum = mlp(
        2, mixed_low, gate_up, down_all, mixed, cotangent, attn_proj, gain_full
    )
    input_sum, attn_sum, gain_sum, mlp_sum = attention_backward(
        3,
        d_proj,
        attn_all,
        every_input,
        mlp_partial,
        down_sum,
        attended,
        raw,
        rotated,
        values,
        head_scales,
        cosine_table,
        sine_table,
        starts,
        head_gains,
        token_gains,
    )
    input_grad = d_mixed + input_sum

    gain_sum = lax.dynamic_index_in_dim(gain_sum, yl, 0, keepdims=False)[:4]
    gain_grad = lax.dynamic_slice_in_dim(gain_sum, lax.axis_index("z") * shard_rows, shard_rows, axis=1)
    attn_grad, attn_first_new, attn_second_new, attn_new = attn_adam(
        attn_weights, attn_first, attn_second, attn_sum
    )
    mlp_grad, mlp_first_new, mlp_second_new, mlp_new = mlp_adam(
        mlp_weights, mlp_first, mlp_second, mlp_sum
    )
    gain_first_new, gain_second_new, gain_new = adam_update(
        gains, gain_first, gain_second, gain_grad, GAIN_RATE, 0.0
    )
    return (
        hidden_out,
        input_grad,
        attn_grad,
        attn_first_new,
        attn_second_new,
        attn_new,
        mlp_grad,
        mlp_first_new,
        mlp_second_new,
        mlp_new,
        gain_grad,
        gain_first_new,
        gain_second_new,
        gain_new,
    )


def solution(mesh):
    split = Mesh(mesh.devices.reshape(2, 4, 4, 2, 2), EVERY)
    tokens, shards, rows = P(EVERY, None), P(None, DP, TENSOR), P(None, DP)
    return jax.shard_map(
        body,
        mesh=split,
        in_specs=(tokens, tokens, P(DP, None), *[shards] * 6, *[rows] * 3),
        out_specs=(tokens, tokens, *[shards] * 8, *[rows] * 4),
        check_vma=False,
    )
```

```python
import functools

import jax
import jax.numpy as jnp
from jax import lax
from jax.experimental import pallas as pl
from jax.experimental.pallas import tpu as pltpu
from jax.sharding import Mesh
from jax.sharding import PartitionSpec as P

HEAD_DIM = 128
STEP = 10
DP = ("yl", "x", "z")
TENSOR = ("yh", "c")
EVERY = ("yl", "x", "z", "yh", "c")
RING = 4
MESH = pl.DeviceIdType.MESH

NORM_EPS = 1e-06
ROPE_BASE = 500000.0
BETA_ONE = 0.9
BETA_TWO = 0.95
ADAM_EPS = 1e-08
WEIGHT_RATE = 0.03
GAIN_RATE = 1.0
WEIGHT_DECAY = 0.1

BF16 = jnp.bfloat16
F32 = jnp.float32
IN_VMEM = pl.BlockSpec(memory_space=pltpu.VMEM)
ANYWHERE = pl.BlockSpec(memory_space=pl.ANY)
VMEM_LIMIT = 60 * 1024 * 1024


class Place:
    def __init__(self):
        self.x, self.z, self.c = (lax.axis_index(a) for a in ("x", "z", "c"))
        self.yl, self.yh = (lax.axis_index(a) for a in ("yl", "yh"))
        self.y = self.yh * 2 + self.yl

    def at(self, axis, step):
        if axis == "y":
            there = (self.y + step + RING) % RING
            return {"yl": there % 2, "yh": there // 2}
        if axis == "c":
            return {"c": 1 - self.c}
        return {axis: (getattr(self, axis) + step + RING) % RING}

    def shift(self, axis, step):
        return (getattr(self, axis) + step + RING) % RING


def greet(devices):
    barrier = pltpu.get_barrier_semaphore()
    for device in devices:
        pl.semaphore_signal(barrier, inc=1, device_id=device, device_id_type=MESH)
    pl.semaphore_wait(barrier, len(devices))


def greet_all(place, axes):
    devices = []
    for axis in axes:
        devices += [place.at(axis, 1)] if axis == "c" else [place.at(axis, 1), place.at(axis, -1)]
    greet(devices)


class Sender:
    def __init__(self, sems):
        self.sems, self.open = sems, []

    def push(self, src, dst, recv_sem, device):
        copy = pltpu.make_async_remote_copy(
            src_ref=src,
            dst_ref=dst,
            send_sem=self.sems.at[len(self.open)],
            recv_sem=recv_sem,
            device_id=device,
            device_id_type=MESH,
        )
        copy.start()
        self.open.append(copy.wait_send)
        return len(self.open) - 1

    def settle(self, numbers):
        for number in numbers:
            self.open[number]()
            self.open[number] = lambda: None

    def keep(self, src, dst):
        copy = pltpu.make_async_copy(src, dst, self.sems.at[len(self.open)])
        copy.start()
        self.open.append(copy.wait)

    def keep_first(self, src, dst):
        copy = pltpu.make_async_copy(src, dst, self.sems.at[len(self.open)])
        copy.start()
        self.open.append(lambda: None)
        return copy

    def arrived(self, dst, recv_sem, device):
        pltpu.make_async_remote_copy(
            src_ref=dst,
            dst_ref=dst,
            send_sem=self.sems.at[0],
            recv_sem=recv_sem,
            device_id=device,
            device_id_type=MESH,
        ).wait_recv()

    def finish(self):
        for wait in self.open:
            wait()


def take_turns(tasks):
    tasks = list(tasks)
    while tasks:
        for task in list(tasks):
            if next(task, "done") == "done":
                tasks.remove(task)


WHOLE, LOW, HIGH = 0, 1, 2
PIECES = 4


def part_of(ref, part, cut):
    rows = ref.shape[-2]
    if part == WHOLE:
        return ref
    return ref.at[pl.ds(0, cut)] if part == LOW else ref.at[pl.ds(cut, rows - cut)]


def plane_gather(place, sender, sems, out, cut):
    rows = out.shape[-2]
    axes = (("x", "z"), ("z", "x"))

    def piece(half, dp, dq):
        p, q = (place.shift(a, d) for a, d in zip(axes[half], (dp, dq)))
        return out.at[half, p, q] if half == 0 else out.at[half, q, p]

    def parts(part):
        if part == WHOLE:
            return True
        return cut > 0 if part == LOW else cut < rows

    def send(half, dp, dq, part, along, step):
        if parts(part):
            ref = part_of(piece(half, dp, dq), part, cut)
            sp, sq = ((dp - step) % RING, dq % RING) if along == 0 else (dp % RING, (dq - step) % RING)
            sender.push(ref, ref, sems.at[half, sp, sq, part], place.at(axes[half][along], step))

    def wait(half, dp, dq, part):
        if parts(part):
            ref = part_of(piece(half, dp, dq), part, cut)
            sender.arrived(ref, sems.at[half, dp % RING, dq % RING, part], place.at("x", 1))

    both = (0, 1)
    for half in both:
        for step in (1, -1):
            send(half, 0, 0, WHOLE, 0, step)
    for half in both:
        for step in (1, -1):
            send(half, 0, 0, WHOLE, 1, step)
    yield
    for step, part in ((1, LOW), (-1, HIGH)):
        for half in both:
            wait(half, -step, 0, WHOLE)
            send(half, -step, 0, part, 0, step)
            for side in (1, -1):
                send(half, -step, 0, WHOLE, 1, side)
    yield
    for half in both:
        for step, part in ((1, LOW), (-1, HIGH)):
            wait(half, 0, -step, WHOLE)
            send(half, 0, -step, part, 1, step)
    yield
    for half in both:
        wait(half, 2, 0, LOW)
        wait(half, 2, 0, HIGH)
        for side in (1, -1):
            send(half, 2, 0, WHOLE, 1, side)
    yield
    for dp in (-1, 1, 2):
        for half in both:
            for step, part in ((1, LOW), (-1, HIGH)):
                wait(half, dp, -step, WHOLE)
                send(half, dp, -step, part, 1, step)
        yield
    for dp in (0, -1, 1, 2):
        for half in both:
            wait(half, dp, 2, LOW)
            wait(half, dp, 2, HIGH)


class RingGather:
    def __init__(self, place, sender, sems, own, out):
        self.place, self.sender, self.sems, self.own, self.out = place, sender, sems, own, out
        self.rows = own.shape[0]
        self.other = place.at("c", 1)
        self.begun, self.forwarded = [], []

    def piece(self, dy, core, part=WHOLE):
        y = self.place.shift("y", dy)
        half = self.rows // 2
        start, size = {WHOLE: (0, self.rows), LOW: (0, half), HIGH: (half, half)}[part]
        return self.out.at[y % 2, y // 2, pl.ds(pl.multiple_of(core * self.rows + start, 16), size)]

    def begin(self):
        place, mine = self.place, self.piece(0, self.place.c)
        for step in (1, -1):
            number = self.sender.push(self.own, mine, self.sems.at[(-step) % RING, WHOLE], place.at("y", step))
            self.begun.append(number)
        self.begun.append(self.sender.push(self.own, mine, self.sems.at[0, 3], self.other))
        self.kept = self.sender.keep_first(self.own, mine)

    def relay(self):
        for step, part in ((1, LOW), (-1, HIGH)):
            ref = self.piece(-step, self.place.c)
            self.sender.arrived(ref, self.sems.at[(-step) % RING, WHOLE], self.other)
            half = self.piece(-step, self.place.c, part)
            self.forwarded += [
                self.sender.push(half, half, self.sems.at[2, part], self.place.at("y", step)),
                self.sender.push(ref, ref, self.sems.at[(-step) % RING, 3], self.other),
            ]

    def relay_far(self):
        for part in (LOW, HIGH):
            self.sender.arrived(self.piece(2, self.place.c, part), self.sems.at[2, part], self.other)
        ref = self.piece(2, self.place.c)
        self.forwarded += [self.sender.push(ref, ref, self.sems.at[2, 3], self.other)]

    def ready(self, dy):
        if dy == 0:
            self.kept.wait()
        self.sender.arrived(self.piece(dy, 1 - self.place.c), self.sems.at[dy % RING, 3], self.other)


def ring_gather(place, sender, sems, own, out):
    gather = RingGather(place, sender, sems, own, out)
    gather.begin()
    yield
    gather.relay()
    yield
    gather.relay_far()
    yield
    for dy in (0, 1, -1, 2):
        gather.ready(dy)


def add_rows(out, terms, rows):
    def step(i, carry):
        window = pl.ds(pl.multiple_of(i * 16, 16), 16)
        total = terms[0][window, :].astype(F32)
        for term in terms[1:]:
            total = total + term[window, :].astype(F32)
        out[window, :] = total.astype(out.dtype)
        return carry

    lax.fori_loop(0, rows // 16, step, 0)


class RingSum:
    def __init__(self, place, sender, sems, partial, kept, from_core, hop, last):
        self.place, self.sender, self.sems, self.partial = place, sender, sems, partial
        self.kept, self.from_core, self.hop, self.last = kept, from_core, hop, last
        self.rows = kept.shape[1]
        self.low, self.high = pl.ds(0, self.rows // 2), pl.ds(self.rows // 2, self.rows // 2)
        self.other = place.at("c", 1)

    def mine(self, dy, core):
        y = self.place.shift("y", dy)
        return self.partial.at[y % 2, y // 2, pl.ds(pl.multiple_of(core * self.rows, 16), self.rows)]

    def offer(self, dy):
        slot = dy % RING
        self.sender.push(
            self.mine(dy, 1 - self.place.c), self.from_core.at[slot], self.sems.at[0, slot], self.other
        )

    def pieces(self):
        columns = self.kept.shape[2]
        return [pl.ds(p * columns // PIECES, columns // PIECES) for p in range(PIECES)]

    def collect(self, dy):
        slot = dy % RING
        kept, low, high = self.kept.at[slot], self.low, self.high
        self.sender.arrived(self.from_core.at[slot], self.sems.at[0, slot], self.other)
        if dy == 0:
            return
        up, down = self.place.at("y", 1), self.place.at("y", -1)
        mine = self.mine(dy, self.place.c)
        if dy == 2:
            for p, columns in enumerate(self.pieces()):
                add_rows(kept.at[:, columns], (mine.at[:, columns], self.from_core.at[slot, :, columns]), self.rows)
                self.sender.push(kept.at[low, columns], self.hop.at[0, :, columns], self.sems.at[1, p], up)
                self.sender.push(
                    kept.at[high, columns], self.hop.at[1, :, columns], self.sems.at[1, PIECES + p], down
                )
            return
        add_rows(kept, (mine, self.from_core.at[slot]), self.rows)
        if dy == 1:
            self.sender.push(kept.at[high], self.last.at[0, high], self.sems.at[2, 1], up)
        else:
            self.sender.push(kept.at[low], self.last.at[1, low], self.sems.at[2, 2], down)

    def relay(self):
        for p, columns in enumerate(self.pieces()):
            for k, slot, part, step in ((0, 1, self.low, 1), (1, 3, self.high, -1)):
                number = k * PIECES + p
                self.sender.arrived(self.hop.at[k, :, columns], self.sems.at[1, number], self.other)
                rows = self.kept.at[slot, part, columns]
                add_rows(rows, (rows, self.hop.at[k, :, columns]), self.rows // 2)
                self.sender.push(
                    rows, self.last.at[k, part, columns], self.sems.at[3, number], self.place.at("y", step)
                )

    def finish(self, out, *others):
        self.sender.arrived(self.last.at[0, self.high], self.sems.at[2, 1], self.other)
        self.sender.arrived(self.last.at[1, self.low], self.sems.at[2, 2], self.other)
        mine = self.mine(0, self.place.c)
        for p, columns in enumerate(self.pieces()):
            for k, part in ((0, self.low), (1, self.high)):
                self.sender.arrived(
                    self.last.at[k, part, columns], self.sems.at[3, k * PIECES + p], self.other
                )
            terms = (mine, self.from_core.at[0], self.last.at[0], self.last.at[1], *others)
            add_rows(out.at[:, columns], [term.at[:, columns] for term in terms], self.rows)


def plane_scatter(place, sender, sems, partial, done, cut, bufs):
    rows = partial.shape[-2]
    hop, last, middle, hop2, last2 = bufs
    low, high = pl.ds(0, cut), pl.ds(cut, rows - cut)
    axes = (("z", "x"), ("x", "z"))
    two_parts = cut < rows
    both = (0, 1)
    other = place.at("x", 1)

    def row(half, du, window):
        u = place.shift(axes[half][0], du)
        return partial.at[half, :, u, window] if half == 0 else partial.at[half, u, :, window]

    def line(half, du, v):
        u = place.shift(axes[half][0], du)
        return partial.at[half, v, u] if half == 0 else partial.at[half, u, v]

    def add(out, terms, count):
        if count % 16:
            total = terms[0][...].astype(F32)
            for term in terms[1:]:
                total = total + term[...].astype(F32)
            out[...] = total.astype(out.dtype)
        else:
            add_rows(out, terms, count)

    for half in both:
        u = axes[half][0]
        sender.push(row(half, 2, low), hop.at[half, 0], sems.at[half, 0], place.at(u, 1))
        if two_parts:
            sender.push(row(half, 2, high), hop.at[half, 1], sems.at[half, 1], place.at(u, -1))
    for half in both:
        u = axes[half][0]
        if two_parts:
            sender.push(row(half, 1, high), last.at[half, 0, :, high], sems.at[half, 2], place.at(u, 1))
        sender.push(row(half, -1, low), last.at[half, 1, :, low], sems.at[half, 3], place.at(u, -1))
    yield
    for half in both:
        u = axes[half][0]
        sender.arrived(hop.at[half, 0], sems.at[half, 0], other)
        for v in range(RING):
            add(hop.at[half, 0, v], (line(half, 1, v).at[low], hop.at[half, 0, v]), cut)
        sender.push(hop.at[half, 0], last.at[half, 0, :, low], sems.at[half, 4], place.at(u, 1))
        if two_parts:
            sender.arrived(hop.at[half, 1], sems.at[half, 1], other)
            for v in range(RING):
                add(
                    hop.at[half, 1, v],
                    (line(half, -1, v).at[high], hop.at[half, 1, v]),
                    rows - cut,
                )
            sender.push(
                hop.at[half, 1], last.at[half, 1, :, high], sems.at[half, 5], place.at(u, -1)
            )
    yield
    for half in both:
        v_axis = axes[half][1]
        if two_parts:
            sender.arrived(last.at[half, 0, :, high], sems.at[half, 2], other)
        sender.arrived(last.at[half, 1, :, low], sems.at[half, 3], other)
        sender.arrived(last.at[half, 0, :, low], sems.at[half, 4], other)
        if two_parts:
            sender.arrived(last.at[half, 1, :, high], sems.at[half, 5], other)
        for dv in (2, 1, -1, 0):
            v = place.shift(v_axis, dv)
            terms = (line(half, 0, v), last.at[half, 0, v], last.at[half, 1, v])
            add(middle.at[half, dv % RING], terms, rows)
            if dv == 2:
                sender.push(
                    middle.at[half, 2, low], hop2.at[half, 0], sems.at[half, 6], place.at(v_axis, 1)
                )
                if two_parts:
                    sender.push(
                        middle.at[half, 2, high],
                        hop2.at[half, 1],
                        sems.at[half, 7],
                        place.at(v_axis, -1),
                    )
            elif dv == 1 and two_parts:
                sender.push(
                    middle.at[half, 1, high], last2.at[half, 0, high], sems.at[half, 8], place.at(v_axis, 1)
                )
            elif dv == -1:
                sender.push(
                    middle.at[half, 3, low], last2.at[half, 1, low], sems.at[half, 9], place.at(v_axis, -1)
                )
    yield
    for half in both:
        v_axis = axes[half][1]
        sender.arrived(hop2.at[half, 0], sems.at[half, 6], other)
        add(hop2.at[half, 0], (middle.at[half, 1, low], hop2.at[half, 0]), cut)
        sender.push(
            hop2.at[half, 0], last2.at[half, 0, low], sems.at[half, 10], place.at(v_axis, 1)
        )
        if two_parts:
            sender.arrived(hop2.at[half, 1], sems.at[half, 7], other)
            add(hop2.at[half, 1], (middle.at[half, 3, high], hop2.at[half, 1]), rows - cut)
            sender.push(
                hop2.at[half, 1], last2.at[half, 1, high], sems.at[half, 11], place.at(v_axis, -1)
            )
    yield
    for half in both:
        if two_parts:
            sender.arrived(last2.at[half, 0, high], sems.at[half, 8], other)
        sender.arrived(last2.at[half, 1, low], sems.at[half, 9], other)
        sender.arrived(last2.at[half, 0, low], sems.at[half, 10], other)
        if two_parts:
            sender.arrived(last2.at[half, 1, high], sems.at[half, 11], other)
        add(done.at[half], (middle.at[half, 0], last2.at[half, 0], last2.at[half, 1]), rows)


def scatter_buffers(rows, columns, dtype):
    cut = rows // 2 if dtype == BF16 else rows
    return [
        pltpu.VMEM((2, 2, RING, cut, columns), dtype),
        pltpu.VMEM((2, 2, RING, rows, columns), dtype),
        pltpu.VMEM((2, RING, rows, columns), dtype),
        pltpu.VMEM((2, 2, cut, columns), dtype),
        pltpu.VMEM((2, 2, rows, columns), dtype),
    ]


def ring_buffers(rows, columns):
    return [
        pltpu.VMEM((RING, rows, columns), BF16),
        pltpu.VMEM((RING, rows, columns), BF16),
        pltpu.VMEM((2, rows // 2, columns), BF16),
        pltpu.VMEM((2, rows, columns), BF16),
    ]


def dma_sems(*shape):
    return pltpu.SemaphoreType.DMA(shape)


def shape_of(*shape, dtype=BF16):
    return jax.ShapeDtypeStruct(shape, dtype)


def call(kernel, number, out_shape, in_specs, out_specs, scratch, args):
    return pl.pallas_call(
        kernel,
        out_shape=out_shape,
        in_specs=in_specs,
        out_specs=out_specs,
        scratch_shapes=scratch,
        compiler_params=pltpu.CompilerParams(
            collective_id=number, has_side_effects=True, vmem_limit_bytes=VMEM_LIMIT
        ),
    )(*args)


NN = (((1,), (0,)), ((), ()))
NT = (((1,), (1,)), ((), ()))
TN = (((0,), (0,)), ((), ()))


def dot(left, right, dims=NN):
    return lax.dot_general(left, right, dims, preferred_element_type=F32)


def in_tiles(width, tile, work):
    for n in range(width // tile):
        work(pl.ds(n * tile, tile))


def refs_of(refs, *counts):
    refs, out = list(refs), []
    for n in counts:
        out.append(refs[:n])
        del refs[:n]
    return out


def by_rows(count, work):
    def step(i, carry):
        work(pl.ds(pl.multiple_of(i * 16, 16), 16))
        return carry

    lax.fori_loop(0, count // 16, step, 0)


def load_weights(sender, source, targets):
    copies = []
    for k, target in targets:
        for yl in range(2):
            copies.append(sender.keep_first(source.at[:, :, k, yl], target.at[yl]))
    return copies


def rows_of(weight, window):
    if len(weight.shape) == 2:
        return weight[window, :]
    run = weight.shape[2] * weight.shape[3]
    first, count = window.start // run, window.size // run
    block = weight[first // RING, pl.ds(first % RING, count), :, :, :]
    return block.reshape(window.size, weight.shape[4])


def columns_of(weight, window):
    block = weight[:, :, :, :, window]
    return block.reshape(-1, window.size)


def mlp_kernel(
    own, gate_up, down, down_pair, mixed_in, cotangent_in, proj_in, gain_rows, hidden_out, d_mixed_out, d_proj_out,
    gains_out, grads_out, down_out, *refs
):
    (
        (x_all, d_all, w_gate, w_up, w_down, gate, up, act, partial, down_partial, tiles),
        (down_proj, mixed, cotangent, proj),
        ring,
        first_buffers,
        second_buffers,
        (sends, gather_sems, sum_sems, gather_sems2, sum_sems2, plane, plane2, tile_sems, plane3),
    ) = refs_of(refs, 11, 4, 4, 5, 5, 9)
    d_own = d_proj_out
    d_gate, d_up = gate, up
    place = Place()
    sender = Sender(sends)
    loads = load_weights(sender, gate_up, ((0, w_gate), (1, w_up)))
    early = down.shape[4]
    w_rest = w_down.at[:, :, :, :, pl.ds(early, down_pair.shape[2])]
    load_pair = sender.keep_first(down_pair, w_rest.at[:, place.x, place.z])
    load_down = sender.keep_first(down, w_down.at[:, :, :, :, pl.ds(0, early)])
    pairs = ((mixed_in, mixed), (cotangent_in, cotangent), (proj_in, proj))
    later = [sender.keep_first(source, target) for source, target in pairs]
    greet_all(place, ("x", "z", "y", "c"))
    gather = RingGather(place, sender, gather_sems, own, x_all)
    total = RingSum(place, sender, sum_sems, partial, *ring)
    gather.begin()
    load_pair.wait()
    rest = plane_gather(place, sender, plane3, w_rest, w_rest.shape[3] // 2)
    next(rest)
    for copy in loads:
        copy.wait()
    load_down.wait()
    tile = 512

    def where(dy):
        y = place.shift("y", dy)
        return y % 2, y // 2

    def at_chip(dy):
        at = where(dy)
        return (*at, slice(None)), (2 * rows, hidden_width)

    def at_neighbours(_):
        return (1 - place.yl, slice(None), slice(None)), (4 * rows, hidden_width)

    rows, hidden_width = own.shape[0], act.shape[-1]

    def forward_hidden(index, shape):
        count = shape[0]

        def hidden(columns):
            tokens = x_all[(*index, slice(None))].reshape(count, -1)
            g = dot(tokens, columns_of(w_gate, columns))
            u = dot(tokens, columns_of(w_up, columns))
            here = (*index, columns)
            held = act[here].shape
            gate[here], up[here] = g.astype(BF16).reshape(held), u.astype(BF16).reshape(held)
            act[here] = (g * jax.nn.sigmoid(g) * u).astype(BF16).reshape(held)

        in_tiles(hidden_width, tile, hidden)

    def forward_project(index, shape):
        def project(columns):
            left = act[(*index, slice(None))].reshape(shape)
            value = dot(left, rows_of(w_down, columns), NT).astype(BF16)
            here = (*index, columns)
            partial[here] = value.reshape(partial[here].shape)

        in_tiles(partial.shape[-1], tile, project)

    def in_turn(gather, total, work, before_far=lambda: None):
        gather.ready(0)
        work(*at_chip(0))
        total.offer(0)
        gather.relay()
        gather.ready(1)
        gather.ready(-1)
        work(*at_neighbours(0))
        total.offer(1)
        total.offer(-1)
        gather.relay_far()
        total.collect(1)
        total.collect(-1)
        gather.ready(2)
        before_far()
        work(*at_chip(2))
        total.offer(2)

    gather.ready(0)
    forward_hidden(*at_chip(0))
    for _ in range(4):
        next(rest)
    gather.relay()
    next(rest)
    gather.ready(1)
    gather.ready(-1)
    next(rest)
    forward_hidden(*at_neighbours(0))
    take_turns((rest,))
    gather.relay_far()
    forward_project(*at_neighbours(0))
    total.offer(1)
    total.offer(-1)
    forward_project(*at_chip(0))
    total.offer(0)
    total.collect(1)
    total.collect(-1)
    gather.ready(2)
    forward_hidden(*at_chip(2))
    forward_project(*at_chip(2))
    total.offer(2)
    total.collect(2)
    total.collect(0)
    total.relay()
    total.finish(down_proj)
    for copy in later:
        copy.wait()
    sender.settle(range(len(sender.open)))
    gains_out[...] = jnp.zeros_like(gains_out)

    def output_norm(rows):
        value, upstream, gain = down_proj[rows, :], cotangent[rows, :].astype(F32), gain_rows[3:4, :]
        scale = norm_scale(value)
        hidden_out[rows, :] = (mixed[rows, :] + value * scale * gain).astype(BF16)
        d_own[rows, :] = norm_back(upstream, value, scale, gain).astype(BF16)
        gains_out[1:2, :] += jnp.sum(upstream * value * scale, axis=0, keepdims=True)

    by_rows(down_proj.shape[0], output_norm)

    gather = RingGather(place, sender, gather_sems2, d_own, d_all)
    total = RingSum(place, sender, sum_sems2, partial, *ring)
    gather.begin()

    def backward(index, shape):
        count = shape[0]

        def hidden(columns):
            d_act = dot(d_all[(*index, slice(None))].reshape(count, -1), columns_of(w_down, columns))
            here = (*index, columns)
            held = gate[here].shape
            g, u = gate[here].astype(F32).reshape(d_act.shape), up[here].astype(F32).reshape(d_act.shape)
            s = jax.nn.sigmoid(g)
            d_gate[here] = (d_act * u * s * (1.0 + g * (1.0 - s))).astype(BF16).reshape(held)
            d_up[here] = (d_act * g * s).astype(BF16).reshape(held)

        in_tiles(hidden_width, tile, hidden)

        def back(columns):
            whole = (*index, slice(None))
            value = dot(d_gate[whole].reshape(shape), rows_of(w_gate, columns), NT)
            value = value + dot(d_up[whole].reshape(shape), rows_of(w_up, columns), NT)
            here = (*index, columns)
            partial[here] = value.astype(BF16).reshape(partial[here].shape)

        in_tiles(partial.shape[-1], tile, back)

    block = 4 * down_partial.shape[3]

    def all_rows(ref, columns=slice(None)):
        value = ref[:, :, :, columns]
        return value.reshape(-1, value.shape[-1])

    def sent(slot, k, i):
        return pltpu.make_async_copy(
            tiles.at[slot, k], grads_out.at[k, i // RING, i % RING], tile_sems.at[slot, k]
        )

    def weight_grads(begin, end):
        for i in range(begin, end):
            slot = i % 2
            for k, right in enumerate((d_gate, d_up)):
                if i >= 2:
                    sent(slot, k, i - 2).wait()
                value = dot(all_rows(x_all, pl.ds(i * block, block)), all_rows(right), TN)
                tiles[slot, k] = value.astype(BF16).reshape(tiles.shape[2:])
                sent(slot, k, i).start()

    half = act.shape[-1] // 2

    def down_grad(p, sems, buffers):
        columns = pl.ds(p * half, half)
        right = all_rows(act, columns)
        for i in range(2 * RING):
            value = dot(all_rows(d_all, pl.ds(i * block, block)), right, TN).astype(BF16)
            down_partial[i // RING, i % RING, :, :, columns] = value.reshape(*down_partial.shape[2:4], half)
        task = plane_scatter(
            place,
            sender,
            sems,
            down_partial.at[:, :, :, :, columns],
            down_out.at[:, :, columns],
            down_partial.shape[3] // 2,
            buffers,
        )
        next(task)
        return task

    tasks = []

    def down_grads():
        tasks.append(down_grad(0, plane, first_buffers))
        tasks.append(down_grad(1, plane2, second_buffers))

    in_turn(gather, total, backward, down_grads)
    task, task2 = tasks
    total.collect(2)
    next(task)
    total.collect(0)
    next(task2)
    weight_grads(0, 3)
    total.relay()
    weight_grads(3, 4)
    next(task)
    weight_grads(4, 6)
    next(task2)
    weight_grads(6, 7)
    next(task)
    weight_grads(7, 8)
    next(task2)
    total.finish(d_mixed_out)
    sender.settle(gather.begun)

    def attention_norm(rows):
        value, gain = proj[rows, :], gain_rows[2:3, :]
        d_mixed = cotangent[rows, :].astype(F32) + d_mixed_out[rows, :]
        d_mixed_out[rows, :] = d_mixed
        scale = norm_scale(value)
        d_proj_out[rows, :] = norm_back(d_mixed, value, scale, gain).astype(BF16)
        gains_out[0:1, :] += jnp.sum(d_mixed * value * scale, axis=0, keepdims=True)

    by_rows(down_proj.shape[0], attention_norm)
    take_turns((task, task2))
    for i in (6, 7):
        for k in range(2):
            sent(i % 2, k, i).wait()
    sender.finish()


def mlp(number, own, gate_up, down, down_pair, mixed, cotangent, proj, gain_rows):
    rows, width = own.shape
    piece, hidden = gate_up.shape[-2:]
    tokens = (2, 2, 2 * rows)
    weight = pltpu.VMEM((2, RING, RING, piece, hidden), BF16)
    wide, narrow = pltpu.VMEM((*tokens, width), BF16), pltpu.VMEM((*tokens, hidden), BF16)
    return call(
        mlp_kernel,
        number,
        (
            shape_of(rows, width),
            shape_of(rows, width, dtype=F32),
            shape_of(rows, width),
            shape_of(8, width, dtype=F32),
            shape_of(2, 2, RING, RING, piece, hidden),
            shape_of(2, piece, hidden),
        ),
        [ANYWHERE] * 7 + [IN_VMEM],
        (IN_VMEM,) * 4 + (ANYWHERE, IN_VMEM),
        [
            wide,
            wide,
            *[weight] * 3,
            *[narrow] * 3,
            wide,
            weight,
            pltpu.VMEM((2, 2, RING, piece, hidden), BF16),
            pltpu.VMEM((rows, width), F32),
            pltpu.VMEM((rows, width), F32),
            pltpu.VMEM((rows, width), BF16),
            pltpu.VMEM((rows, width), F32),
            *ring_buffers(rows, width),
            *scatter_buffers(piece, hidden // 2, BF16),
            *scatter_buffers(piece, hidden // 2, BF16),
            dma_sems(176),
            dma_sems(RING, 4),
            dma_sems(4, 2 * PIECES),
            dma_sems(RING, 4),
            dma_sems(4, 2 * PIECES),
            dma_sems(2, 12),
            dma_sems(2, 12),
            dma_sems(2, 2),
            dma_sems(2, RING, RING, 3),
        ],
        (own, gate_up, down, down_pair, mixed, cotangent, proj, gain_rows),
    )


def ring_product(place, total, values, weight, partial, others, before_near=lambda: None):
    def compute(dy):
        y = place.shift("y", dy)
        at = (y % 2, y // 2)

        def tile(columns):
            partial[(*at, slice(None), columns)] = dot(values[at], rows_of(weight, columns), NT).astype(BF16)

        in_tiles(partial.shape[-1], 512, tile)
        total.offer(dy)

    compute(2)
    before_near()
    compute(1)
    total.collect(2)
    compute(-1)
    total.collect(1)
    compute(0)
    total.collect(-1)
    total.collect(0)
    for task in others:
        next(task)
    total.relay()


def flat(weight):
    return weight.reshape(-1, weight.shape[-1])


def exact(left, right, dims):
    return lax.dot_general(
        left, right, dims, precision=lax.Precision.HIGHEST, preferred_element_type=F32
    )


def half_roll(values):
    return pltpu.roll(values, HEAD_DIM // 2, 1)


def near_devices(place):
    return [place.at(axis, step) for axis in ("x", "z") for step in (1, -1)]


class Octet:
    peers = [(dy, dc) for dy in (0, 1, 3, 2) for dc in (0, 1) if dy or dc]

    def __init__(self, place, sender, own, slots, sems):
        self.place, self.sender, self.own, self.slots, self.sems = place, sender, own, slots, sems

    @staticmethod
    def device(place, dy, dc):
        y = place.shift("y", dy)
        return {"yl": y % 2, "yh": y // 2, "c": (place.c + dc) % 2}

    def send(self):
        for dy, dc in self.peers:
            slot = ((RING - dy) % RING) * 2 + dc
            device = self.device(self.place, dy, dc)
            self.sender.push(self.own, self.slots.at[slot], self.sems.at[slot], device)

    def total(self):
        for dy, dc in self.peers:
            slot = dy * 2 + dc
            self.sender.arrived(self.slots.at[slot], self.sems.at[slot], self.device(self.place, dy, dc))
        value = self.own[...]
        for dy, dc in self.peers:
            value = value + self.slots[dy * 2 + dc]
        return value


def one_hot_rows(k):
    return (lax.broadcasted_iota(jnp.int32, (8, HEAD_DIM), 0) == k).astype(F32)


def masked(scores, starts, i):
    tile, count = scores.shape
    keys = lax.broadcasted_iota(jnp.int32, (tile, count), 1)
    queries = lax.broadcasted_iota(jnp.int32, (tile, count), 0) + i * tile
    return jnp.where((keys >= starts) & (keys <= queries), scores, -1e30)


def softmax(scores):
    exponent = jnp.exp(scores - jnp.max(scores, axis=-1, keepdims=True))
    return exponent / jnp.sum(exponent, axis=-1, keepdims=True)


def attention_forward_kernel(
    own, attn, down, gain, cosine_in, sine_in, starts_in, proj_out, mixed_out, low_out, gain_rows, head_out, x_out,
    weight_out, raw_out, rot_out, value_out, scale_out, attended_out, down_out, pair_out, *refs
):
    (
        (x_all, weight, raw, rot, values, scales, attended, partial, sums, slots, down_all, gain_all),
        (cosine, sine, starts, hidden),
        ring,
        (sends, gather_sems, sum_sems, octet_sems, attn_plane, gain_plane, plane, swap),
    ) = refs_of(refs, 12, 4, 4, 8)
    place = Place()
    sender = Sender(sends)
    _, heads, _, block_rows, _ = raw.shape
    inner = heads * HEAD_DIM
    tile = block_rows // 2
    pairs = ((cosine_in, cosine), (sine_in, sine), (starts_in, starts), (own, hidden))
    later = [sender.keep_first(source, target) for source, target in pairs]
    partner = {"yl": 1 - place.yl}
    me, you = place.yl, 1 - place.yl
    half = down_all.shape[4]
    early, later_half = pl.ds(0, half), pl.ds(half, half)
    shards = ((attn, weight), (gain, gain_all), (down.at[:, :, early], down_all))
    mine = [
        sender.keep_first(source if k == 1 else source.at[me], target.at[me, place.x, place.z])
        for k, (source, target) in enumerate(shards)
    ]
    greet(near_devices(place) + [Octet.device(place, *peer) for peer in Octet.peers])
    for k, (source, target) in enumerate(shards[:2]):
        sender.push(
            source if k == 1 else source.at[you], target.at[me, place.x, place.z], swap.at[k], partner
        )
    gather = RingGather(place, sender, gather_sems, own, x_all)
    gather.begin()
    for copy in mine:
        copy.wait()
    for k, (_, target) in enumerate(shards[:2]):
        sender.arrived(target.at[you, place.x, place.z], swap.at[k], partner)
    attn_task = plane_gather(place, sender, attn_plane, weight, weight.shape[3] // 2)
    gain_task = plane_gather(place, sender, gain_plane, gain_all, gain_all.shape[3])
    next(attn_task)
    next(gain_task)
    sender.push(down.at[you, :, early], down_all.at[me, place.x, place.z], swap.at[2], partner)
    sender.push(down.at[you, :, later_half], pair_out.at[me], swap.at[3], partner)
    sender.keep(down.at[me, :, later_half], pair_out.at[me])

    def gather_all():
        gather.relay()
        yield
        gather.relay_far()
        yield
        for dy in (0, 1, -1, 2):
            gather.ready(dy)

    take_turns((gain_task, attn_task, gather_all()))
    sender.keep(x_all, x_out)
    sender.keep(weight, weight_out)
    for yl in range(2):
        for x in range(RING):
            for h in range(2):
                lanes = pl.ds(((yl * RING + x) * 2 + h) * HEAD_DIM, HEAD_DIM)
                gain_rows[:, lanes] = gain_all[yl, x, 2 * h] + gain_all[yl, x, 2 * h + 1]
    first_column = (place.yh * 2 + place.c) * (2 * inner) + place.yl * inner

    def head_gain(k, h):
        start = pl.multiple_of(first_column + h * HEAD_DIM, HEAD_DIM)
        return gain_rows[k : k + 1, pl.ds(start, HEAD_DIM)]

    for h in range(heads):
        start = pl.multiple_of(first_column + h * HEAD_DIM, HEAD_DIM)
        head_out[:, pl.ds(h * HEAD_DIM, HEAD_DIM)] = gain_rows[:, pl.ds(start, HEAD_DIM)]
    sender.arrived(down_all.at[you, place.x, place.z], swap.at[2], partner)
    down_task = plane_gather(place, sender, plane, down_all, down_all.shape[3] // 2)
    next(down_task)
    total = RingSum(place, sender, sum_sems, partial, *ring)
    ones = [one_hot_rows(k) for k in range(2)]

    def project(t, carry):
        a, b = t // 2, t % 2
        window = pl.ds(pl.multiple_of(b * tile, tile), tile)
        value = dot(x_all[a, b], columns_of(weight, pl.ds(0, 2 * inner)))
        row_sums = jnp.zeros((8, tile), F32)
        for k in range(2):
            for h in range(heads):
                column = k * inner + h * HEAD_DIM
                part = value[:, column : column + HEAD_DIM]
                raw[k, h, a, window, :] = part
                row_sums = row_sums + exact(ones[k], part * part, NT)
        sums[:, pl.ds(pl.multiple_of(t * tile, tile), tile)] = row_sums
        return carry

    def project_value(t, carry):
        a, b = t // 2, t % 2
        window = pl.ds(pl.multiple_of(b * tile, tile), tile)
        value = dot(x_all[a, b], columns_of(weight, pl.ds(2 * inner, inner))).astype(BF16)
        for h in range(heads):
            values[h, a, window, :] = value[:, h * HEAD_DIM : (h + 1) * HEAD_DIM]
        return carry

    lax.fori_loop(0, 4, project, 0)
    octet = Octet(place, sender, sums, slots, octet_sems)
    octet.send()
    sender.keep(raw, raw_out)
    lax.fori_loop(0, 4, project_value, 0)
    sender.keep(values, value_out)
    next(down_task)
    for copy in later:
        copy.wait()
    row_scales = lax.rsqrt(octet.total() / x_all.shape[3] + NORM_EPS)
    for b in range(2):
        for k in range(2):
            scale = exact(row_scales[:, b * block_rows : (b + 1) * block_rows], ones[k], TN)
            scales[k, b] = scale
            for h in range(heads):
                value = raw[k, h, b] * scale * head_gain(k, h)
                rot[k, h, b] = (value * cosine[b] + half_roll(value) * sine[b]).astype(BF16)
    sender.keep(scales, scale_out)
    sender.keep(rot, rot_out)
    next(down_task)

    def attention(b):
        for h in range(heads):
            key, value = rot[1, h, b], values[h, b]
            for i in range(2):
                window, count = pl.ds(i * tile, tile), (i + 1) * tile
                scores = dot(rot[0, h, b, window, :], key[:count], NT) * HEAD_DIM ** (-0.5)
                probs = softmax(masked(scores, starts[b, window, 0:1], i)).astype(BF16)
                attended[b, i, :, pl.ds(h * HEAD_DIM, HEAD_DIM)] = dot(probs, value[:count]).astype(BF16)

    attention(place.yl)
    out_weight = weight.at[:, :, :, :, pl.ds(3 * inner, inner)]
    ring_product(place, total, attended, out_weight, partial, (), lambda: attention(1 - place.yl))
    sender.keep(attended, attended_out)
    take_turns((down_task,))
    sender.keep(down_all, down_out)
    total.finish(proj_out)

    def mix(rows):
        value = proj_out[rows, :]
        mixed = hidden[rows, :].astype(F32) + value * norm_scale(value) * gain_rows[2:3, :]
        mixed_out[rows, :] = mixed
        low_out[rows, :] = mixed.astype(BF16)

    by_rows(proj_out.shape[0], mix)
    sender.arrived(pair_out.at[you], swap.at[3], partner)
    sender.finish()


def attention_forward(number, own, attn, down, gain, cosine, sine, starts):
    rows, width = own.shape
    inner = attn.shape[2] // 4
    heads = inner // HEAD_DIM
    tokens = (2, 2, 2 * rows)
    raw = (2, heads, 2, 4 * rows, HEAD_DIM)
    values, scales, attended = raw[1:], (2, 2, 4 * rows, HEAD_DIM), (*tokens, inner)
    weight = (2, RING, RING, *attn.shape[1:])
    piece = down.shape[1], down.shape[2] // 2
    down_all = (2, RING, RING, *piece)
    return call(
        attention_forward_kernel,
        number,
        (
            shape_of(rows, width, dtype=F32),
            shape_of(rows, width, dtype=F32),
            shape_of(rows, width),
            shape_of(8, width, dtype=F32),
            shape_of(8, inner, dtype=F32),
            shape_of(*tokens, width),
            shape_of(*weight),
            shape_of(*raw, dtype=F32),
            shape_of(*raw),
            shape_of(*values),
            shape_of(*scales, dtype=F32),
            shape_of(*attended),
            shape_of(*down_all),
            shape_of(2, *piece),
        ),
        [ANYWHERE] * 7,
        (IN_VMEM,) * 5 + (ANYWHERE,) * 9,
        [
            pltpu.VMEM((*tokens, width), BF16),
            pltpu.VMEM(weight, BF16),
            pltpu.VMEM(raw, F32),
            pltpu.VMEM(raw, BF16),
            pltpu.VMEM(values, BF16),
            pltpu.VMEM(scales, F32),
            pltpu.VMEM(attended, BF16),
            pltpu.VMEM((*tokens, width), BF16),
            pltpu.VMEM((8, 8 * rows), F32),
            pltpu.VMEM((8, 8, 8 * rows), F32),
            pltpu.VMEM(down_all, BF16),
            pltpu.VMEM((2, RING, RING, *gain.shape), F32),
            *[pltpu.VMEM(other.shape, other.dtype) for other in (cosine, sine, starts, own)],
            *ring_buffers(rows, width),
            dma_sems(208),
            dma_sems(RING, 4),
            dma_sems(4, 2 * PIECES),
            dma_sems(8),
            dma_sems(2, RING, RING, 3),
            dma_sems(2, RING, RING, 3),
            dma_sems(2, RING, RING, 3),
            dma_sems(4),
        ],
        (own, attn, down, gain, cosine, sine, starts),
    )


def attention_backward_kernel(
    own, weight, inputs, d_mixed_in, mlp_in, down, attended_in, raw_in, rot_in, values_in, scales_in,
    cosines_in, sines_in, starts_in, head_gains, token_gains, out, attn_out, gain_out, mlp_out, *refs
):
    (
        (shared, own_weight, attn_partial, gate_partial, up_partial, d_att, back, d_qkv, sums, slots, d_mixed),
        staged,
        (gain_partial, gain_rows, gain_slots, attn_done, gain_done, mlp_done),
        ring,
        buffers,
        late_buffers,
        gate_buffers,
        up_buffers,
        gain_buffers,
        (sends, gather_sems, sum_sems, octet_sems, gain_sems, swap, plane, late_plane, gain_plane, gate_plane),
        (up_plane,),
    ) = refs_of(refs, 11, 8, 6, 4, 5, 5, 5, 5, 5, 10, 1)
    attended, raw_all, rot, values, scales, cosines, sines, starts = staged
    d_all = x_all = partial = shared
    place = Place()
    sender = Sender(sends)
    _, heads, _, block_rows, _ = rot.shape
    width = d_qkv.shape[-1]
    inner = heads * HEAD_DIM
    rows = attn_partial.shape[3]
    block = RING * rows
    mlp_loads = [sender.keep_first(mlp_in.at[0], gate_partial), sender.keep_first(mlp_in.at[1], up_partial)]
    load = sender.keep_first(weight, own_weight)
    sources = (attended_in, raw_in, rot_in, values_in, scales_in, cosines_in, sines_in, starts_in)
    later = [sender.keep_first(source, target) for source, target in zip(sources, staged)]
    sender.keep(d_mixed_in, d_mixed)
    mixed_number = len(sender.open) - 1
    partner = {"yl": 1 - place.yl}
    me, you = place.yl, 1 - place.yl
    greet(near_devices(place) + [Octet.device(place, *peer) for peer in Octet.peers])
    gather = RingGather(place, sender, gather_sems, own, d_all)
    total = RingSum(place, sender, sum_sems, partial, *ring)
    gather.begin()
    sender.push(down.at[you], mlp_out.at[2, me], swap.at[3], partner)
    sender.keep(down.at[me], mlp_out.at[2, me])
    mlp = []
    for k, (sems, bufs, summand) in enumerate(
        ((gate_plane, gate_buffers, gate_partial), (up_plane, up_buffers, up_partial))
    ):
        mlp_loads[k].wait()
        task = plane_scatter(place, sender, sems, summand, mlp_done.at[k], rows // 2, bufs)
        next(task)
        mlp.append(task)
    gate_task, up_task = mlp
    load.wait()
    gain_partial[...] = jnp.zeros_like(gain_partial)
    gain_rows[...] = jnp.zeros_like(gain_rows)
    for k in range(2 * RING):
        for z in range(RING):
            gain_partial[k // RING, k % RING, z, 2:4, :] = token_gains[0:2, k * block : (k + 1) * block]

    def compute(dy):
        gather.ready(dy)
        y = place.shift("y", dy)
        at = (y % 2, y // 2)
        d_att[at] = dot(d_all[at], own_weight[:, pl.ds(width, inner)]).astype(BF16)

    tile = block_rows // 2
    score_factor = HEAD_DIM ** (-0.5)
    ones = [one_hot_rows(k) for k in range(2)]

    def attention(b):
        row_sums = jnp.zeros((8, block_rows), F32)
        cosine, sine = cosines[b], sines[b]
        for h in range(heads):
            lanes = pl.ds(h * HEAD_DIM, HEAD_DIM)
            key, value = rot[1, h, b], values[h, b]
            d_query, d_key, d_value = [], [None, None], [None, None]
            for i in range(2):
                window = pl.ds(i * tile, tile)
                query, upstream = rot[0, h, b, window, :], d_att[b, i, :, lanes]
                count = (i + 1) * tile
                scores = dot(query, key[:count], NT) * score_factor
                probs = softmax(masked(scores, starts[b, window, 0:1], i))
                d_probs = dot(upstream, value[:count], NT)
                row_dot = jnp.sum(probs * d_probs, axis=-1, keepdims=True)
                d_scores = (probs * (d_probs - row_dot) * score_factor).astype(BF16)
                probs = probs.astype(BF16)
                d_query.append(dot(d_scores, key[:count]))
                for j in range(i + 1):
                    part = slice(j * tile, (j + 1) * tile)
                    for sums_of, left, right in ((d_key, d_scores, query), (d_value, probs, upstream)):
                        term = dot(left[:, part], right, TN)
                        sums_of[j] = term if sums_of[j] is None else sums_of[j] + term
            for i in range(2):
                d_qkv[b, i, :, pl.ds(2 * inner + h * HEAD_DIM, HEAD_DIM)] = d_value[i].astype(BF16)
            for k, parts in enumerate((d_query, d_key)):
                turned = jnp.concatenate(parts, axis=0)
                turned = turned * cosine - half_roll(turned) * sine
                raw = raw_all[k, h, b]
                gain_rows[k : k + 1, lanes] += jnp.sum(turned * raw * scales[k, b], axis=0, keepdims=True)
                turned = turned * head_gains[k : k + 1, lanes]
                back[k, h, b] = turned
                row_sums = row_sums + exact(ones[k], turned * raw, NT)
        sums[:, pl.ds(pl.multiple_of(b * block_rows, block_rows), block_rows)] = row_sums

    compute(0)
    gather.relay()
    compute(1)
    compute(-1)
    next(gate_task)
    for copy in later:
        copy.wait()
    attention(1 - place.yl)
    gather.relay_far()
    compute(2)
    next(up_task)
    attention(place.yl)
    octet = Octet(place, sender, sums, slots, octet_sems)
    octet.send()
    first = (place.yh * 2 + place.c) * 2 + place.yl
    for z in range(RING):
        gain_partial[first // RING, first % RING, z, 0:2, :] = gain_rows[0:2, :]
    gains = plane_scatter(place, sender, gain_plane, gain_partial, gain_done, gain_done.shape[1], gain_buffers)
    next(gains)

    def flat_tokens(ref, columns=slice(None)):
        value = ref[:, :, :, columns]
        return value.reshape(-1, value.shape[-1])

    def weight_grads(left_ref, right, start):
        size = right.shape[1]
        for i in range(2 * RING):
            left = flat_tokens(left_ref, pl.ds(i * block, block))
            value = dot(left, right, TN).astype(BF16)
            attn_partial[i // RING, i % RING, :, :, pl.ds(start, size)] = value.reshape(RING, rows, size)

    weight_grads(d_all, flat_tokens(attended), width)
    sender.settle(gather.forwarded)
    load = sender.keep_first(inputs, x_all)
    next(gate_task)
    load.wait()

    def attn_scatter(columns, sems, bufs):
        task = plane_scatter(
            place,
            sender,
            sems,
            attn_partial.at[:, :, :, :, columns],
            attn_done.at[:, :, columns],
            rows // 2,
            bufs,
        )
        next(task)
        return task

    weight_grads(x_all, flat_tokens(d_qkv, pl.ds(2 * inner, inner)), 2 * inner)
    early = attn_scatter(pl.ds(2 * inner, 2 * inner), plane, buffers)
    row_sums = octet.total()
    for b in range(2):
        for k in range(2):
            column = exact(row_sums[:, b * block_rows : (b + 1) * block_rows], ones[k], TN)
            for h in range(heads):
                scale = scales[k, b]
                value = scale * back[k, h, b] - raw_all[k, h, b] * (scale * scale * scale * column / own.shape[1])
                value = value.astype(BF16)
                for i in range(2):
                    d_qkv[b, i, :, pl.ds(k * inner + h * HEAD_DIM, HEAD_DIM)] = value[
                        i * tile : (i + 1) * tile
                    ]
    weight_grads(x_all, flat_tokens(d_qkv, pl.ds(0, 2 * inner)), 0)
    late = attn_scatter(pl.ds(0, 2 * inner), late_plane, late_buffers)
    next(gate_task)
    next(up_task)
    next(early)
    ring_product(
        place, total, d_qkv, own_weight.at[:, pl.ds(0, width)], partial, (late, up_task, gains)
    )
    take_turns((gate_task, up_task))
    for k in range(2):
        sender.push(mlp_done.at[k, you], mlp_out.at[k, me], swap.at[1 + k], partner)
        sender.keep(mlp_done.at[k, me], mlp_out.at[k, me])
    take_turns((early, gains, late))
    sender.push(attn_done.at[you], attn_out.at[me], swap.at[0], partner)
    sender.keep(attn_done.at[me], attn_out.at[me])
    everyone = Octet(place, sender, gain_done, gain_slots, gain_sems)
    everyone.send()
    sender.settle([mixed_number])
    total.finish(out, d_mixed)
    gain_out[...] = everyone.total()
    sender.arrived(attn_out.at[you], swap.at[0], partner)
    for k in range(3):
        sender.arrived(mlp_out.at[k, you], swap.at[1 + k], partner)
    sender.finish()


def attention_backward(number, own, weight, inputs, d_mixed, mlp_partial, down, attended, *others):
    rows, width = own.shape
    tokens = (2, 2, 2 * rows)
    inner = attended.shape[3]
    heads = inner // HEAD_DIM
    shard = width // 32, weight.shape[1]
    gain_tile = (8, 4 * shard[0])
    return call(
        attention_backward_kernel,
        number,
        (
            shape_of(rows, width, dtype=F32),
            shape_of(2, *shard),
            shape_of(2, *gain_tile, dtype=F32),
            shape_of(3, 2, *shard),
        ),
        [ANYWHERE] * 14 + [IN_VMEM] * 2,
        (IN_VMEM,) * 4,
        [
            pltpu.VMEM((*tokens, width), BF16),
            pltpu.VMEM(weight.shape, BF16),
            pltpu.VMEM((2, RING, RING, *shard), BF16),
            pltpu.VMEM(mlp_partial.shape[1:], BF16),
            pltpu.VMEM(mlp_partial.shape[1:], BF16),
            pltpu.VMEM((*tokens, inner), BF16),
            pltpu.VMEM((2, heads, 2, 4 * rows, HEAD_DIM), F32),
            pltpu.VMEM((*tokens, 3 * inner), BF16),
            pltpu.VMEM((8, 8 * rows), F32),
            pltpu.VMEM((8, 8, 8 * rows), F32),
            pltpu.VMEM((rows, width), F32),
            *[pltpu.VMEM(other.shape, other.dtype) for other in (attended, *others[:7])],
            pltpu.VMEM((2, RING, RING, *gain_tile), F32),
            pltpu.VMEM((8, inner), F32),
            pltpu.VMEM((8, 2, *gain_tile), F32),
            pltpu.VMEM((2, *shard), BF16),
            pltpu.VMEM((2, *gain_tile), F32),
            pltpu.VMEM((2, 2, *shard), BF16),
            *ring_buffers(rows, width),
            *scatter_buffers(shard[0], shard[1] // 2, BF16),
            *scatter_buffers(shard[0], shard[1] // 2, BF16),
            *scatter_buffers(*shard, BF16),
            *scatter_buffers(*shard, BF16),
            *scatter_buffers(*gain_tile, F32),
            dma_sems(224),
            dma_sems(RING, 4),
            dma_sems(4, 2 * PIECES),
            dma_sems(8),
            dma_sems(8),
            dma_sems(5),
            dma_sems(2, 12),
            dma_sems(2, 12),
            dma_sems(2, 12),
            dma_sems(2, 12),
            dma_sems(2, 12),
        ],
        (own, weight, inputs, d_mixed, mlp_partial, down, attended, *others),
    )


def norm_scale(values):
    return lax.rsqrt(jnp.mean(values * values, axis=-1, keepdims=True) + NORM_EPS)


def norm_back(upstream, values, scales, gain_row):
    scaled_grad = upstream * gain_row
    return scales * scaled_grad - values * scales**3 * jnp.mean(
        scaled_grad * values, axis=-1, keepdims=True
    )


def doc_layout(lengths, group_size):
    positions = jnp.arange(group_size, dtype=jnp.int32)
    doc_ends = jnp.cumsum(lengths)
    passed = (positions[:, None] >= doc_ends[None, :]).astype(jnp.int32)
    segment = jnp.sum(passed, axis=-1)
    begins = jnp.sum(passed * lengths[None, :], axis=-1)
    return (segment, positions - begins)


def rope_tables(offsets):
    frequency = ROPE_BASE ** (-jnp.arange(0, HEAD_DIM, 2).astype(jnp.float32) / HEAD_DIM)
    angles = offsets.astype(jnp.float32)[:, None] * frequency[None, :]
    cosine, sine = jnp.cos(angles), jnp.sin(angles)
    return (
        jnp.concatenate([cosine, cosine], axis=-1),
        jnp.concatenate([sine, sine], axis=-1),
    )


def half_turn(values):
    middle = values.shape[-1] // 2
    return jnp.concatenate([-values[..., middle:], values[..., :middle]], axis=-1)


def rotate(values, cosine_table, sine_table):
    return values * cosine_table + half_turn(values) * sine_table


def unrotate(values, cosine_table, sine_table):
    return values * cosine_table - half_turn(values) * sine_table


def product(left, right):
    return jnp.dot(left, right, preferred_element_type=F32)


def row_product(left, right):
    return lax.dot_general(left, right, (((1,), (1,)), ((), ())), preferred_element_type=F32)


def col_product(left, right):
    return lax.dot_general(left, right, (((0,), (0,)), ((), ())), preferred_element_type=F32)


def adam_update(weights_old, first_old, second_old, gradient, rate, decay):
    first_new = BETA_ONE * first_old + (1.0 - BETA_ONE) * gradient
    second_new = BETA_TWO * second_old + (1.0 - BETA_TWO) * gradient * gradient
    ratio = (
        first_new
        / (1.0 - BETA_ONE**STEP)
        / (jnp.sqrt(second_new / (1.0 - BETA_TWO**STEP)) + ADAM_EPS)
    )
    return (first_new, second_new, weights_old - rate * (ratio + decay * weights_old))


def mlp_adam_kernel(weights, first, second, sums, grad_out, first_out, second_out, new_out):
    half = sums.shape[3]
    for h in range(2):
        part = slice(None), slice(None), slice(h * half, (h + 1) * half)
        gradient = sums[:, h].astype(F32)
        grad_out[part] = gradient
        first_out[part], second_out[part], new_out[part] = adam_update(
            weights[part], first[part], second[part], gradient, WEIGHT_RATE, WEIGHT_DECAY
        )


def mlp_adam(weights, first, second, sums):
    count, rows, columns = weights.shape
    state = pl.BlockSpec((1, rows, columns), lambda m: (m, 0, 0))
    return pl.pallas_call(
        mlp_adam_kernel,
        out_shape=(shape_of(*weights.shape, dtype=F32),) * 4,
        grid=(count,),
        in_specs=[state] * 3 + [pl.BlockSpec((1, *sums.shape[1:]), lambda m: (m, 0, 0, 0))],
        out_specs=(state,) * 4,
        compiler_params=pltpu.CompilerParams(vmem_limit_bytes=VMEM_LIMIT),
    )(weights, first, second, sums)


def attn_adam_kernel(weights, first, second, sums, grad_out, first_out, second_out, new_out):
    inner = weights.shape[2]
    for m in range(weights.shape[0]):
        gradient = sums[0, :, m * inner : (m + 1) * inner].astype(F32)
        grad_out[m] = gradient
        first_out[m], second_out[m], new_out[m] = adam_update(
            weights[m], first[m], second[m], gradient, WEIGHT_RATE, WEIGHT_DECAY
        )


def attn_adam(weights, first, second, sums):
    count, rows, columns = weights.shape
    state = pl.BlockSpec((count, rows, columns // 2), lambda h: (0, 0, h))
    return pl.pallas_call(
        attn_adam_kernel,
        out_shape=(shape_of(*weights.shape, dtype=F32),) * 4,
        grid=(2,),
        in_specs=[state] * 3 + [pl.BlockSpec((1, *sums.shape[1:]), lambda h: (h, 0, 0))],
        out_specs=(state,) * 4,
        compiler_params=pltpu.CompilerParams(vmem_limit_bytes=VMEM_LIMIT),
    )(weights, first, second, sums)


def body(
    hidden_in,
    cotangent,
    doc_lengths,
    attn_weights,
    attn_first,
    attn_second,
    mlp_weights,
    mlp_first,
    mlp_second,
    gains,
    gain_first,
    gain_second,
):
    row_count, model_width = hidden_in.shape
    shard_rows = attn_weights.shape[1]
    heads_width = attn_weights.shape[2] // 2
    hidden_width = mlp_weights.shape[2] // 2
    token_count = 8 * row_count
    block_rows = token_count // 2
    head_count = heads_width // HEAD_DIM
    score_factor = HEAD_DIM ** (-0.5)
    yl, yh, core = (lax.axis_index(a) for a in ("yl", "yh", "c"))

    attn_halves = (
        attn_weights.astype(BF16)
        .reshape(4, shard_rows, 2, heads_width)
        .transpose(2, 1, 0, 3)
        .reshape(2, shard_rows, 4 * heads_width)
    )
    left, right = mlp_weights[:2, :, :hidden_width], mlp_weights[:2, :, hidden_width:]
    mine = jnp.where(yl == 0, left, right).astype(BF16)
    yours = jnp.where(yl == 0, right, left).astype(BF16)
    arrived = lax.ppermute(yours, "yl", [(0, 1), (1, 0)])
    down_halves = mlp_weights[2].astype(BF16).reshape(shard_rows, 2, hidden_width).transpose(1, 0, 2)
    gain_low = lax.reduce_precision(gains, 8, 7)
    odd = lax.axis_index("z") % 2
    gain_tile = jnp.concatenate([jnp.where(odd == 0, gain_low, 0.0), jnp.where(odd == 1, gain_low, 0.0)], axis=1)
    gain_tile = jnp.pad(gain_tile, ((0, 4), (0, 0)))
    theirs = lax.ppermute(doc_lengths, "yl", [(0, 1), (1, 0)])
    lengths = jnp.where(yl == 0, jnp.stack([doc_lengths[0], theirs[0]]), jnp.stack([theirs[0], doc_lengths[0]]))
    _, offsets = jax.vmap(lambda one: doc_layout(one, block_rows))(lengths)
    cosine_table, sine_table = rope_tables(offsets.reshape(-1))
    sine_table = sine_table * jnp.where(jnp.arange(HEAD_DIM) < HEAD_DIM // 2, -1.0, 1.0)
    cosine_table = cosine_table.reshape(2, block_rows, HEAD_DIM)
    sine_table = sine_table.reshape(2, block_rows, HEAD_DIM)
    starts = jnp.broadcast_to((jnp.arange(block_rows) - offsets)[:, :, None], (2, block_rows, HEAD_DIM))

    arrived, cosine_table, sine_table, starts, attn_halves, gain_tile, down_halves = lax.optimization_barrier(
        (arrived, cosine_table, sine_table, starts, attn_halves, gain_tile, down_halves)
    )
    pair = jnp.stack(
        [jnp.where(yl == 0, mine, arrived), jnp.where(yl == 0, arrived, mine)], axis=1
    )
    gate_up = lax.all_gather(pair.reshape(-1, hidden_width), ("x", "z"), tiled=True)
    gate_up = gate_up.reshape(RING, RING, 2, 2, shard_rows, hidden_width)

    (
        attn_proj, mixed, mixed_low, gain_full, head_gains, every_input, attn_all, raw, rotated, values,
        head_scales, attended, down_half, down_pair,
    ) = attention_forward(
        1, hidden_in, attn_halves, down_halves, gain_tile, cosine_table, sine_table, starts
    )
    attn_all = flat(attn_all)
    hidden_out, d_mixed, d_proj, token_gains, mlp_partial, down_sum = mlp(
        2, mixed_low, gate_up, down_half, down_pair, mixed, cotangent, attn_proj, gain_full
    )
    input_grad, attn_sum, gain_sum, mlp_sum = attention_backward(
        3,
        d_proj,
        attn_all,
        every_input,
        d_mixed,
        mlp_partial,
        down_sum,
        attended,
        raw,
        rotated,
        values,
        head_scales,
        cosine_table,
        sine_table,
        starts,
        head_gains,
        token_gains,
    )

    gain_sum = lax.dynamic_index_in_dim(gain_sum, yl, 0, keepdims=False)[:4]
    gain_grad = lax.dynamic_slice_in_dim(gain_sum, lax.axis_index("z") * shard_rows, shard_rows, axis=1)
    attn_grad, attn_first_new, attn_second_new, attn_new = attn_adam(
        attn_weights, attn_first, attn_second, attn_sum
    )
    mlp_grad, mlp_first_new, mlp_second_new, mlp_new = mlp_adam(
        mlp_weights, mlp_first, mlp_second, mlp_sum
    )
    gain_first_new, gain_second_new, gain_new = adam_update(
        gains, gain_first, gain_second, gain_grad, GAIN_RATE, 0.0
    )
    return (
        hidden_out,
        input_grad,
        attn_grad,
        attn_first_new,
        attn_second_new,
        attn_new,
        mlp_grad,
        mlp_first_new,
        mlp_second_new,
        mlp_new,
        gain_grad,
        gain_first_new,
        gain_second_new,
        gain_new,
    )


def solution(mesh):
    split = Mesh(mesh.devices.reshape(2, 4, 4, 2, 2), EVERY)
    tokens, shards, rows = P(EVERY, None), P(None, DP, TENSOR), P(None, DP)
    return jax.shard_map(
        body,
        mesh=split,
        in_specs=(tokens, tokens, P(DP, None), *[shards] * 6, *[rows] * 3),
        out_specs=(tokens, tokens, *[shards] * 8, *[rows] * 4),
        check_vma=False,
    )
```

```python
import functools

import jax
import jax.numpy as jnp
from jax import lax
from jax.experimental import pallas as pl
from jax.experimental.pallas import tpu as pltpu
from jax.sharding import Mesh
from jax.sharding import PartitionSpec as P

HEAD_DIM = 128
STEP = 10
DP = ("yl", "x", "z")
TENSOR = ("yh", "c")
EVERY = ("yl", "x", "z", "yh", "c")
RING = 4
MESH = pl.DeviceIdType.MESH

NORM_EPS = 1e-06
ROPE_BASE = 500000.0
BETA_ONE = 0.9
BETA_TWO = 0.95
ADAM_EPS = 1e-08
WEIGHT_RATE = 0.03
GAIN_RATE = 1.0
WEIGHT_DECAY = 0.1

BF16 = jnp.bfloat16
F32 = jnp.float32
IN_VMEM = pl.BlockSpec(memory_space=pltpu.VMEM)
ANYWHERE = pl.BlockSpec(memory_space=pl.ANY)
VMEM_LIMIT = 60 * 1024 * 1024


class Place:
    def __init__(self):
        self.x, self.z, self.c = (lax.axis_index(a) for a in ("x", "z", "c"))
        self.yl, self.yh = (lax.axis_index(a) for a in ("yl", "yh"))
        self.y = self.yh * 2 + self.yl

    def at(self, axis, step):
        if axis == "y":
            there = (self.y + step + RING) % RING
            return {"yl": there % 2, "yh": there // 2}
        if axis == "c":
            return {"c": 1 - self.c}
        return {axis: (getattr(self, axis) + step + RING) % RING}

    def shift(self, axis, step):
        return (getattr(self, axis) + step + RING) % RING


def greet(devices):
    barrier = pltpu.get_barrier_semaphore()
    for device in devices:
        pl.semaphore_signal(barrier, inc=1, device_id=device, device_id_type=MESH)
    pl.semaphore_wait(barrier, len(devices))


def greet_all(place, axes):
    devices = []
    for axis in axes:
        devices += [place.at(axis, 1)] if axis == "c" else [place.at(axis, 1), place.at(axis, -1)]
    greet(devices)


class Sender:
    def __init__(self, sems):
        self.sems, self.open = sems, []

    def push(self, src, dst, recv_sem, device):
        copy = pltpu.make_async_remote_copy(
            src_ref=src,
            dst_ref=dst,
            send_sem=self.sems.at[len(self.open)],
            recv_sem=recv_sem,
            device_id=device,
            device_id_type=MESH,
        )
        copy.start()
        self.open.append(copy.wait_send)
        return len(self.open) - 1

    def settle(self, numbers):
        for number in numbers:
            self.open[number]()
            self.open[number] = lambda: None

    def keep(self, src, dst):
        copy = pltpu.make_async_copy(src, dst, self.sems.at[len(self.open)])
        copy.start()
        self.open.append(copy.wait)

    def keep_first(self, src, dst):
        copy = pltpu.make_async_copy(src, dst, self.sems.at[len(self.open)])
        copy.start()
        self.open.append(lambda: None)
        return copy

    def arrived(self, dst, recv_sem, device):
        pltpu.make_async_remote_copy(
            src_ref=dst,
            dst_ref=dst,
            send_sem=self.sems.at[0],
            recv_sem=recv_sem,
            device_id=device,
            device_id_type=MESH,
        ).wait_recv()

    def finish(self):
        for wait in self.open:
            wait()


def take_turns(tasks):
    tasks = list(tasks)
    while tasks:
        for task in list(tasks):
            if next(task, "done") == "done":
                tasks.remove(task)


WHOLE, LOW, HIGH = 0, 1, 2
PIECES = 4


def part_of(ref, part, cut):
    rows = ref.shape[-2]
    if part == WHOLE:
        return ref
    return ref.at[pl.ds(0, cut)] if part == LOW else ref.at[pl.ds(cut, rows - cut)]


def plane_gather(place, sender, sems, out, cut):
    rows = out.shape[-2]
    axes = (("x", "z"), ("z", "x"))

    def piece(half, dp, dq):
        p, q = (place.shift(a, d) for a, d in zip(axes[half], (dp, dq)))
        return out.at[half, p, q] if half == 0 else out.at[half, q, p]

    def parts(part):
        if part == WHOLE:
            return True
        return cut > 0 if part == LOW else cut < rows

    def send(half, dp, dq, part, along, step):
        if parts(part):
            ref = part_of(piece(half, dp, dq), part, cut)
            sp, sq = ((dp - step) % RING, dq % RING) if along == 0 else (dp % RING, (dq - step) % RING)
            sender.push(ref, ref, sems.at[half, sp, sq, part], place.at(axes[half][along], step))

    def wait(half, dp, dq, part):
        if parts(part):
            ref = part_of(piece(half, dp, dq), part, cut)
            sender.arrived(ref, sems.at[half, dp % RING, dq % RING, part], place.at("x", 1))

    both = (0, 1)
    for half in both:
        for step in (1, -1):
            send(half, 0, 0, WHOLE, 0, step)
    for half in both:
        for step in (1, -1):
            send(half, 0, 0, WHOLE, 1, step)
    yield
    for step, part in ((1, LOW), (-1, HIGH)):
        for half in both:
            wait(half, -step, 0, WHOLE)
            send(half, -step, 0, part, 0, step)
            for side in (1, -1):
                send(half, -step, 0, WHOLE, 1, side)
    yield
    for half in both:
        for step, part in ((1, LOW), (-1, HIGH)):
            wait(half, 0, -step, WHOLE)
            send(half, 0, -step, part, 1, step)
    yield
    for half in both:
        wait(half, 2, 0, LOW)
        wait(half, 2, 0, HIGH)
        for side in (1, -1):
            send(half, 2, 0, WHOLE, 1, side)
    yield
    for dp in (-1, 1, 2):
        for half in both:
            for step, part in ((1, LOW), (-1, HIGH)):
                wait(half, dp, -step, WHOLE)
                send(half, dp, -step, part, 1, step)
        yield
    for dp in (0, -1, 1, 2):
        for half in both:
            wait(half, dp, 2, LOW)
            wait(half, dp, 2, HIGH)


class RingGather:
    def __init__(self, place, sender, sems, own, out):
        self.place, self.sender, self.sems, self.own, self.out = place, sender, sems, own, out
        self.rows = own.shape[0]
        self.other = place.at("c", 1)
        self.begun, self.forwarded = [], []

    def piece(self, dy, core, part=WHOLE):
        y = self.place.shift("y", dy)
        half = self.rows // 2
        start, size = {WHOLE: (0, self.rows), LOW: (0, half), HIGH: (half, half)}[part]
        return self.out.at[y % 2, y // 2, pl.ds(pl.multiple_of(core * self.rows + start, 16), size)]

    def begin(self):
        place, mine = self.place, self.piece(0, self.place.c)
        for step in (1, -1):
            number = self.sender.push(self.own, mine, self.sems.at[(-step) % RING, WHOLE], place.at("y", step))
            self.begun.append(number)
        self.begun.append(self.sender.push(self.own, mine, self.sems.at[0, 3], self.other))
        self.kept = self.sender.keep_first(self.own, mine)

    def relay(self):
        for step, part in ((1, LOW), (-1, HIGH)):
            ref = self.piece(-step, self.place.c)
            self.sender.arrived(ref, self.sems.at[(-step) % RING, WHOLE], self.other)
            half = self.piece(-step, self.place.c, part)
            self.forwarded += [
                self.sender.push(half, half, self.sems.at[2, part], self.place.at("y", step)),
                self.sender.push(ref, ref, self.sems.at[(-step) % RING, 3], self.other),
            ]

    def relay_far(self):
        for part in (LOW, HIGH):
            self.sender.arrived(self.piece(2, self.place.c, part), self.sems.at[2, part], self.other)
        ref = self.piece(2, self.place.c)
        self.forwarded += [self.sender.push(ref, ref, self.sems.at[2, 3], self.other)]

    def ready(self, dy):
        if dy == 0:
            self.kept.wait()
        self.sender.arrived(self.piece(dy, 1 - self.place.c), self.sems.at[dy % RING, 3], self.other)


def ring_gather(place, sender, sems, own, out):
    gather = RingGather(place, sender, sems, own, out)
    gather.begin()
    yield
    gather.relay()
    yield
    gather.relay_far()
    yield
    for dy in (0, 1, -1, 2):
        gather.ready(dy)


def add_rows(out, terms, rows):
    def step(i, carry):
        window = pl.ds(pl.multiple_of(i * 16, 16), 16)
        total = terms[0][window, :].astype(F32)
        for term in terms[1:]:
            total = total + term[window, :].astype(F32)
        out[window, :] = total.astype(out.dtype)
        return carry

    lax.fori_loop(0, rows // 16, step, 0)


class RingSum:
    def __init__(self, place, sender, sems, partial, kept, from_core, hop, last):
        self.place, self.sender, self.sems, self.partial = place, sender, sems, partial
        self.kept, self.from_core, self.hop, self.last = kept, from_core, hop, last
        self.rows = kept.shape[1]
        self.low, self.high = pl.ds(0, self.rows // 2), pl.ds(self.rows // 2, self.rows // 2)
        self.other = place.at("c", 1)

    def mine(self, dy, core):
        y = self.place.shift("y", dy)
        return self.partial.at[y % 2, y // 2, pl.ds(pl.multiple_of(core * self.rows, 16), self.rows)]

    def offer(self, dy):
        slot = dy % RING
        self.sender.push(
            self.mine(dy, 1 - self.place.c), self.from_core.at[slot], self.sems.at[0, slot], self.other
        )

    def pieces(self):
        columns = self.kept.shape[2]
        return [pl.ds(p * columns // PIECES, columns // PIECES) for p in range(PIECES)]

    def collect(self, dy):
        slot = dy % RING
        kept, low, high = self.kept.at[slot], self.low, self.high
        self.sender.arrived(self.from_core.at[slot], self.sems.at[0, slot], self.other)
        if dy == 0:
            return
        up, down = self.place.at("y", 1), self.place.at("y", -1)
        mine = self.mine(dy, self.place.c)
        if dy == 2:
            for p, columns in enumerate(self.pieces()):
                add_rows(kept.at[:, columns], (mine.at[:, columns], self.from_core.at[slot, :, columns]), self.rows)
                self.sender.push(kept.at[low, columns], self.hop.at[0, :, columns], self.sems.at[1, p], up)
                self.sender.push(
                    kept.at[high, columns], self.hop.at[1, :, columns], self.sems.at[1, PIECES + p], down
                )
            return
        add_rows(kept, (mine, self.from_core.at[slot]), self.rows)
        if dy == 1:
            self.sender.push(kept.at[high], self.last.at[0, high], self.sems.at[2, 1], up)
        else:
            self.sender.push(kept.at[low], self.last.at[1, low], self.sems.at[2, 2], down)

    def relay(self):
        for p, columns in enumerate(self.pieces()):
            for k, slot, part, step in ((0, 1, self.low, 1), (1, 3, self.high, -1)):
                number = k * PIECES + p
                self.sender.arrived(self.hop.at[k, :, columns], self.sems.at[1, number], self.other)
                rows = self.kept.at[slot, part, columns]
                add_rows(rows, (rows, self.hop.at[k, :, columns]), self.rows // 2)
                self.sender.push(
                    rows, self.last.at[k, part, columns], self.sems.at[3, number], self.place.at("y", step)
                )

    def finish(self, out, *others):
        self.sender.arrived(self.last.at[0, self.high], self.sems.at[2, 1], self.other)
        self.sender.arrived(self.last.at[1, self.low], self.sems.at[2, 2], self.other)
        mine = self.mine(0, self.place.c)
        for p, columns in enumerate(self.pieces()):
            for k, part in ((0, self.low), (1, self.high)):
                self.sender.arrived(
                    self.last.at[k, part, columns], self.sems.at[3, k * PIECES + p], self.other
                )
            terms = (mine, self.from_core.at[0], self.last.at[0], self.last.at[1], *others)
            add_rows(out.at[:, columns], [term.at[:, columns] for term in terms], self.rows)


def plane_scatter(place, sender, sems, partial, done, cut, bufs, source=None):
    rows = partial.shape[-2]
    hop, last, middle, hop2, last2 = bufs
    low, high = pl.ds(0, cut), pl.ds(cut, rows - cut)
    axes = (("z", "x"), ("x", "z"))
    two_parts = cut < rows
    both = (0, 1)
    other = place.at("x", 1)

    source = partial if source is None else source

    def row(half, du, window):
        u = place.shift(axes[half][0], du)
        return source.at[half, :, u, window] if half == 0 else source.at[half, u, :, window]

    def line(half, du, v):
        u = place.shift(axes[half][0], du)
        return partial.at[half, v, u] if half == 0 else partial.at[half, u, v]

    def add(out, terms, count):
        if count % 16:
            total = terms[0][...].astype(F32)
            for term in terms[1:]:
                total = total + term[...].astype(F32)
            out[...] = total.astype(out.dtype)
        else:
            add_rows(out, terms, count)

    for half in both:
        u = axes[half][0]
        sender.push(row(half, 2, low), hop.at[half, 0], sems.at[half, 0], place.at(u, 1))
        if two_parts:
            sender.push(row(half, 2, high), hop.at[half, 1], sems.at[half, 1], place.at(u, -1))
    for half in both:
        u = axes[half][0]
        if two_parts:
            sender.push(row(half, 1, high), last.at[half, 0, :, high], sems.at[half, 2], place.at(u, 1))
        sender.push(row(half, -1, low), last.at[half, 1, :, low], sems.at[half, 3], place.at(u, -1))
    yield
    for half in both:
        u = axes[half][0]
        sender.arrived(hop.at[half, 0], sems.at[half, 0], other)
        for v in range(RING):
            add(hop.at[half, 0, v], (line(half, 1, v).at[low], hop.at[half, 0, v]), cut)
        sender.push(hop.at[half, 0], last.at[half, 0, :, low], sems.at[half, 4], place.at(u, 1))
        if two_parts:
            sender.arrived(hop.at[half, 1], sems.at[half, 1], other)
            for v in range(RING):
                add(
                    hop.at[half, 1, v],
                    (line(half, -1, v).at[high], hop.at[half, 1, v]),
                    rows - cut,
                )
            sender.push(
                hop.at[half, 1], last.at[half, 1, :, high], sems.at[half, 5], place.at(u, -1)
            )
    yield
    for half in both:
        v_axis = axes[half][1]
        if two_parts:
            sender.arrived(last.at[half, 0, :, high], sems.at[half, 2], other)
        sender.arrived(last.at[half, 1, :, low], sems.at[half, 3], other)
        sender.arrived(last.at[half, 0, :, low], sems.at[half, 4], other)
        if two_parts:
            sender.arrived(last.at[half, 1, :, high], sems.at[half, 5], other)
        for dv in (2, 1, -1, 0):
            v = place.shift(v_axis, dv)
            terms = (line(half, 0, v), last.at[half, 0, v], last.at[half, 1, v])
            add(middle.at[half, dv % RING], terms, rows)
            if dv == 2:
                sender.push(
                    middle.at[half, 2, low], hop2.at[half, 0], sems.at[half, 6], place.at(v_axis, 1)
                )
                if two_parts:
                    sender.push(
                        middle.at[half, 2, high],
                        hop2.at[half, 1],
                        sems.at[half, 7],
                        place.at(v_axis, -1),
                    )
            elif dv == 1 and two_parts:
                sender.push(
                    middle.at[half, 1, high], last2.at[half, 0, high], sems.at[half, 8], place.at(v_axis, 1)
                )
            elif dv == -1:
                sender.push(
                    middle.at[half, 3, low], last2.at[half, 1, low], sems.at[half, 9], place.at(v_axis, -1)
                )
    yield
    for half in both:
        v_axis = axes[half][1]
        sender.arrived(hop2.at[half, 0], sems.at[half, 6], other)
        add(hop2.at[half, 0], (middle.at[half, 1, low], hop2.at[half, 0]), cut)
        sender.push(
            hop2.at[half, 0], last2.at[half, 0, low], sems.at[half, 10], place.at(v_axis, 1)
        )
        if two_parts:
            sender.arrived(hop2.at[half, 1], sems.at[half, 7], other)
            add(hop2.at[half, 1], (middle.at[half, 3, high], hop2.at[half, 1]), rows - cut)
            sender.push(
                hop2.at[half, 1], last2.at[half, 1, high], sems.at[half, 11], place.at(v_axis, -1)
            )
    yield
    for half in both:
        if two_parts:
            sender.arrived(last2.at[half, 0, high], sems.at[half, 8], other)
        sender.arrived(last2.at[half, 1, low], sems.at[half, 9], other)
        sender.arrived(last2.at[half, 0, low], sems.at[half, 10], other)
        if two_parts:
            sender.arrived(last2.at[half, 1, high], sems.at[half, 11], other)
        add(done.at[half], (middle.at[half, 0], last2.at[half, 0], last2.at[half, 1]), rows)


def scatter_buffers(rows, columns, dtype):
    cut = rows // 2 if dtype == BF16 else rows
    return [
        pltpu.VMEM((2, 2, RING, cut, columns), dtype),
        pltpu.VMEM((2, 2, RING, rows, columns), dtype),
        pltpu.VMEM((2, RING, rows, columns), dtype),
        pltpu.VMEM((2, 2, cut, columns), dtype),
        pltpu.VMEM((2, 2, rows, columns), dtype),
    ]


def ring_buffers(rows, columns):
    return [
        pltpu.VMEM((RING, rows, columns), BF16),
        pltpu.VMEM((RING, rows, columns), BF16),
        pltpu.VMEM((2, rows // 2, columns), BF16),
        pltpu.VMEM((2, rows, columns), BF16),
    ]


def dma_sems(*shape):
    return pltpu.SemaphoreType.DMA(shape)


def shape_of(*shape, dtype=BF16):
    return jax.ShapeDtypeStruct(shape, dtype)


def call(kernel, number, out_shape, in_specs, out_specs, scratch, args):
    return pl.pallas_call(
        kernel,
        out_shape=out_shape,
        in_specs=in_specs,
        out_specs=out_specs,
        scratch_shapes=scratch,
        compiler_params=pltpu.CompilerParams(
            collective_id=number, has_side_effects=True, vmem_limit_bytes=VMEM_LIMIT
        ),
    )(*args)


NN = (((1,), (0,)), ((), ()))
NT = (((1,), (1,)), ((), ()))
TN = (((0,), (0,)), ((), ()))


def dot(left, right, dims=NN):
    return lax.dot_general(left, right, dims, preferred_element_type=F32)


def in_tiles(width, tile, work):
    for n in range(width // tile):
        work(pl.ds(n * tile, tile))


def refs_of(refs, *counts):
    refs, out = list(refs), []
    for n in counts:
        out.append(refs[:n])
        del refs[:n]
    return out


def by_rows(count, work):
    def step(i, carry):
        work(pl.ds(pl.multiple_of(i * 16, 16), 16))
        return carry

    lax.fori_loop(0, count // 16, step, 0)


def load_weights(sender, source, targets):
    copies = []
    for k, target in targets:
        for yl in range(2):
            copies.append(sender.keep_first(source.at[:, :, k, yl], target.at[yl]))
    return copies


def rows_of(weight, window):
    if len(weight.shape) == 2:
        return weight[window, :]
    run = weight.shape[2] * weight.shape[3]
    first, count = window.start // run, window.size // run
    block = weight[first // RING, pl.ds(first % RING, count), :, :, :]
    return block.reshape(window.size, weight.shape[4])


def columns_of(weight, window):
    block = weight[:, :, :, :, window]
    return block.reshape(-1, window.size)


def mlp_kernel(
    own, gate_up, down, down_pair, mixed_in, cotangent_in, proj_in, gain_rows, hidden_out, d_mixed_out, d_proj_out,
    gains_out, grads_out, down_out, *refs
):
    (
        (x_all, d_all, w_gate, w_up, w_down, gate, up, act, partial, down_partial, tiles),
        (down_proj, mixed, cotangent, proj),
        ring,
        first_buffers,
        second_buffers,
        (sends, gather_sems, sum_sems, gather_sems2, sum_sems2, plane, plane2, tile_sems, plane3),
    ) = refs_of(refs, 11, 4, 4, 5, 5, 9)
    d_own = d_proj_out
    d_gate, d_up = gate, up
    place = Place()
    sender = Sender(sends)
    early = down.shape[4]
    w_rest = w_down.at[:, :, :, :, pl.ds(early, down_pair.shape[2])]
    load_pair = sender.keep_first(down_pair, w_rest.at[:, place.x, place.z])
    loads = load_weights(sender, gate_up, ((0, w_gate), (1, w_up)))
    load_down = sender.keep_first(down, w_down.at[:, :, :, :, pl.ds(0, early)])
    greet_all(place, ("x", "z", "y", "c"))
    gather = RingGather(place, sender, gather_sems, own, x_all)
    total = RingSum(place, sender, sum_sems, partial, *ring)
    gather.begin()
    load_pair.wait()
    rest = plane_gather(place, sender, plane3, w_rest, w_rest.shape[3] // 2)
    next(rest)
    pairs = ((mixed_in, mixed), (cotangent_in, cotangent), (proj_in, proj))
    later = [sender.keep_first(source, target) for source, target in pairs]
    for copy in loads:
        copy.wait()
    load_down.wait()
    tile = 512

    def where(dy):
        y = place.shift("y", dy)
        return y % 2, y // 2

    def at_chip(dy):
        at = where(dy)
        return (*at, slice(None)), (2 * rows, hidden_width)

    def at_neighbours(_):
        return (1 - place.yl, slice(None), slice(None)), (4 * rows, hidden_width)

    rows, hidden_width = own.shape[0], act.shape[-1]

    def forward_hidden(index, shape):
        count = shape[0]

        def hidden(columns):
            tokens = x_all[(*index, slice(None))].reshape(count, -1)
            g = dot(tokens, columns_of(w_gate, columns))
            u = dot(tokens, columns_of(w_up, columns))
            here = (*index, columns)
            held = act[here].shape
            gate[here], up[here] = g.astype(BF16).reshape(held), u.astype(BF16).reshape(held)
            act[here] = (g * jax.nn.sigmoid(g) * u).astype(BF16).reshape(held)

        in_tiles(hidden_width, tile, hidden)

    def forward_project(index, shape):
        def project(columns):
            left = act[(*index, slice(None))].reshape(shape)
            value = dot(left, rows_of(w_down, columns), NT).astype(BF16)
            here = (*index, columns)
            partial[here] = value.reshape(partial[here].shape)

        in_tiles(partial.shape[-1], tile, project)

    def in_turn(gather, total, work, before_far=lambda: None):
        gather.ready(0)
        work(*at_chip(0))
        total.offer(0)
        gather.relay()
        gather.ready(1)
        gather.ready(-1)
        work(*at_neighbours(0))
        total.offer(1)
        total.offer(-1)
        gather.relay_far()
        total.collect(1)
        total.collect(-1)
        gather.ready(2)
        before_far()
        work(*at_chip(2))
        total.offer(2)

    gather.ready(0)
    forward_hidden(*at_chip(0))
    for _ in range(4):
        next(rest)
    gather.relay()
    next(rest)
    gather.ready(1)
    gather.ready(-1)
    next(rest)
    forward_hidden(*at_neighbours(0))
    take_turns((rest,))
    gather.relay_far()
    forward_project(*at_neighbours(0))
    total.offer(1)
    total.offer(-1)
    forward_project(*at_chip(0))
    total.offer(0)
    total.collect(1)
    total.collect(-1)
    gather.ready(2)
    forward_hidden(*at_chip(2))
    forward_project(*at_chip(2))
    total.offer(2)
    total.collect(2)
    total.collect(0)
    total.relay()
    total.finish(down_proj)
    for copy in later:
        copy.wait()
    sender.settle(range(len(sender.open)))
    gains_out[...] = jnp.zeros_like(gains_out)

    def output_norm(rows):
        value, upstream, gain = down_proj[rows, :], cotangent[rows, :].astype(F32), gain_rows[3:4, :]
        scale = norm_scale(value)
        hidden_out[rows, :] = (mixed[rows, :] + value * scale * gain).astype(BF16)
        d_own[rows, :] = norm_back(upstream, value, scale, gain).astype(BF16)
        gains_out[1:2, :] += jnp.sum(upstream * value * scale, axis=0, keepdims=True)

    by_rows(down_proj.shape[0], output_norm)

    gather = RingGather(place, sender, gather_sems2, d_own, d_all)
    total = RingSum(place, sender, sum_sems2, partial, *ring)
    gather.begin()

    def backward(index, shape):
        count = shape[0]

        def hidden(columns):
            d_act = dot(d_all[(*index, slice(None))].reshape(count, -1), columns_of(w_down, columns))
            here = (*index, columns)
            held = gate[here].shape
            g, u = gate[here].astype(F32).reshape(d_act.shape), up[here].astype(F32).reshape(d_act.shape)
            s = jax.nn.sigmoid(g)
            d_gate[here] = (d_act * u * s * (1.0 + g * (1.0 - s))).astype(BF16).reshape(held)
            d_up[here] = (d_act * g * s).astype(BF16).reshape(held)

        in_tiles(hidden_width, tile, hidden)

        def back(columns):
            whole = (*index, slice(None))
            value = dot(d_gate[whole].reshape(shape), rows_of(w_gate, columns), NT)
            value = value + dot(d_up[whole].reshape(shape), rows_of(w_up, columns), NT)
            here = (*index, columns)
            partial[here] = value.astype(BF16).reshape(partial[here].shape)

        in_tiles(partial.shape[-1], tile, back)

    block = 4 * down_partial.shape[3]

    def all_rows(ref, columns=slice(None)):
        value = ref[:, :, :, columns]
        return value.reshape(-1, value.shape[-1])

    def sent(slot, k, i):
        return pltpu.make_async_copy(
            tiles.at[slot, k], grads_out.at[k, i // RING, i % RING], tile_sems.at[slot, k]
        )

    def weight_grads(begin, end):
        for i in range(begin, end):
            slot = i % 2
            for k, right in enumerate((d_gate, d_up)):
                if i >= 2:
                    sent(slot, k, i - 2).wait()
                value = dot(all_rows(x_all, pl.ds(i * block, block)), all_rows(right), TN)
                tiles[slot, k] = value.astype(BF16).reshape(tiles.shape[2:])
                sent(slot, k, i).start()

    half = act.shape[-1] // 2

    def down_sum(p, sems, buffers):
        columns = pl.ds(p * half, half)
        task = plane_scatter(
            place,
            sender,
            sems,
            down_partial.at[:, :, :, :, columns],
            down_out.at[:, :, columns],
            down_partial.shape[3] // 2,
            buffers,
        )
        next(task)
        return task

    tasks = []

    def down_grads():
        for i in range(2 * RING):
            value = dot(all_rows(d_all, pl.ds(i * block, block)), all_rows(act), TN).astype(BF16)
            down_partial[i // RING, i % RING] = value.reshape(down_partial.shape[2:])
        tasks.append(down_sum(0, plane, first_buffers))
        tasks.append(down_sum(1, plane2, second_buffers))

    in_turn(gather, total, backward, down_grads)
    task, task2 = tasks
    total.collect(2)
    next(task)
    total.collect(0)
    next(task2)
    weight_grads(0, 3)
    total.relay()
    weight_grads(3, 4)
    next(task)
    weight_grads(4, 6)
    next(task2)
    weight_grads(6, 7)
    next(task)
    weight_grads(7, 8)
    next(task2)
    total.finish(d_mixed_out)
    sender.settle(gather.begun)

    def attention_norm(rows):
        value, gain = proj[rows, :], gain_rows[2:3, :]
        d_mixed = cotangent[rows, :].astype(F32) + d_mixed_out[rows, :]
        d_mixed_out[rows, :] = d_mixed
        scale = norm_scale(value)
        d_proj_out[rows, :] = norm_back(d_mixed, value, scale, gain).astype(BF16)
        gains_out[0:1, :] += jnp.sum(d_mixed * value * scale, axis=0, keepdims=True)

    by_rows(down_proj.shape[0], attention_norm)
    take_turns((task, task2))
    for i in (6, 7):
        for k in range(2):
            sent(i % 2, k, i).wait()
    sender.finish()


def mlp(number, own, gate_up, down, down_pair, mixed, cotangent, proj, gain_rows):
    rows, width = own.shape
    piece, hidden = gate_up.shape[-2:]
    tokens = (2, 2, 2 * rows)
    weight = pltpu.VMEM((2, RING, RING, piece, hidden), BF16)
    wide, narrow = pltpu.VMEM((*tokens, width), BF16), pltpu.VMEM((*tokens, hidden), BF16)
    return call(
        mlp_kernel,
        number,
        (
            shape_of(rows, width),
            shape_of(rows, width, dtype=F32),
            shape_of(rows, width),
            shape_of(8, width, dtype=F32),
            shape_of(2, 2, RING, RING, piece, hidden),
            shape_of(2, piece, hidden),
        ),
        [ANYWHERE] * 7 + [IN_VMEM],
        (IN_VMEM,) * 4 + (ANYWHERE, IN_VMEM),
        [
            wide,
            wide,
            *[weight] * 3,
            *[narrow] * 3,
            wide,
            weight,
            pltpu.VMEM((2, 2, RING, piece, hidden), BF16),
            pltpu.VMEM((rows, width), F32),
            pltpu.VMEM((rows, width), F32),
            pltpu.VMEM((rows, width), BF16),
            pltpu.VMEM((rows, width), F32),
            *ring_buffers(rows, width),
            *scatter_buffers(piece, hidden // 2, BF16),
            *scatter_buffers(piece, hidden // 2, BF16),
            dma_sems(176),
            dma_sems(RING, 4),
            dma_sems(4, 2 * PIECES),
            dma_sems(RING, 4),
            dma_sems(4, 2 * PIECES),
            dma_sems(2, 12),
            dma_sems(2, 12),
            dma_sems(2, 2),
            dma_sems(2, RING, RING, 3),
        ],
        (own, gate_up, down, down_pair, mixed, cotangent, proj, gain_rows),
    )


def ring_product(place, total, values, weight, partial, others, before_near=lambda: None):
    def compute(dy):
        y = place.shift("y", dy)
        at = (y % 2, y // 2)

        def tile(columns):
            partial[(*at, slice(None), columns)] = dot(values[at], rows_of(weight, columns), NT).astype(BF16)

        in_tiles(partial.shape[-1], 512, tile)
        total.offer(dy)

    compute(2)
    before_near()
    compute(1)
    total.collect(2)
    compute(-1)
    total.collect(1)
    compute(0)
    total.collect(-1)
    total.collect(0)
    for task in others:
        next(task)
    total.relay()


def flat(weight):
    return weight.reshape(-1, weight.shape[-1])


def exact(left, right, dims):
    return lax.dot_general(
        left, right, dims, precision=lax.Precision.HIGHEST, preferred_element_type=F32
    )


def half_roll(values):
    return pltpu.roll(values, HEAD_DIM // 2, 1)


def near_devices(place):
    return [place.at(axis, step) for axis in ("x", "z") for step in (1, -1)]


class Octet:
    peers = [(dy, dc) for dy in (0, 1, 3, 2) for dc in (0, 1) if dy or dc]

    def __init__(self, place, sender, own, slots, sems):
        self.place, self.sender, self.own, self.slots, self.sems = place, sender, own, slots, sems

    @staticmethod
    def device(place, dy, dc):
        y = place.shift("y", dy)
        return {"yl": y % 2, "yh": y // 2, "c": (place.c + dc) % 2}

    def send(self):
        for dy, dc in self.peers:
            slot = ((RING - dy) % RING) * 2 + dc
            device = self.device(self.place, dy, dc)
            self.sender.push(self.own, self.slots.at[slot], self.sems.at[slot], device)

    def total(self):
        for dy, dc in self.peers:
            slot = dy * 2 + dc
            self.sender.arrived(self.slots.at[slot], self.sems.at[slot], self.device(self.place, dy, dc))
        value = self.own[...]
        for dy, dc in self.peers:
            value = value + self.slots[dy * 2 + dc]
        return value


def one_hot_rows(k):
    return (lax.broadcasted_iota(jnp.int32, (8, HEAD_DIM), 0) == k).astype(F32)


def masked(scores, starts, i):
    tile, count = scores.shape
    keys = lax.broadcasted_iota(jnp.int32, (tile, count), 1)
    queries = lax.broadcasted_iota(jnp.int32, (tile, count), 0) + i * tile
    return jnp.where((keys >= starts) & (keys <= queries), scores, -1e30)


def softmax(scores):
    exponent = jnp.exp(scores - jnp.max(scores, axis=-1, keepdims=True))
    return exponent / jnp.sum(exponent, axis=-1, keepdims=True)


def attention_forward_kernel(
    own, attn, down, gain, cosine_in, sine_in, starts_in, proj_out, mixed_out, low_out, gain_rows, head_out, x_out,
    weight_out, raw_out, rot_out, value_out, scale_out, attended_out, down_out, pair_out, *refs
):
    (
        (x_all, weight, raw, rot, values, scales, attended, partial, sums, slots, down_all, gain_all),
        (cosine, sine, starts, hidden),
        ring,
        (sends, gather_sems, sum_sems, octet_sems, attn_plane, gain_plane, plane, swap),
    ) = refs_of(refs, 12, 4, 4, 8)
    place = Place()
    sender = Sender(sends)
    _, heads, _, block_rows, _ = raw.shape
    inner = heads * HEAD_DIM
    tile = block_rows // 2
    partner = {"yl": 1 - place.yl}
    me, you = place.yl, 1 - place.yl
    half = down_all.shape[4]
    early, later_half = pl.ds(0, half), pl.ds(half, half)
    shards = ((attn, weight), (gain, gain_all), (down.at[:, :, early], down_all))
    mine = [
        sender.keep_first(source if k == 1 else source.at[me], target.at[me, place.x, place.z])
        for k, (source, target) in enumerate(shards)
    ]
    greet(near_devices(place) + [Octet.device(place, *peer) for peer in Octet.peers])
    for k, (source, target) in enumerate(shards[:2]):
        sender.push(
            source if k == 1 else source.at[you], target.at[me, place.x, place.z], swap.at[k], partner
        )
    gather = RingGather(place, sender, gather_sems, own, x_all)
    gather.begin()
    for copy in mine:
        copy.wait()
    for k, (_, target) in enumerate(shards[:2]):
        sender.arrived(target.at[you, place.x, place.z], swap.at[k], partner)
    attn_task = plane_gather(place, sender, attn_plane, weight, weight.shape[3] // 2)
    gain_task = plane_gather(place, sender, gain_plane, gain_all, gain_all.shape[3])
    next(attn_task)
    next(gain_task)
    pairs = ((cosine_in, cosine), (sine_in, sine), (starts_in, starts), (own, hidden))
    later = [sender.keep_first(source, target) for source, target in pairs]
    sender.push(down.at[you, :, early], down_all.at[me, place.x, place.z], swap.at[2], partner)
    sender.push(down.at[you, :, later_half], pair_out.at[me], swap.at[3], partner)
    sender.keep(down.at[me, :, later_half], pair_out.at[me])

    def gather_all():
        gather.relay()
        yield
        gather.relay_far()
        yield
        for dy in (0, 1, -1, 2):
            gather.ready(dy)

    take_turns((gain_task, attn_task, gather_all()))
    sender.keep(x_all, x_out)
    sender.keep(weight, weight_out)
    for yl in range(2):
        for x in range(RING):
            for h in range(2):
                lanes = pl.ds(((yl * RING + x) * 2 + h) * HEAD_DIM, HEAD_DIM)
                gain_rows[:, lanes] = gain_all[yl, x, 2 * h] + gain_all[yl, x, 2 * h + 1]
    first_column = (place.yh * 2 + place.c) * (2 * inner) + place.yl * inner

    def head_gain(k, h):
        start = pl.multiple_of(first_column + h * HEAD_DIM, HEAD_DIM)
        return gain_rows[k : k + 1, pl.ds(start, HEAD_DIM)]

    for h in range(heads):
        start = pl.multiple_of(first_column + h * HEAD_DIM, HEAD_DIM)
        head_out[:, pl.ds(h * HEAD_DIM, HEAD_DIM)] = gain_rows[:, pl.ds(start, HEAD_DIM)]
    sender.arrived(down_all.at[you, place.x, place.z], swap.at[2], partner)
    down_task = plane_gather(place, sender, plane, down_all, down_all.shape[3] // 2)
    next(down_task)
    total = RingSum(place, sender, sum_sems, partial, *ring)
    ones = [one_hot_rows(k) for k in range(2)]

    def project(t, carry):
        a, b = t // 2, t % 2
        window = pl.ds(pl.multiple_of(b * tile, tile), tile)
        value = dot(x_all[a, b], columns_of(weight, pl.ds(0, 2 * inner)))
        row_sums = jnp.zeros((8, tile), F32)
        for k in range(2):
            for h in range(heads):
                column = k * inner + h * HEAD_DIM
                part = value[:, column : column + HEAD_DIM]
                raw[k, h, a, window, :] = part
                row_sums = row_sums + exact(ones[k], part * part, NT)
        sums[:, pl.ds(pl.multiple_of(t * tile, tile), tile)] = row_sums
        return carry

    def project_value(t, carry):
        a, b = t // 2, t % 2
        window = pl.ds(pl.multiple_of(b * tile, tile), tile)
        value = dot(x_all[a, b], columns_of(weight, pl.ds(2 * inner, inner))).astype(BF16)
        for h in range(heads):
            values[h, a, window, :] = value[:, h * HEAD_DIM : (h + 1) * HEAD_DIM]
        return carry

    lax.fori_loop(0, 4, project, 0)
    octet = Octet(place, sender, sums, slots, octet_sems)
    octet.send()
    sender.keep(raw, raw_out)
    lax.fori_loop(0, 4, project_value, 0)
    sender.keep(values, value_out)
    next(down_task)
    for copy in later:
        copy.wait()
    row_scales = lax.rsqrt(octet.total() / x_all.shape[3] + NORM_EPS)
    for b in range(2):
        for k in range(2):
            scale = exact(row_scales[:, b * block_rows : (b + 1) * block_rows], ones[k], TN)
            scales[k, b] = scale
            for h in range(heads):
                value = raw[k, h, b] * scale * head_gain(k, h)
                rot[k, h, b] = (value * cosine[b] + half_roll(value) * sine[b]).astype(BF16)
    sender.keep(scales, scale_out)
    sender.keep(rot, rot_out)
    next(down_task)

    def attention(b):
        for h in range(heads):
            key, value = rot[1, h, b], values[h, b]
            for i in range(2):
                window, count = pl.ds(i * tile, tile), (i + 1) * tile
                scores = dot(rot[0, h, b, window, :], key[:count], NT) * HEAD_DIM ** (-0.5)
                probs = softmax(masked(scores, starts[b, window, 0:1], i)).astype(BF16)
                attended[b, i, :, pl.ds(h * HEAD_DIM, HEAD_DIM)] = dot(probs, value[:count]).astype(BF16)

    attention(place.yl)
    out_weight = weight.at[:, :, :, :, pl.ds(3 * inner, inner)]
    ring_product(place, total, attended, out_weight, partial, (), lambda: attention(1 - place.yl))
    sender.keep(attended, attended_out)
    take_turns((down_task,))
    sender.keep(down_all, down_out)
    total.finish(proj_out)

    def mix(rows):
        value = proj_out[rows, :]
        mixed = hidden[rows, :].astype(F32) + value * norm_scale(value) * gain_rows[2:3, :]
        mixed_out[rows, :] = mixed
        low_out[rows, :] = mixed.astype(BF16)

    by_rows(proj_out.shape[0], mix)
    sender.arrived(pair_out.at[you], swap.at[3], partner)
    sender.finish()


def attention_forward(number, own, attn, down, gain, cosine, sine, starts):
    rows, width = own.shape
    inner = attn.shape[2] // 4
    heads = inner // HEAD_DIM
    tokens = (2, 2, 2 * rows)
    raw = (2, heads, 2, 4 * rows, HEAD_DIM)
    values, scales, attended = raw[1:], (2, 2, 4 * rows, HEAD_DIM), (*tokens, inner)
    weight = (2, RING, RING, *attn.shape[1:])
    piece = down.shape[1], down.shape[2] // 2
    down_all = (2, RING, RING, *piece)
    return call(
        attention_forward_kernel,
        number,
        (
            shape_of(rows, width, dtype=F32),
            shape_of(rows, width, dtype=F32),
            shape_of(rows, width),
            shape_of(8, width, dtype=F32),
            shape_of(8, inner, dtype=F32),
            shape_of(*tokens, width),
            shape_of(*weight),
            shape_of(*raw, dtype=F32),
            shape_of(*raw),
            shape_of(*values),
            shape_of(*scales, dtype=F32),
            shape_of(*attended),
            shape_of(*down_all),
            shape_of(2, *piece),
        ),
        [ANYWHERE] * 7,
        (IN_VMEM,) * 5 + (ANYWHERE,) * 9,
        [
            pltpu.VMEM((*tokens, width), BF16),
            pltpu.VMEM(weight, BF16),
            pltpu.VMEM(raw, F32),
            pltpu.VMEM(raw, BF16),
            pltpu.VMEM(values, BF16),
            pltpu.VMEM(scales, F32),
            pltpu.VMEM(attended, BF16),
            pltpu.VMEM((*tokens, width), BF16),
            pltpu.VMEM((8, 8 * rows), F32),
            pltpu.VMEM((8, 8, 8 * rows), F32),
            pltpu.VMEM(down_all, BF16),
            pltpu.VMEM((2, RING, RING, *gain.shape), F32),
            *[pltpu.VMEM(other.shape, other.dtype) for other in (cosine, sine, starts, own)],
            *ring_buffers(rows, width),
            dma_sems(208),
            dma_sems(RING, 4),
            dma_sems(4, 2 * PIECES),
            dma_sems(8),
            dma_sems(2, RING, RING, 3),
            dma_sems(2, RING, RING, 3),
            dma_sems(2, RING, RING, 3),
            dma_sems(4),
        ],
        (own, attn, down, gain, cosine, sine, starts),
    )


def attention_backward_kernel(
    own, weight, inputs, d_mixed_in, mlp_in, down, attended_in, raw_in, rot_in, values_in, scales_in,
    cosines_in, sines_in, starts_in, head_gains, token_gains, out, attn_out, gain_out, mlp_out, *refs
):
    (
        (shared, own_weight, attn_partial, gate_partial, up_partial, d_att, back, d_qkv, sums, slots, d_mixed),
        staged,
        (gain_partial, gain_rows, gain_slots, attn_done, gain_done, mlp_done),
        ring,
        buffers,
        late_buffers,
        gate_buffers,
        up_buffers,
        gain_buffers,
        (sends, gather_sems, sum_sems, octet_sems, gain_sems, swap, plane, late_plane, gain_plane, gate_plane),
        (up_plane,),
    ) = refs_of(refs, 11, 8, 6, 4, 5, 5, 5, 5, 5, 10, 1)
    attended, raw_all, rot, values, scales, cosines, sines, starts = staged
    d_all = x_all = partial = shared
    place = Place()
    sender = Sender(sends)
    _, heads, _, block_rows, _ = rot.shape
    width = d_qkv.shape[-1]
    inner = heads * HEAD_DIM
    rows = attn_partial.shape[3]
    block = RING * rows
    mlp_loads = [sender.keep_first(mlp_in.at[0], gate_partial), sender.keep_first(mlp_in.at[1], up_partial)]
    partner = {"yl": 1 - place.yl}
    me, you = place.yl, 1 - place.yl
    greet(near_devices(place) + [Octet.device(place, *peer) for peer in Octet.peers])
    gather = RingGather(place, sender, gather_sems, own, d_all)
    total = RingSum(place, sender, sum_sems, partial, *ring)
    gather.begin()
    sender.push(down.at[you], mlp_out.at[2, me], swap.at[3], partner)
    sender.keep(down.at[me], mlp_out.at[2, me])
    mlp = []
    for k, (sems, bufs, summand) in enumerate(
        ((gate_plane, gate_buffers, gate_partial), (up_plane, up_buffers, up_partial))
    ):
        task = plane_scatter(
            place, sender, sems, summand, mlp_done.at[k], rows // 2, bufs, mlp_in.at[k]
        )
        next(task)
        mlp.append(task)
    gate_task, up_task = mlp
    load = sender.keep_first(weight, own_weight)
    sources = (attended_in, raw_in, rot_in, values_in, scales_in, cosines_in, sines_in, starts_in)
    later = [sender.keep_first(source, target) for source, target in zip(sources, staged)]
    sender.keep(d_mixed_in, d_mixed)
    mixed_number = len(sender.open) - 1
    load.wait()
    gain_partial[...] = jnp.zeros_like(gain_partial)
    gain_rows[...] = jnp.zeros_like(gain_rows)
    for k in range(2 * RING):
        for z in range(RING):
            gain_partial[k // RING, k % RING, z, 2:4, :] = token_gains[0:2, k * block : (k + 1) * block]

    def compute(dy):
        gather.ready(dy)
        y = place.shift("y", dy)
        at = (y % 2, y // 2)
        d_att[at] = dot(d_all[at], own_weight[:, pl.ds(width, inner)]).astype(BF16)

    tile = block_rows // 2
    score_factor = HEAD_DIM ** (-0.5)
    ones = [one_hot_rows(k) for k in range(2)]

    def attention(b):
        row_sums = jnp.zeros((8, block_rows), F32)
        cosine, sine = cosines[b], sines[b]
        for h in range(heads):
            lanes = pl.ds(h * HEAD_DIM, HEAD_DIM)
            key, value = rot[1, h, b], values[h, b]
            d_query, d_key, d_value = [], [None, None], [None, None]
            for i in range(2):
                window = pl.ds(i * tile, tile)
                query, upstream = rot[0, h, b, window, :], d_att[b, i, :, lanes]
                count = (i + 1) * tile
                scores = dot(query, key[:count], NT) * score_factor
                probs = softmax(masked(scores, starts[b, window, 0:1], i))
                d_probs = dot(upstream, value[:count], NT)
                row_dot = jnp.sum(probs * d_probs, axis=-1, keepdims=True)
                d_scores = (probs * (d_probs - row_dot) * score_factor).astype(BF16)
                probs = probs.astype(BF16)
                d_query.append(dot(d_scores, key[:count]))
                for j in range(i + 1):
                    part = slice(j * tile, (j + 1) * tile)
                    for sums_of, left, right in ((d_key, d_scores, query), (d_value, probs, upstream)):
                        term = dot(left[:, part], right, TN)
                        sums_of[j] = term if sums_of[j] is None else sums_of[j] + term
            for i in range(2):
                d_qkv[b, i, :, pl.ds(2 * inner + h * HEAD_DIM, HEAD_DIM)] = d_value[i].astype(BF16)
            for k, parts in enumerate((d_query, d_key)):
                turned = jnp.concatenate(parts, axis=0)
                turned = turned * cosine - half_roll(turned) * sine
                raw = raw_all[k, h, b]
                gain_rows[k : k + 1, lanes] += jnp.sum(turned * raw * scales[k, b], axis=0, keepdims=True)
                turned = turned * head_gains[k : k + 1, lanes]
                back[k, h, b] = turned
                row_sums = row_sums + exact(ones[k], turned * raw, NT)
        sums[:, pl.ds(pl.multiple_of(b * block_rows, block_rows), block_rows)] = row_sums

    compute(0)
    gather.relay()
    compute(1)
    compute(-1)
    for copy in mlp_loads + later:
        copy.wait()
    next(gate_task)
    attention(1 - place.yl)
    gather.relay_far()
    compute(2)
    next(up_task)
    attention(place.yl)
    octet = Octet(place, sender, sums, slots, octet_sems)
    octet.send()
    first = (place.yh * 2 + place.c) * 2 + place.yl
    for z in range(RING):
        gain_partial[first // RING, first % RING, z, 0:2, :] = gain_rows[0:2, :]
    gains = plane_scatter(place, sender, gain_plane, gain_partial, gain_done, gain_done.shape[1], gain_buffers)
    next(gains)

    def flat_tokens(ref, columns=slice(None)):
        value = ref[:, :, :, columns]
        return value.reshape(-1, value.shape[-1])

    def weight_grads(left_ref, right, start):
        size = right.shape[1]
        for i in range(2 * RING):
            left = flat_tokens(left_ref, pl.ds(i * block, block))
            value = dot(left, right, TN).astype(BF16)
            attn_partial[i // RING, i % RING, :, :, pl.ds(start, size)] = value.reshape(RING, rows, size)

    weight_grads(d_all, flat_tokens(attended), width)
    sender.settle(gather.forwarded)
    load = sender.keep_first(inputs, x_all)
    next(gate_task)
    load.wait()

    def attn_scatter(columns, sems, bufs):
        task = plane_scatter(
            place,
            sender,
            sems,
            attn_partial.at[:, :, :, :, columns],
            attn_done.at[:, :, columns],
            rows // 2,
            bufs,
        )
        next(task)
        return task

    weight_grads(x_all, flat_tokens(d_qkv, pl.ds(2 * inner, inner)), 2 * inner)
    early = attn_scatter(pl.ds(2 * inner, 2 * inner), plane, buffers)
    row_sums = octet.total()
    for b in range(2):
        for k in range(2):
            column = exact(row_sums[:, b * block_rows : (b + 1) * block_rows], ones[k], TN)
            for h in range(heads):
                scale = scales[k, b]
                value = scale * back[k, h, b] - raw_all[k, h, b] * (scale * scale * scale * column / own.shape[1])
                value = value.astype(BF16)
                for i in range(2):
                    d_qkv[b, i, :, pl.ds(k * inner + h * HEAD_DIM, HEAD_DIM)] = value[
                        i * tile : (i + 1) * tile
                    ]
    weight_grads(x_all, flat_tokens(d_qkv, pl.ds(0, 2 * inner)), 0)
    late = attn_scatter(pl.ds(0, 2 * inner), late_plane, late_buffers)
    next(gate_task)
    next(up_task)
    next(early)
    ring_product(
        place, total, d_qkv, own_weight.at[:, pl.ds(0, width)], partial, (late, up_task, gains)
    )
    take_turns((gate_task, up_task))
    for k in range(2):
        sender.push(mlp_done.at[k, you], mlp_out.at[k, me], swap.at[1 + k], partner)
        sender.keep(mlp_done.at[k, me], mlp_out.at[k, me])
    take_turns((early, gains, late))
    sender.push(attn_done.at[you], attn_out.at[me], swap.at[0], partner)
    sender.keep(attn_done.at[me], attn_out.at[me])
    everyone = Octet(place, sender, gain_done, gain_slots, gain_sems)
    everyone.send()
    sender.settle([mixed_number])
    total.finish(out, d_mixed)
    gain_out[...] = everyone.total()
    sender.arrived(attn_out.at[you], swap.at[0], partner)
    for k in range(3):
        sender.arrived(mlp_out.at[k, you], swap.at[1 + k], partner)
    sender.finish()


def attention_backward(number, own, weight, inputs, d_mixed, mlp_partial, down, attended, *others):
    rows, width = own.shape
    tokens = (2, 2, 2 * rows)
    inner = attended.shape[3]
    heads = inner // HEAD_DIM
    shard = width // 32, weight.shape[1]
    gain_tile = (8, 4 * shard[0])
    return call(
        attention_backward_kernel,
        number,
        (
            shape_of(rows, width, dtype=F32),
            shape_of(2, *shard),
            shape_of(2, *gain_tile, dtype=F32),
            shape_of(3, 2, *shard),
        ),
        [ANYWHERE] * 14 + [IN_VMEM] * 2,
        (IN_VMEM,) * 4,
        [
            pltpu.VMEM((*tokens, width), BF16),
            pltpu.VMEM(weight.shape, BF16),
            pltpu.VMEM((2, RING, RING, *shard), BF16),
            pltpu.VMEM(mlp_partial.shape[1:], BF16),
            pltpu.VMEM(mlp_partial.shape[1:], BF16),
            pltpu.VMEM((*tokens, inner), BF16),
            pltpu.VMEM((2, heads, 2, 4 * rows, HEAD_DIM), F32),
            pltpu.VMEM((*tokens, 3 * inner), BF16),
            pltpu.VMEM((8, 8 * rows), F32),
            pltpu.VMEM((8, 8, 8 * rows), F32),
            pltpu.VMEM((rows, width), F32),
            *[pltpu.VMEM(other.shape, other.dtype) for other in (attended, *others[:7])],
            pltpu.VMEM((2, RING, RING, *gain_tile), F32),
            pltpu.VMEM((8, inner), F32),
            pltpu.VMEM((8, 2, *gain_tile), F32),
            pltpu.VMEM((2, *shard), BF16),
            pltpu.VMEM((2, *gain_tile), F32),
            pltpu.VMEM((2, 2, *shard), BF16),
            *ring_buffers(rows, width),
            *scatter_buffers(shard[0], shard[1] // 2, BF16),
            *scatter_buffers(shard[0], shard[1] // 2, BF16),
            *scatter_buffers(*shard, BF16),
            *scatter_buffers(*shard, BF16),
            *scatter_buffers(*gain_tile, F32),
            dma_sems(224),
            dma_sems(RING, 4),
            dma_sems(4, 2 * PIECES),
            dma_sems(8),
            dma_sems(8),
            dma_sems(5),
            dma_sems(2, 12),
            dma_sems(2, 12),
            dma_sems(2, 12),
            dma_sems(2, 12),
            dma_sems(2, 12),
        ],
        (own, weight, inputs, d_mixed, mlp_partial, down, attended, *others),
    )


def norm_scale(values):
    return lax.rsqrt(jnp.mean(values * values, axis=-1, keepdims=True) + NORM_EPS)


def norm_back(upstream, values, scales, gain_row):
    scaled_grad = upstream * gain_row
    return scales * scaled_grad - values * scales**3 * jnp.mean(
        scaled_grad * values, axis=-1, keepdims=True
    )


def doc_layout(lengths, group_size):
    positions = jnp.arange(group_size, dtype=jnp.int32)
    doc_ends = jnp.cumsum(lengths)
    passed = (positions[:, None] >= doc_ends[None, :]).astype(jnp.int32)
    segment = jnp.sum(passed, axis=-1)
    begins = jnp.sum(passed * lengths[None, :], axis=-1)
    return (segment, positions - begins)


def rope_tables(offsets):
    frequency = ROPE_BASE ** (-jnp.arange(0, HEAD_DIM, 2).astype(jnp.float32) / HEAD_DIM)
    angles = offsets.astype(jnp.float32)[:, None] * frequency[None, :]
    cosine, sine = jnp.cos(angles), jnp.sin(angles)
    return (
        jnp.concatenate([cosine, cosine], axis=-1),
        jnp.concatenate([sine, sine], axis=-1),
    )


def half_turn(values):
    middle = values.shape[-1] // 2
    return jnp.concatenate([-values[..., middle:], values[..., :middle]], axis=-1)


def rotate(values, cosine_table, sine_table):
    return values * cosine_table + half_turn(values) * sine_table


def unrotate(values, cosine_table, sine_table):
    return values * cosine_table - half_turn(values) * sine_table


def product(left, right):
    return jnp.dot(left, right, preferred_element_type=F32)


def row_product(left, right):
    return lax.dot_general(left, right, (((1,), (1,)), ((), ())), preferred_element_type=F32)


def col_product(left, right):
    return lax.dot_general(left, right, (((0,), (0,)), ((), ())), preferred_element_type=F32)


def adam_update(weights_old, first_old, second_old, gradient, rate, decay):
    first_new = BETA_ONE * first_old + (1.0 - BETA_ONE) * gradient
    second_new = BETA_TWO * second_old + (1.0 - BETA_TWO) * gradient * gradient
    ratio = (
        first_new
        / (1.0 - BETA_ONE**STEP)
        / (jnp.sqrt(second_new / (1.0 - BETA_TWO**STEP)) + ADAM_EPS)
    )
    return (first_new, second_new, weights_old - rate * (ratio + decay * weights_old))


def mlp_adam_kernel(weights, first, second, sums, grad_out, first_out, second_out, new_out):
    half = sums.shape[3]
    for h in range(2):
        part = slice(None), slice(None), slice(h * half, (h + 1) * half)
        gradient = sums[:, h].astype(F32)
        grad_out[part] = gradient
        first_out[part], second_out[part], new_out[part] = adam_update(
            weights[part], first[part], second[part], gradient, WEIGHT_RATE, WEIGHT_DECAY
        )


def mlp_adam(weights, first, second, sums):
    count, rows, columns = weights.shape
    state = pl.BlockSpec((1, rows, columns), lambda m: (m, 0, 0))
    return pl.pallas_call(
        mlp_adam_kernel,
        out_shape=(shape_of(*weights.shape, dtype=F32),) * 4,
        grid=(count,),
        in_specs=[state] * 3 + [pl.BlockSpec((1, *sums.shape[1:]), lambda m: (m, 0, 0, 0))],
        out_specs=(state,) * 4,
        compiler_params=pltpu.CompilerParams(vmem_limit_bytes=VMEM_LIMIT),
    )(weights, first, second, sums)


def attn_adam_kernel(weights, first, second, sums, grad_out, first_out, second_out, new_out):
    inner = weights.shape[2]
    for m in range(weights.shape[0]):
        gradient = sums[0, :, m * inner : (m + 1) * inner].astype(F32)
        grad_out[m] = gradient
        first_out[m], second_out[m], new_out[m] = adam_update(
            weights[m], first[m], second[m], gradient, WEIGHT_RATE, WEIGHT_DECAY
        )


def attn_adam(weights, first, second, sums):
    count, rows, columns = weights.shape
    state = pl.BlockSpec((count, rows, columns // 2), lambda h: (0, 0, h))
    return pl.pallas_call(
        attn_adam_kernel,
        out_shape=(shape_of(*weights.shape, dtype=F32),) * 4,
        grid=(2,),
        in_specs=[state] * 3 + [pl.BlockSpec((1, *sums.shape[1:]), lambda h: (h, 0, 0))],
        out_specs=(state,) * 4,
        compiler_params=pltpu.CompilerParams(vmem_limit_bytes=VMEM_LIMIT),
    )(weights, first, second, sums)


def body(
    hidden_in,
    cotangent,
    doc_lengths,
    attn_weights,
    attn_first,
    attn_second,
    mlp_weights,
    mlp_first,
    mlp_second,
    gains,
    gain_first,
    gain_second,
):
    row_count, model_width = hidden_in.shape
    shard_rows = attn_weights.shape[1]
    heads_width = attn_weights.shape[2] // 2
    hidden_width = mlp_weights.shape[2] // 2
    token_count = 8 * row_count
    block_rows = token_count // 2
    head_count = heads_width // HEAD_DIM
    score_factor = HEAD_DIM ** (-0.5)
    yl, yh, core = (lax.axis_index(a) for a in ("yl", "yh", "c"))

    attn_halves = (
        attn_weights.astype(BF16)
        .reshape(4, shard_rows, 2, heads_width)
        .transpose(2, 1, 0, 3)
        .reshape(2, shard_rows, 4 * heads_width)
    )
    left, right = mlp_weights[:2, :, :hidden_width], mlp_weights[:2, :, hidden_width:]
    mine = jnp.where(yl == 0, left, right).astype(BF16)
    yours = jnp.where(yl == 0, right, left).astype(BF16)
    arrived = lax.ppermute(yours, "yl", [(0, 1), (1, 0)])
    down_halves = mlp_weights[2].astype(BF16).reshape(shard_rows, 2, hidden_width).transpose(1, 0, 2)
    gain_low = lax.reduce_precision(gains, 8, 7)
    odd = lax.axis_index("z") % 2
    gain_tile = jnp.concatenate([jnp.where(odd == 0, gain_low, 0.0), jnp.where(odd == 1, gain_low, 0.0)], axis=1)
    gain_tile = jnp.pad(gain_tile, ((0, 4), (0, 0)))
    theirs = lax.ppermute(doc_lengths, "yl", [(0, 1), (1, 0)])
    lengths = jnp.where(yl == 0, jnp.stack([doc_lengths[0], theirs[0]]), jnp.stack([theirs[0], doc_lengths[0]]))
    _, offsets = jax.vmap(lambda one: doc_layout(one, block_rows))(lengths)
    cosine_table, sine_table = rope_tables(offsets.reshape(-1))
    sine_table = sine_table * jnp.where(jnp.arange(HEAD_DIM) < HEAD_DIM // 2, -1.0, 1.0)
    cosine_table = cosine_table.reshape(2, block_rows, HEAD_DIM)
    sine_table = sine_table.reshape(2, block_rows, HEAD_DIM)
    starts = jnp.broadcast_to((jnp.arange(block_rows) - offsets)[:, :, None], (2, block_rows, HEAD_DIM))

    arrived, cosine_table, sine_table, starts, attn_halves, gain_tile, down_halves = lax.optimization_barrier(
        (arrived, cosine_table, sine_table, starts, attn_halves, gain_tile, down_halves)
    )
    pair = jnp.stack(
        [jnp.where(yl == 0, mine, arrived), jnp.where(yl == 0, arrived, mine)], axis=1
    )
    gate_up = lax.all_gather(pair.reshape(-1, hidden_width), ("x", "z"), tiled=True)
    gate_up = gate_up.reshape(RING, RING, 2, 2, shard_rows, hidden_width)

    (
        attn_proj, mixed, mixed_low, gain_full, head_gains, every_input, attn_all, raw, rotated, values,
        head_scales, attended, down_half, down_pair,
    ) = attention_forward(
        1, hidden_in, attn_halves, down_halves, gain_tile, cosine_table, sine_table, starts
    )
    attn_all = flat(attn_all)
    hidden_out, d_mixed, d_proj, token_gains, mlp_partial, down_sum = mlp(
        2, mixed_low, gate_up, down_half, down_pair, mixed, cotangent, attn_proj, gain_full
    )
    input_grad, attn_sum, gain_sum, mlp_sum = attention_backward(
        3,
        d_proj,
        attn_all,
        every_input,
        d_mixed,
        mlp_partial,
        down_sum,
        attended,
        raw,
        rotated,
        values,
        head_scales,
        cosine_table,
        sine_table,
        starts,
        head_gains,
        token_gains,
    )

    gain_sum = lax.dynamic_index_in_dim(gain_sum, yl, 0, keepdims=False)[:4]
    gain_grad = lax.dynamic_slice_in_dim(gain_sum, lax.axis_index("z") * shard_rows, shard_rows, axis=1)
    attn_grad, attn_first_new, attn_second_new, attn_new = attn_adam(
        attn_weights, attn_first, attn_second, attn_sum
    )
    mlp_grad, mlp_first_new, mlp_second_new, mlp_new = mlp_adam(
        mlp_weights, mlp_first, mlp_second, mlp_sum
    )
    gain_first_new, gain_second_new, gain_new = adam_update(
        gains, gain_first, gain_second, gain_grad, GAIN_RATE, 0.0
    )
    return (
        hidden_out,
        input_grad,
        attn_grad,
        attn_first_new,
        attn_second_new,
        attn_new,
        mlp_grad,
        mlp_first_new,
        mlp_second_new,
        mlp_new,
        gain_grad,
        gain_first_new,
        gain_second_new,
        gain_new,
    )


def solution(mesh):
    split = Mesh(mesh.devices.reshape(2, 4, 4, 2, 2), EVERY)
    tokens, shards, rows = P(EVERY, None), P(None, DP, TENSOR), P(None, DP)
    return jax.shard_map(
        body,
        mesh=split,
        in_specs=(tokens, tokens, P(DP, None), *[shards] * 6, *[rows] * 3),
        out_specs=(tokens, tokens, *[shards] * 8, *[rows] * 4),
        check_vma=False,
    )
```

```python
import functools

import jax
import jax.numpy as jnp
from jax import lax
from jax.experimental import pallas as pl
from jax.experimental.pallas import tpu as pltpu
from jax.sharding import Mesh
from jax.sharding import PartitionSpec as P

HEAD_DIM = 128
STEP = 10
DP = ("yl", "x", "z")
TENSOR = ("yh", "c")
EVERY = ("yl", "x", "z", "yh", "c")
RING = 4
MESH = pl.DeviceIdType.MESH

NORM_EPS = 1e-06
ROPE_BASE = 500000.0
BETA_ONE = 0.9
BETA_TWO = 0.95
ADAM_EPS = 1e-08
WEIGHT_RATE = 0.03
GAIN_RATE = 1.0
WEIGHT_DECAY = 0.1

BF16 = jnp.bfloat16
F32 = jnp.float32
IN_VMEM = pl.BlockSpec(memory_space=pltpu.VMEM)
ANYWHERE = pl.BlockSpec(memory_space=pl.ANY)
VMEM_LIMIT = 60 * 1024 * 1024


class Place:
    def __init__(self):
        self.x, self.z, self.c = (lax.axis_index(a) for a in ("x", "z", "c"))
        self.yl, self.yh = (lax.axis_index(a) for a in ("yl", "yh"))
        self.y = self.yh * 2 + self.yl

    def at(self, axis, step):
        if axis == "y":
            there = (self.y + step + RING) % RING
            return {"yl": there % 2, "yh": there // 2}
        if axis == "c":
            return {"c": 1 - self.c}
        return {axis: (getattr(self, axis) + step + RING) % RING}

    def shift(self, axis, step):
        return (getattr(self, axis) + step + RING) % RING


def greet(devices):
    barrier = pltpu.get_barrier_semaphore()
    for device in devices:
        pl.semaphore_signal(barrier, inc=1, device_id=device, device_id_type=MESH)
    pl.semaphore_wait(barrier, len(devices))


def greet_all(place, axes):
    devices = []
    for axis in axes:
        devices += [place.at(axis, 1)] if axis == "c" else [place.at(axis, 1), place.at(axis, -1)]
    greet(devices)


class Sender:
    def __init__(self, sems):
        self.sems, self.open = sems, []

    def push(self, src, dst, recv_sem, device):
        copy = pltpu.make_async_remote_copy(
            src_ref=src,
            dst_ref=dst,
            send_sem=self.sems.at[len(self.open)],
            recv_sem=recv_sem,
            device_id=device,
            device_id_type=MESH,
        )
        copy.start()
        self.open.append(copy.wait_send)
        return len(self.open) - 1

    def settle(self, numbers):
        for number in numbers:
            self.open[number]()
            self.open[number] = lambda: None

    def keep(self, src, dst):
        copy = pltpu.make_async_copy(src, dst, self.sems.at[len(self.open)])
        copy.start()
        self.open.append(copy.wait)

    def keep_first(self, src, dst):
        copy = pltpu.make_async_copy(src, dst, self.sems.at[len(self.open)])
        copy.start()
        self.open.append(lambda: None)
        return copy

    def arrived(self, dst, recv_sem, device):
        pltpu.make_async_remote_copy(
            src_ref=dst,
            dst_ref=dst,
            send_sem=self.sems.at[0],
            recv_sem=recv_sem,
            device_id=device,
            device_id_type=MESH,
        ).wait_recv()

    def finish(self):
        for wait in self.open:
            wait()


def take_turns(tasks):
    tasks = list(tasks)
    while tasks:
        for task in list(tasks):
            if next(task, "done") == "done":
                tasks.remove(task)


WHOLE, LOW, HIGH = 0, 1, 2
PIECES = 4


def part_of(ref, part, cut):
    rows = ref.shape[-2]
    if part == WHOLE:
        return ref
    return ref.at[pl.ds(0, cut)] if part == LOW else ref.at[pl.ds(cut, rows - cut)]


def plane_gather(place, sender, sems, out, cut):
    rows = out.shape[-2]
    axes = (("x", "z"), ("z", "x"))

    def piece(half, dp, dq):
        p, q = (place.shift(a, d) for a, d in zip(axes[half], (dp, dq)))
        return out.at[half, p, q] if half == 0 else out.at[half, q, p]

    def parts(part):
        if part == WHOLE:
            return True
        return cut > 0 if part == LOW else cut < rows

    def send(half, dp, dq, part, along, step):
        if parts(part):
            ref = part_of(piece(half, dp, dq), part, cut)
            sp, sq = ((dp - step) % RING, dq % RING) if along == 0 else (dp % RING, (dq - step) % RING)
            sender.push(ref, ref, sems.at[half, sp, sq, part], place.at(axes[half][along], step))

    def wait(half, dp, dq, part):
        if parts(part):
            ref = part_of(piece(half, dp, dq), part, cut)
            sender.arrived(ref, sems.at[half, dp % RING, dq % RING, part], place.at("x", 1))

    both = (0, 1)
    for half in both:
        for step in (1, -1):
            send(half, 0, 0, WHOLE, 0, step)
    for half in both:
        for step in (1, -1):
            send(half, 0, 0, WHOLE, 1, step)
    yield
    for step, part in ((1, LOW), (-1, HIGH)):
        for half in both:
            wait(half, -step, 0, WHOLE)
            send(half, -step, 0, part, 0, step)
            for side in (1, -1):
                send(half, -step, 0, WHOLE, 1, side)
    yield
    for half in both:
        for step, part in ((1, LOW), (-1, HIGH)):
            wait(half, 0, -step, WHOLE)
            send(half, 0, -step, part, 1, step)
    yield
    for half in both:
        wait(half, 2, 0, LOW)
        wait(half, 2, 0, HIGH)
        for side in (1, -1):
            send(half, 2, 0, WHOLE, 1, side)
    yield
    for dp in (-1, 1, 2):
        for half in both:
            for step, part in ((1, LOW), (-1, HIGH)):
                wait(half, dp, -step, WHOLE)
                send(half, dp, -step, part, 1, step)
        yield
    for dp in (0, -1, 1, 2):
        for half in both:
            wait(half, dp, 2, LOW)
            wait(half, dp, 2, HIGH)


class RingGather:
    def __init__(self, place, sender, sems, own, out):
        self.place, self.sender, self.sems, self.own, self.out = place, sender, sems, own, out
        self.rows = own.shape[0]
        self.other = place.at("c", 1)
        self.begun, self.forwarded = [], []

    def piece(self, dy, core, part=WHOLE):
        y = self.place.shift("y", dy)
        half = self.rows // 2
        start, size = {WHOLE: (0, self.rows), LOW: (0, half), HIGH: (half, half)}[part]
        return self.out.at[y % 2, y // 2, pl.ds(pl.multiple_of(core * self.rows + start, 16), size)]

    def begin(self):
        place, mine = self.place, self.piece(0, self.place.c)
        for step in (1, -1):
            number = self.sender.push(self.own, mine, self.sems.at[(-step) % RING, WHOLE], place.at("y", step))
            self.begun.append(number)
        self.begun.append(self.sender.push(self.own, mine, self.sems.at[0, 3], self.other))
        self.kept = self.sender.keep_first(self.own, mine)

    def relay(self):
        for step, part in ((1, LOW), (-1, HIGH)):
            ref = self.piece(-step, self.place.c)
            self.sender.arrived(ref, self.sems.at[(-step) % RING, WHOLE], self.other)
            half = self.piece(-step, self.place.c, part)
            self.forwarded += [
                self.sender.push(half, half, self.sems.at[2, part], self.place.at("y", step)),
                self.sender.push(ref, ref, self.sems.at[(-step) % RING, 3], self.other),
            ]

    def relay_far(self):
        for part in (LOW, HIGH):
            self.sender.arrived(self.piece(2, self.place.c, part), self.sems.at[2, part], self.other)
        ref = self.piece(2, self.place.c)
        self.forwarded += [self.sender.push(ref, ref, self.sems.at[2, 3], self.other)]

    def ready(self, dy):
        if dy == 0:
            self.kept.wait()
        self.sender.arrived(self.piece(dy, 1 - self.place.c), self.sems.at[dy % RING, 3], self.other)


def ring_gather(place, sender, sems, own, out):
    gather = RingGather(place, sender, sems, own, out)
    gather.begin()
    yield
    gather.relay()
    yield
    gather.relay_far()
    yield
    for dy in (0, 1, -1, 2):
        gather.ready(dy)


def add_rows(out, terms, rows):
    def step(i, carry):
        window = pl.ds(pl.multiple_of(i * 16, 16), 16)
        total = terms[0][window, :].astype(F32)
        for term in terms[1:]:
            total = total + term[window, :].astype(F32)
        out[window, :] = total.astype(out.dtype)
        return carry

    lax.fori_loop(0, rows // 16, step, 0)


class RingSum:
    def __init__(self, place, sender, sems, partial, kept, from_core, hop, last):
        self.place, self.sender, self.sems, self.partial = place, sender, sems, partial
        self.kept, self.from_core, self.hop, self.last = kept, from_core, hop, last
        self.rows = kept.shape[1]
        self.low, self.high = pl.ds(0, self.rows // 2), pl.ds(self.rows // 2, self.rows // 2)
        self.other = place.at("c", 1)

    def mine(self, dy, core):
        y = self.place.shift("y", dy)
        return self.partial.at[y % 2, y // 2, pl.ds(pl.multiple_of(core * self.rows, 16), self.rows)]

    def offer(self, dy):
        slot = dy % RING
        self.sender.push(
            self.mine(dy, 1 - self.place.c), self.from_core.at[slot], self.sems.at[0, slot], self.other
        )

    def pieces(self):
        columns = self.kept.shape[2]
        return [pl.ds(p * columns // PIECES, columns // PIECES) for p in range(PIECES)]

    def collect(self, dy):
        slot = dy % RING
        kept, low, high = self.kept.at[slot], self.low, self.high
        self.sender.arrived(self.from_core.at[slot], self.sems.at[0, slot], self.other)
        if dy == 0:
            return
        up, down = self.place.at("y", 1), self.place.at("y", -1)
        mine = self.mine(dy, self.place.c)
        if dy == 2:
            for p, columns in enumerate(self.pieces()):
                add_rows(kept.at[:, columns], (mine.at[:, columns], self.from_core.at[slot, :, columns]), self.rows)
                self.sender.push(kept.at[low, columns], self.hop.at[0, :, columns], self.sems.at[1, p], up)
                self.sender.push(
                    kept.at[high, columns], self.hop.at[1, :, columns], self.sems.at[1, PIECES + p], down
                )
            return
        add_rows(kept, (mine, self.from_core.at[slot]), self.rows)
        if dy == 1:
            self.sender.push(kept.at[high], self.last.at[0, high], self.sems.at[2, 1], up)
        else:
            self.sender.push(kept.at[low], self.last.at[1, low], self.sems.at[2, 2], down)

    def relay(self):
        for p, columns in enumerate(self.pieces()):
            for k, slot, part, step in ((0, 1, self.low, 1), (1, 3, self.high, -1)):
                number = k * PIECES + p
                self.sender.arrived(self.hop.at[k, :, columns], self.sems.at[1, number], self.other)
                rows = self.kept.at[slot, part, columns]
                add_rows(rows, (rows, self.hop.at[k, :, columns]), self.rows // 2)
                self.sender.push(
                    rows, self.last.at[k, part, columns], self.sems.at[3, number], self.place.at("y", step)
                )

    def finish(self, out, *others):
        self.sender.arrived(self.last.at[0, self.high], self.sems.at[2, 1], self.other)
        self.sender.arrived(self.last.at[1, self.low], self.sems.at[2, 2], self.other)
        mine = self.mine(0, self.place.c)
        for p, columns in enumerate(self.pieces()):
            for k, part in ((0, self.low), (1, self.high)):
                self.sender.arrived(
                    self.last.at[k, part, columns], self.sems.at[3, k * PIECES + p], self.other
                )
            terms = (mine, self.from_core.at[0], self.last.at[0], self.last.at[1], *others)
            add_rows(out.at[:, columns], [term.at[:, columns] for term in terms], self.rows)


def plane_scatter(place, sender, sems, partial, done, cut, bufs):
    rows = partial.shape[-2]
    hop, last, middle, hop2, last2 = bufs
    low, high = pl.ds(0, cut), pl.ds(cut, rows - cut)
    axes = (("z", "x"), ("x", "z"))
    two_parts = cut < rows
    both = (0, 1)
    other = place.at("x", 1)

    def row(half, du, window):
        u = place.shift(axes[half][0], du)
        return partial.at[half, :, u, window] if half == 0 else partial.at[half, u, :, window]

    def line(half, du, v):
        u = place.shift(axes[half][0], du)
        return partial.at[half, v, u] if half == 0 else partial.at[half, u, v]

    def add(out, terms, count):
        if count % 16:
            total = terms[0][...].astype(F32)
            for term in terms[1:]:
                total = total + term[...].astype(F32)
            out[...] = total.astype(out.dtype)
        else:
            add_rows(out, terms, count)

    for half in both:
        u = axes[half][0]
        sender.push(row(half, 2, low), hop.at[half, 0], sems.at[half, 0], place.at(u, 1))
        if two_parts:
            sender.push(row(half, 2, high), hop.at[half, 1], sems.at[half, 1], place.at(u, -1))
    for half in both:
        u = axes[half][0]
        if two_parts:
            sender.push(row(half, 1, high), last.at[half, 0, :, high], sems.at[half, 2], place.at(u, 1))
        sender.push(row(half, -1, low), last.at[half, 1, :, low], sems.at[half, 3], place.at(u, -1))
    yield
    for half in both:
        u = axes[half][0]
        sender.arrived(hop.at[half, 0], sems.at[half, 0], other)
        for v in range(RING):
            add(hop.at[half, 0, v], (line(half, 1, v).at[low], hop.at[half, 0, v]), cut)
        sender.push(hop.at[half, 0], last.at[half, 0, :, low], sems.at[half, 4], place.at(u, 1))
        if two_parts:
            sender.arrived(hop.at[half, 1], sems.at[half, 1], other)
            for v in range(RING):
                add(
                    hop.at[half, 1, v],
                    (line(half, -1, v).at[high], hop.at[half, 1, v]),
                    rows - cut,
                )
            sender.push(
                hop.at[half, 1], last.at[half, 1, :, high], sems.at[half, 5], place.at(u, -1)
            )
    yield
    for half in both:
        v_axis = axes[half][1]
        if two_parts:
            sender.arrived(last.at[half, 0, :, high], sems.at[half, 2], other)
        sender.arrived(last.at[half, 1, :, low], sems.at[half, 3], other)
        sender.arrived(last.at[half, 0, :, low], sems.at[half, 4], other)
        if two_parts:
            sender.arrived(last.at[half, 1, :, high], sems.at[half, 5], other)
        for dv in (2, 1, -1, 0):
            v = place.shift(v_axis, dv)
            terms = (line(half, 0, v), last.at[half, 0, v], last.at[half, 1, v])
            add(middle.at[half, dv % RING], terms, rows)
            if dv == 2:
                sender.push(
                    middle.at[half, 2, low], hop2.at[half, 0], sems.at[half, 6], place.at(v_axis, 1)
                )
                if two_parts:
                    sender.push(
                        middle.at[half, 2, high],
                        hop2.at[half, 1],
                        sems.at[half, 7],
                        place.at(v_axis, -1),
                    )
            elif dv == 1 and two_parts:
                sender.push(
                    middle.at[half, 1, high], last2.at[half, 0, high], sems.at[half, 8], place.at(v_axis, 1)
                )
            elif dv == -1:
                sender.push(
                    middle.at[half, 3, low], last2.at[half, 1, low], sems.at[half, 9], place.at(v_axis, -1)
                )
    yield
    for half in both:
        v_axis = axes[half][1]
        sender.arrived(hop2.at[half, 0], sems.at[half, 6], other)
        add(hop2.at[half, 0], (middle.at[half, 1, low], hop2.at[half, 0]), cut)
        sender.push(
            hop2.at[half, 0], last2.at[half, 0, low], sems.at[half, 10], place.at(v_axis, 1)
        )
        if two_parts:
            sender.arrived(hop2.at[half, 1], sems.at[half, 7], other)
            add(hop2.at[half, 1], (middle.at[half, 3, high], hop2.at[half, 1]), rows - cut)
            sender.push(
                hop2.at[half, 1], last2.at[half, 1, high], sems.at[half, 11], place.at(v_axis, -1)
            )
    yield
    for half in both:
        if two_parts:
            sender.arrived(last2.at[half, 0, high], sems.at[half, 8], other)
        sender.arrived(last2.at[half, 1, low], sems.at[half, 9], other)
        sender.arrived(last2.at[half, 0, low], sems.at[half, 10], other)
        if two_parts:
            sender.arrived(last2.at[half, 1, high], sems.at[half, 11], other)
        add(done.at[half], (middle.at[half, 0], last2.at[half, 0], last2.at[half, 1]), rows)


def scatter_buffers(rows, columns, dtype):
    cut = rows // 2 if dtype == BF16 else rows
    return [
        pltpu.VMEM((2, 2, RING, cut, columns), dtype),
        pltpu.VMEM((2, 2, RING, rows, columns), dtype),
        pltpu.VMEM((2, RING, rows, columns), dtype),
        pltpu.VMEM((2, 2, cut, columns), dtype),
        pltpu.VMEM((2, 2, rows, columns), dtype),
    ]


def ring_buffers(rows, columns):
    return [
        pltpu.VMEM((RING, rows, columns), BF16),
        pltpu.VMEM((RING, rows, columns), BF16),
        pltpu.VMEM((2, rows // 2, columns), BF16),
        pltpu.VMEM((2, rows, columns), BF16),
    ]


def dma_sems(*shape):
    return pltpu.SemaphoreType.DMA(shape)


def shape_of(*shape, dtype=BF16):
    return jax.ShapeDtypeStruct(shape, dtype)


def call(kernel, number, out_shape, in_specs, out_specs, scratch, args):
    return pl.pallas_call(
        kernel,
        out_shape=out_shape,
        in_specs=in_specs,
        out_specs=out_specs,
        scratch_shapes=scratch,
        compiler_params=pltpu.CompilerParams(
            collective_id=number, has_side_effects=True, vmem_limit_bytes=VMEM_LIMIT
        ),
    )(*args)


NN = (((1,), (0,)), ((), ()))
NT = (((1,), (1,)), ((), ()))
TN = (((0,), (0,)), ((), ()))


def dot(left, right, dims=NN):
    return lax.dot_general(left, right, dims, preferred_element_type=F32)


def in_tiles(width, tile, work):
    for n in range(width // tile):
        work(pl.ds(n * tile, tile))


def refs_of(refs, *counts):
    refs, out = list(refs), []
    for n in counts:
        out.append(refs[:n])
        del refs[:n]
    return out


def by_rows(count, work):
    def step(i, carry):
        work(pl.ds(pl.multiple_of(i * 16, 16), 16))
        return carry

    lax.fori_loop(0, count // 16, step, 0)


def load_weights(sender, source, targets):
    copies = []
    for k, target in targets:
        for yl in range(2):
            copies.append(sender.keep_first(source.at[:, :, k, yl], target.at[yl]))
    return copies


def rows_of(weight, window):
    if len(weight.shape) == 2:
        return weight[window, :]
    run = weight.shape[2] * weight.shape[3]
    first, count = window.start // run, window.size // run
    block = weight[first // RING, pl.ds(first % RING, count), :, :, :]
    return block.reshape(window.size, weight.shape[4])


def columns_of(weight, window):
    block = weight[:, :, :, :, window]
    return block.reshape(-1, window.size)


def mlp_kernel(
    own, gate_up, down, down_pair, mixed_in, cotangent_in, proj_in, gain_rows, hidden_out, d_mixed_out, d_proj_out,
    gains_out, grads_out, down_out, *refs
):
    (
        (x_all, d_all, w_gate, w_up, w_down, gate, up, act, partial, down_partial, tiles),
        (down_proj, mixed, cotangent, proj),
        ring,
        first_buffers,
        second_buffers,
        (sends, gather_sems, sum_sems, gather_sems2, sum_sems2, plane, plane2, tile_sems, plane3),
    ) = refs_of(refs, 11, 4, 4, 5, 5, 9)
    d_own = d_proj_out
    d_gate, d_up = gate, up
    place = Place()
    sender = Sender(sends)
    loads = load_weights(sender, gate_up, ((0, w_gate), (1, w_up)))
    early = down.shape[4]
    w_rest = w_down.at[:, :, :, :, pl.ds(early, down_pair.shape[2])]
    load_pair = sender.keep_first(down_pair, w_rest.at[:, place.x, place.z])
    load_down = sender.keep_first(down, w_down.at[:, :, :, :, pl.ds(0, early)])
    pairs = ((mixed_in, mixed), (cotangent_in, cotangent), (proj_in, proj))
    later = [sender.keep_first(source, target) for source, target in pairs]
    greet_all(place, ("x", "z", "y", "c"))
    gather = RingGather(place, sender, gather_sems, own, x_all)
    total = RingSum(place, sender, sum_sems, partial, *ring)
    gather.begin()
    load_pair.wait()
    rest = plane_gather(place, sender, plane3, w_rest, w_rest.shape[3] // 2)
    next(rest)
    for copy in loads:
        copy.wait()
    load_down.wait()
    tile = 512

    def where(dy):
        y = place.shift("y", dy)
        return y % 2, y // 2

    def at_chip(dy):
        at = where(dy)
        return (*at, slice(None)), (2 * rows, hidden_width)

    def at_neighbours(_):
        return (1 - place.yl, slice(None), slice(None)), (4 * rows, hidden_width)

    rows, hidden_width = own.shape[0], act.shape[-1]

    def forward_hidden(index, shape):
        count = shape[0]

        def hidden(columns):
            tokens = x_all[(*index, slice(None))].reshape(count, -1)
            g = dot(tokens, columns_of(w_gate, columns))
            u = dot(tokens, columns_of(w_up, columns))
            here = (*index, columns)
            held = act[here].shape
            gate[here], up[here] = g.astype(BF16).reshape(held), u.astype(BF16).reshape(held)
            act[here] = (g * jax.nn.sigmoid(g) * u).astype(BF16).reshape(held)

        in_tiles(hidden_width, tile, hidden)

    def forward_project(index, shape):
        def project(columns):
            left = act[(*index, slice(None))].reshape(shape)
            value = dot(left, rows_of(w_down, columns), NT).astype(BF16)
            here = (*index, columns)
            partial[here] = value.reshape(partial[here].shape)

        in_tiles(partial.shape[-1], tile, project)

    def in_turn(gather, total, work, before_far=lambda: None):
        gather.ready(0)
        work(*at_chip(0))
        total.offer(0)
        gather.relay()
        gather.ready(1)
        gather.ready(-1)
        work(*at_neighbours(0))
        total.offer(1)
        total.offer(-1)
        gather.relay_far()
        total.collect(1)
        total.collect(-1)
        gather.ready(2)
        before_far()
        work(*at_chip(2))
        total.offer(2)

    gather.ready(0)
    forward_hidden(*at_chip(0))
    for _ in range(4):
        next(rest)
    gather.relay()
    next(rest)
    gather.ready(1)
    gather.ready(-1)
    next(rest)
    forward_hidden(*at_neighbours(0))
    take_turns((rest,))
    gather.relay_far()
    forward_project(*at_neighbours(0))
    total.offer(1)
    total.offer(-1)
    forward_project(*at_chip(0))
    total.offer(0)
    total.collect(1)
    total.collect(-1)
    gather.ready(2)
    forward_hidden(*at_chip(2))
    forward_project(*at_chip(2))
    total.offer(2)
    total.collect(2)
    total.collect(0)
    total.relay()
    total.finish(down_proj)
    for copy in later:
        copy.wait()
    sender.settle(range(len(sender.open)))
    gains_out[...] = jnp.zeros_like(gains_out)

    def output_norm(rows):
        value, upstream, gain = down_proj[rows, :], cotangent[rows, :].astype(F32), gain_rows[3:4, :]
        scale = norm_scale(value)
        hidden_out[rows, :] = (mixed[rows, :] + value * scale * gain).astype(BF16)
        d_own[rows, :] = norm_back(upstream, value, scale, gain).astype(BF16)
        gains_out[1:2, :] += jnp.sum(upstream * value * scale, axis=0, keepdims=True)

    by_rows(down_proj.shape[0], output_norm)

    gather = RingGather(place, sender, gather_sems2, d_own, d_all)
    total = RingSum(place, sender, sum_sems2, partial, *ring)
    gather.begin()

    def backward(index, shape):
        count = shape[0]

        def hidden(columns):
            d_act = dot(d_all[(*index, slice(None))].reshape(count, -1), columns_of(w_down, columns))
            here = (*index, columns)
            held = gate[here].shape
            g, u = gate[here].astype(F32).reshape(d_act.shape), up[here].astype(F32).reshape(d_act.shape)
            s = jax.nn.sigmoid(g)
            d_gate[here] = (d_act * u * s * (1.0 + g * (1.0 - s))).astype(BF16).reshape(held)
            d_up[here] = (d_act * g * s).astype(BF16).reshape(held)

        in_tiles(hidden_width, tile, hidden)

        def back(columns):
            whole = (*index, slice(None))
            value = dot(d_gate[whole].reshape(shape), rows_of(w_gate, columns), NT)
            value = value + dot(d_up[whole].reshape(shape), rows_of(w_up, columns), NT)
            here = (*index, columns)
            partial[here] = value.astype(BF16).reshape(partial[here].shape)

        in_tiles(partial.shape[-1], tile, back)

    block = 4 * down_partial.shape[3]

    def all_rows(ref, columns=slice(None)):
        value = ref[:, :, :, columns]
        return value.reshape(-1, value.shape[-1])

    def sent(slot, k, i):
        return pltpu.make_async_copy(
            tiles.at[slot, k], grads_out.at[k, i // RING, i % RING], tile_sems.at[slot, k]
        )

    def weight_grads(begin, end):
        for i in range(begin, end):
            slot = i % 2
            for k, right in enumerate((d_gate, d_up)):
                if i >= 2:
                    sent(slot, k, i - 2).wait()
                value = dot(all_rows(x_all, pl.ds(i * block, block)), all_rows(right), TN)
                tiles[slot, k] = value.astype(BF16).reshape(tiles.shape[2:])
                sent(slot, k, i).start()

    half = act.shape[-1] // 2

    def down_grad(p, sems, buffers):
        columns = pl.ds(p * half, half)
        right = all_rows(act, columns)
        for i in range(2 * RING):
            value = dot(all_rows(d_all, pl.ds(i * block, block)), right, TN).astype(BF16)
            down_partial[i // RING, i % RING, :, :, columns] = value.reshape(*down_partial.shape[2:4], half)
        task = plane_scatter(
            place,
            sender,
            sems,
            down_partial.at[:, :, :, :, columns],
            down_out.at[:, :, columns],
            down_partial.shape[3] // 2,
            buffers,
        )
        next(task)
        return task

    tasks = []

    def down_grads():
        tasks.append(down_grad(0, plane, first_buffers))
        tasks.append(down_grad(1, plane2, second_buffers))

    in_turn(gather, total, backward, down_grads)
    task, task2 = tasks
    total.collect(2)
    next(task)
    total.collect(0)
    next(task2)
    weight_grads(0, 3)
    total.relay()
    weight_grads(3, 4)
    next(task)
    weight_grads(4, 6)
    next(task2)
    weight_grads(6, 7)
    next(task)
    weight_grads(7, 8)
    next(task2)
    total.finish(d_mixed_out)
    sender.settle(gather.begun)

    def attention_norm(rows):
        value, gain = proj[rows, :], gain_rows[2:3, :]
        d_mixed = cotangent[rows, :].astype(F32) + d_mixed_out[rows, :]
        d_mixed_out[rows, :] = d_mixed
        scale = norm_scale(value)
        d_proj_out[rows, :] = norm_back(d_mixed, value, scale, gain).astype(BF16)
        gains_out[0:1, :] += jnp.sum(d_mixed * value * scale, axis=0, keepdims=True)

    by_rows(down_proj.shape[0], attention_norm)
    take_turns((task, task2))
    for i in (6, 7):
        for k in range(2):
            sent(i % 2, k, i).wait()
    sender.finish()


def mlp(number, own, gate_up, down, down_pair, mixed, cotangent, proj, gain_rows):
    rows, width = own.shape
    piece, hidden = gate_up.shape[-2:]
    tokens = (2, 2, 2 * rows)
    weight = pltpu.VMEM((2, RING, RING, piece, hidden), BF16)
    wide, narrow = pltpu.VMEM((*tokens, width), BF16), pltpu.VMEM((*tokens, hidden), BF16)
    return call(
        mlp_kernel,
        number,
        (
            shape_of(rows, width),
            shape_of(rows, width, dtype=F32),
            shape_of(rows, width),
            shape_of(8, width, dtype=F32),
            shape_of(2, 2, RING, RING, piece, hidden),
            shape_of(2, piece, hidden),
        ),
        [ANYWHERE] * 7 + [IN_VMEM],
        (IN_VMEM,) * 4 + (ANYWHERE, IN_VMEM),
        [
            wide,
            wide,
            *[weight] * 3,
            *[narrow] * 3,
            wide,
            weight,
            pltpu.VMEM((2, 2, RING, piece, hidden), BF16),
            pltpu.VMEM((rows, width), F32),
            pltpu.VMEM((rows, width), F32),
            pltpu.VMEM((rows, width), BF16),
            pltpu.VMEM((rows, width), F32),
            *ring_buffers(rows, width),
            *scatter_buffers(piece, hidden // 2, BF16),
            *scatter_buffers(piece, hidden // 2, BF16),
            dma_sems(176),
            dma_sems(RING, 4),
            dma_sems(4, 2 * PIECES),
            dma_sems(RING, 4),
            dma_sems(4, 2 * PIECES),
            dma_sems(2, 12),
            dma_sems(2, 12),
            dma_sems(2, 2),
            dma_sems(2, RING, RING, 3),
        ],
        (own, gate_up, down, down_pair, mixed, cotangent, proj, gain_rows),
    )


def ring_product(place, total, values, weight, partial, others, before_near=lambda: None):
    def compute(dy):
        y = place.shift("y", dy)
        at = (y % 2, y // 2)

        def tile(columns):
            partial[(*at, slice(None), columns)] = dot(values[at], rows_of(weight, columns), NT).astype(BF16)

        in_tiles(partial.shape[-1], 512, tile)
        total.offer(dy)

    compute(2)
    before_near()
    compute(1)
    total.collect(2)
    compute(-1)
    total.collect(1)
    compute(0)
    total.collect(-1)
    total.collect(0)
    for task in others:
        next(task)
    total.relay()


def flat(weight):
    return weight.reshape(-1, weight.shape[-1])


def exact(left, right, dims):
    return lax.dot_general(
        left, right, dims, precision=lax.Precision.HIGHEST, preferred_element_type=F32
    )


def half_roll(values):
    return pltpu.roll(values, HEAD_DIM // 2, 1)


def near_devices(place):
    return [place.at(axis, step) for axis in ("x", "z") for step in (1, -1)]


class Octet:
    peers = [(dy, dc) for dy in (0, 1, 3, 2) for dc in (0, 1) if dy or dc]

    def __init__(self, place, sender, own, slots, sems):
        self.place, self.sender, self.own, self.slots, self.sems = place, sender, own, slots, sems

    @staticmethod
    def device(place, dy, dc):
        y = place.shift("y", dy)
        return {"yl": y % 2, "yh": y // 2, "c": (place.c + dc) % 2}

    def send(self):
        for dy, dc in self.peers:
            slot = ((RING - dy) % RING) * 2 + dc
            device = self.device(self.place, dy, dc)
            self.sender.push(self.own, self.slots.at[slot], self.sems.at[slot], device)

    def total(self):
        for dy, dc in self.peers:
            slot = dy * 2 + dc
            self.sender.arrived(self.slots.at[slot], self.sems.at[slot], self.device(self.place, dy, dc))
        value = self.own[...]
        for dy, dc in self.peers:
            value = value + self.slots[dy * 2 + dc]
        return value


def one_hot_rows(k):
    return (lax.broadcasted_iota(jnp.int32, (8, HEAD_DIM), 0) == k).astype(F32)


def masked(scores, starts, i):
    tile, count = scores.shape
    keys = lax.broadcasted_iota(jnp.int32, (tile, count), 1)
    queries = lax.broadcasted_iota(jnp.int32, (tile, count), 0) + i * tile
    return jnp.where((keys >= starts) & (keys <= queries), scores, -1e30)


def softmax(scores):
    exponent = jnp.exp(scores - jnp.max(scores, axis=-1, keepdims=True))
    return exponent / jnp.sum(exponent, axis=-1, keepdims=True)


def attention_forward_kernel(
    own, attn, down, gain, cosine_in, sine_in, starts_in, proj_out, mixed_out, low_out, gain_rows, head_out, x_out,
    weight_out, raw_out, rot_out, value_out, scale_out, attended_out, down_out, pair_out, *refs
):
    (
        (x_all, weight, raw, rot, values, scales, attended, partial, sums, slots, down_all, gain_all),
        (cosine, sine, starts, hidden),
        ring,
        (sends, gather_sems, sum_sems, octet_sems, attn_plane, gain_plane, plane, swap),
    ) = refs_of(refs, 12, 4, 4, 8)
    place = Place()
    sender = Sender(sends)
    _, heads, _, block_rows, _ = raw.shape
    inner = heads * HEAD_DIM
    tile = block_rows // 2
    pairs = ((cosine_in, cosine), (sine_in, sine), (starts_in, starts), (own, hidden))
    later = [sender.keep_first(source, target) for source, target in pairs]
    partner = {"yl": 1 - place.yl}
    me, you = place.yl, 1 - place.yl
    half = down_all.shape[4]
    early, later_half = pl.ds(0, half), pl.ds(half, half)
    shards = ((attn, weight), (gain, gain_all), (down.at[:, :, early], down_all))
    mine = [
        sender.keep_first(source if k == 1 else source.at[me], target.at[me, place.x, place.z])
        for k, (source, target) in enumerate(shards)
    ]
    greet(near_devices(place) + [Octet.device(place, *peer) for peer in Octet.peers])
    for k, (source, target) in enumerate(shards[:2]):
        sender.push(
            source if k == 1 else source.at[you], target.at[me, place.x, place.z], swap.at[k], partner
        )
    gather = RingGather(place, sender, gather_sems, own, x_all)
    gather.begin()
    for copy in mine:
        copy.wait()
    for k, (_, target) in enumerate(shards[:2]):
        sender.arrived(target.at[you, place.x, place.z], swap.at[k], partner)
    attn_task = plane_gather(place, sender, attn_plane, weight, weight.shape[3] // 2)
    gain_task = plane_gather(place, sender, gain_plane, gain_all, gain_all.shape[3])
    next(attn_task)
    next(gain_task)
    sender.push(down.at[you, :, early], down_all.at[me, place.x, place.z], swap.at[2], partner)
    sender.push(down.at[you, :, later_half], pair_out.at[me], swap.at[3], partner)
    sender.keep(down.at[me, :, later_half], pair_out.at[me])

    def gather_all():
        gather.relay()
        yield
        gather.relay_far()
        yield
        for dy in (0, 1, -1, 2):
            gather.ready(dy)

    take_turns((gain_task, attn_task, gather_all()))
    sender.keep(x_all, x_out)
    sender.keep(weight, weight_out)
    for yl in range(2):
        for x in range(RING):
            for h in range(2):
                lanes = pl.ds(((yl * RING + x) * 2 + h) * HEAD_DIM, HEAD_DIM)
                gain_rows[:, lanes] = gain_all[yl, x, 2 * h] + gain_all[yl, x, 2 * h + 1]
    first_column = (place.yh * 2 + place.c) * (2 * inner) + place.yl * inner

    def head_gain(k, h):
        start = pl.multiple_of(first_column + h * HEAD_DIM, HEAD_DIM)
        return gain_rows[k : k + 1, pl.ds(start, HEAD_DIM)]

    for h in range(heads):
        start = pl.multiple_of(first_column + h * HEAD_DIM, HEAD_DIM)
        head_out[:, pl.ds(h * HEAD_DIM, HEAD_DIM)] = gain_rows[:, pl.ds(start, HEAD_DIM)]
    sender.arrived(down_all.at[you, place.x, place.z], swap.at[2], partner)
    down_task = plane_gather(place, sender, plane, down_all, down_all.shape[3] // 2)
    next(down_task)
    total = RingSum(place, sender, sum_sems, partial, *ring)
    ones = [one_hot_rows(k) for k in range(2)]

    def project(t, carry):
        a, b = t // 2, t % 2
        window = pl.ds(pl.multiple_of(b * tile, tile), tile)
        value = dot(x_all[a, b], columns_of(weight, pl.ds(0, 2 * inner)))
        row_sums = jnp.zeros((8, tile), F32)
        for k in range(2):
            for h in range(heads):
                column = k * inner + h * HEAD_DIM
                part = value[:, column : column + HEAD_DIM]
                raw[k, h, a, window, :] = part
                row_sums = row_sums + exact(ones[k], part * part, NT)
        sums[:, pl.ds(pl.multiple_of(t * tile, tile), tile)] = row_sums
        return carry

    def project_value(t, carry):
        a, b = t // 2, t % 2
        window = pl.ds(pl.multiple_of(b * tile, tile), tile)
        value = dot(x_all[a, b], columns_of(weight, pl.ds(2 * inner, inner))).astype(BF16)
        for h in range(heads):
            values[h, a, window, :] = value[:, h * HEAD_DIM : (h + 1) * HEAD_DIM]
        return carry

    lax.fori_loop(0, 4, project, 0)
    octet = Octet(place, sender, sums, slots, octet_sems)
    octet.send()
    sender.keep(raw, raw_out)
    lax.fori_loop(0, 4, project_value, 0)
    sender.keep(values, value_out)
    next(down_task)
    for copy in later:
        copy.wait()
    row_scales = lax.rsqrt(octet.total() / x_all.shape[3] + NORM_EPS)
    for b in range(2):
        for k in range(2):
            scale = exact(row_scales[:, b * block_rows : (b + 1) * block_rows], ones[k], TN)
            scales[k, b] = scale
            for h in range(heads):
                value = raw[k, h, b] * scale * head_gain(k, h)
                rot[k, h, b] = (value * cosine[b] + half_roll(value) * sine[b]).astype(BF16)
    sender.keep(scales, scale_out)
    sender.keep(rot, rot_out)
    next(down_task)

    def attention(b):
        for h in range(heads):
            key, value = rot[1, h, b], values[h, b]
            for i in range(2):
                window, count = pl.ds(i * tile, tile), (i + 1) * tile
                scores = dot(rot[0, h, b, window, :], key[:count], NT) * HEAD_DIM ** (-0.5)
                probs = softmax(masked(scores, starts[b, window, 0:1], i)).astype(BF16)
                attended[b, i, :, pl.ds(h * HEAD_DIM, HEAD_DIM)] = dot(probs, value[:count]).astype(BF16)

    attention(place.yl)
    out_weight = weight.at[:, :, :, :, pl.ds(3 * inner, inner)]
    ring_product(place, total, attended, out_weight, partial, (), lambda: attention(1 - place.yl))
    sender.keep(attended, attended_out)
    take_turns((down_task,))
    sender.keep(down_all, down_out)
    total.finish(proj_out)

    def mix(rows):
        value = proj_out[rows, :]
        mixed = hidden[rows, :].astype(F32) + value * norm_scale(value) * gain_rows[2:3, :]
        mixed_out[rows, :] = mixed
        low_out[rows, :] = mixed.astype(BF16)

    by_rows(proj_out.shape[0], mix)
    sender.arrived(pair_out.at[you], swap.at[3], partner)
    sender.finish()


def attention_forward(number, own, attn, down, gain, cosine, sine, starts):
    rows, width = own.shape
    inner = attn.shape[2] // 4
    heads = inner // HEAD_DIM
    tokens = (2, 2, 2 * rows)
    raw = (2, heads, 2, 4 * rows, HEAD_DIM)
    values, scales, attended = raw[1:], (2, 2, 4 * rows, HEAD_DIM), (*tokens, inner)
    weight = (2, RING, RING, *attn.shape[1:])
    piece = down.shape[1], down.shape[2] // 2
    down_all = (2, RING, RING, *piece)
    return call(
        attention_forward_kernel,
        number,
        (
            shape_of(rows, width, dtype=F32),
            shape_of(rows, width, dtype=F32),
            shape_of(rows, width),
            shape_of(8, width, dtype=F32),
            shape_of(8, inner, dtype=F32),
            shape_of(*tokens, width),
            shape_of(*weight),
            shape_of(*raw, dtype=F32),
            shape_of(*raw),
            shape_of(*values),
            shape_of(*scales, dtype=F32),
            shape_of(*attended),
            shape_of(*down_all),
            shape_of(2, *piece),
        ),
        [ANYWHERE] * 7,
        (IN_VMEM,) * 5 + (ANYWHERE,) * 9,
        [
            pltpu.VMEM((*tokens, width), BF16),
            pltpu.VMEM(weight, BF16),
            pltpu.VMEM(raw, F32),
            pltpu.VMEM(raw, BF16),
            pltpu.VMEM(values, BF16),
            pltpu.VMEM(scales, F32),
            pltpu.VMEM(attended, BF16),
            pltpu.VMEM((*tokens, width), BF16),
            pltpu.VMEM((8, 8 * rows), F32),
            pltpu.VMEM((8, 8, 8 * rows), F32),
            pltpu.VMEM(down_all, BF16),
            pltpu.VMEM((2, RING, RING, *gain.shape), F32),
            *[pltpu.VMEM(other.shape, other.dtype) for other in (cosine, sine, starts, own)],
            *ring_buffers(rows, width),
            dma_sems(208),
            dma_sems(RING, 4),
            dma_sems(4, 2 * PIECES),
            dma_sems(8),
            dma_sems(2, RING, RING, 3),
            dma_sems(2, RING, RING, 3),
            dma_sems(2, RING, RING, 3),
            dma_sems(4),
        ],
        (own, attn, down, gain, cosine, sine, starts),
    )


def attention_backward_kernel(
    own, weight, inputs, mlp_in, down, attended_in, raw_in, rot_in, values_in, scales_in,
    cosines_in, sines_in, starts_in, head_gains, token_gains, out, attn_out, gain_out, mlp_out, *refs
):
    (
        (shared, own_weight, attn_partial, gate_partial, up_partial, d_att, back, d_qkv, sums, slots),
        staged,
        (gain_partial, gain_rows, gain_slots, attn_done, gain_done, mlp_done),
        ring,
        buffers,
        late_buffers,
        gate_buffers,
        up_buffers,
        gain_buffers,
        (sends, gather_sems, sum_sems, octet_sems, gain_sems, swap, plane, late_plane, gain_plane, gate_plane),
        (up_plane,),
    ) = refs_of(refs, 10, 8, 6, 4, 5, 5, 5, 5, 5, 10, 1)
    attended, raw_all, rot, values, scales, cosines, sines, starts = staged
    d_all = x_all = partial = shared
    place = Place()
    sender = Sender(sends)
    _, heads, _, block_rows, _ = rot.shape
    width = d_qkv.shape[-1]
    inner = heads * HEAD_DIM
    rows = attn_partial.shape[3]
    block = RING * rows
    mlp_loads = [sender.keep_first(mlp_in.at[0], gate_partial), sender.keep_first(mlp_in.at[1], up_partial)]
    load = sender.keep_first(weight, own_weight)
    sources = (attended_in, raw_in, rot_in, values_in, scales_in, cosines_in, sines_in, starts_in)
    later = [sender.keep_first(source, target) for source, target in zip(sources, staged)]
    partner = {"yl": 1 - place.yl}
    me, you = place.yl, 1 - place.yl
    greet(near_devices(place) + [Octet.device(place, *peer) for peer in Octet.peers])
    gather = RingGather(place, sender, gather_sems, own, d_all)
    total = RingSum(place, sender, sum_sems, partial, *ring)
    gather.begin()
    sender.push(down.at[you], mlp_out.at[2, me], swap.at[3], partner)
    sender.keep(down.at[me], mlp_out.at[2, me])
    mlp = []
    for k, (sems, bufs, summand) in enumerate(
        ((gate_plane, gate_buffers, gate_partial), (up_plane, up_buffers, up_partial))
    ):
        mlp_loads[k].wait()
        task = plane_scatter(place, sender, sems, summand, mlp_done.at[k], rows // 2, bufs)
        next(task)
        mlp.append(task)
    gate_task, up_task = mlp
    load.wait()
    gain_partial[...] = jnp.zeros_like(gain_partial)
    gain_rows[...] = jnp.zeros_like(gain_rows)
    for k in range(2 * RING):
        for z in range(RING):
            gain_partial[k // RING, k % RING, z, 2:4, :] = token_gains[0:2, k * block : (k + 1) * block]

    def compute(dy):
        gather.ready(dy)
        y = place.shift("y", dy)
        at = (y % 2, y // 2)
        d_att[at] = dot(d_all[at], own_weight[:, pl.ds(width, inner)]).astype(BF16)

    tile = block_rows // 2
    score_factor = HEAD_DIM ** (-0.5)
    ones = [one_hot_rows(k) for k in range(2)]

    def attention(b):
        row_sums = jnp.zeros((8, block_rows), F32)
        cosine, sine = cosines[b], sines[b]
        for h in range(heads):
            lanes = pl.ds(h * HEAD_DIM, HEAD_DIM)
            key, value = rot[1, h, b], values[h, b]
            d_query, d_key, d_value = [], [None, None], [None, None]
            for i in range(2):
                window = pl.ds(i * tile, tile)
                query, upstream = rot[0, h, b, window, :], d_att[b, i, :, lanes]
                count = (i + 1) * tile
                scores = dot(query, key[:count], NT) * score_factor
                probs = softmax(masked(scores, starts[b, window, 0:1], i))
                d_probs = dot(upstream, value[:count], NT)
                row_dot = jnp.sum(probs * d_probs, axis=-1, keepdims=True)
                d_scores = (probs * (d_probs - row_dot) * score_factor).astype(BF16)
                probs = probs.astype(BF16)
                d_query.append(dot(d_scores, key[:count]))
                for j in range(i + 1):
                    part = slice(j * tile, (j + 1) * tile)
                    for sums_of, left, right in ((d_key, d_scores, query), (d_value, probs, upstream)):
                        term = dot(left[:, part], right, TN)
                        sums_of[j] = term if sums_of[j] is None else sums_of[j] + term
            for i in range(2):
                d_qkv[b, i, :, pl.ds(2 * inner + h * HEAD_DIM, HEAD_DIM)] = d_value[i].astype(BF16)
            for k, parts in enumerate((d_query, d_key)):
                turned = jnp.concatenate(parts, axis=0)
                turned = turned * cosine - half_roll(turned) * sine
                raw = raw_all[k, h, b]
                gain_rows[k : k + 1, lanes] += jnp.sum(turned * raw * scales[k, b], axis=0, keepdims=True)
                turned = turned * head_gains[k : k + 1, lanes]
                back[k, h, b] = turned
                row_sums = row_sums + exact(ones[k], turned * raw, NT)
        sums[:, pl.ds(pl.multiple_of(b * block_rows, block_rows), block_rows)] = row_sums

    compute(0)
    gather.relay()
    compute(1)
    compute(-1)
    next(gate_task)
    for copy in later:
        copy.wait()
    attention(1 - place.yl)
    gather.relay_far()
    compute(2)
    next(up_task)
    attention(place.yl)
    octet = Octet(place, sender, sums, slots, octet_sems)
    octet.send()
    first = (place.yh * 2 + place.c) * 2 + place.yl
    for z in range(RING):
        gain_partial[first // RING, first % RING, z, 0:2, :] = gain_rows[0:2, :]
    gains = plane_scatter(place, sender, gain_plane, gain_partial, gain_done, gain_done.shape[1], gain_buffers)
    next(gains)

    def flat_tokens(ref, columns=slice(None)):
        value = ref[:, :, :, columns]
        return value.reshape(-1, value.shape[-1])

    def weight_grads(left_ref, right, start):
        size = right.shape[1]
        for i in range(2 * RING):
            left = flat_tokens(left_ref, pl.ds(i * block, block))
            value = dot(left, right, TN).astype(BF16)
            attn_partial[i // RING, i % RING, :, :, pl.ds(start, size)] = value.reshape(RING, rows, size)

    weight_grads(d_all, flat_tokens(attended), width)
    sender.settle(gather.forwarded)
    load = sender.keep_first(inputs, x_all)
    next(gate_task)
    load.wait()

    def attn_scatter(columns, sems, bufs):
        task = plane_scatter(
            place,
            sender,
            sems,
            attn_partial.at[:, :, :, :, columns],
            attn_done.at[:, :, columns],
            rows // 2,
            bufs,
        )
        next(task)
        return task

    weight_grads(x_all, flat_tokens(d_qkv, pl.ds(2 * inner, inner)), 2 * inner)
    early = attn_scatter(pl.ds(2 * inner, 2 * inner), plane, buffers)
    row_sums = octet.total()
    for b in range(2):
        for k in range(2):
            column = exact(row_sums[:, b * block_rows : (b + 1) * block_rows], ones[k], TN)
            for h in range(heads):
                scale = scales[k, b]
                value = scale * back[k, h, b] - raw_all[k, h, b] * (scale * scale * scale * column / own.shape[1])
                value = value.astype(BF16)
                for i in range(2):
                    d_qkv[b, i, :, pl.ds(k * inner + h * HEAD_DIM, HEAD_DIM)] = value[
                        i * tile : (i + 1) * tile
                    ]
    weight_grads(x_all, flat_tokens(d_qkv, pl.ds(0, 2 * inner)), 0)
    late = attn_scatter(pl.ds(0, 2 * inner), late_plane, late_buffers)
    next(gate_task)
    next(up_task)
    next(early)
    ring_product(
        place, total, d_qkv, own_weight.at[:, pl.ds(0, width)], partial, (late, up_task, gains)
    )
    take_turns((gate_task, up_task))
    for k in range(2):
        sender.push(mlp_done.at[k, you], mlp_out.at[k, me], swap.at[1 + k], partner)
        sender.keep(mlp_done.at[k, me], mlp_out.at[k, me])
    take_turns((early, gains, late))
    sender.push(attn_done.at[you], attn_out.at[me], swap.at[0], partner)
    sender.keep(attn_done.at[me], attn_out.at[me])
    everyone = Octet(place, sender, gain_done, gain_slots, gain_sems)
    everyone.send()
    total.finish(out)
    gain_out[...] = everyone.total()
    sender.arrived(attn_out.at[you], swap.at[0], partner)
    for k in range(3):
        sender.arrived(mlp_out.at[k, you], swap.at[1 + k], partner)
    sender.finish()


def attention_backward(number, own, weight, inputs, mlp_partial, down, attended, *others):
    rows, width = own.shape
    tokens = (2, 2, 2 * rows)
    inner = attended.shape[3]
    heads = inner // HEAD_DIM
    shard = width // 32, weight.shape[1]
    gain_tile = (8, 4 * shard[0])
    return call(
        attention_backward_kernel,
        number,
        (
            shape_of(rows, width, dtype=F32),
            shape_of(2, *shard),
            shape_of(2, *gain_tile, dtype=F32),
            shape_of(3, 2, *shard),
        ),
        [ANYWHERE] * 13 + [IN_VMEM] * 2,
        (IN_VMEM,) * 4,
        [
            pltpu.VMEM((*tokens, width), BF16),
            pltpu.VMEM(weight.shape, BF16),
            pltpu.VMEM((2, RING, RING, *shard), BF16),
            pltpu.VMEM(mlp_partial.shape[1:], BF16),
            pltpu.VMEM(mlp_partial.shape[1:], BF16),
            pltpu.VMEM((*tokens, inner), BF16),
            pltpu.VMEM((2, heads, 2, 4 * rows, HEAD_DIM), F32),
            pltpu.VMEM((*tokens, 3 * inner), BF16),
            pltpu.VMEM((8, 8 * rows), F32),
            pltpu.VMEM((8, 8, 8 * rows), F32),
            *[pltpu.VMEM(other.shape, other.dtype) for other in (attended, *others[:7])],
            pltpu.VMEM((2, RING, RING, *gain_tile), F32),
            pltpu.VMEM((8, inner), F32),
            pltpu.VMEM((8, 2, *gain_tile), F32),
            pltpu.VMEM((2, *shard), BF16),
            pltpu.VMEM((2, *gain_tile), F32),
            pltpu.VMEM((2, 2, *shard), BF16),
            *ring_buffers(rows, width),
            *scatter_buffers(shard[0], shard[1] // 2, BF16),
            *scatter_buffers(shard[0], shard[1] // 2, BF16),
            *scatter_buffers(*shard, BF16),
            *scatter_buffers(*shard, BF16),
            *scatter_buffers(*gain_tile, F32),
            dma_sems(224),
            dma_sems(RING, 4),
            dma_sems(4, 2 * PIECES),
            dma_sems(8),
            dma_sems(8),
            dma_sems(5),
            dma_sems(2, 12),
            dma_sems(2, 12),
            dma_sems(2, 12),
            dma_sems(2, 12),
            dma_sems(2, 12),
        ],
        (own, weight, inputs, mlp_partial, down, attended, *others),
    )


def norm_scale(values):
    return lax.rsqrt(jnp.mean(values * values, axis=-1, keepdims=True) + NORM_EPS)


def norm_back(upstream, values, scales, gain_row):
    scaled_grad = upstream * gain_row
    return scales * scaled_grad - values * scales**3 * jnp.mean(
        scaled_grad * values, axis=-1, keepdims=True
    )


def doc_layout(lengths, group_size):
    positions = jnp.arange(group_size, dtype=jnp.int32)
    doc_ends = jnp.cumsum(lengths)
    passed = (positions[:, None] >= doc_ends[None, :]).astype(jnp.int32)
    segment = jnp.sum(passed, axis=-1)
    begins = jnp.sum(passed * lengths[None, :], axis=-1)
    return (segment, positions - begins)


def rope_tables(offsets):
    frequency = ROPE_BASE ** (-jnp.arange(0, HEAD_DIM, 2).astype(jnp.float32) / HEAD_DIM)
    angles = offsets.astype(jnp.float32)[:, None] * frequency[None, :]
    cosine, sine = jnp.cos(angles), jnp.sin(angles)
    return (
        jnp.concatenate([cosine, cosine], axis=-1),
        jnp.concatenate([sine, sine], axis=-1),
    )


def half_turn(values):
    middle = values.shape[-1] // 2
    return jnp.concatenate([-values[..., middle:], values[..., :middle]], axis=-1)


def rotate(values, cosine_table, sine_table):
    return values * cosine_table + half_turn(values) * sine_table


def unrotate(values, cosine_table, sine_table):
    return values * cosine_table - half_turn(values) * sine_table


def product(left, right):
    return jnp.dot(left, right, preferred_element_type=F32)


def row_product(left, right):
    return lax.dot_general(left, right, (((1,), (1,)), ((), ())), preferred_element_type=F32)


def col_product(left, right):
    return lax.dot_general(left, right, (((0,), (0,)), ((), ())), preferred_element_type=F32)


def adam_update(weights_old, first_old, second_old, gradient, rate, decay):
    first_new = BETA_ONE * first_old + (1.0 - BETA_ONE) * gradient
    second_new = BETA_TWO * second_old + (1.0 - BETA_TWO) * gradient * gradient
    ratio = (
        first_new
        / (1.0 - BETA_ONE**STEP)
        / (jnp.sqrt(second_new / (1.0 - BETA_TWO**STEP)) + ADAM_EPS)
    )
    return (first_new, second_new, weights_old - rate * (ratio + decay * weights_old))


def mlp_adam_kernel(weights, first, second, sums, grad_out, first_out, second_out, new_out):
    half = sums.shape[3]
    for h in range(2):
        part = slice(None), slice(None), slice(h * half, (h + 1) * half)
        gradient = sums[:, h].astype(F32)
        grad_out[part] = gradient
        first_out[part], second_out[part], new_out[part] = adam_update(
            weights[part], first[part], second[part], gradient, WEIGHT_RATE, WEIGHT_DECAY
        )


def mlp_adam(weights, first, second, sums):
    count, rows, columns = weights.shape
    state = pl.BlockSpec((1, rows, columns), lambda m: (m, 0, 0))
    return pl.pallas_call(
        mlp_adam_kernel,
        out_shape=(shape_of(*weights.shape, dtype=F32),) * 4,
        grid=(count,),
        in_specs=[state] * 3 + [pl.BlockSpec((1, *sums.shape[1:]), lambda m: (m, 0, 0, 0))],
        out_specs=(state,) * 4,
        compiler_params=pltpu.CompilerParams(vmem_limit_bytes=VMEM_LIMIT),
    )(weights, first, second, sums)


def attn_adam_kernel(weights, first, second, sums, grad_out, first_out, second_out, new_out):
    inner = weights.shape[2]
    for m in range(weights.shape[0]):
        gradient = sums[0, :, m * inner : (m + 1) * inner].astype(F32)
        grad_out[m] = gradient
        first_out[m], second_out[m], new_out[m] = adam_update(
            weights[m], first[m], second[m], gradient, WEIGHT_RATE, WEIGHT_DECAY
        )


def attn_adam(weights, first, second, sums):
    count, rows, columns = weights.shape
    state = pl.BlockSpec((count, rows, columns // 2), lambda h: (0, 0, h))
    return pl.pallas_call(
        attn_adam_kernel,
        out_shape=(shape_of(*weights.shape, dtype=F32),) * 4,
        grid=(2,),
        in_specs=[state] * 3 + [pl.BlockSpec((1, *sums.shape[1:]), lambda h: (h, 0, 0))],
        out_specs=(state,) * 4,
        compiler_params=pltpu.CompilerParams(vmem_limit_bytes=VMEM_LIMIT),
    )(weights, first, second, sums)


def body(
    hidden_in,
    cotangent,
    doc_lengths,
    attn_weights,
    attn_first,
    attn_second,
    mlp_weights,
    mlp_first,
    mlp_second,
    gains,
    gain_first,
    gain_second,
):
    row_count, model_width = hidden_in.shape
    shard_rows = attn_weights.shape[1]
    heads_width = attn_weights.shape[2] // 2
    hidden_width = mlp_weights.shape[2] // 2
    token_count = 8 * row_count
    block_rows = token_count // 2
    head_count = heads_width // HEAD_DIM
    score_factor = HEAD_DIM ** (-0.5)
    yl, yh, core = (lax.axis_index(a) for a in ("yl", "yh", "c"))

    attn_halves = (
        attn_weights.astype(BF16)
        .reshape(4, shard_rows, 2, heads_width)
        .transpose(2, 1, 0, 3)
        .reshape(2, shard_rows, 4 * heads_width)
    )
    left, right = mlp_weights[:2, :, :hidden_width], mlp_weights[:2, :, hidden_width:]
    mine = jnp.where(yl == 0, left, right).astype(BF16)
    yours = jnp.where(yl == 0, right, left).astype(BF16)
    arrived = lax.ppermute(yours, "yl", [(0, 1), (1, 0)])
    down_halves = mlp_weights[2].astype(BF16).reshape(shard_rows, 2, hidden_width).transpose(1, 0, 2)
    gain_low = lax.reduce_precision(gains, 8, 7)
    odd = lax.axis_index("z") % 2
    gain_tile = jnp.concatenate([jnp.where(odd == 0, gain_low, 0.0), jnp.where(odd == 1, gain_low, 0.0)], axis=1)
    gain_tile = jnp.pad(gain_tile, ((0, 4), (0, 0)))
    theirs = lax.ppermute(doc_lengths, "yl", [(0, 1), (1, 0)])
    lengths = jnp.where(yl == 0, jnp.stack([doc_lengths[0], theirs[0]]), jnp.stack([theirs[0], doc_lengths[0]]))
    _, offsets = jax.vmap(lambda one: doc_layout(one, block_rows))(lengths)
    cosine_table, sine_table = rope_tables(offsets.reshape(-1))
    sine_table = sine_table * jnp.where(jnp.arange(HEAD_DIM) < HEAD_DIM // 2, -1.0, 1.0)
    cosine_table = cosine_table.reshape(2, block_rows, HEAD_DIM)
    sine_table = sine_table.reshape(2, block_rows, HEAD_DIM)
    starts = jnp.broadcast_to((jnp.arange(block_rows) - offsets)[:, :, None], (2, block_rows, HEAD_DIM))

    arrived, cosine_table, sine_table, starts, attn_halves, gain_tile, down_halves = lax.optimization_barrier(
        (arrived, cosine_table, sine_table, starts, attn_halves, gain_tile, down_halves)
    )
    pair = jnp.stack(
        [jnp.where(yl == 0, mine, arrived), jnp.where(yl == 0, arrived, mine)], axis=1
    )
    gate_up = lax.all_gather(pair.reshape(-1, hidden_width), ("x", "z"), tiled=True)
    gate_up = gate_up.reshape(RING, RING, 2, 2, shard_rows, hidden_width)

    (
        attn_proj, mixed, mixed_low, gain_full, head_gains, every_input, attn_all, raw, rotated, values,
        head_scales, attended, down_half, down_pair,
    ) = attention_forward(
        1, hidden_in, attn_halves, down_halves, gain_tile, cosine_table, sine_table, starts
    )
    attn_all = flat(attn_all)
    hidden_out, d_mixed, d_proj, token_gains, mlp_partial, down_sum = mlp(
        2, mixed_low, gate_up, down_half, down_pair, mixed, cotangent, attn_proj, gain_full
    )
    input_sum, attn_sum, gain_sum, mlp_sum = attention_backward(
        3,
        d_proj,
        attn_all,
        every_input,
        mlp_partial,
        down_sum,
        attended,
        raw,
        rotated,
        values,
        head_scales,
        cosine_table,
        sine_table,
        starts,
        head_gains,
        token_gains,
    )

    gain_sum = lax.dynamic_index_in_dim(gain_sum, yl, 0, keepdims=False)[:4]
    gain_grad = lax.dynamic_slice_in_dim(gain_sum, lax.axis_index("z") * shard_rows, shard_rows, axis=1)
    input_grad = d_mixed + input_sum
    attn_grad, attn_first_new, attn_second_new, attn_new = attn_adam(
        attn_weights, attn_first, attn_second, attn_sum
    )
    mlp_grad, mlp_first_new, mlp_second_new, mlp_new = mlp_adam(
        mlp_weights, mlp_first, mlp_second, mlp_sum
    )
    gain_first_new, gain_second_new, gain_new = adam_update(
        gains, gain_first, gain_second, gain_grad, GAIN_RATE, 0.0
    )
    return (
        hidden_out,
        input_grad,
        attn_grad,
        attn_first_new,
        attn_second_new,
        attn_new,
        mlp_grad,
        mlp_first_new,
        mlp_second_new,
        mlp_new,
        gain_grad,
        gain_first_new,
        gain_second_new,
        gain_new,
    )


def solution(mesh):
    split = Mesh(mesh.devices.reshape(2, 4, 4, 2, 2), EVERY)
    tokens, shards, rows = P(EVERY, None), P(None, DP, TENSOR), P(None, DP)
    return jax.shard_map(
        body,
        mesh=split,
        in_specs=(tokens, tokens, P(DP, None), *[shards] * 6, *[rows] * 3),
        out_specs=(tokens, tokens, *[shards] * 8, *[rows] * 4),
        check_vma=False,
    )
```

```python
import functools

import jax
import jax.numpy as jnp
from jax import lax
from jax.experimental import pallas as pl
from jax.experimental.pallas import tpu as pltpu
from jax.sharding import Mesh
from jax.sharding import PartitionSpec as P

HEAD_DIM = 128
STEP = 10
DP = ("yl", "x", "z")
TENSOR = ("yh", "c")
EVERY = ("yl", "x", "z", "yh", "c")
RING = 4
MESH = pl.DeviceIdType.MESH

NORM_EPS = 1e-06
ROPE_BASE = 500000.0
BETA_ONE = 0.9
BETA_TWO = 0.95
ADAM_EPS = 1e-08
WEIGHT_RATE = 0.03
GAIN_RATE = 1.0
WEIGHT_DECAY = 0.1

BF16 = jnp.bfloat16
F32 = jnp.float32
IN_VMEM = pl.BlockSpec(memory_space=pltpu.VMEM)
ANYWHERE = pl.BlockSpec(memory_space=pl.ANY)
VMEM_LIMIT = 60 * 1024 * 1024


class Place:
    def __init__(self):
        self.x, self.z, self.c = (lax.axis_index(a) for a in ("x", "z", "c"))
        self.yl, self.yh = (lax.axis_index(a) for a in ("yl", "yh"))
        self.y = self.yh * 2 + self.yl

    def at(self, axis, step):
        if axis == "y":
            there = (self.y + step + RING) % RING
            return {"yl": there % 2, "yh": there // 2}
        if axis == "c":
            return {"c": 1 - self.c}
        return {axis: (getattr(self, axis) + step + RING) % RING}

    def shift(self, axis, step):
        return (getattr(self, axis) + step + RING) % RING


def greet(devices):
    barrier = pltpu.get_barrier_semaphore()
    for device in devices:
        pl.semaphore_signal(barrier, inc=1, device_id=device, device_id_type=MESH)
    pl.semaphore_wait(barrier, len(devices))


def greet_all(place, axes):
    devices = []
    for axis in axes:
        devices += [place.at(axis, 1)] if axis == "c" else [place.at(axis, 1), place.at(axis, -1)]
    greet(devices)


class Sender:
    def __init__(self, sems):
        self.sems, self.open = sems, []

    def push(self, src, dst, recv_sem, device):
        copy = pltpu.make_async_remote_copy(
            src_ref=src,
            dst_ref=dst,
            send_sem=self.sems.at[len(self.open)],
            recv_sem=recv_sem,
            device_id=device,
            device_id_type=MESH,
        )
        copy.start()
        self.open.append(copy.wait_send)
        return len(self.open) - 1

    def settle(self, numbers):
        for number in numbers:
            self.open[number]()
            self.open[number] = lambda: None

    def keep(self, src, dst):
        copy = pltpu.make_async_copy(src, dst, self.sems.at[len(self.open)])
        copy.start()
        self.open.append(copy.wait)

    def keep_first(self, src, dst):
        copy = pltpu.make_async_copy(src, dst, self.sems.at[len(self.open)])
        copy.start()
        self.open.append(lambda: None)
        return copy

    def arrived(self, dst, recv_sem, device):
        pltpu.make_async_remote_copy(
            src_ref=dst,
            dst_ref=dst,
            send_sem=self.sems.at[0],
            recv_sem=recv_sem,
            device_id=device,
            device_id_type=MESH,
        ).wait_recv()

    def finish(self):
        for wait in self.open:
            wait()


def take_turns(tasks):
    tasks = list(tasks)
    while tasks:
        for task in list(tasks):
            if next(task, "done") == "done":
                tasks.remove(task)


WHOLE, LOW, HIGH = 0, 1, 2
PIECES = 4


def part_of(ref, part, cut):
    rows = ref.shape[-2]
    if part == WHOLE:
        return ref
    return ref.at[pl.ds(0, cut)] if part == LOW else ref.at[pl.ds(cut, rows - cut)]


def plane_gather(place, sender, sems, out, cut):
    rows = out.shape[-2]
    axes = (("x", "z"), ("z", "x"))

    def piece(half, dp, dq):
        p, q = (place.shift(a, d) for a, d in zip(axes[half], (dp, dq)))
        return out.at[half, p, q] if half == 0 else out.at[half, q, p]

    def parts(part):
        if part == WHOLE:
            return True
        return cut > 0 if part == LOW else cut < rows

    def send(half, dp, dq, part, along, step):
        if parts(part):
            ref = part_of(piece(half, dp, dq), part, cut)
            sp, sq = ((dp - step) % RING, dq % RING) if along == 0 else (dp % RING, (dq - step) % RING)
            sender.push(ref, ref, sems.at[half, sp, sq, part], place.at(axes[half][along], step))

    def wait(half, dp, dq, part):
        if parts(part):
            ref = part_of(piece(half, dp, dq), part, cut)
            sender.arrived(ref, sems.at[half, dp % RING, dq % RING, part], place.at("x", 1))

    both = (0, 1)
    for half in both:
        for step in (1, -1):
            send(half, 0, 0, WHOLE, 0, step)
    for half in both:
        for step in (1, -1):
            send(half, 0, 0, WHOLE, 1, step)
    yield
    for step, part in ((1, LOW), (-1, HIGH)):
        for half in both:
            wait(half, -step, 0, WHOLE)
            send(half, -step, 0, part, 0, step)
            for side in (1, -1):
                send(half, -step, 0, WHOLE, 1, side)
    yield
    for half in both:
        for step, part in ((1, LOW), (-1, HIGH)):
            wait(half, 0, -step, WHOLE)
            send(half, 0, -step, part, 1, step)
    yield
    for half in both:
        wait(half, 2, 0, LOW)
        wait(half, 2, 0, HIGH)
        for side in (1, -1):
            send(half, 2, 0, WHOLE, 1, side)
    yield
    for dp in (-1, 1, 2):
        for half in both:
            for step, part in ((1, LOW), (-1, HIGH)):
                wait(half, dp, -step, WHOLE)
                send(half, dp, -step, part, 1, step)
        yield
    for dp in (0, -1, 1, 2):
        for half in both:
            wait(half, dp, 2, LOW)
            wait(half, dp, 2, HIGH)


class RingGather:
    def __init__(self, place, sender, sems, own, out):
        self.place, self.sender, self.sems, self.own, self.out = place, sender, sems, own, out
        self.rows = own.shape[0]
        self.other = place.at("c", 1)
        self.begun, self.forwarded = [], []

    def piece(self, dy, core, part=WHOLE):
        y = self.place.shift("y", dy)
        half = self.rows // 2
        start, size = {WHOLE: (0, self.rows), LOW: (0, half), HIGH: (half, half)}[part]
        return self.out.at[y % 2, y // 2, pl.ds(pl.multiple_of(core * self.rows + start, 16), size)]

    def begin(self):
        place, mine = self.place, self.piece(0, self.place.c)
        for step in (1, -1):
            number = self.sender.push(self.own, mine, self.sems.at[(-step) % RING, WHOLE], place.at("y", step))
            self.begun.append(number)
        self.begun.append(self.sender.push(self.own, mine, self.sems.at[0, 3], self.other))
        self.kept = self.sender.keep_first(self.own, mine)

    def relay(self):
        for step, part in ((1, LOW), (-1, HIGH)):
            ref = self.piece(-step, self.place.c)
            self.sender.arrived(ref, self.sems.at[(-step) % RING, WHOLE], self.other)
            half = self.piece(-step, self.place.c, part)
            self.forwarded += [
                self.sender.push(half, half, self.sems.at[2, part], self.place.at("y", step)),
                self.sender.push(ref, ref, self.sems.at[(-step) % RING, 3], self.other),
            ]

    def relay_far(self):
        for part in (LOW, HIGH):
            self.sender.arrived(self.piece(2, self.place.c, part), self.sems.at[2, part], self.other)
        ref = self.piece(2, self.place.c)
        self.forwarded += [self.sender.push(ref, ref, self.sems.at[2, 3], self.other)]

    def ready(self, dy):
        if dy == 0:
            self.kept.wait()
        self.sender.arrived(self.piece(dy, 1 - self.place.c), self.sems.at[dy % RING, 3], self.other)


def ring_gather(place, sender, sems, own, out):
    gather = RingGather(place, sender, sems, own, out)
    gather.begin()
    yield
    gather.relay()
    yield
    gather.relay_far()
    yield
    for dy in (0, 1, -1, 2):
        gather.ready(dy)


def add_rows(out, terms, rows):
    def step(i, carry):
        window = pl.ds(pl.multiple_of(i * 16, 16), 16)
        total = terms[0][window, :].astype(F32)
        for term in terms[1:]:
            total = total + term[window, :].astype(F32)
        out[window, :] = total.astype(out.dtype)
        return carry

    lax.fori_loop(0, rows // 16, step, 0)


class RingSum:
    def __init__(self, place, sender, sems, partial, kept, from_core, hop, last):
        self.place, self.sender, self.sems, self.partial = place, sender, sems, partial
        self.kept, self.from_core, self.hop, self.last = kept, from_core, hop, last
        self.rows = kept.shape[1]
        self.low, self.high = pl.ds(0, self.rows // 2), pl.ds(self.rows // 2, self.rows // 2)
        self.other = place.at("c", 1)

    def mine(self, dy, core):
        y = self.place.shift("y", dy)
        return self.partial.at[y % 2, y // 2, pl.ds(pl.multiple_of(core * self.rows, 16), self.rows)]

    def offer(self, dy):
        slot = dy % RING
        self.sender.push(
            self.mine(dy, 1 - self.place.c), self.from_core.at[slot], self.sems.at[0, slot], self.other
        )

    def pieces(self):
        columns = self.kept.shape[2]
        return [pl.ds(p * columns // PIECES, columns // PIECES) for p in range(PIECES)]

    def collect(self, dy):
        slot = dy % RING
        kept, low, high = self.kept.at[slot], self.low, self.high
        self.sender.arrived(self.from_core.at[slot], self.sems.at[0, slot], self.other)
        if dy == 0:
            return
        up, down = self.place.at("y", 1), self.place.at("y", -1)
        mine = self.mine(dy, self.place.c)
        if dy == 2:
            for p, columns in enumerate(self.pieces()):
                add_rows(kept.at[:, columns], (mine.at[:, columns], self.from_core.at[slot, :, columns]), self.rows)
                self.sender.push(kept.at[low, columns], self.hop.at[0, :, columns], self.sems.at[1, p], up)
                self.sender.push(
                    kept.at[high, columns], self.hop.at[1, :, columns], self.sems.at[1, PIECES + p], down
                )
            return
        add_rows(kept, (mine, self.from_core.at[slot]), self.rows)
        if dy == 1:
            self.sender.push(kept.at[high], self.last.at[0, high], self.sems.at[2, 1], up)
        else:
            self.sender.push(kept.at[low], self.last.at[1, low], self.sems.at[2, 2], down)

    def relay(self):
        for p, columns in enumerate(self.pieces()):
            for k, slot, part, step in ((0, 1, self.low, 1), (1, 3, self.high, -1)):
                number = k * PIECES + p
                self.sender.arrived(self.hop.at[k, :, columns], self.sems.at[1, number], self.other)
                rows = self.kept.at[slot, part, columns]
                add_rows(rows, (rows, self.hop.at[k, :, columns]), self.rows // 2)
                self.sender.push(
                    rows, self.last.at[k, part, columns], self.sems.at[3, number], self.place.at("y", step)
                )

    def finish(self, out, *others):
        self.sender.arrived(self.last.at[0, self.high], self.sems.at[2, 1], self.other)
        self.sender.arrived(self.last.at[1, self.low], self.sems.at[2, 2], self.other)
        mine = self.mine(0, self.place.c)
        for p, columns in enumerate(self.pieces()):
            for k, part in ((0, self.low), (1, self.high)):
                self.sender.arrived(
                    self.last.at[k, part, columns], self.sems.at[3, k * PIECES + p], self.other
                )
            terms = (mine, self.from_core.at[0], self.last.at[0], self.last.at[1], *others)
            add_rows(out.at[:, columns], [term.at[:, columns] for term in terms], self.rows)


def plane_scatter(place, sender, sems, partial, done, cut, bufs):
    rows = partial.shape[-2]
    hop, last, middle, hop2, last2 = bufs
    low, high = pl.ds(0, cut), pl.ds(cut, rows - cut)
    axes = (("z", "x"), ("x", "z"))
    two_parts = cut < rows
    both = (0, 1)
    other = place.at("x", 1)

    def row(half, du, window):
        u = place.shift(axes[half][0], du)
        return partial.at[half, :, u, window] if half == 0 else partial.at[half, u, :, window]

    def line(half, du, v):
        u = place.shift(axes[half][0], du)
        return partial.at[half, v, u] if half == 0 else partial.at[half, u, v]

    def add(out, terms, count):
        if count % 16:
            total = terms[0][...].astype(F32)
            for term in terms[1:]:
                total = total + term[...].astype(F32)
            out[...] = total.astype(out.dtype)
        else:
            add_rows(out, terms, count)

    for half in both:
        u = axes[half][0]
        sender.push(row(half, 2, low), hop.at[half, 0], sems.at[half, 0], place.at(u, 1))
        if two_parts:
            sender.push(row(half, 2, high), hop.at[half, 1], sems.at[half, 1], place.at(u, -1))
    for half in both:
        u = axes[half][0]
        if two_parts:
            sender.push(row(half, 1, high), last.at[half, 0, :, high], sems.at[half, 2], place.at(u, 1))
        sender.push(row(half, -1, low), last.at[half, 1, :, low], sems.at[half, 3], place.at(u, -1))
    yield
    for half in both:
        u = axes[half][0]
        sender.arrived(hop.at[half, 0], sems.at[half, 0], other)
        for v in range(RING):
            add(hop.at[half, 0, v], (line(half, 1, v).at[low], hop.at[half, 0, v]), cut)
        sender.push(hop.at[half, 0], last.at[half, 0, :, low], sems.at[half, 4], place.at(u, 1))
        if two_parts:
            sender.arrived(hop.at[half, 1], sems.at[half, 1], other)
            for v in range(RING):
                add(
                    hop.at[half, 1, v],
                    (line(half, -1, v).at[high], hop.at[half, 1, v]),
                    rows - cut,
                )
            sender.push(
                hop.at[half, 1], last.at[half, 1, :, high], sems.at[half, 5], place.at(u, -1)
            )
    yield
    for half in both:
        v_axis = axes[half][1]
        if two_parts:
            sender.arrived(last.at[half, 0, :, high], sems.at[half, 2], other)
        sender.arrived(last.at[half, 1, :, low], sems.at[half, 3], other)
        sender.arrived(last.at[half, 0, :, low], sems.at[half, 4], other)
        if two_parts:
            sender.arrived(last.at[half, 1, :, high], sems.at[half, 5], other)
        for dv in (2, 1, -1, 0):
            v = place.shift(v_axis, dv)
            terms = (line(half, 0, v), last.at[half, 0, v], last.at[half, 1, v])
            add(middle.at[half, dv % RING], terms, rows)
            if dv == 2:
                sender.push(
                    middle.at[half, 2, low], hop2.at[half, 0], sems.at[half, 6], place.at(v_axis, 1)
                )
                if two_parts:
                    sender.push(
                        middle.at[half, 2, high],
                        hop2.at[half, 1],
                        sems.at[half, 7],
                        place.at(v_axis, -1),
                    )
            elif dv == 1 and two_parts:
                sender.push(
                    middle.at[half, 1, high], last2.at[half, 0, high], sems.at[half, 8], place.at(v_axis, 1)
                )
            elif dv == -1:
                sender.push(
                    middle.at[half, 3, low], last2.at[half, 1, low], sems.at[half, 9], place.at(v_axis, -1)
                )
    yield
    for half in both:
        v_axis = axes[half][1]
        sender.arrived(hop2.at[half, 0], sems.at[half, 6], other)
        add(hop2.at[half, 0], (middle.at[half, 1, low], hop2.at[half, 0]), cut)
        sender.push(
            hop2.at[half, 0], last2.at[half, 0, low], sems.at[half, 10], place.at(v_axis, 1)
        )
        if two_parts:
            sender.arrived(hop2.at[half, 1], sems.at[half, 7], other)
            add(hop2.at[half, 1], (middle.at[half, 3, high], hop2.at[half, 1]), rows - cut)
            sender.push(
                hop2.at[half, 1], last2.at[half, 1, high], sems.at[half, 11], place.at(v_axis, -1)
            )
    yield
    for half in both:
        if two_parts:
            sender.arrived(last2.at[half, 0, high], sems.at[half, 8], other)
        sender.arrived(last2.at[half, 1, low], sems.at[half, 9], other)
        sender.arrived(last2.at[half, 0, low], sems.at[half, 10], other)
        if two_parts:
            sender.arrived(last2.at[half, 1, high], sems.at[half, 11], other)
        add(done.at[half], (middle.at[half, 0], last2.at[half, 0], last2.at[half, 1]), rows)


def scatter_buffers(rows, columns, dtype):
    cut = rows // 2 if dtype == BF16 else rows
    return [
        pltpu.VMEM((2, 2, RING, cut, columns), dtype),
        pltpu.VMEM((2, 2, RING, rows, columns), dtype),
        pltpu.VMEM((2, RING, rows, columns), dtype),
        pltpu.VMEM((2, 2, cut, columns), dtype),
        pltpu.VMEM((2, 2, rows, columns), dtype),
    ]


def ring_buffers(rows, columns):
    return [
        pltpu.VMEM((RING, rows, columns), BF16),
        pltpu.VMEM((RING, rows, columns), BF16),
        pltpu.VMEM((2, rows // 2, columns), BF16),
        pltpu.VMEM((2, rows, columns), BF16),
    ]


def dma_sems(*shape):
    return pltpu.SemaphoreType.DMA(shape)


def shape_of(*shape, dtype=BF16):
    return jax.ShapeDtypeStruct(shape, dtype)


def call(kernel, number, out_shape, in_specs, out_specs, scratch, args):
    return pl.pallas_call(
        kernel,
        out_shape=out_shape,
        in_specs=in_specs,
        out_specs=out_specs,
        scratch_shapes=scratch,
        compiler_params=pltpu.CompilerParams(
            collective_id=number, has_side_effects=True, vmem_limit_bytes=VMEM_LIMIT
        ),
    )(*args)


NN = (((1,), (0,)), ((), ()))
NT = (((1,), (1,)), ((), ()))
TN = (((0,), (0,)), ((), ()))


def dot(left, right, dims=NN):
    return lax.dot_general(left, right, dims, preferred_element_type=F32)


def in_tiles(width, tile, work):
    for n in range(width // tile):
        work(pl.ds(n * tile, tile))


def refs_of(refs, *counts):
    refs, out = list(refs), []
    for n in counts:
        out.append(refs[:n])
        del refs[:n]
    return out


def by_rows(count, work):
    def step(i, carry):
        work(pl.ds(pl.multiple_of(i * 16, 16), 16))
        return carry

    lax.fori_loop(0, count // 16, step, 0)


def load_weights(sender, source, targets):
    copies = []
    for k, target in targets:
        for yl in range(2):
            copies.append(sender.keep_first(source.at[:, :, k, yl], target.at[yl]))
    return copies


def rows_of(weight, window):
    if len(weight.shape) == 2:
        return weight[window, :]
    run = weight.shape[2] * weight.shape[3]
    first, count = window.start // run, window.size // run
    block = weight[first // RING, pl.ds(first % RING, count), :, :, :]
    return block.reshape(window.size, weight.shape[4])


def columns_of(weight, window):
    block = weight[:, :, :, :, window]
    return block.reshape(-1, window.size)


def mlp_kernel(
    own, gate_up, down, down_pair, mixed_in, cotangent_in, proj_in, gain_rows, hidden_out, d_mixed_out, d_proj_out,
    gains_out, grads_out, down_out, *refs
):
    (
        (x_all, d_all, w_gate, w_up, w_down, gate, up, act, partial, down_partial, tiles),
        (down_proj, mixed, cotangent, proj),
        ring,
        first_buffers,
        second_buffers,
        (sends, gather_sems, sum_sems, gather_sems2, sum_sems2, plane, plane2, tile_sems, plane3),
    ) = refs_of(refs, 11, 4, 4, 5, 5, 9)
    d_own = d_proj_out
    d_gate, d_up = gate, up
    place = Place()
    sender = Sender(sends)
    loads = load_weights(sender, gate_up, ((0, w_gate), (1, w_up)))
    early = down.shape[4]
    w_rest = w_down.at[:, :, :, :, pl.ds(early, down_pair.shape[2])]
    load_pair = sender.keep_first(down_pair, w_rest.at[:, place.x, place.z])
    load_down = sender.keep_first(down, w_down.at[:, :, :, :, pl.ds(0, early)])
    pairs = ((mixed_in, mixed), (cotangent_in, cotangent), (proj_in, proj))
    later = [sender.keep_first(source, target) for source, target in pairs]
    greet_all(place, ("x", "z", "y", "c"))
    gather = RingGather(place, sender, gather_sems, own, x_all)
    total = RingSum(place, sender, sum_sems, partial, *ring)
    gather.begin()
    load_pair.wait()
    rest = plane_gather(place, sender, plane3, w_rest, w_rest.shape[3] // 2)
    next(rest)
    for copy in loads:
        copy.wait()
    load_down.wait()
    tile = 512

    def where(dy):
        y = place.shift("y", dy)
        return y % 2, y // 2

    def at_chip(dy):
        at = where(dy)
        return (*at, slice(None)), (2 * rows, hidden_width)

    def at_neighbours(_):
        return (1 - place.yl, slice(None), slice(None)), (4 * rows, hidden_width)

    rows, hidden_width = own.shape[0], act.shape[-1]

    def forward_hidden(index, shape):
        count = shape[0]

        def hidden(columns):
            tokens = x_all[(*index, slice(None))].reshape(count, -1)
            g = dot(tokens, columns_of(w_gate, columns))
            u = dot(tokens, columns_of(w_up, columns))
            here = (*index, columns)
            held = act[here].shape
            gate[here], up[here] = g.astype(BF16).reshape(held), u.astype(BF16).reshape(held)
            act[here] = (g * jax.nn.sigmoid(g) * u).astype(BF16).reshape(held)

        in_tiles(hidden_width, tile, hidden)

    def forward_project(index, shape):
        def project(columns):
            left = act[(*index, slice(None))].reshape(shape)
            value = dot(left, rows_of(w_down, columns), NT).astype(BF16)
            here = (*index, columns)
            partial[here] = value.reshape(partial[here].shape)

        in_tiles(partial.shape[-1], tile, project)

    def in_turn(gather, total, work, before_far=lambda: None):
        gather.ready(0)
        work(*at_chip(0))
        total.offer(0)
        gather.relay()
        gather.ready(1)
        gather.ready(-1)
        work(*at_neighbours(0))
        total.offer(1)
        total.offer(-1)
        gather.relay_far()
        total.collect(1)
        total.collect(-1)
        gather.ready(2)
        before_far()
        work(*at_chip(2))
        total.offer(2)

    gather.ready(0)
    forward_hidden(*at_chip(0))
    for _ in range(4):
        next(rest)
    gather.relay()
    next(rest)
    gather.ready(1)
    gather.ready(-1)
    next(rest)
    forward_hidden(*at_neighbours(0))
    take_turns((rest,))
    gather.relay_far()
    forward_project(*at_neighbours(0))
    total.offer(1)
    total.offer(-1)
    forward_project(*at_chip(0))
    total.offer(0)
    total.collect(1)
    total.collect(-1)
    gather.ready(2)
    forward_hidden(*at_chip(2))
    forward_project(*at_chip(2))
    total.offer(2)
    total.collect(2)
    total.collect(0)
    total.relay()
    total.finish(down_proj)
    for copy in later:
        copy.wait()
    sender.settle(range(len(sender.open)))
    gains_out[...] = jnp.zeros_like(gains_out)

    def output_norm(rows):
        value, upstream, gain = down_proj[rows, :], cotangent[rows, :].astype(F32), gain_rows[3:4, :]
        scale = norm_scale(value)
        hidden_out[rows, :] = (mixed[rows, :] + value * scale * gain).astype(BF16)
        d_own[rows, :] = norm_back(upstream, value, scale, gain).astype(BF16)
        gains_out[1:2, :] += jnp.sum(upstream * value * scale, axis=0, keepdims=True)

    by_rows(down_proj.shape[0], output_norm)

    gather = RingGather(place, sender, gather_sems2, d_own, d_all)
    total = RingSum(place, sender, sum_sems2, partial, *ring)
    gather.begin()

    def backward(index, shape):
        count = shape[0]

        def hidden(columns):
            d_act = dot(d_all[(*index, slice(None))].reshape(count, -1), columns_of(w_down, columns))
            here = (*index, columns)
            held = gate[here].shape
            g, u = gate[here].astype(F32).reshape(d_act.shape), up[here].astype(F32).reshape(d_act.shape)
            s = jax.nn.sigmoid(g)
            d_gate[here] = (d_act * u * s * (1.0 + g * (1.0 - s))).astype(BF16).reshape(held)
            d_up[here] = (d_act * g * s).astype(BF16).reshape(held)

        in_tiles(hidden_width, tile, hidden)

        def back(columns):
            whole = (*index, slice(None))
            value = dot(d_gate[whole].reshape(shape), rows_of(w_gate, columns), NT)
            value = value + dot(d_up[whole].reshape(shape), rows_of(w_up, columns), NT)
            here = (*index, columns)
            partial[here] = value.astype(BF16).reshape(partial[here].shape)

        in_tiles(partial.shape[-1], tile, back)

    block = 4 * down_partial.shape[3]

    def all_rows(ref, columns=slice(None)):
        value = ref[:, :, :, columns]
        return value.reshape(-1, value.shape[-1])

    def sent(slot, k, i):
        return pltpu.make_async_copy(
            tiles.at[slot, k], grads_out.at[k, i // RING, i % RING], tile_sems.at[slot, k]
        )

    def weight_grads(begin, end):
        for i in range(begin, end):
            slot = i % 2
            for k, right in enumerate((d_gate, d_up)):
                if i >= 2:
                    sent(slot, k, i - 2).wait()
                value = dot(all_rows(x_all, pl.ds(i * block, block)), all_rows(right), TN)
                tiles[slot, k] = value.astype(BF16).reshape(tiles.shape[2:])
                sent(slot, k, i).start()

    half = act.shape[-1] // 2

    def down_grad(p, sems, buffers):
        columns = pl.ds(p * half, half)
        right = all_rows(act, columns)
        for i in range(2 * RING):
            value = dot(all_rows(d_all, pl.ds(i * block, block)), right, TN).astype(BF16)
            down_partial[i // RING, i % RING, :, :, columns] = value.reshape(*down_partial.shape[2:4], half)
        task = plane_scatter(
            place,
            sender,
            sems,
            down_partial.at[:, :, :, :, columns],
            down_out.at[:, :, columns],
            down_partial.shape[3] // 2,
            buffers,
        )
        next(task)
        return task

    tasks = []

    def down_grads():
        tasks.append(down_grad(0, plane, first_buffers))
        tasks.append(down_grad(1, plane2, second_buffers))

    in_turn(gather, total, backward, down_grads)
    task, task2 = tasks
    total.collect(2)
    next(task)
    total.collect(0)
    next(task2)
    weight_grads(0, 3)
    total.relay()
    weight_grads(3, 4)
    next(task)
    weight_grads(4, 6)
    next(task2)
    weight_grads(6, 7)
    next(task)
    weight_grads(7, 8)
    next(task2)
    total.finish(d_mixed_out)
    sender.settle(gather.begun)

    def attention_norm(rows):
        value, gain = proj[rows, :], gain_rows[2:3, :]
        d_mixed = cotangent[rows, :].astype(F32) + d_mixed_out[rows, :]
        d_mixed_out[rows, :] = d_mixed
        scale = norm_scale(value)
        d_proj_out[rows, :] = norm_back(d_mixed, value, scale, gain).astype(BF16)
        gains_out[0:1, :] += jnp.sum(d_mixed * value * scale, axis=0, keepdims=True)

    by_rows(down_proj.shape[0], attention_norm)
    take_turns((task, task2))
    for i in (6, 7):
        for k in range(2):
            sent(i % 2, k, i).wait()
    sender.finish()


def mlp(number, own, gate_up, down, down_pair, mixed, cotangent, proj, gain_rows):
    rows, width = own.shape
    piece, hidden = gate_up.shape[-2:]
    tokens = (2, 2, 2 * rows)
    weight = pltpu.VMEM((2, RING, RING, piece, hidden), BF16)
    wide, narrow = pltpu.VMEM((*tokens, width), BF16), pltpu.VMEM((*tokens, hidden), BF16)
    return call(
        mlp_kernel,
        number,
        (
            shape_of(rows, width),
            shape_of(rows, width, dtype=F32),
            shape_of(rows, width),
            shape_of(8, width, dtype=F32),
            shape_of(2, 2, RING, RING, piece, hidden),
            shape_of(2, piece, hidden),
        ),
        [ANYWHERE] * 7 + [IN_VMEM],
        (IN_VMEM,) * 4 + (ANYWHERE, IN_VMEM),
        [
            wide,
            wide,
            *[weight] * 3,
            *[narrow] * 3,
            wide,
            weight,
            pltpu.VMEM((2, 2, RING, piece, hidden), BF16),
            pltpu.VMEM((rows, width), F32),
            pltpu.VMEM((rows, width), F32),
            pltpu.VMEM((rows, width), BF16),
            pltpu.VMEM((rows, width), F32),
            *ring_buffers(rows, width),
            *scatter_buffers(piece, hidden // 2, BF16),
            *scatter_buffers(piece, hidden // 2, BF16),
            dma_sems(176),
            dma_sems(RING, 4),
            dma_sems(4, 2 * PIECES),
            dma_sems(RING, 4),
            dma_sems(4, 2 * PIECES),
            dma_sems(2, 12),
            dma_sems(2, 12),
            dma_sems(2, 2),
            dma_sems(2, RING, RING, 3),
        ],
        (own, gate_up, down, down_pair, mixed, cotangent, proj, gain_rows),
    )


def ring_product(place, total, values, weight, partial, others, before_near=lambda: None):
    def compute(dy):
        y = place.shift("y", dy)
        at = (y % 2, y // 2)

        def tile(columns):
            partial[(*at, slice(None), columns)] = dot(values[at], rows_of(weight, columns), NT).astype(BF16)

        in_tiles(partial.shape[-1], 512, tile)
        total.offer(dy)

    compute(2)
    before_near()
    compute(1)
    total.collect(2)
    compute(-1)
    total.collect(1)
    compute(0)
    total.collect(-1)
    total.collect(0)
    for task in others:
        next(task)
    total.relay()


def flat(weight):
    return weight.reshape(-1, weight.shape[-1])


def exact(left, right, dims):
    return lax.dot_general(
        left, right, dims, precision=lax.Precision.HIGHEST, preferred_element_type=F32
    )


def half_roll(values):
    return pltpu.roll(values, HEAD_DIM // 2, 1)


def near_devices(place):
    return [place.at(axis, step) for axis in ("x", "z") for step in (1, -1)]


class Octet:
    peers = [(dy, dc) for dy in (0, 1, 3, 2) for dc in (0, 1) if dy or dc]

    def __init__(self, place, sender, own, slots, sems):
        self.place, self.sender, self.own, self.slots, self.sems = place, sender, own, slots, sems

    @staticmethod
    def device(place, dy, dc):
        y = place.shift("y", dy)
        return {"yl": y % 2, "yh": y // 2, "c": (place.c + dc) % 2}

    def send(self):
        for dy, dc in self.peers:
            slot = ((RING - dy) % RING) * 2 + dc
            device = self.device(self.place, dy, dc)
            self.sender.push(self.own, self.slots.at[slot], self.sems.at[slot], device)

    def total(self):
        for dy, dc in self.peers:
            slot = dy * 2 + dc
            self.sender.arrived(self.slots.at[slot], self.sems.at[slot], self.device(self.place, dy, dc))
        value = self.own[...]
        for dy, dc in self.peers:
            value = value + self.slots[dy * 2 + dc]
        return value


def one_hot_rows(k):
    return (lax.broadcasted_iota(jnp.int32, (8, HEAD_DIM), 0) == k).astype(F32)


def masked(scores, starts, i):
    tile, count = scores.shape
    keys = lax.broadcasted_iota(jnp.int32, (tile, count), 1)
    queries = lax.broadcasted_iota(jnp.int32, (tile, count), 0) + i * tile
    return jnp.where((keys >= starts) & (keys <= queries), scores, -1e30)


def softmax(scores):
    exponent = jnp.exp(scores - jnp.max(scores, axis=-1, keepdims=True))
    return exponent / jnp.sum(exponent, axis=-1, keepdims=True)


def attention_forward_kernel(
    own, attn, down, gain, cosine_in, sine_in, starts_in, proj_out, mixed_out, low_out, gain_rows, head_out, x_out,
    weight_out, raw_out, rot_out, value_out, scale_out, attended_out, down_out, pair_out, *refs
):
    (
        (x_all, weight, raw, rot, values, scales, attended, partial, sums, slots, down_all, gain_all),
        (cosine, sine, starts, hidden),
        ring,
        (sends, gather_sems, sum_sems, octet_sems, attn_plane, gain_plane, plane, swap),
    ) = refs_of(refs, 12, 4, 4, 8)
    place = Place()
    sender = Sender(sends)
    _, heads, _, block_rows, _ = raw.shape
    inner = heads * HEAD_DIM
    tile = block_rows // 2
    pairs = ((cosine_in, cosine), (sine_in, sine), (starts_in, starts), (own, hidden))
    later = [sender.keep_first(source, target) for source, target in pairs]
    partner = {"yl": 1 - place.yl}
    me, you = place.yl, 1 - place.yl
    half = down_all.shape[4]
    early, later_half = pl.ds(0, half), pl.ds(half, half)
    shards = ((attn, weight), (gain, gain_all), (down.at[:, :, early], down_all))
    mine = [
        sender.keep_first(source if k == 1 else source.at[me], target.at[me, place.x, place.z])
        for k, (source, target) in enumerate(shards)
    ]
    greet(near_devices(place) + [Octet.device(place, *peer) for peer in Octet.peers])
    for k, (source, target) in enumerate(shards[:2]):
        sender.push(
            source if k == 1 else source.at[you], target.at[me, place.x, place.z], swap.at[k], partner
        )
    gather = RingGather(place, sender, gather_sems, own, x_all)
    gather.begin()
    for copy in mine:
        copy.wait()
    for k, (_, target) in enumerate(shards[:2]):
        sender.arrived(target.at[you, place.x, place.z], swap.at[k], partner)
    attn_task = plane_gather(place, sender, attn_plane, weight, weight.shape[3] // 2)
    gain_task = plane_gather(place, sender, gain_plane, gain_all, gain_all.shape[3])
    next(attn_task)
    next(gain_task)
    sender.push(down.at[you, :, early], down_all.at[me, place.x, place.z], swap.at[2], partner)
    sender.push(down.at[you, :, later_half], pair_out.at[me], swap.at[3], partner)
    sender.keep(down.at[me, :, later_half], pair_out.at[me])

    def gather_all():
        gather.relay()
        yield
        gather.relay_far()
        yield
        for dy in (0, 1, -1, 2):
            gather.ready(dy)

    take_turns((gain_task, attn_task, gather_all()))
    sender.keep(x_all, x_out)
    sender.keep(weight, weight_out)
    for yl in range(2):
        for x in range(RING):
            for h in range(2):
                lanes = pl.ds(((yl * RING + x) * 2 + h) * HEAD_DIM, HEAD_DIM)
                gain_rows[:, lanes] = gain_all[yl, x, 2 * h] + gain_all[yl, x, 2 * h + 1]
    first_column = (place.yh * 2 + place.c) * (2 * inner) + place.yl * inner

    def head_gain(k, h):
        start = pl.multiple_of(first_column + h * HEAD_DIM, HEAD_DIM)
        return gain_rows[k : k + 1, pl.ds(start, HEAD_DIM)]

    for h in range(heads):
        start = pl.multiple_of(first_column + h * HEAD_DIM, HEAD_DIM)
        head_out[:, pl.ds(h * HEAD_DIM, HEAD_DIM)] = gain_rows[:, pl.ds(start, HEAD_DIM)]
    sender.arrived(down_all.at[you, place.x, place.z], swap.at[2], partner)
    down_task = plane_gather(place, sender, plane, down_all, down_all.shape[3] // 2)
    next(down_task)
    total = RingSum(place, sender, sum_sems, partial, *ring)
    ones = [one_hot_rows(k) for k in range(2)]

    def project(t, carry):
        a, b = t // 2, t % 2
        window = pl.ds(pl.multiple_of(b * tile, tile), tile)
        value = dot(x_all[a, b], columns_of(weight, pl.ds(0, 2 * inner)))
        row_sums = jnp.zeros((8, tile), F32)
        for k in range(2):
            for h in range(heads):
                column = k * inner + h * HEAD_DIM
                part = value[:, column : column + HEAD_DIM]
                raw[k, h, a, window, :] = part
                row_sums = row_sums + exact(ones[k], part * part, NT)
        sums[:, pl.ds(pl.multiple_of(t * tile, tile), tile)] = row_sums
        return carry

    def project_value(t, carry):
        a, b = t // 2, t % 2
        window = pl.ds(pl.multiple_of(b * tile, tile), tile)
        value = dot(x_all[a, b], columns_of(weight, pl.ds(2 * inner, inner))).astype(BF16)
        for h in range(heads):
            values[h, a, window, :] = value[:, h * HEAD_DIM : (h + 1) * HEAD_DIM]
        return carry

    lax.fori_loop(0, 4, project, 0)
    octet = Octet(place, sender, sums, slots, octet_sems)
    octet.send()
    sender.keep(raw, raw_out)
    lax.fori_loop(0, 4, project_value, 0)
    sender.keep(values, value_out)
    next(down_task)
    for copy in later:
        copy.wait()
    row_scales = lax.rsqrt(octet.total() / x_all.shape[3] + NORM_EPS)
    for b in range(2):
        for k in range(2):
            scale = exact(row_scales[:, b * block_rows : (b + 1) * block_rows], ones[k], TN)
            scales[k, b] = scale
            for h in range(heads):
                value = raw[k, h, b] * scale * head_gain(k, h)
                rot[k, h, b] = (value * cosine[b] + half_roll(value) * sine[b]).astype(BF16)
    sender.keep(scales, scale_out)
    sender.keep(rot, rot_out)
    next(down_task)

    def attention(b):
        for h in range(heads):
            key, value = rot[1, h, b], values[h, b]
            for i in range(2):
                window, count = pl.ds(i * tile, tile), (i + 1) * tile
                scores = dot(rot[0, h, b, window, :], key[:count], NT) * HEAD_DIM ** (-0.5)
                probs = softmax(masked(scores, starts[b, window, 0:1], i)).astype(BF16)
                attended[b, i, :, pl.ds(h * HEAD_DIM, HEAD_DIM)] = dot(probs, value[:count]).astype(BF16)

    attention(place.yl)
    out_weight = weight.at[:, :, :, :, pl.ds(3 * inner, inner)]
    ring_product(place, total, attended, out_weight, partial, (), lambda: attention(1 - place.yl))
    sender.keep(attended, attended_out)
    take_turns((down_task,))
    sender.keep(down_all, down_out)
    total.finish(proj_out)

    def mix(rows):
        value = proj_out[rows, :]
        mixed = hidden[rows, :].astype(F32) + value * norm_scale(value) * gain_rows[2:3, :]
        mixed_out[rows, :] = mixed
        low_out[rows, :] = mixed.astype(BF16)

    by_rows(proj_out.shape[0], mix)
    sender.arrived(pair_out.at[you], swap.at[3], partner)
    sender.finish()


def attention_forward(number, own, attn, down, gain, cosine, sine, starts):
    rows, width = own.shape
    inner = attn.shape[2] // 4
    heads = inner // HEAD_DIM
    tokens = (2, 2, 2 * rows)
    raw = (2, heads, 2, 4 * rows, HEAD_DIM)
    values, scales, attended = raw[1:], (2, 2, 4 * rows, HEAD_DIM), (*tokens, inner)
    weight = (2, RING, RING, *attn.shape[1:])
    piece = down.shape[1], down.shape[2] // 2
    down_all = (2, RING, RING, *piece)
    return call(
        attention_forward_kernel,
        number,
        (
            shape_of(rows, width, dtype=F32),
            shape_of(rows, width, dtype=F32),
            shape_of(rows, width),
            shape_of(8, width, dtype=F32),
            shape_of(8, inner, dtype=F32),
            shape_of(*tokens, width),
            shape_of(*weight),
            shape_of(*raw, dtype=F32),
            shape_of(*raw),
            shape_of(*values),
            shape_of(*scales, dtype=F32),
            shape_of(*attended),
            shape_of(*down_all),
            shape_of(2, *piece),
        ),
        [ANYWHERE] * 7,
        (IN_VMEM,) * 5 + (ANYWHERE,) * 9,
        [
            pltpu.VMEM((*tokens, width), BF16),
            pltpu.VMEM(weight, BF16),
            pltpu.VMEM(raw, F32),
            pltpu.VMEM(raw, BF16),
            pltpu.VMEM(values, BF16),
            pltpu.VMEM(scales, F32),
            pltpu.VMEM(attended, BF16),
            pltpu.VMEM((*tokens, width), BF16),
            pltpu.VMEM((8, 8 * rows), F32),
            pltpu.VMEM((8, 8, 8 * rows), F32),
            pltpu.VMEM(down_all, BF16),
            pltpu.VMEM((2, RING, RING, *gain.shape), F32),
            *[pltpu.VMEM(other.shape, other.dtype) for other in (cosine, sine, starts, own)],
            *ring_buffers(rows, width),
            dma_sems(208),
            dma_sems(RING, 4),
            dma_sems(4, 2 * PIECES),
            dma_sems(8),
            dma_sems(2, RING, RING, 3),
            dma_sems(2, RING, RING, 3),
            dma_sems(2, RING, RING, 3),
            dma_sems(4),
        ],
        (own, attn, down, gain, cosine, sine, starts),
    )


def attention_backward_kernel(
    own, weight, inputs, d_mixed_in, mlp_in, down, attended_in, raw_in, rot_in, values_in, scales_in,
    cosines_in, sines_in, starts_in, head_gains, token_gains, out, attn_out, gain_out, mlp_out, *refs
):
    (
        (shared, own_weight, attn_partial, gate_partial, up_partial, d_att, back, d_qkv, sums, slots, d_mixed),
        staged,
        (gain_partial, gain_rows, gain_slots, attn_done, gain_done, mlp_done),
        ring,
        buffers,
        late_buffers,
        gate_buffers,
        up_buffers,
        gain_buffers,
        (sends, gather_sems, sum_sems, octet_sems, gain_sems, swap, plane, late_plane, gain_plane, gate_plane),
        (up_plane,),
    ) = refs_of(refs, 11, 8, 6, 4, 5, 5, 5, 5, 5, 10, 1)
    attended, raw_all, rot, values, scales, cosines, sines, starts = staged
    d_all = x_all = partial = shared
    place = Place()
    sender = Sender(sends)
    _, heads, _, block_rows, _ = rot.shape
    width = d_qkv.shape[-1]
    inner = heads * HEAD_DIM
    rows = attn_partial.shape[3]
    block = RING * rows
    mlp_loads = [sender.keep_first(mlp_in.at[0], gate_partial), sender.keep_first(mlp_in.at[1], up_partial)]
    load = sender.keep_first(weight, own_weight)
    sources = (attended_in, raw_in, rot_in, values_in, scales_in, cosines_in, sines_in, starts_in)
    later = [sender.keep_first(source, target) for source, target in zip(sources, staged)]
    sender.keep(d_mixed_in, d_mixed)
    mixed_number = len(sender.open) - 1
    partner = {"yl": 1 - place.yl}
    me, you = place.yl, 1 - place.yl
    greet(near_devices(place) + [Octet.device(place, *peer) for peer in Octet.peers])
    gather = RingGather(place, sender, gather_sems, own, d_all)
    total = RingSum(place, sender, sum_sems, partial, *ring)
    gather.begin()
    sender.push(down.at[you], mlp_out.at[2, me], swap.at[3], partner)
    sender.keep(down.at[me], mlp_out.at[2, me])
    mlp = []
    for k, (sems, bufs, summand) in enumerate(
        ((gate_plane, gate_buffers, gate_partial), (up_plane, up_buffers, up_partial))
    ):
        mlp_loads[k].wait()
        task = plane_scatter(place, sender, sems, summand, mlp_done.at[k], rows // 2, bufs)
        next(task)
        mlp.append(task)
    gate_task, up_task = mlp
    load.wait()
    gain_partial[...] = jnp.zeros_like(gain_partial)
    gain_rows[...] = jnp.zeros_like(gain_rows)
    for k in range(2 * RING):
        for z in range(RING):
            gain_partial[k // RING, k % RING, z, 2:4, :] = token_gains[0:2, k * block : (k + 1) * block]

    def compute(dy):
        gather.ready(dy)
        y = place.shift("y", dy)
        at = (y % 2, y // 2)
        d_att[at] = dot(d_all[at], own_weight[:, pl.ds(width, inner)]).astype(BF16)

    tile = block_rows // 2
    score_factor = HEAD_DIM ** (-0.5)
    ones = [one_hot_rows(k) for k in range(2)]

    def attention(b, between=lambda: None):
        row_sums = jnp.zeros((8, block_rows), F32)
        cosine, sine = cosines[b], sines[b]
        for h in range(heads):
            lanes = pl.ds(h * HEAD_DIM, HEAD_DIM)
            key, value = rot[1, h, b], values[h, b]
            d_query, d_key, d_value = [], [None, None], [None, None]
            for i in range(2):
                window = pl.ds(i * tile, tile)
                query, upstream = rot[0, h, b, window, :], d_att[b, i, :, lanes]
                count = (i + 1) * tile
                scores = dot(query, key[:count], NT) * score_factor
                probs = softmax(masked(scores, starts[b, window, 0:1], i))
                d_probs = dot(upstream, value[:count], NT)
                row_dot = jnp.sum(probs * d_probs, axis=-1, keepdims=True)
                d_scores = (probs * (d_probs - row_dot) * score_factor).astype(BF16)
                probs = probs.astype(BF16)
                d_query.append(dot(d_scores, key[:count]))
                for j in range(i + 1):
                    part = slice(j * tile, (j + 1) * tile)
                    for sums_of, left, right in ((d_key, d_scores, query), (d_value, probs, upstream)):
                        term = dot(left[:, part], right, TN)
                        sums_of[j] = term if sums_of[j] is None else sums_of[j] + term
            for i in range(2):
                d_qkv[b, i, :, pl.ds(2 * inner + h * HEAD_DIM, HEAD_DIM)] = d_value[i].astype(BF16)
            for k, parts in enumerate((d_query, d_key)):
                turned = jnp.concatenate(parts, axis=0)
                turned = turned * cosine - half_roll(turned) * sine
                raw = raw_all[k, h, b]
                gain_rows[k : k + 1, lanes] += jnp.sum(turned * raw * scales[k, b], axis=0, keepdims=True)
                turned = turned * head_gains[k : k + 1, lanes]
                back[k, h, b] = turned
                row_sums = row_sums + exact(ones[k], turned * raw, NT)
            if h == 0:
                between()
        sums[:, pl.ds(pl.multiple_of(b * block_rows, block_rows), block_rows)] = row_sums

    compute(0)
    gather.relay()
    compute(1)
    compute(-1)
    for copy in later:
        copy.wait()
    attention(1 - place.yl, gather.relay_far)
    next(gate_task)
    compute(2)
    attention(place.yl)
    octet = Octet(place, sender, sums, slots, octet_sems)
    octet.send()
    next(up_task)
    first = (place.yh * 2 + place.c) * 2 + place.yl
    for z in range(RING):
        gain_partial[first // RING, first % RING, z, 0:2, :] = gain_rows[0:2, :]
    gains = plane_scatter(place, sender, gain_plane, gain_partial, gain_done, gain_done.shape[1], gain_buffers)
    next(gains)

    def flat_tokens(ref, columns=slice(None)):
        value = ref[:, :, :, columns]
        return value.reshape(-1, value.shape[-1])

    def weight_grads(left_ref, right, start):
        size = right.shape[1]
        for i in range(2 * RING):
            left = flat_tokens(left_ref, pl.ds(i * block, block))
            value = dot(left, right, TN).astype(BF16)
            attn_partial[i // RING, i % RING, :, :, pl.ds(start, size)] = value.reshape(RING, rows, size)

    weight_grads(d_all, flat_tokens(attended), width)
    sender.settle(gather.forwarded)
    load = sender.keep_first(inputs, x_all)
    next(gate_task)
    load.wait()

    def attn_scatter(columns, sems, bufs):
        task = plane_scatter(
            place,
            sender,
            sems,
            attn_partial.at[:, :, :, :, columns],
            attn_done.at[:, :, columns],
            rows // 2,
            bufs,
        )
        next(task)
        return task

    weight_grads(x_all, flat_tokens(d_qkv, pl.ds(2 * inner, inner)), 2 * inner)
    early = attn_scatter(pl.ds(2 * inner, 2 * inner), plane, buffers)
    row_sums = octet.total()
    for b in range(2):
        for k in range(2):
            column = exact(row_sums[:, b * block_rows : (b + 1) * block_rows], ones[k], TN)
            for h in range(heads):
                scale = scales[k, b]
                value = scale * back[k, h, b] - raw_all[k, h, b] * (scale * scale * scale * column / own.shape[1])
                value = value.astype(BF16)
                for i in range(2):
                    d_qkv[b, i, :, pl.ds(k * inner + h * HEAD_DIM, HEAD_DIM)] = value[
                        i * tile : (i + 1) * tile
                    ]
    weight_grads(x_all, flat_tokens(d_qkv, pl.ds(0, 2 * inner)), 0)
    late = attn_scatter(pl.ds(0, 2 * inner), late_plane, late_buffers)
    next(gate_task)
    next(up_task)
    next(early)
    ring_product(
        place, total, d_qkv, own_weight.at[:, pl.ds(0, width)], partial, (late, up_task, gains)
    )
    take_turns((gate_task, up_task))
    for k in range(2):
        sender.push(mlp_done.at[k, you], mlp_out.at[k, me], swap.at[1 + k], partner)
        sender.keep(mlp_done.at[k, me], mlp_out.at[k, me])
    take_turns((early, gains, late))
    sender.push(attn_done.at[you], attn_out.at[me], swap.at[0], partner)
    sender.keep(attn_done.at[me], attn_out.at[me])
    everyone = Octet(place, sender, gain_done, gain_slots, gain_sems)
    everyone.send()
    sender.settle([mixed_number])
    total.finish(out, d_mixed)
    gain_out[...] = everyone.total()
    sender.arrived(attn_out.at[you], swap.at[0], partner)
    for k in range(3):
        sender.arrived(mlp_out.at[k, you], swap.at[1 + k], partner)
    sender.finish()


def attention_backward(number, own, weight, inputs, d_mixed, mlp_partial, down, attended, *others):
    rows, width = own.shape
    tokens = (2, 2, 2 * rows)
    inner = attended.shape[3]
    heads = inner // HEAD_DIM
    shard = width // 32, weight.shape[1]
    gain_tile = (8, 4 * shard[0])
    return call(
        attention_backward_kernel,
        number,
        (
            shape_of(rows, width, dtype=F32),
            shape_of(2, *shard),
            shape_of(2, *gain_tile, dtype=F32),
            shape_of(3, 2, *shard),
        ),
        [ANYWHERE] * 14 + [IN_VMEM] * 2,
        (IN_VMEM,) * 4,
        [
            pltpu.VMEM((*tokens, width), BF16),
            pltpu.VMEM(weight.shape, BF16),
            pltpu.VMEM((2, RING, RING, *shard), BF16),
            pltpu.VMEM(mlp_partial.shape[1:], BF16),
            pltpu.VMEM(mlp_partial.shape[1:], BF16),
            pltpu.VMEM((*tokens, inner), BF16),
            pltpu.VMEM((2, heads, 2, 4 * rows, HEAD_DIM), F32),
            pltpu.VMEM((*tokens, 3 * inner), BF16),
            pltpu.VMEM((8, 8 * rows), F32),
            pltpu.VMEM((8, 8, 8 * rows), F32),
            pltpu.VMEM((rows, width), F32),
            *[pltpu.VMEM(other.shape, other.dtype) for other in (attended, *others[:7])],
            pltpu.VMEM((2, RING, RING, *gain_tile), F32),
            pltpu.VMEM((8, inner), F32),
            pltpu.VMEM((8, 2, *gain_tile), F32),
            pltpu.VMEM((2, *shard), BF16),
            pltpu.VMEM((2, *gain_tile), F32),
            pltpu.VMEM((2, 2, *shard), BF16),
            *ring_buffers(rows, width),
            *scatter_buffers(shard[0], shard[1] // 2, BF16),
            *scatter_buffers(shard[0], shard[1] // 2, BF16),
            *scatter_buffers(*shard, BF16),
            *scatter_buffers(*shard, BF16),
            *scatter_buffers(*gain_tile, F32),
            dma_sems(224),
            dma_sems(RING, 4),
            dma_sems(4, 2 * PIECES),
            dma_sems(8),
            dma_sems(8),
            dma_sems(5),
            dma_sems(2, 12),
            dma_sems(2, 12),
            dma_sems(2, 12),
            dma_sems(2, 12),
            dma_sems(2, 12),
        ],
        (own, weight, inputs, d_mixed, mlp_partial, down, attended, *others),
    )


def norm_scale(values):
    return lax.rsqrt(jnp.mean(values * values, axis=-1, keepdims=True) + NORM_EPS)


def norm_back(upstream, values, scales, gain_row):
    scaled_grad = upstream * gain_row
    return scales * scaled_grad - values * scales**3 * jnp.mean(
        scaled_grad * values, axis=-1, keepdims=True
    )


def doc_layout(lengths, group_size):
    positions = jnp.arange(group_size, dtype=jnp.int32)
    doc_ends = jnp.cumsum(lengths)
    passed = (positions[:, None] >= doc_ends[None, :]).astype(jnp.int32)
    segment = jnp.sum(passed, axis=-1)
    begins = jnp.sum(passed * lengths[None, :], axis=-1)
    return (segment, positions - begins)


def rope_tables(offsets):
    frequency = ROPE_BASE ** (-jnp.arange(0, HEAD_DIM, 2).astype(jnp.float32) / HEAD_DIM)
    angles = offsets.astype(jnp.float32)[:, None] * frequency[None, :]
    cosine, sine = jnp.cos(angles), jnp.sin(angles)
    return (
        jnp.concatenate([cosine, cosine], axis=-1),
        jnp.concatenate([sine, sine], axis=-1),
    )


def half_turn(values):
    middle = values.shape[-1] // 2
    return jnp.concatenate([-values[..., middle:], values[..., :middle]], axis=-1)


def rotate(values, cosine_table, sine_table):
    return values * cosine_table + half_turn(values) * sine_table


def unrotate(values, cosine_table, sine_table):
    return values * cosine_table - half_turn(values) * sine_table


def product(left, right):
    return jnp.dot(left, right, preferred_element_type=F32)


def row_product(left, right):
    return lax.dot_general(left, right, (((1,), (1,)), ((), ())), preferred_element_type=F32)


def col_product(left, right):
    return lax.dot_general(left, right, (((0,), (0,)), ((), ())), preferred_element_type=F32)


def adam_update(weights_old, first_old, second_old, gradient, rate, decay):
    first_new = BETA_ONE * first_old + (1.0 - BETA_ONE) * gradient
    second_new = BETA_TWO * second_old + (1.0 - BETA_TWO) * gradient * gradient
    ratio = (
        first_new
        / (1.0 - BETA_ONE**STEP)
        / (jnp.sqrt(second_new / (1.0 - BETA_TWO**STEP)) + ADAM_EPS)
    )
    return (first_new, second_new, weights_old - rate * (ratio + decay * weights_old))


def mlp_adam_kernel(weights, first, second, sums, grad_out, first_out, second_out, new_out):
    half = sums.shape[3]
    for h in range(2):
        part = slice(None), slice(None), slice(h * half, (h + 1) * half)
        gradient = sums[:, h].astype(F32)
        grad_out[part] = gradient
        first_out[part], second_out[part], new_out[part] = adam_update(
            weights[part], first[part], second[part], gradient, WEIGHT_RATE, WEIGHT_DECAY
        )


def mlp_adam(weights, first, second, sums):
    count, rows, columns = weights.shape
    state = pl.BlockSpec((1, rows, columns), lambda m: (m, 0, 0))
    return pl.pallas_call(
        mlp_adam_kernel,
        out_shape=(shape_of(*weights.shape, dtype=F32),) * 4,
        grid=(count,),
        in_specs=[state] * 3 + [pl.BlockSpec((1, *sums.shape[1:]), lambda m: (m, 0, 0, 0))],
        out_specs=(state,) * 4,
        compiler_params=pltpu.CompilerParams(vmem_limit_bytes=VMEM_LIMIT),
    )(weights, first, second, sums)


def attn_adam_kernel(weights, first, second, sums, grad_out, first_out, second_out, new_out):
    inner = weights.shape[2]
    for m in range(weights.shape[0]):
        gradient = sums[0, :, m * inner : (m + 1) * inner].astype(F32)
        grad_out[m] = gradient
        first_out[m], second_out[m], new_out[m] = adam_update(
            weights[m], first[m], second[m], gradient, WEIGHT_RATE, WEIGHT_DECAY
        )


def attn_adam(weights, first, second, sums):
    count, rows, columns = weights.shape
    state = pl.BlockSpec((count, rows, columns // 2), lambda h: (0, 0, h))
    return pl.pallas_call(
        attn_adam_kernel,
        out_shape=(shape_of(*weights.shape, dtype=F32),) * 4,
        grid=(2,),
        in_specs=[state] * 3 + [pl.BlockSpec((1, *sums.shape[1:]), lambda h: (h, 0, 0))],
        out_specs=(state,) * 4,
        compiler_params=pltpu.CompilerParams(vmem_limit_bytes=VMEM_LIMIT),
    )(weights, first, second, sums)


def body(
    hidden_in,
    cotangent,
    doc_lengths,
    attn_weights,
    attn_first,
    attn_second,
    mlp_weights,
    mlp_first,
    mlp_second,
    gains,
    gain_first,
    gain_second,
):
    row_count, model_width = hidden_in.shape
    shard_rows = attn_weights.shape[1]
    heads_width = attn_weights.shape[2] // 2
    hidden_width = mlp_weights.shape[2] // 2
    token_count = 8 * row_count
    block_rows = token_count // 2
    head_count = heads_width // HEAD_DIM
    score_factor = HEAD_DIM ** (-0.5)
    yl, yh, core = (lax.axis_index(a) for a in ("yl", "yh", "c"))

    attn_halves = (
        attn_weights.astype(BF16)
        .reshape(4, shard_rows, 2, heads_width)
        .transpose(2, 1, 0, 3)
        .reshape(2, shard_rows, 4 * heads_width)
    )
    left, right = mlp_weights[:2, :, :hidden_width], mlp_weights[:2, :, hidden_width:]
    mine = jnp.where(yl == 0, left, right).astype(BF16)
    yours = jnp.where(yl == 0, right, left).astype(BF16)
    arrived = lax.ppermute(yours, "yl", [(0, 1), (1, 0)])
    down_halves = mlp_weights[2].astype(BF16).reshape(shard_rows, 2, hidden_width).transpose(1, 0, 2)
    gain_low = lax.reduce_precision(gains, 8, 7)
    odd = lax.axis_index("z") % 2
    gain_tile = jnp.concatenate([jnp.where(odd == 0, gain_low, 0.0), jnp.where(odd == 1, gain_low, 0.0)], axis=1)
    gain_tile = jnp.pad(gain_tile, ((0, 4), (0, 0)))
    theirs = lax.ppermute(doc_lengths, "yl", [(0, 1), (1, 0)])
    lengths = jnp.where(yl == 0, jnp.stack([doc_lengths[0], theirs[0]]), jnp.stack([theirs[0], doc_lengths[0]]))
    _, offsets = jax.vmap(lambda one: doc_layout(one, block_rows))(lengths)
    cosine_table, sine_table = rope_tables(offsets.reshape(-1))
    sine_table = sine_table * jnp.where(jnp.arange(HEAD_DIM) < HEAD_DIM // 2, -1.0, 1.0)
    cosine_table = cosine_table.reshape(2, block_rows, HEAD_DIM)
    sine_table = sine_table.reshape(2, block_rows, HEAD_DIM)
    starts = jnp.broadcast_to((jnp.arange(block_rows) - offsets)[:, :, None], (2, block_rows, HEAD_DIM))

    arrived, cosine_table, sine_table, starts, attn_halves, gain_tile, down_halves = lax.optimization_barrier(
        (arrived, cosine_table, sine_table, starts, attn_halves, gain_tile, down_halves)
    )
    pair = jnp.stack(
        [jnp.where(yl == 0, mine, arrived), jnp.where(yl == 0, arrived, mine)], axis=1
    )
    gate_up = lax.all_gather(pair.reshape(-1, hidden_width), ("x", "z"), tiled=True)
    gate_up = gate_up.reshape(RING, RING, 2, 2, shard_rows, hidden_width)

    (
        attn_proj, mixed, mixed_low, gain_full, head_gains, every_input, attn_all, raw, rotated, values,
        head_scales, attended, down_half, down_pair,
    ) = attention_forward(
        1, hidden_in, attn_halves, down_halves, gain_tile, cosine_table, sine_table, starts
    )
    attn_all = flat(attn_all)
    hidden_out, d_mixed, d_proj, token_gains, mlp_partial, down_sum = mlp(
        2, mixed_low, gate_up, down_half, down_pair, mixed, cotangent, attn_proj, gain_full
    )
    input_grad, attn_sum, gain_sum, mlp_sum = attention_backward(
        3,
        d_proj,
        attn_all,
        every_input,
        d_mixed,
        mlp_partial,
        down_sum,
        attended,
        raw,
        rotated,
        values,
        head_scales,
        cosine_table,
        sine_table,
        starts,
        head_gains,
        token_gains,
    )

    gain_sum = lax.dynamic_index_in_dim(gain_sum, yl, 0, keepdims=False)[:4]
    gain_grad = lax.dynamic_slice_in_dim(gain_sum, lax.axis_index("z") * shard_rows, shard_rows, axis=1)
    attn_grad, attn_first_new, attn_second_new, attn_new = attn_adam(
        attn_weights, attn_first, attn_second, attn_sum
    )
    mlp_grad, mlp_first_new, mlp_second_new, mlp_new = mlp_adam(
        mlp_weights, mlp_first, mlp_second, mlp_sum
    )
    gain_first_new, gain_second_new, gain_new = adam_update(
        gains, gain_first, gain_second, gain_grad, GAIN_RATE, 0.0
    )
    return (
        hidden_out,
        input_grad,
        attn_grad,
        attn_first_new,
        attn_second_new,
        attn_new,
        mlp_grad,
        mlp_first_new,
        mlp_second_new,
        mlp_new,
        gain_grad,
        gain_first_new,
        gain_second_new,
        gain_new,
    )


def solution(mesh):
    split = Mesh(mesh.devices.reshape(2, 4, 4, 2, 2), EVERY)
    tokens, shards, rows = P(EVERY, None), P(None, DP, TENSOR), P(None, DP)
    return jax.shard_map(
        body,
        mesh=split,
        in_specs=(tokens, tokens, P(DP, None), *[shards] * 6, *[rows] * 3),
        out_specs=(tokens, tokens, *[shards] * 8, *[rows] * 4),
        check_vma=False,
    )
```
